32 devices in a mesh: seq: 16 (over z, y, x), rep: 2 (over core).
Axes of the slice: x: 2, y: 2, z: 4, core: 2. Of those that a mesh axis runs over, the one named last changes fastest.
Arguments:
- tokens: bfloat16 [2, 32768, 768], P('rep', 'seq'), may hold values from -8.5 to 8.5
- cotangent: bfloat16 [2, 32768, 768], P('rep', 'seq'), may hold values from -6 to 6
- attn_w: float32 [4, 768, 768], P(None, ('seq', 'rep')), may hold values from -0.21650635 to 0.21650635
- w_up: float32 [768, 3072], P(('seq', 'rep')), may hold values from -0.21875 to 0.21875
- w_down: float32 [3072, 768], P(('seq', 'rep')), may hold values from -0.109375 to 0.109375
- vectors: float32 [768, 35], P(('seq', 'rep')), may hold values from -1.5 to 1.5, as said below
- attn_m: float32 [4, 768, 768], P(None, ('seq', 'rep')), may hold values from -46.08 to 46.08
- attn_v: float32 [4, 768, 768], P(None, ('seq', 'rep')), may hold values from 1.31072 to 52.4288
- up_m: float32 [768, 3072], P(('seq', 'rep')), may hold values from -80 to 80
- up_v: float32 [768, 3072], P(('seq', 'rep')), may hold values from 13.1072 to 65.536
- down_m: float32 [3072, 768], P(('seq', 'rep')), may hold values from -64 to 64
- down_v: float32 [3072, 768], P(('seq', 'rep')), may hold values from 9.8304 to 52.4288
- vec_m: float32 [768, 35], P(('seq', 'rep')), may hold values from -160 to 160
- vec_v: float32 [768, 35], P(('seq', 'rep')), may hold values from 32.768 to 262.144
Outputs:
- output: bfloat16 [2, 32768, 768], P('rep', 'seq')
- input_grad: bfloat16 [2, 32768, 768], P('rep', 'seq')
- attn_new: float32 [4, 768, 768], P(None, ('seq', 'rep'))
- attn_m_new: float32 [4, 768, 768], P(None, ('seq', 'rep'))
- attn_v_new: float32 [4, 768, 768], P(None, ('seq', 'rep'))
- up_new: float32 [768, 3072], P(('seq', 'rep'))
- up_m_new: float32 [768, 3072], P(('seq', 'rep'))
- up_v_new: float32 [768, 3072], P(('seq', 'rep'))
- down_new: float32 [3072, 768], P(('seq', 'rep'))
- down_m_new: float32 [3072, 768], P(('seq', 'rep'))
- down_v_new: float32 [3072, 768], P(('seq', 'rep'))
- vec_new: float32 [768, 35], P(('seq', 'rep'))
- vec_m_new: float32 [768, 35], P(('seq', 'rep'))
- vec_v_new: float32 [768, 35], P(('seq', 'rep'))
The draws below stay inside these ranges and needn't reach their ends.
Inputs may be any that keep to these rules, and one draw needn't show every extreme that they name: `vectors`: columns 0 and 1 lie near 1; the other 33 columns are of order 1 / sqrt(33).
All inputs are finite; a program needn't handle non-finite values.
Results may differ from the reference program's by a relative error of at most 0.012.
Values may be sent and summed in bfloat16 or wider, within the bound.
A program may use at most 320 MiB of HBM per device.

```python
import math
import jax
import jax.numpy as jnp
from jax import lax

MODEL_DIM = 768
H = 12
HD = 64
FF = 3072
M = 64
KC = 33
NSITER = 6
STEP = 10
NTOK = 32768
ITEM_TOKENS = 32768
SEGLEN = 512
ALLTOK = 65536
N_REP = 2


def draw_vectors(key, part):
    key = jax.random.fold_in(key, 11)
    gain_key, tap_key = jax.random.split(key)
    gain_cols = 1.0 + 0.1 * jnp.clip(jax.random.normal(gain_key, (MODEL_DIM, 2), jnp.float32), -3.5, 3.5)
    tap_values = jnp.clip(jax.random.normal(tap_key, (MODEL_DIM, KC), jnp.float32), -4.0, 4.0) / KC ** 0.5
    return jnp.concatenate([gain_cols, tap_values], axis=1)


def draw_tokens(key, part):
    key = jax.random.fold_in(key, 12)
    shared_key, scale_key, noise_key = jax.random.split(key, 3)
    segments = N_REP * NTOK // SEGLEN
    shared = jnp.clip(jax.random.normal(shared_key, (segments, 1, MODEL_DIM), jnp.float32), -4.0, 4.0)
    token_scale = jax.random.uniform(scale_key, (segments, SEGLEN, 1), jnp.float32, 0.5, 1.5)
    noise = 0.6 * jnp.clip(jax.random.normal(noise_key, (segments, SEGLEN, MODEL_DIM), jnp.float32), -4.0, 4.0)
    values = shared * token_scale + noise
    return values.reshape(N_REP, NTOK, MODEL_DIM).astype(jnp.bfloat16)


def draw_attn_w(key, part):
    key = jax.random.fold_in(key, 13)
    block_scale = jnp.array([1.4, 1.4, 1.0, 1.0], jnp.float32)[:, None, None] / MODEL_DIM ** 0.5
    base = jnp.clip(jax.random.normal(key, (4, MODEL_DIM, MODEL_DIM), jnp.float32), -4.0, 4.0)
    return base * block_scale


def draw_attn_m(key, part):
    key = jax.random.fold_in(key, 14)
    block_scale = jnp.array([0.015, 0.015, 0.03, 0.03], jnp.float32)[:, None, None] * ALLTOK ** 0.5
    base = jnp.clip(jax.random.normal(key, (4, MODEL_DIM, MODEL_DIM), jnp.float32), -6.0, 6.0)
    return base * block_scale


def draw_attn_v(key, part):
    key = jax.random.fold_in(key, 15)
    low_end = jnp.log(jnp.array([2e-05, 2e-05, 2e-05, 2e-05], jnp.float32))[:, None, None]
    high_end = jnp.log(jnp.array([0.0003, 0.0003, 0.0008, 0.0008], jnp.float32))[:, None, None]
    fraction = jax.random.uniform(key, (4, MODEL_DIM, MODEL_DIM), jnp.float32, 0.0, 1.0)
    return jnp.exp(low_end + fraction * (high_end - low_end)) * ALLTOK


def shard_levels(stream_key, dims, shards, least, top_value):
    factor_of, own = 1.0, jax.random.fold_in(stream_key, 6)
    for axis_at, parts in shards:
        heights = jnp.exp(jax.random.uniform(jax.random.fold_in(own, axis_at), (parts,), jnp.float32, least / len(shards), top_value / len(shards)))
        factor_of = factor_of * jnp.repeat(heights, dims[axis_at] // parts).reshape([-1 if axis == axis_at else 1 for axis in range(len(dims))])
    return factor_of


def centred(rng, dims, scale, reach, cuts=(), kind=jnp.bfloat16):
    loudness = shard_levels(rng, dims, cuts, -0.22, 0.18) if cuts else 1.0
    values = jax.random.normal(rng, dims, jnp.float32) * scale * loudness
    return jnp.minimum(jnp.maximum(values, -reach), reach).astype(kind)


def setup_inputs(seed: int = 0) -> dict:
    key_of = jax.random.split(jax.random.key(seed), 15)
    tokens = draw_tokens(jax.random.fold_in(key_of[14], 71), 0)
    cotangent = centred(key_of[1], (N_REP, NTOK, MODEL_DIM), 1.0, 6.0, ((0, 2), (1, 16)))
    attn_w = draw_attn_w(jax.random.fold_in(key_of[14], 71), 0)
    w_up = centred(key_of[3], (MODEL_DIM, FF), MODEL_DIM ** -0.5, 0.21875, ((0, 32),), jnp.float32)
    w_down = centred(key_of[4], (FF, MODEL_DIM), FF ** -0.5, 0.109375, ((0, 32),), jnp.float32)
    vectors = draw_vectors(jax.random.fold_in(key_of[14], 71), 0)
    attn_m = draw_attn_m(jax.random.fold_in(key_of[14], 71), 0)
    attn_v = draw_attn_v(jax.random.fold_in(key_of[14], 71), 0)
    up_m = centred(key_of[8], (MODEL_DIM, FF), (0.05 * ALLTOK ** 0.5), 80.0, ((0, 32),), jnp.float32)
    up_v = jnp.clip(jnp.exp(math.log(65.536) - 1.609438 * jax.random.uniform(key_of[9], (MODEL_DIM, FF), jnp.float32) ** shard_levels(key_of[9], (MODEL_DIM, FF), ((0, 32),), -0.2, 0.2)), 13.1072, 65.536)
    down_m = centred(key_of[10], (FF, MODEL_DIM), (0.04 * ALLTOK ** 0.5), 64.0, ((0, 32),), jnp.float32)
    down_v = jnp.clip(jnp.exp(math.log(52.4288) - 1.67397636 * jax.random.uniform(key_of[11], (FF, MODEL_DIM), jnp.float32) ** shard_levels(key_of[11], (FF, MODEL_DIM), ((0, 32),), -0.2, 0.2)), 9.8304, 52.4288)
    vec_m = centred(key_of[12], (MODEL_DIM, 2 + KC), (0.1 * ALLTOK ** 0.5), 160.0, ((0, 32),), jnp.float32)
    vec_v = jnp.clip(jnp.exp(math.log(262.144) - 2.0794415 * jax.random.uniform(key_of[13], (MODEL_DIM, 2 + KC), jnp.float32) ** shard_levels(key_of[13], (MODEL_DIM, 2 + KC), ((0, 32),), -0.2, 0.2)), 32.768, 262.144)
    return {"tokens": tokens, "cotangent": cotangent, "attn_w": attn_w, "w_up": w_up, "w_down": w_down, "vectors": vectors, "attn_m": attn_m, "attn_v": attn_v, "up_m": up_m, "up_v": up_v, "down_m": down_m, "down_v": down_v, "vec_m": vec_m, "vec_v": vec_v}


EPS_NORM = 1e-05
BETA_ONE = 0.9
BETA_TWO = 0.999
ADAM_EPS = 1e-08
LEARN_RATE = 0.03
VECTOR_RATE = 0.15
DECAY_RATE = 0.1

@jax.custom_vjp
def low(v):
    return lax.optimization_barrier(v.astype(jnp.bfloat16)).astype(jnp.float32)

@jax.custom_vjp
def low_back(v):
    return v

def low_keep(v):
    return (low(v), None)

def low_pass(kept, grad):
    return (grad,)

def back_keep(v):
    return (v, None)

def back_low(kept, grad):
    return (low(grad),)
low.defvjp(low_keep, low_pass)
low_back.defvjp(back_keep, back_low)

def matmul(left_side, right_side):
    return jnp.dot(left_side, right_side, precision=lax.Precision.HIGHEST)

def layer_norm(values, gain_vec):
    center = values - lax.optimization_barrier(jnp.mean(values, axis=-1, keepdims=True))
    spread = lax.optimization_barrier(jnp.mean(center * center, axis=-1, keepdims=True))
    return center * lax.rsqrt(spread + EPS_NORM) * gain_vec

def pseudo_inverse(matrix):
    column_sums = lax.optimization_barrier(jnp.sum(matrix, axis=1))
    bound_value = jnp.sqrt(lax.optimization_barrier(jnp.sum(column_sums * column_sums, axis=-1)))
    iterate = jnp.swapaxes(matrix, 1, 2) / bound_value[:, None, None]
    identity = jnp.eye(matrix.shape[-1], dtype=matrix.dtype)
    for sweep_index in range(NSITER):
        product = jnp.einsum('hij,hjk->hik', matrix, iterate, precision=lax.Precision.HIGHEST)
        inner_term = 7.0 * identity - product
        inner_term = 15.0 * identity - jnp.einsum('hij,hjk->hik', product, inner_term, precision=lax.Precision.HIGHEST)
        inner_term = 13.0 * identity - jnp.einsum('hij,hjk->hik', product, inner_term, precision=lax.Precision.HIGHEST)
        iterate = 0.25 * jnp.einsum('hij,hjk->hik', iterate, inner_term, precision=lax.Precision.HIGHEST)
    return iterate

def sequence_layer(params, sequence):
    attn_w, w_up, w_down, vectors = params
    gain_one = vectors[:, 0]
    gain_two = vectors[:, 1]
    kernel = vectors[:, 2:]
    qk_scale = HD ** (-0.25)
    radius = (KC - 1) // 2
    highest_precision = lax.Precision.HIGHEST
    normed = low(layer_norm(sequence, gain_one))
    queries = low(low_back(matmul(normed, attn_w[0]) * qk_scale))
    keys_all = low(low_back(matmul(normed, attn_w[1]) * qk_scale))
    values = low(low_back(matmul(normed, attn_w[2])))
    marks_q = low(lax.optimization_barrier(jnp.mean(queries.reshape(M, SEGLEN, MODEL_DIM), axis=1)))
    marks_k = low(lax.optimization_barrier(jnp.mean(keys_all.reshape(M, SEGLEN, MODEL_DIM), axis=1)))
    query_heads = queries.reshape(ITEM_TOKENS, H, HD)
    key_heads = keys_all.reshape(ITEM_TOKENS, H, HD)
    value_heads = values.reshape(ITEM_TOKENS, H, HD)
    landmark_query_heads = marks_q.reshape(M, H, HD)
    landmark_key_heads = marks_k.reshape(M, H, HD)
    score_matrix = low_back(jnp.einsum('ijo,njo->ijn', query_heads, landmark_key_heads, precision=highest_precision))
    weights_single = low(jax.nn.softmax(score_matrix, axis=-1))
    kernel_weights = jax.nn.softmax(jnp.einsum('fwz,uwz->wfu', landmark_query_heads, landmark_key_heads, precision=highest_precision), axis=-1)
    inverse_matrix = pseudo_inverse(kernel_weights)
    second_score_matrix = low_back(jnp.einsum('czf,qzf->zcq', landmark_query_heads, key_heads, precision=highest_precision))
    exponent_values = jnp.exp(second_score_matrix)
    summed_rows = jnp.einsum('iuo,oiz->iuz', low(exponent_values), value_heads, precision=highest_precision)
    totals = lax.optimization_barrier(jnp.sum(exponent_values, axis=-1))
    value_mixture = summed_rows / totals[..., None]
    landmark_output = low(jnp.einsum('zgw,zwx->zgx', inverse_matrix, value_mixture, precision=highest_precision))
    attended_rows = jnp.einsum('loy,oyv->lov', weights_single, landmark_output, precision=highest_precision).reshape(ITEM_TOKENS, MODEL_DIM)
    padded = jnp.pad(values, ((radius, radius), (0, 0)))
    convolved = jnp.zeros((ITEM_TOKENS, MODEL_DIM), jnp.float32)
    for tap_index in range(KC):
        convolved = convolved + kernel[:, tap_index] * padded[tap_index:tap_index + ITEM_TOKENS]
    mixture = low(low_back(attended_rows + convolved))
    residual = sequence + low_back(matmul(mixture, attn_w[3]))
    normed_two = low(layer_norm(residual, gain_two))
    hidden = low(jax.nn.gelu(low_back(matmul(normed_two, w_up)), approximate=False))
    return residual + matmul(hidden, w_down)

def forward(attn_w, w_up, w_down, vectors, inputs):
    params = (low(attn_w), low(w_up), low(w_down), low(vectors))
    sequences = inputs.reshape(-1, ITEM_TOKENS, MODEL_DIM)
    outputs = lax.map(jax.checkpoint(lambda seq_item: sequence_layer(params, seq_item)), sequences)
    return outputs.reshape(inputs.shape)

def adam_step(weight, grad_vec, moment, second, rate_value):
    moment_new = BETA_ONE * moment + (1.0 - BETA_ONE) * grad_vec
    second_new = BETA_TWO * second + (1.0 - BETA_TWO) * grad_vec * grad_vec
    first_hat = moment_new / (1.0 - BETA_ONE ** STEP)
    second_hat = second_new / (1.0 - BETA_TWO ** STEP)
    weight_new = weight - rate_value * (first_hat / (jnp.sqrt(second_hat) + ADAM_EPS) + DECAY_RATE * weight)
    return (weight_new, moment_new, second_new)

def reference(tokens, cotangent, attn_w, w_up, w_down, vectors, attn_m, attn_v, up_m, up_v, down_m, down_v, vec_m, vec_v):
    inputs = tokens.astype(jnp.float32)
    outputs, pullback = jax.vjp(forward, attn_w, w_up, w_down, vectors, inputs)
    grads = pullback(cotangent.astype(jnp.float32))
    attn_new, attn_m_new, attn_v_new = adam_step(attn_w, grads[0], attn_m, attn_v, LEARN_RATE)
    up_new, up_m_new, up_v_new = adam_step(w_up, grads[1], up_m, up_v, LEARN_RATE)
    down_new, down_m_new, down_v_new = adam_step(w_down, grads[2], down_m, down_v, LEARN_RATE)
    vec_new, vec_m_new, vec_v_new = adam_step(vectors, grads[3], vec_m, vec_v, VECTOR_RATE)
    return (outputs.astype(jnp.bfloat16), grads[4].astype(jnp.bfloat16), attn_new, attn_m_new, attn_v_new, up_new, up_m_new, up_v_new, down_new, down_m_new, down_v_new, vec_new, vec_m_new, vec_v_new)
```

```python
import functools

import jax
import jax.numpy as jnp
from jax import lax
from jax.experimental import pallas as pl
from jax.experimental.pallas import tpu as pltpu
from jax.sharding import PartitionSpec as P

H = 12
HD = 64
M = 64
KC = 33
NSITER = 6
STEP = 10
EPS_NORM = 1e-05
BETA_ONE = 0.9
BETA_TWO = 0.999
ADAM_EPS = 1e-08
LEARN_RATE = 0.03
VECTOR_RATE = 0.15
DECAY_RATE = 0.1

F32 = jnp.float32
BF16 = jnp.bfloat16
GROUP = 256
NG = 3
RAD = 16
QK_SCALE = HD ** (-0.25)
HI = lax.Precision.HIGHEST
VMEM_LIMIT = 58 * 1024 * 1024


def dot(a, b, precision=None):
    return lax.dot_general(a, b, (((1,), (0,)), ((), ())), precision=precision, preferred_element_type=F32)


def dot_nt(a, b, precision=None):
    return lax.dot_general(a, b, (((1,), (1,)), ((), ())), precision=precision, preferred_element_type=F32)


def dot_tn(a, b, precision=None):
    return lax.dot_general(a, b, (((0,), (0,)), ((), ())), precision=precision, preferred_element_type=F32)


def head_mask(shape=(GROUP, GROUP)):
    rows = lax.broadcasted_iota(jnp.int32, shape, 0)
    cols = lax.broadcasted_iota(jnp.int32, shape, 1)
    return lax.shift_right_logical(rows, 6) == lax.shift_right_logical(cols, 6)


def spread(wide):
    tall = jnp.concatenate([wide, wide, wide, wide], axis=0)
    return jnp.where(head_mask(), tall, jnp.zeros_like(tall))


def collect(full):
    kept = jnp.where(head_mask(), full, jnp.zeros_like(full))
    return (kept[0:64] + kept[64:128]) + (kept[128:192] + kept[192:256])


def flip(wide):
    turned = jnp.transpose(spread(wide))
    return (turned[0:64] + turned[64:128]) + (turned[128:192] + turned[192:256])


def gs(g):
    return slice(g * GROUP, (g + 1) * GROUP)


def half_reduce(x, op, init):
    parts = []
    for c in range(x.shape[1] // 128):
        col = x[:, c * 128 : (c + 1) * 128]
        low = lax.broadcasted_iota(jnp.int32, col.shape, 1) < 64
        a = op(jnp.where(low, col, init), axis=1, keepdims=True)
        b = op(jnp.where(low, init, col), axis=1, keepdims=True)
        parts.append(jnp.where(low, a, b))
    return jnp.concatenate(parts, axis=1)


def normalize(x):
    center = x - jnp.mean(x, axis=-1, keepdims=True)
    inv = lax.rsqrt(jnp.mean(center * center, axis=-1, keepdims=True) + EPS_NORM)
    return center * inv, inv


def norm_back(up, normal, inv, gain):
    scaled = up * gain
    centered = scaled - jnp.mean(scaled, axis=-1, keepdims=True)
    return inv * (centered - normal * jnp.mean(scaled * normal, axis=-1, keepdims=True))


def rowsum8(x):
    return jnp.sum(x.reshape(x.shape[0] // 8, 8, x.shape[1]), axis=0)


def gelu_parts(a):
    z = jnp.abs(a)
    t = 1.0 / (1.0 + (0.3275911 * 0.7071067811865476) * z)
    e = jnp.exp(-0.5 * a * a)
    poly = t * (0.127414796 + t * (-0.142248368 + t * (0.7107068705 + t * (-0.7265760135 + t * 0.5307027145))))
    tail = poly * e
    phi = jnp.where(a >= 0, 1.0 - tail, tail)
    return a * phi, phi + a * (e * 0.3989422804014327)


def whole(shape):
    zeros = (0,) * len(shape)
    return pl.BlockSpec(shape, lambda i: zeros, pipeline_mode=pl.Buffered(1))


def rows(tile, width):
    return pl.BlockSpec((tile, width), lambda i: (i, 0))


def sds(shape, dtype):
    return jax.ShapeDtypeStruct(shape, dtype)


def params():
    return pltpu.CompilerParams(dimension_semantics=("arbitrary",), vmem_limit_bytes=VMEM_LIMIT)


def project_kernel(x_ref, w_ref, gain_ref, h_ref, q_ref, k_ref, v_ref, mean_ref):
    i = pl.program_id(0)
    x = x_ref[...].astype(F32)
    normal, _ = normalize(x)
    h = (normal * gain_ref[0:1, :]).astype(BF16)
    h_ref[...] = h
    q = (dot(h, w_ref[0]) * QK_SCALE).astype(BF16)
    q_ref[...] = q
    mean_ref[pl.ds(i, 1), :] = jnp.mean(q.astype(F32), axis=0, keepdims=True)
    k = (dot(h, w_ref[1]) * QK_SCALE).astype(BF16)
    k_ref[...] = k
    mean_ref[pl.ds(i + 4, 1), :] = jnp.mean(k.astype(F32), axis=0, keepdims=True)
    v_ref[...] = dot(h, w_ref[2]).astype(BF16)


def project(x, w_attn, gains):
    t, d = x.shape
    tile = t // 4
    return pl.pallas_call(
        project_kernel,
        grid=(4,),
        in_specs=[rows(tile, d), whole(w_attn.shape), whole(gains.shape)],
        out_specs=[rows(tile, d)] * 4 + [whole((8, d))],
        out_shape=[sds((t, d), BF16)] * 4 + [sds((8, d), F32)],
        compiler_params=params(),
        name="project",
    )(x, w_attn, gains)


def pinv_kernel(mq_ref, mk_ref, a_ref, p_ref, z_ref, az_ref, t2_ref, t3_ref):
    eye = jnp.where(
        (lax.broadcasted_iota(jnp.int32, (M, GROUP), 1) & 63) == lax.broadcasted_iota(jnp.int32, (M, GROUP), 0),
        1.0,
        0.0,
    )
    ones = jnp.where(head_mask(), 1.0, 0.0)
    a, z = [], []
    for g in range(NG):
        s = dot_nt(mq_ref[:, gs(g)], spread(mk_ref[:, gs(g)]))
        e = jnp.exp(s - half_reduce(s, jnp.max, -jnp.inf))
        ag = e / half_reduce(e, jnp.sum, 0.0)
        a_ref[:, gs(g)] = ag
        col = jnp.sum(ag, axis=0, keepdims=True)
        sq = dot(jnp.broadcast_to(col * col, (8, GROUP)), ones, HI)[0:1]
        a.append(ag)
        z.append(flip(ag) / jnp.sqrt(sq))
    for it in range(NSITER):
        for g in range(NG):
            z_ref[it, :, gs(g)] = z[g]
        az = [dot(a[g], spread(z[g]), HI) for g in range(NG)]
        t1 = [7.0 * eye - az[g] for g in range(NG)]
        t2 = [15.0 * eye - dot(az[g], spread(t1[g]), HI) for g in range(NG)]
        t3 = [13.0 * eye - dot(az[g], spread(t2[g]), HI) for g in range(NG)]
        z = [0.25 * dot(z[g], spread(t3[g]), HI) for g in range(NG)]
        for g in range(NG):
            az_ref[it, :, gs(g)] = az[g]
            t2_ref[it, :, gs(g)] = t2[g]
            t3_ref[it, :, gs(g)] = t3[g]
    for g in range(NG):
        p_ref[:, gs(g)] = z[g]


def pinv(mq, mk):
    d = mq.shape[1]
    vm = pl.BlockSpec(memory_space=pltpu.VMEM)
    return pl.pallas_call(
        pinv_kernel,
        in_specs=[vm] * 2,
        out_specs=[vm] * 6,
        out_shape=[sds((M, d), F32)] * 2 + [sds((NSITER, M, d), F32)] * 4,
        compiler_params=pltpu.CompilerParams(vmem_limit_bytes=VMEM_LIMIT),
        name="pinv",
    )(mq, mk)


def pinv_back_kernel(mq_ref, mk_ref, a_ref, p_ref, z_ref, az_ref, t2_ref, t3_ref, gw_ref, u_ref, zt_ref, dq_ref, dk_ref, *, inv_n):
    eye = jnp.where(
        (lax.broadcasted_iota(jnp.int32, (M, GROUP), 1) & 63) == lax.broadcasted_iota(jnp.int32, (M, GROUP), 0),
        1.0,
        0.0,
    )
    ones = jnp.where(head_mask(), 1.0, 0.0)
    R = range(NG)
    a = [a_ref[:, gs(g)] for g in R]
    gz = []
    for g in R:
        bv = u_ref[:, gs(g)] / widen(zt_ref[...], g)
        gz.append(flip(dot_nt(gw_ref[:, gs(g)], spread(bv), HI)))
    da = [jnp.zeros((M, GROUP), F32) for _ in R]
    for it in reversed(range(NSITER)):
        z = [z_ref[it, :, gs(g)] for g in R]
        az = [az_ref[it, :, gs(g)] for g in R]
        t2 = [t2_ref[it, :, gs(g)] for g in R]
        t3 = [t3_ref[it, :, gs(g)] for g in R]
        bg = [spread(0.25 * gz[g]) for g in R]
        d3 = [dot(0.25 * gz[g], spread(z[g]), HI) for g in R]
        baz = [spread(az[g]) for g in R]
        d2 = [-dot(d3[g], baz[g], HI) for g in R]
        d1 = [-dot(d2[g], baz[g], HI) for g in R]
        daz = [
            -dot(t2[g], spread(d3[g]), HI) - dot(7.0 * eye - az[g], spread(d2[g]), HI) - d1[g] for g in R
        ]
        da = [da[g] + dot(z[g], spread(daz[g]), HI) for g in R]
        gz = [dot(t3[g], bg[g], HI) + dot(daz[g], spread(a[g]), HI) for g in R]
    for g in R:
        col = jnp.sum(a[g], axis=0, keepdims=True)
        sq = dot(jnp.broadcast_to(col * col, (8, GROUP)), ones, HI)[0:1]
        bound = jnp.sqrt(sq)
        tot = jnp.sum(gz[g] * a[g], axis=0, keepdims=True)
        tot = dot(jnp.broadcast_to(tot, (8, GROUP)), ones, HI)[0:1]
        full = flip(da[g]) + gz[g] / bound - (tot / (bound * bound * bound)) * col
        ds = a[g] * (full - half_reduce(full * a[g], jnp.sum, 0.0))
        dq_ref[:, gs(g)] = dot(ds, spread(mk_ref[:, gs(g)].astype(F32)), HI) * inv_n
        dk_ref[:, gs(g)] = dot(flip(ds), spread(mq_ref[:, gs(g)].astype(F32)), HI) * inv_n


def pinv_back(mq, mk, saved, gw, u, zt, inv_n):
    d = mq.shape[1]
    vm = pl.BlockSpec(memory_space=pltpu.VMEM)
    return pl.pallas_call(
        functools.partial(pinv_back_kernel, inv_n=inv_n),
        in_specs=[vm] * 11,
        out_specs=[vm] * 2,
        out_shape=[sds((M, d), F32)] * 2,
        compiler_params=pltpu.CompilerParams(vmem_limit_bytes=VMEM_LIMIT),
        name="pinv_back",
    )(mq, mk, *saved, gw, u, zt)


def widen(zt, g):
    return jnp.concatenate(
        [jnp.broadcast_to(zt[:, h : h + 1], (M, HD)) for h in range(4 * g, 4 * g + 4)], axis=1
    )


def attend_kernel(q_ref, k_ref, v_ref, mq_ref, mk_ref, f_ref, e_ref, u_ref, zt_ref, uacc, zacc):
    i = pl.program_id(0)
    n = pl.num_programs(0)

    @pl.when(i == 0)
    def _():
        uacc[...] = jnp.zeros_like(uacc)
        zacc[...] = jnp.zeros_like(zacc)

    ones_bd = jnp.where(head_mask(), 1.0, 0.0).astype(BF16)
    ones = jnp.ones((q_ref.shape[0], 128), BF16)
    for g in range(NG):
        s = dot_nt(q_ref[:, gs(g)], spread(mk_ref[:, gs(g)]))
        ex = jnp.exp(s - half_reduce(s, jnp.max, -jnp.inf))
        den = dot(ex.astype(BF16), ones_bd)
        f_ref[:, gs(g)] = (ex / den).astype(BF16)
        e = jnp.exp(dot_nt(k_ref[:, gs(g)], spread(mq_ref[:, gs(g)]))).astype(BF16)
        e_ref[:, gs(g)] = e
        uacc[g] += dot_tn(e, v_ref[:, gs(g)])
        zacc[g] += dot_tn(e, ones)

    @pl.when(i == n - 1)
    def _():
        lane = lax.broadcasted_iota(jnp.int32, (M, 128), 1)
        total = jnp.zeros((M, 128), F32)
        for g in range(NG):
            u_ref[:, gs(g)] = collect(uacc[g])
            for h in range(4):
                total = total + jnp.where(lane == 4 * g + h, zacc[g, h * 64 : h * 64 + 64, :], 0.0)
        zt_ref[...] = total


def attend(q, k, v, mq, mk):
    t, d = q.shape
    tile = t // 4
    return pl.pallas_call(
        attend_kernel,
        grid=(4,),
        in_specs=[rows(tile, d)] * 3 + [whole((M, d))] * 2,
        out_specs=[rows(tile, d)] * 2 + [whole((M, d)), whole((M, 128))],
        out_shape=[sds((t, d), BF16)] * 2 + [sds((M, d), F32), sds((M, 128), F32)],
        scratch_shapes=[pltpu.VMEM((NG, GROUP, GROUP), F32), pltpu.VMEM((NG, GROUP, 128), F32)],
        compiler_params=params(),
        name="attend",
    )(q, k, v, mq, mk)


CHUNK = 64


def fill_extended(ext, body_ref, left_ref, right_ref, i, n, tile):
    start = pl.multiple_of(i * tile, tile)
    for c in range(ext.shape[0]):
        cols = slice(c * 128, (c + 1) * 128)
        ext[c, RAD : RAD + tile, :] = body_ref[pl.ds(start, tile), cols].astype(F32)
        before = body_ref[pl.ds(pl.multiple_of(jnp.maximum(start - RAD, 0), RAD), RAD), cols].astype(F32)
        ext[c, 0:RAD, :] = jnp.where(i == 0, left_ref[:, cols].astype(F32), before)
        last = body_ref.shape[0] - RAD
        after = body_ref[pl.ds(pl.multiple_of(jnp.minimum(start + tile, last), RAD), RAD), cols].astype(F32)
        ext[c, RAD + tile : 2 * RAD + tile, :] = jnp.where(i == n - 1, right_ref[:, cols].astype(F32), after)


def conv_forward(ext, tap_ref, out, tile):
    def step(r, _):
        base = pl.multiple_of(r * CHUNK, CHUNK)
        for c in range(ext.shape[0]):
            cols = slice(c * 128, (c + 1) * 128)
            acc = jnp.zeros((CHUNK, 128), F32)
            for b in range(8):
                reach = 4 if b == 0 else 3
                win = ext[c, pl.ds(base + b, CHUNK + 8 * reach), :]
                for m in range(reach + 1):
                    o = 8 * m + b
                    acc = acc + tap_ref[o : o + 1, cols] * win[8 * m : 8 * m + CHUNK]
            out[c, pl.ds(base, CHUNK), :] = acc
        return 0

    lax.fori_loop(0, tile // CHUNK, step, 0)


def conv_backward(vext, gext, tap_ref, out, tapacc, tile):
    def step(r, _):
        base = pl.multiple_of(r * CHUNK, CHUNK)
        for c in range(vext.shape[0]):
            cols = slice(c * 128, (c + 1) * 128)
            acc = jnp.zeros((CHUNK, 128), F32)
            here = gext[c, pl.ds(base + RAD, CHUNK), :]
            for b in range(8):
                reach = 4 if b == 0 else 3
                win = gext[c, pl.ds(base + b, CHUNK + 8 * reach), :]
                for m in range(reach + 1):
                    o = KC - 1 - (8 * m + b)
                    acc = acc + tap_ref[o : o + 1, cols] * win[8 * m : 8 * m + CHUNK]
                win = vext[c, pl.ds(base + b, CHUNK + 8 * reach), :]
                for m in range(reach + 1):
                    o = 8 * m + b
                    tapacc[o, :, cols] += rowsum8(here * win[8 * m : 8 * m + CHUNK])
            out[c, pl.ds(base, CHUNK), :] = acc
        return 0

    lax.fori_loop(0, tile // CHUNK, step, 0)


FCHUNK = 512


def middle_kernel(
    x_ref, dy_ref, f_ref, q_ref, v_ref, left_ref, right_ref, wo_ref, up_ref, down_ref, gain_ref, tap_ref,
    mk_ref, u_ref, zt_ref, p_ref,
    out_ref, act_ref, da_ref, h2_ref, mix_ref, dx_ref, dmix_ref, dqf_ref, gw_ref, dkt_ref, dg_ref,
    ext, conv, wbd, gwacc, dktacc, dgacc, oacc, hacc,
):
    i = pl.program_id(0)
    n = pl.num_programs(0)
    tile = x_ref.shape[0]
    d = x_ref.shape[1]

    @pl.when(i == 0)
    def _():
        gwacc[...] = jnp.zeros_like(gwacc)
        dktacc[...] = jnp.zeros_like(dktacc)
        dgacc[...] = jnp.zeros_like(dgacc)
        for g in range(NG):
            bv = u_ref[:, gs(g)] / widen(zt_ref[...], g)
            wbd[g] = spread(dot(p_ref[:, gs(g)], spread(bv), HI)).astype(BF16)

    fill_extended(ext, v_ref, left_ref, right_ref, i, n, tile)
    conv_forward(ext, tap_ref, conv, tile)
    for g in range(NG):
        att = dot(f_ref[:, gs(g)], wbd[g])
        for s in range(2):
            c = 2 * g + s
            mix_ref[:, c * 128 : (c + 1) * 128] = (att[:, s * 128 : (s + 1) * 128] + conv[c]).astype(BF16)
    x1 = x_ref[...].astype(F32) + dot(mix_ref[...], wo_ref[...])
    normal, inv = normalize(x1)
    gain = gain_ref[1:2, :]
    h2 = (normal * gain).astype(BF16)
    h2_ref[...] = h2
    dy = dy_ref[...]
    ff = up_ref.shape[1]
    for j in range(ff // FCHUNK):
        cols = slice(j * FCHUNK, (j + 1) * FCHUNK)
        a = dot(h2, up_ref[:, cols])
        act, slope = gelu_parts(a)
        act = act.astype(BF16)
        act_ref[:, cols] = act
        da = (dot_nt(dy, down_ref[cols, :]) * slope).astype(BF16)
        da_ref[:, cols] = da
        o = dot(act, down_ref[cols, :])
        h = dot_nt(da, up_ref[:, cols])
        if j == 0:
            oacc[...] = o
            hacc[...] = h
        else:
            oacc[...] += o
            hacc[...] += h
    out_ref[...] = (x1 + oacc[...]).astype(BF16)
    dh2 = hacc[...]
    dgacc[...] += rowsum8(dh2 * normal)
    dx1 = norm_back(dh2, normal, inv, gain) + dy.astype(F32)
    do = dx1.astype(BF16)
    dx_ref[...] = do
    dmix = dot_nt(do, wo_ref[...]).astype(BF16)
    dmix_ref[...] = dmix
    ones_bd = jnp.where(head_mask(), 1.0, 0.0).astype(BF16)
    for g in range(NG):
        dm = dmix[:, gs(g)]
        f = f_ref[:, gs(g)]
        df = dot_nt(dm, wbd[g])
        gwacc[g] += dot_tn(f, dm)
        ff32 = f.astype(F32)
        prod = df * ff32
        hi = prod.astype(BF16)
        lo = (prod - hi.astype(F32)).astype(BF16)
        ds = (ff32 * (df - (dot(hi, ones_bd) + dot(lo, ones_bd)))).astype(BF16)
        dqf_ref[:, gs(g)] = dot(ds, spread(mk_ref[:, gs(g)])).astype(BF16)
        dktacc[g] += dot_tn(ds, q_ref[:, gs(g)])

    @pl.when(i == n - 1)
    def _():
        for g in range(NG):
            gw_ref[:, gs(g)] = collect(gwacc[g])
            dkt_ref[:, gs(g)] = collect(dktacc[g])
        dg_ref[...] = jnp.broadcast_to(jnp.sum(dgacc[...], axis=0, keepdims=True), (8, d))


def middle(x, dy, f, q, v, left, right, wo, up, down, gains, taps, mk, u, zt, p):
    t, d = x.shape
    ff = up.shape[1]
    tile = 256
    r = rows(tile, d)
    rf = rows(tile, ff)
    return pl.pallas_call(
        middle_kernel,
        grid=(t // tile,),
        in_specs=[r, r, r, r, whole((t, d)), whole((RAD, d)), whole((RAD, d)), whole((d, d)), whole(up.shape), whole(down.shape),
                  whole(gains.shape), whole(taps.shape), whole((M, d)), whole((M, d)), whole((M, 128)), whole((M, d))],
        out_specs=[r, rf, rf, r, r, r, r, r, whole((M, d)), whole((M, d)), whole((8, d))],
        out_shape=[sds((t, d), BF16), sds((t, ff), BF16), sds((t, ff), BF16)] + [sds((t, d), BF16)] * 5
        + [sds((M, d), F32), sds((M, d), F32), sds((8, d), F32)],
        scratch_shapes=[
            pltpu.VMEM((6, tile + 2 * RAD, 128), F32),
            pltpu.VMEM((6, tile, 128), F32),
            pltpu.VMEM((NG, GROUP, GROUP), BF16),
            pltpu.VMEM((NG, GROUP, GROUP), F32),
            pltpu.VMEM((NG, GROUP, GROUP), F32),
            pltpu.VMEM((8, d), F32),
            pltpu.VMEM((tile, d), F32),
            pltpu.VMEM((tile, d), F32),
        ],
        compiler_params=params(),
        name="middle",
    )(x, dy, f, q, v, left, right, wo, up, down, gains, taps, mk, u, zt, p)


def back_kernel(
    e_ref, k_ref, v_ref, vl_ref, vr_ref, g_ref, gl_ref, gr_ref, tap_ref, mq_ref, u_ref, zt_ref, p_ref, gw_ref,
    dv_ref, dkb_ref, dqt_ref, dtap_ref,
    vext, gext, conv, tapacc, dubd, rowadd, dqtacc,
):
    i = pl.program_id(0)
    n = pl.num_programs(0)
    tile = e_ref.shape[0]

    @pl.when(i == 0)
    def _():
        dqtacc[...] = jnp.zeros_like(dqtacc)
        tapacc[...] = jnp.zeros_like(tapacc)
        for g in range(NG):
            z = widen(zt_ref[...], g)
            bv = u_ref[:, gs(g)] / z
            dbv = dot(flip(p_ref[:, gs(g)]), spread(gw_ref[:, gs(g)]), HI)
            dubd[g] = spread(dbv / z).astype(BF16)
            rowadd[g] = dot_nt(jnp.ones((8, GROUP), F32), spread(dbv * bv / z), HI)

    fill_extended(vext, v_ref, vl_ref, vr_ref, i, n, tile)
    fill_extended(gext, g_ref, gl_ref, gr_ref, i, n, tile)
    conv_backward(vext, gext, tap_ref, conv, tapacc, tile)
    here = pl.ds(pl.multiple_of(i * tile, tile), tile)
    for g in range(NG):
        e = e_ref[:, gs(g)]
        de = dot_nt(v_ref[here, gs(g)], dubd[g]) - rowadd[g, 0:1, :]
        ds = (e.astype(F32) * de).astype(BF16)
        dvb = dot(e, dubd[g])
        for s in range(2):
            c = 2 * g + s
            dv_ref[:, c * 128 : (c + 1) * 128] = (dvb[:, s * 128 : (s + 1) * 128] + conv[c]).astype(BF16)
        dkb_ref[:, gs(g)] = dot(ds, spread(mq_ref[:, gs(g)])).astype(BF16)
        dqtacc[g] += dot_tn(ds, k_ref[:, gs(g)])

    @pl.when(i == n - 1)
    def _():
        for g in range(NG):
            dqt_ref[:, gs(g)] = collect(dqtacc[g])
        dtap_ref[...] = jnp.sum(tapacc[...], axis=1)


def back(e, k, v, vl, vr, dmix, gl, gr, taps, mq, u, zt, p, gw):
    t, d = e.shape
    tile = 256
    r = rows(tile, d)
    w = whole((M, d))
    return pl.pallas_call(
        back_kernel,
        grid=(t // tile,),
        in_specs=[r, r, whole((t, d)), whole((RAD, d)), whole((RAD, d)), whole((t, d)), whole((RAD, d)), whole((RAD, d)),
                  whole(taps.shape), w, w, whole((M, 128)), w, w],
        out_specs=[r, r, w, whole((40, d))],
        out_shape=[sds((t, d), BF16), sds((t, d), BF16), sds((M, d), F32), sds((40, d), F32)],
        scratch_shapes=[
            pltpu.VMEM((6, tile + 2 * RAD, 128), F32),
            pltpu.VMEM((6, tile + 2 * RAD, 128), F32),
            pltpu.VMEM((6, tile, 128), F32),
            pltpu.VMEM((40, 8, d), F32),
            pltpu.VMEM((NG, GROUP, GROUP), BF16),
            pltpu.VMEM((NG, 8, GROUP), F32),
            pltpu.VMEM((NG, GROUP, GROUP), F32),
        ],
        compiler_params=params(),
        name="back",
    )(e, k, v, vl, vr, dmix, gl, gr, taps, mq, u, zt, p, gw)


def last_kernel(x_ref, dx_ref, dqf_ref, dkb_ref, dv_ref, own_ref, w_ref, gain_ref, dq_ref, dk_ref, ig_ref, dg_ref, dgacc, *, seg_len, rows_dev):
    i = pl.program_id(0)
    n = pl.num_programs(0)
    tile, d = x_ref.shape

    @pl.when(i == 0)
    def _():
        dgacc[...] = jnp.zeros_like(dgacc)

    at = i * rows_dev // 4
    scale = 1.0 / seg_len
    dq = (dqf_ref[...].astype(F32) + own_ref[pl.ds(at, 1), :] * scale).astype(BF16)
    dk = (dkb_ref[...].astype(F32) + own_ref[pl.ds(at + 4, 1), :] * scale).astype(BF16)
    dq_ref[...] = dq
    dk_ref[...] = dk
    dh = (dot_nt(dq, w_ref[0]) + dot_nt(dk, w_ref[1])) * QK_SCALE + dot_nt(dv_ref[...], w_ref[2])
    normal, inv = normalize(x_ref[...].astype(F32))
    dgacc[...] += rowsum8(dh * normal)
    ig = norm_back(dh, normal, inv, gain_ref[0:1, :]) + dx_ref[...].astype(F32)
    ig_ref[...] = ig.astype(BF16)

    @pl.when(i == n - 1)
    def _():
        dg_ref[...] = jnp.broadcast_to(jnp.sum(dgacc[...], axis=0, keepdims=True), (8, d))


def last(x, dx, dqf, dkb, dv, own, w_attn, gains, seg_len, rows_dev):
    t, d = x.shape
    tile = t // 4
    r = rows(tile, d)
    return pl.pallas_call(
        functools.partial(last_kernel, seg_len=seg_len, rows_dev=rows_dev),
        grid=(4,),
        in_specs=[r, r, r, r, r, whole((8, d)), whole(w_attn.shape), whole(gains.shape)],
        out_specs=[r, r, r, whole((8, d))],
        out_shape=[sds((t, d), BF16)] * 3 + [sds((8, d), F32)],
        scratch_shapes=[pltpu.VMEM((8, d), F32)],
        compiler_params=params(),
        name="last",
    )(x, dx, dqf, dkb, dv, own, w_attn, gains)


def adam_step(weight, grad_vec, moment, second, rate_value):
    moment_new = BETA_ONE * moment + (1.0 - BETA_ONE) * grad_vec
    second_new = BETA_TWO * second + (1.0 - BETA_TWO) * grad_vec * grad_vec
    first_hat = moment_new / (1.0 - BETA_ONE**STEP)
    second_hat = second_new / (1.0 - BETA_TWO**STEP)
    weight_new = weight - rate_value * (
        first_hat / (jnp.sqrt(second_hat) + ADAM_EPS) + DECAY_RATE * weight
    )
    return (weight_new, moment_new, second_new)


def halos(cells, index, count):
    left = lax.ppermute(cells[-RAD:], "seq", [(i, (i + 1) % count) for i in range(count)])
    right = lax.ppermute(cells[:RAD], "seq", [((i + 1) % count, i) for i in range(count)])
    left = jnp.where(index > 0, left, jnp.zeros_like(left))
    right = jnp.where(index < count - 1, right, jnp.zeros_like(right))
    return left, right


def per_device(tokens, cotangent, attn_w, w_up, w_down, vectors, attn_m, attn_v, up_m, up_v, down_m, down_v, vec_m, vec_v):
    both = ("seq", "rep")
    x = tokens[0]
    dy = cotangent[0]
    t, d = x.shape
    count = lax.axis_size("seq")
    index = lax.axis_index("seq")
    rows_dev = max(M // count, 1)
    per_mark = count * rows_dev // M
    seg_len = t * count // M

    w_attn = lax.all_gather(attn_w.astype(BF16), both, axis=1, tiled=True)
    up = lax.all_gather(w_up.astype(BF16), both, axis=0, tiled=True)
    down = lax.all_gather(w_down.astype(BF16), both, axis=0, tiled=True)
    vec = lax.all_gather(vectors.astype(BF16), both, axis=0, tiled=True)
    vec_t = jnp.transpose(vec.astype(F32))
    gains = jnp.concatenate([vec_t[:2], jnp.zeros((6, d), F32)], axis=0)
    taps = jnp.concatenate([vec_t[2:], jnp.zeros((7, d), F32)], axis=0)

    h1, q, k, v, means = project(x, w_attn, gains)
    marks = lax.all_gather(means, "seq", axis=0)
    marks = jnp.transpose(marks.reshape(count, 2, 4, d), (1, 0, 2, 3)).reshape(2, M, count * 4 // M, d)
    marks = jnp.mean(marks, axis=2).astype(BF16)
    mq, mk = marks[0], marks[1]
    vl, vr = halos(v, index, count)
    f, e, u, zt = attend(q, k, v, mq, mk)
    u, zt = lax.psum((u, zt), "seq")
    a, p, zs, azs, t2s, t3s = pinv(mq, mk)
    out, act, da, h2, mix, dx, dmix, dqf, gw, dkt, dg2 = middle(
        x, dy, f, q, v, vl, vr, w_attn[3], up, down, gains, taps, mk, u, zt, p
    )
    gw = lax.psum(gw, "seq")
    gl, gr = halos(dmix, index, count)
    dot_xla = functools.partial(jnp.einsum, "ta,tb->ab", preferred_element_type=F32)
    g_down = dot_xla(act, dy).astype(BF16)
    g_up = dot_xla(h2, da).astype(BF16)
    g_o = dot_xla(mix, dx)
    dqt_a, dkt_a = pinv_back(mq, mk, (a, p, zs, azs, t2s, t3s), gw, u, zt, 1.0 / count)
    dv, dkb, dqt, dtap = back(e, k, v, vl, vr, dmix, gl, gr, taps, mq, u, zt, p, gw)
    spread_marks = jnp.stack([dqt + dqt_a, dkt + dkt_a])
    spread_marks = jnp.repeat(spread_marks, per_mark, axis=1).reshape(2, count, rows_dev, d)
    spread_marks = jnp.transpose(spread_marks, (1, 0, 2, 3))
    own = lax.psum_scatter(spread_marks, "seq", scatter_dimension=0, tiled=True)[0]
    own = jnp.pad(own, ((0, 0), (0, 4 - rows_dev), (0, 0))).reshape(8, d)
    dq, dk, ig, dg1 = last(x, dx, dqf, dkb, dv, own, w_attn, gains, seg_len, rows_dev)
    g_q = dot_xla(h1, dq) * QK_SCALE
    g_k = dot_xla(h1, dk) * QK_SCALE
    g_v = dot_xla(h1, dv)
    g_attn = jnp.stack([g_q, g_k, g_v, g_o]).astype(BF16)
    g_vec = jnp.transpose(jnp.concatenate([dg1[:1], dg2[:1], dtap[:KC]], axis=0))
    red_attn = lax.psum_scatter(g_attn, both, scatter_dimension=1, tiled=True).astype(F32)
    red_up = lax.psum_scatter(g_up, both, scatter_dimension=0, tiled=True).astype(F32)
    red_down = lax.psum_scatter(g_down, both, scatter_dimension=0, tiled=True).astype(F32)
    red_vec = lax.psum_scatter(g_vec, both, scatter_dimension=0, tiled=True)
    return (
        out[None],
        ig[None],
        *adam_step(attn_w, red_attn, attn_m, attn_v, LEARN_RATE),
        *adam_step(w_up, red_up, up_m, up_v, LEARN_RATE),
        *adam_step(w_down, red_down, down_m, down_v, LEARN_RATE),
        *adam_step(vectors, red_vec, vec_m, vec_v, VECTOR_RATE),
    )


def solution(mesh):
    tok = P("rep", "seq", None)
    att = P(None, ("seq", "rep"), None)
    mat = P(("seq", "rep"), None)
    return jax.shard_map(
        per_device,
        mesh=mesh,
        in_specs=(tok, tok, att, mat, mat, mat, att, att, mat, mat, mat, mat, mat, mat),
        out_specs=(tok, tok, att, att, att) + (mat,) * 9,
        check_vma=False,
    )
```

```python
import functools

import jax
import jax.numpy as jnp
from jax import lax
from jax.experimental import pallas as pl
from jax.experimental.pallas import tpu as pltpu
from jax.sharding import PartitionSpec as P

H = 12
HD = 64
M = 64
KC = 33
NSITER = 6
STEP = 10
EPS_NORM = 1e-05
BETA_ONE = 0.9
BETA_TWO = 0.999
ADAM_EPS = 1e-08
LEARN_RATE = 0.03
VECTOR_RATE = 0.15
DECAY_RATE = 0.1

F32 = jnp.float32
BF16 = jnp.bfloat16
GROUP = 256
NG = 3
RAD = 16
QK_SCALE = HD ** (-0.25)
HI = lax.Precision.HIGHEST
VMEM_LIMIT = 58 * 1024 * 1024


def dot(a, b, precision=None):
    return lax.dot_general(a, b, (((1,), (0,)), ((), ())), precision=precision, preferred_element_type=F32)


def dot_nt(a, b, precision=None):
    return lax.dot_general(a, b, (((1,), (1,)), ((), ())), precision=precision, preferred_element_type=F32)


def dot_tn(a, b, precision=None):
    return lax.dot_general(a, b, (((0,), (0,)), ((), ())), precision=precision, preferred_element_type=F32)


def head_mask(shape=(GROUP, GROUP)):
    rows = lax.broadcasted_iota(jnp.int32, shape, 0)
    cols = lax.broadcasted_iota(jnp.int32, shape, 1)
    return lax.shift_right_logical(rows, 6) == lax.shift_right_logical(cols, 6)


def spread(wide):
    tall = jnp.concatenate([wide, wide, wide, wide], axis=0)
    return jnp.where(head_mask(), tall, jnp.zeros_like(tall))


def collect(full):
    kept = jnp.where(head_mask(), full, jnp.zeros_like(full))
    return (kept[0:64] + kept[64:128]) + (kept[128:192] + kept[192:256])


def flip(wide):
    turned = jnp.transpose(spread(wide))
    return (turned[0:64] + turned[64:128]) + (turned[128:192] + turned[192:256])


def gs(g):
    return slice(g * GROUP, (g + 1) * GROUP)


def half_reduce(x, op, init):
    parts = []
    for c in range(x.shape[1] // 128):
        col = x[:, c * 128 : (c + 1) * 128]
        low = lax.broadcasted_iota(jnp.int32, col.shape, 1) < 64
        a = op(jnp.where(low, col, init), axis=1, keepdims=True)
        b = op(jnp.where(low, init, col), axis=1, keepdims=True)
        parts.append(jnp.where(low, a, b))
    return jnp.concatenate(parts, axis=1)


def normalize(x):
    center = x - jnp.mean(x, axis=-1, keepdims=True)
    inv = lax.rsqrt(jnp.mean(center * center, axis=-1, keepdims=True) + EPS_NORM)
    return center * inv, inv


def norm_back(up, normal, inv, gain):
    scaled = up * gain
    centered = scaled - jnp.mean(scaled, axis=-1, keepdims=True)
    return inv * (centered - normal * jnp.mean(scaled * normal, axis=-1, keepdims=True))


def rowsum8(x):
    return jnp.sum(x.reshape(x.shape[0] // 8, 8, x.shape[1]), axis=0)


def gelu_parts(a):
    z = jnp.abs(a)
    t = 1.0 / (1.0 + (0.3275911 * 0.7071067811865476) * z)
    e = jnp.exp(-0.5 * a * a)
    poly = t * (0.127414796 + t * (-0.142248368 + t * (0.7107068705 + t * (-0.7265760135 + t * 0.5307027145))))
    tail = poly * e
    phi = jnp.where(a >= 0, 1.0 - tail, tail)
    return a * phi, phi + a * (e * 0.3989422804014327)


def whole(shape):
    zeros = (0,) * len(shape)
    return pl.BlockSpec(shape, lambda i: zeros, pipeline_mode=pl.Buffered(1))


def rows(tile, width):
    return pl.BlockSpec((tile, width), lambda i: (i, 0))


def sds(shape, dtype):
    return jax.ShapeDtypeStruct(shape, dtype)


def params():
    return pltpu.CompilerParams(dimension_semantics=("arbitrary",), vmem_limit_bytes=VMEM_LIMIT)


def project_kernel(x_ref, w_ref, gain_ref, h_ref, q_ref, k_ref, v_ref, mean_ref):
    i = pl.program_id(0)
    x = x_ref[...].astype(F32)
    normal, _ = normalize(x)
    h = (normal * gain_ref[0:1, :]).astype(BF16)
    h_ref[...] = h
    q = (dot(h, w_ref[0]) * QK_SCALE).astype(BF16)
    q_ref[...] = q
    mean_ref[pl.ds(i, 1), :] = jnp.mean(q.astype(F32), axis=0, keepdims=True)
    k = (dot(h, w_ref[1]) * QK_SCALE).astype(BF16)
    k_ref[...] = k
    mean_ref[pl.ds(i + 4, 1), :] = jnp.mean(k.astype(F32), axis=0, keepdims=True)
    v_ref[...] = dot(h, w_ref[2]).astype(BF16)


def project(x, w_attn, gains):
    t, d = x.shape
    tile = t // 4
    return pl.pallas_call(
        project_kernel,
        grid=(4,),
        in_specs=[rows(tile, d), whole(w_attn.shape), whole(gains.shape)],
        out_specs=[rows(tile, d)] * 4 + [whole((8, d))],
        out_shape=[sds((t, d), BF16)] * 4 + [sds((8, d), F32)],
        compiler_params=params(),
        name="project",
    )(x, w_attn, gains)


def pinv_kernel(mq_ref, mk_ref, a_ref, p_ref, z_ref, az_ref, t2_ref, t3_ref):
    eye = jnp.where(
        (lax.broadcasted_iota(jnp.int32, (M, GROUP), 1) & 63) == lax.broadcasted_iota(jnp.int32, (M, GROUP), 0),
        1.0,
        0.0,
    )
    ones = jnp.where(head_mask(), 1.0, 0.0)
    a, z = [], []
    for g in range(NG):
        s = dot_nt(mq_ref[:, gs(g)], spread(mk_ref[:, gs(g)]))
        e = jnp.exp(s - half_reduce(s, jnp.max, -jnp.inf))
        ag = e / half_reduce(e, jnp.sum, 0.0)
        a_ref[:, gs(g)] = ag
        col = jnp.sum(ag, axis=0, keepdims=True)
        sq = dot(jnp.broadcast_to(col * col, (8, GROUP)), ones, HI)[0:1]
        a.append(ag)
        z.append(flip(ag) / jnp.sqrt(sq))
    for it in range(NSITER):
        for g in range(NG):
            z_ref[it, :, gs(g)] = z[g]
        az = [dot(a[g], spread(z[g]), HI) for g in range(NG)]
        t1 = [7.0 * eye - az[g] for g in range(NG)]
        t2 = [15.0 * eye - dot(az[g], spread(t1[g]), HI) for g in range(NG)]
        t3 = [13.0 * eye - dot(az[g], spread(t2[g]), HI) for g in range(NG)]
        z = [0.25 * dot(z[g], spread(t3[g]), HI) for g in range(NG)]
        for g in range(NG):
            az_ref[it, :, gs(g)] = az[g]
            t2_ref[it, :, gs(g)] = t2[g]
            t3_ref[it, :, gs(g)] = t3[g]
    for g in range(NG):
        p_ref[:, gs(g)] = z[g]


def pinv(mq, mk):
    d = mq.shape[1]
    vm = pl.BlockSpec(memory_space=pltpu.VMEM)
    return pl.pallas_call(
        pinv_kernel,
        in_specs=[vm] * 2,
        out_specs=[vm] * 6,
        out_shape=[sds((M, d), F32)] * 2 + [sds((NSITER, M, d), F32)] * 4,
        compiler_params=pltpu.CompilerParams(vmem_limit_bytes=VMEM_LIMIT),
        name="pinv",
    )(mq, mk)


def pinv_back_kernel(mq_ref, mk_ref, a_ref, p_ref, z_ref, az_ref, t2_ref, t3_ref, gw_ref, u_ref, zt_ref, dq_ref, dk_ref, *, inv_n):
    eye = jnp.where(
        (lax.broadcasted_iota(jnp.int32, (M, GROUP), 1) & 63) == lax.broadcasted_iota(jnp.int32, (M, GROUP), 0),
        1.0,
        0.0,
    )
    ones = jnp.where(head_mask(), 1.0, 0.0)
    R = range(NG)
    a = [a_ref[:, gs(g)] for g in R]
    gz = []
    for g in R:
        bv = u_ref[:, gs(g)] / widen(zt_ref[...], g)
        gz.append(flip(dot_nt(gw_ref[:, gs(g)], spread(bv), HI)))
    da = [jnp.zeros((M, GROUP), F32) for _ in R]
    for it in reversed(range(NSITER)):
        z = [z_ref[it, :, gs(g)] for g in R]
        az = [az_ref[it, :, gs(g)] for g in R]
        t2 = [t2_ref[it, :, gs(g)] for g in R]
        t3 = [t3_ref[it, :, gs(g)] for g in R]
        bg = [spread(0.25 * gz[g]) for g in R]
        d3 = [dot(0.25 * gz[g], spread(z[g]), HI) for g in R]
        baz = [spread(az[g]) for g in R]
        d2 = [-dot(d3[g], baz[g], HI) for g in R]
        d1 = [-dot(d2[g], baz[g], HI) for g in R]
        daz = [
            -dot(t2[g], spread(d3[g]), HI) - dot(7.0 * eye - az[g], spread(d2[g]), HI) - d1[g] for g in R
        ]
        da = [da[g] + dot(z[g], spread(daz[g]), HI) for g in R]
        gz = [dot(t3[g], bg[g], HI) + dot(daz[g], spread(a[g]), HI) for g in R]
    for g in R:
        col = jnp.sum(a[g], axis=0, keepdims=True)
        sq = dot(jnp.broadcast_to(col * col, (8, GROUP)), ones, HI)[0:1]
        bound = jnp.sqrt(sq)
        tot = jnp.sum(gz[g] * a[g], axis=0, keepdims=True)
        tot = dot(jnp.broadcast_to(tot, (8, GROUP)), ones, HI)[0:1]
        full = flip(da[g]) + gz[g] / bound - (tot / (bound * bound * bound)) * col
        ds = a[g] * (full - half_reduce(full * a[g], jnp.sum, 0.0))
        dq_ref[:, gs(g)] = dot(ds, spread(mk_ref[:, gs(g)].astype(F32)), HI) * inv_n
        dk_ref[:, gs(g)] = dot(flip(ds), spread(mq_ref[:, gs(g)].astype(F32)), HI) * inv_n


def pinv_back(mq, mk, saved, gw, u, zt, inv_n):
    d = mq.shape[1]
    vm = pl.BlockSpec(memory_space=pltpu.VMEM)
    return pl.pallas_call(
        functools.partial(pinv_back_kernel, inv_n=inv_n),
        in_specs=[vm] * 11,
        out_specs=[vm] * 2,
        out_shape=[sds((M, d), F32)] * 2,
        compiler_params=pltpu.CompilerParams(vmem_limit_bytes=VMEM_LIMIT),
        name="pinv_back",
    )(mq, mk, *saved, gw, u, zt)


def widen(zt, g):
    return jnp.concatenate(
        [jnp.broadcast_to(zt[:, h : h + 1], (M, HD)) for h in range(4 * g, 4 * g + 4)], axis=1
    )


def attend_kernel(q_ref, k_ref, v_ref, mq_ref, mk_ref, f_ref, e_ref, u_ref, zt_ref, uacc, zacc):
    i = pl.program_id(0)
    n = pl.num_programs(0)

    @pl.when(i == 0)
    def _():
        uacc[...] = jnp.zeros_like(uacc)
        zacc[...] = jnp.zeros_like(zacc)

    ones_bd = jnp.where(head_mask(), 1.0, 0.0).astype(BF16)
    ones = jnp.ones((q_ref.shape[0], 128), BF16)
    for g in range(NG):
        s = dot_nt(q_ref[:, gs(g)], spread(mk_ref[:, gs(g)]))
        ex = jnp.exp(s - half_reduce(s, jnp.max, -jnp.inf))
        den = dot(ex.astype(BF16), ones_bd)
        f_ref[:, gs(g)] = (ex / den).astype(BF16)
        e = jnp.exp(dot_nt(k_ref[:, gs(g)], spread(mq_ref[:, gs(g)]))).astype(BF16)
        e_ref[:, gs(g)] = e
        uacc[g] += dot_tn(e, v_ref[:, gs(g)])
        zacc[g] += dot_tn(e, ones)

    @pl.when(i == n - 1)
    def _():
        lane = lax.broadcasted_iota(jnp.int32, (M, 128), 1)
        total = jnp.zeros((M, 128), F32)
        for g in range(NG):
            u_ref[:, gs(g)] = collect(uacc[g])
            for h in range(4):
                total = total + jnp.where(lane == 4 * g + h, zacc[g, h * 64 : h * 64 + 64, :], 0.0)
        zt_ref[...] = total


def attend(q, k, v, mq, mk):
    t, d = q.shape
    tile = t // 4
    return pl.pallas_call(
        attend_kernel,
        grid=(4,),
        in_specs=[rows(tile, d)] * 3 + [whole((M, d))] * 2,
        out_specs=[rows(tile, d)] * 2 + [whole((M, d)), whole((M, 128))],
        out_shape=[sds((t, d), BF16)] * 2 + [sds((M, d), F32), sds((M, 128), F32)],
        scratch_shapes=[pltpu.VMEM((NG, GROUP, GROUP), F32), pltpu.VMEM((NG, GROUP, 128), F32)],
        compiler_params=params(),
        name="attend",
    )(q, k, v, mq, mk)


CHUNK = 64


def fill_extended(ext, body_ref, left_ref, right_ref, i, n, tile):
    start = pl.multiple_of(i * tile, tile)
    for c in range(ext.shape[0]):
        cols = slice(c * 128, (c + 1) * 128)
        ext[c, RAD : RAD + tile, :] = body_ref[pl.ds(start, tile), cols].astype(F32)
        before = body_ref[pl.ds(pl.multiple_of(jnp.maximum(start - RAD, 0), RAD), RAD), cols].astype(F32)
        ext[c, 0:RAD, :] = jnp.where(i == 0, left_ref[:, cols].astype(F32), before)
        last = body_ref.shape[0] - RAD
        after = body_ref[pl.ds(pl.multiple_of(jnp.minimum(start + tile, last), RAD), RAD), cols].astype(F32)
        ext[c, RAD + tile : 2 * RAD + tile, :] = jnp.where(i == n - 1, right_ref[:, cols].astype(F32), after)


def conv_forward(ext, tap_ref, out, tile):
    def step(r, _):
        base = pl.multiple_of(r * CHUNK, CHUNK)
        for c in range(ext.shape[0]):
            cols = slice(c * 128, (c + 1) * 128)
            acc = jnp.zeros((CHUNK, 128), F32)
            for b in range(8):
                reach = 4 if b == 0 else 3
                win = ext[c, pl.ds(base + b, CHUNK + 8 * reach), :]
                for m in range(reach + 1):
                    o = 8 * m + b
                    acc = acc + tap_ref[o : o + 1, cols] * win[8 * m : 8 * m + CHUNK]
            out[c, pl.ds(base, CHUNK), :] = acc
        return 0

    lax.fori_loop(0, tile // CHUNK, step, 0)


def conv_backward(vext, gext, tap_ref, out, tapacc, tile):
    def step(r, _):
        base = pl.multiple_of(r * CHUNK, CHUNK)
        for c in range(vext.shape[0]):
            cols = slice(c * 128, (c + 1) * 128)
            acc = jnp.zeros((CHUNK, 128), F32)
            here = gext[c, pl.ds(base + RAD, CHUNK), :]
            for b in range(8):
                reach = 4 if b == 0 else 3
                win = gext[c, pl.ds(base + b, CHUNK + 8 * reach), :]
                for m in range(reach + 1):
                    o = KC - 1 - (8 * m + b)
                    acc = acc + tap_ref[o : o + 1, cols] * win[8 * m : 8 * m + CHUNK]
                win = vext[c, pl.ds(base + b, CHUNK + 8 * reach), :]
                for m in range(reach + 1):
                    o = 8 * m + b
                    tapacc[o, :, cols] += rowsum8(here * win[8 * m : 8 * m + CHUNK])
            out[c, pl.ds(base, CHUNK), :] = acc
        return 0

    lax.fori_loop(0, tile // CHUNK, step, 0)


FCHUNK = 512


def middle_kernel(
    x_ref, dy_ref, f_ref, q_ref, v_ref, left_ref, right_ref, wo_ref, up_ref, down_ref, gain_ref, tap_ref,
    mk_ref, u_ref, zt_ref, p_ref,
    out_ref, act_ref, da_ref, h2_ref, mix_ref, dx_ref, dmix_ref, dqf_ref, gw_ref, dkt_ref, dg_ref,
    ext, conv, wbd, gwacc, dktacc, dgacc, oacc, hacc,
):
    i = pl.program_id(0)
    n = pl.num_programs(0)
    tile = x_ref.shape[0]
    d = x_ref.shape[1]

    @pl.when(i == 0)
    def _():
        gwacc[...] = jnp.zeros_like(gwacc)
        dktacc[...] = jnp.zeros_like(dktacc)
        dgacc[...] = jnp.zeros_like(dgacc)
        for g in range(NG):
            bv = u_ref[:, gs(g)] / widen(zt_ref[...], g)
            wbd[g] = spread(dot(p_ref[:, gs(g)], spread(bv), HI)).astype(BF16)

    fill_extended(ext, v_ref, left_ref, right_ref, i, n, tile)
    conv_forward(ext, tap_ref, conv, tile)
    for g in range(NG):
        att = dot(f_ref[:, gs(g)], wbd[g])
        for s in range(2):
            c = 2 * g + s
            mix_ref[:, c * 128 : (c + 1) * 128] = (att[:, s * 128 : (s + 1) * 128] + conv[c]).astype(BF16)
    x1 = x_ref[...].astype(F32) + dot(mix_ref[...], wo_ref[...])
    normal, inv = normalize(x1)
    gain = gain_ref[1:2, :]
    h2 = (normal * gain).astype(BF16)
    h2_ref[...] = h2
    dy = dy_ref[...]
    ff = up_ref.shape[1]
    for j in range(ff // FCHUNK):
        cols = slice(j * FCHUNK, (j + 1) * FCHUNK)
        a = dot(h2, up_ref[:, cols])
        act, slope = gelu_parts(a)
        act = act.astype(BF16)
        act_ref[:, cols] = act
        da = (dot_nt(dy, down_ref[cols, :]) * slope).astype(BF16)
        da_ref[:, cols] = da
        o = dot(act, down_ref[cols, :])
        h = dot_nt(da, up_ref[:, cols])
        if j == 0:
            oacc[...] = o
            hacc[...] = h
        else:
            oacc[...] += o
            hacc[...] += h
    out_ref[...] = (x1 + oacc[...]).astype(BF16)
    dh2 = hacc[...]
    dgacc[...] += rowsum8(dh2 * normal)
    dx1 = norm_back(dh2, normal, inv, gain) + dy.astype(F32)
    do = dx1.astype(BF16)
    dx_ref[...] = do
    dmix = dot_nt(do, wo_ref[...]).astype(BF16)
    dmix_ref[...] = dmix
    ones_bd = jnp.where(head_mask(), 1.0, 0.0).astype(BF16)
    for g in range(NG):
        dm = dmix[:, gs(g)]
        f = f_ref[:, gs(g)]
        df = dot_nt(dm, wbd[g])
        gwacc[g] += dot_tn(f, dm)
        ff32 = f.astype(F32)
        prod = df * ff32
        hi = prod.astype(BF16)
        lo = (prod - hi.astype(F32)).astype(BF16)
        ds = (ff32 * (df - (dot(hi, ones_bd) + dot(lo, ones_bd)))).astype(BF16)
        dqf_ref[:, gs(g)] = dot(ds, spread(mk_ref[:, gs(g)])).astype(BF16)
        dktacc[g] += dot_tn(ds, q_ref[:, gs(g)])

    @pl.when(i == n - 1)
    def _():
        for g in range(NG):
            gw_ref[:, gs(g)] = collect(gwacc[g])
            dkt_ref[:, gs(g)] = collect(dktacc[g])
        dg_ref[...] = jnp.broadcast_to(jnp.sum(dgacc[...], axis=0, keepdims=True), (8, d))


def middle(x, dy, f, q, v, left, right, wo, up, down, gains, taps, mk, u, zt, p):
    t, d = x.shape
    ff = up.shape[1]
    tile = 256
    r = rows(tile, d)
    rf = rows(tile, ff)
    return pl.pallas_call(
        middle_kernel,
        grid=(t // tile,),
        in_specs=[r, r, r, r, whole((t, d)), whole((RAD, d)), whole((RAD, d)), whole((d, d)), whole(up.shape), whole(down.shape),
                  whole(gains.shape), whole(taps.shape), whole((M, d)), whole((M, d)), whole((M, 128)), whole((M, d))],
        out_specs=[r, rf, rf, r, r, r, r, r, whole((M, d)), whole((M, d)), whole((8, d))],
        out_shape=[sds((t, d), BF16), sds((t, ff), BF16), sds((t, ff), BF16)] + [sds((t, d), BF16)] * 5
        + [sds((M, d), F32), sds((M, d), F32), sds((8, d), F32)],
        scratch_shapes=[
            pltpu.VMEM((6, tile + 2 * RAD, 128), F32),
            pltpu.VMEM((6, tile, 128), F32),
            pltpu.VMEM((NG, GROUP, GROUP), BF16),
            pltpu.VMEM((NG, GROUP, GROUP), F32),
            pltpu.VMEM((NG, GROUP, GROUP), F32),
            pltpu.VMEM((8, d), F32),
            pltpu.VMEM((tile, d), F32),
            pltpu.VMEM((tile, d), F32),
        ],
        compiler_params=params(),
        name="middle",
    )(x, dy, f, q, v, left, right, wo, up, down, gains, taps, mk, u, zt, p)


def back_kernel(
    e_ref, k_ref, v_ref, vl_ref, vr_ref, g_ref, gl_ref, gr_ref, tap_ref, mq_ref, u_ref, zt_ref, p_ref, gw_ref,
    dv_ref, dkb_ref, dqt_ref, dtap_ref,
    vext, gext, conv, tapacc, dubd, rowadd, dqtacc,
):
    i = pl.program_id(0)
    n = pl.num_programs(0)
    tile = e_ref.shape[0]

    @pl.when(i == 0)
    def _():
        dqtacc[...] = jnp.zeros_like(dqtacc)
        tapacc[...] = jnp.zeros_like(tapacc)
        for g in range(NG):
            z = widen(zt_ref[...], g)
            bv = u_ref[:, gs(g)] / z
            dbv = dot(flip(p_ref[:, gs(g)]), spread(gw_ref[:, gs(g)]), HI)
            dubd[g] = spread(dbv / z).astype(BF16)
            rowadd[g] = dot_nt(jnp.ones((8, GROUP), F32), spread(dbv * bv / z), HI)

    fill_extended(vext, v_ref, vl_ref, vr_ref, i, n, tile)
    fill_extended(gext, g_ref, gl_ref, gr_ref, i, n, tile)
    conv_backward(vext, gext, tap_ref, conv, tapacc, tile)
    here = pl.ds(pl.multiple_of(i * tile, tile), tile)
    for g in range(NG):
        e = e_ref[:, gs(g)]
        de = dot_nt(v_ref[here, gs(g)], dubd[g]) - rowadd[g, 0:1, :]
        ds = (e.astype(F32) * de).astype(BF16)
        dvb = dot(e, dubd[g])
        for s in range(2):
            c = 2 * g + s
            dv_ref[:, c * 128 : (c + 1) * 128] = (dvb[:, s * 128 : (s + 1) * 128] + conv[c]).astype(BF16)
        dkb_ref[:, gs(g)] = dot(ds, spread(mq_ref[:, gs(g)])).astype(BF16)
        dqtacc[g] += dot_tn(ds, k_ref[:, gs(g)])

    @pl.when(i == n - 1)
    def _():
        for g in range(NG):
            dqt_ref[:, gs(g)] = collect(dqtacc[g])
        dtap_ref[...] = jnp.sum(tapacc[...], axis=1)


def back(e, k, v, vl, vr, dmix, gl, gr, taps, mq, u, zt, p, gw):
    t, d = e.shape
    tile = 256
    r = rows(tile, d)
    w = whole((M, d))
    return pl.pallas_call(
        back_kernel,
        grid=(t // tile,),
        in_specs=[r, r, whole((t, d)), whole((RAD, d)), whole((RAD, d)), whole((t, d)), whole((RAD, d)), whole((RAD, d)),
                  whole(taps.shape), w, w, whole((M, 128)), w, w],
        out_specs=[r, r, w, whole((40, d))],
        out_shape=[sds((t, d), BF16), sds((t, d), BF16), sds((M, d), F32), sds((40, d), F32)],
        scratch_shapes=[
            pltpu.VMEM((6, tile + 2 * RAD, 128), F32),
            pltpu.VMEM((6, tile + 2 * RAD, 128), F32),
            pltpu.VMEM((6, tile, 128), F32),
            pltpu.VMEM((40, 8, d), F32),
            pltpu.VMEM((NG, GROUP, GROUP), BF16),
            pltpu.VMEM((NG, 8, GROUP), F32),
            pltpu.VMEM((NG, GROUP, GROUP), F32),
        ],
        compiler_params=params(),
        name="back",
    )(e, k, v, vl, vr, dmix, gl, gr, taps, mq, u, zt, p, gw)


def last_kernel(x_ref, dx_ref, dqf_ref, dkb_ref, dv_ref, own_ref, w_ref, gain_ref, dq_ref, dk_ref, ig_ref, dg_ref, dgacc, *, seg_len, rows_dev):
    i = pl.program_id(0)
    n = pl.num_programs(0)
    tile, d = x_ref.shape

    @pl.when(i == 0)
    def _():
        dgacc[...] = jnp.zeros_like(dgacc)

    at = i * rows_dev // 4
    scale = 1.0 / seg_len
    dq = (dqf_ref[...].astype(F32) + own_ref[pl.ds(at, 1), :] * scale).astype(BF16)
    dk = (dkb_ref[...].astype(F32) + own_ref[pl.ds(at + 4, 1), :] * scale).astype(BF16)
    dq_ref[...] = dq
    dk_ref[...] = dk
    dh = (dot_nt(dq, w_ref[0]) + dot_nt(dk, w_ref[1])) * QK_SCALE + dot_nt(dv_ref[...], w_ref[2])
    normal, inv = normalize(x_ref[...].astype(F32))
    dgacc[...] += rowsum8(dh * normal)
    ig = norm_back(dh, normal, inv, gain_ref[0:1, :]) + dx_ref[...].astype(F32)
    ig_ref[...] = ig.astype(BF16)

    @pl.when(i == n - 1)
    def _():
        dg_ref[...] = jnp.broadcast_to(jnp.sum(dgacc[...], axis=0, keepdims=True), (8, d))


def last(x, dx, dqf, dkb, dv, own, w_attn, gains, seg_len, rows_dev):
    t, d = x.shape
    tile = t // 4
    r = rows(tile, d)
    return pl.pallas_call(
        functools.partial(last_kernel, seg_len=seg_len, rows_dev=rows_dev),
        grid=(4,),
        in_specs=[r, r, r, r, r, whole((8, d)), whole(w_attn.shape), whole(gains.shape)],
        out_specs=[r, r, r, whole((8, d))],
        out_shape=[sds((t, d), BF16)] * 3 + [sds((8, d), F32)],
        scratch_shapes=[pltpu.VMEM((8, d), F32)],
        compiler_params=params(),
        name="last",
    )(x, dx, dqf, dkb, dv, own, w_attn, gains)


MESH = pl.DeviceIdType.MESH


def remote(src, dst, send, recv, where):
    return pltpu.make_async_remote_copy(
        src_ref=src, dst_ref=dst, send_sem=send, recv_sem=recv, device_id=where, device_id_type=MESH
    )


def greet(peers):
    bar = pltpu.get_barrier_semaphore()
    for peer in peers:
        pl.semaphore_signal(bar, inc=1, device_id=peer, device_id_type=MESH)
    pl.semaphore_wait(bar, len(peers))


def greet_all(me, n):
    bar = pltpu.get_barrier_semaphore()

    def hello(j, _):
        pl.semaphore_signal(bar, inc=1, device_id={"seq": lax.rem(me + j, n)}, device_id_type=MESH)
        return 0

    lax.fori_loop(1, n, hello, 0)
    pl.semaphore_wait(bar, n - 1)


def each_peer(me, n, make, act):
    def body(j, _):
        act(make(j, lax.rem(me + j, n)))
        return 0

    lax.fori_loop(1, n, body, 0)


def halo_copies(body_ref, left_ref, right_ref, me, n, sems):
    t = body_ref.shape[0]
    right = {"seq": lax.rem(me + 1, n)}
    left = {"seq": lax.rem(me + n - 1, n)}
    return (
        remote(body_ref.at[pl.ds(t - RAD, RAD)], left_ref, sems.at[0], sems.at[1], right),
        remote(body_ref.at[pl.ds(0, RAD)], right_ref, sems.at[2], sems.at[3], left),
    )


def mask_halos(left_ref, right_ref, me, n):
    left_ref[...] = jnp.where(me > 0, left_ref[...], jnp.zeros_like(left_ref))
    right_ref[...] = jnp.where(me < n - 1, right_ref[...], jnp.zeros_like(right_ref))


def marks_kernel(mean_ref, v_ref, mq_ref, mk_ref, left_ref, right_ref, pay, slots, send, recv, hsem, *, n):
    me = lax.axis_index("seq")
    d = mean_ref.shape[1]
    half = d // 2
    greet_all(me, n)
    halos = halo_copies(v_ref, left_ref, right_ref, me, n, hsem)
    pay[...] = jnp.concatenate([mean_ref[:, :half], mean_ref[:, half:]], axis=0).astype(BF16)

    def make(j, peer):
        return remote(pay, slots.at[me], send.at[j], recv.at[j], {"seq": peer})

    each_peer(me, n, make, lambda c: c.start())
    for c in halos:
        c.start()
    slots[pl.ds(me, 1)] = pay[...][None]
    each_peer(me, n, make, lambda c: c.wait())
    per = 4 * n // M
    for out, base in ((mq_ref, 0), (mk_ref, 4)):
        if per == 1:
            got = [slots[i].astype(F32) for i in range(n)]
            for h in range(2):
                tall = jnp.concatenate([x[8 * h + base : 8 * h + base + 4] for x in got], axis=0)
                out[:, h * half : (h + 1) * half] = tall.astype(BF16)
        else:
            for h in range(2):
                lines = []
                for m in range(M):
                    total = jnp.zeros((1, half), F32)
                    for s in range(per // 4):
                        part = slots[m * (per // 4) + s].astype(F32)[8 * h + base : 8 * h + base + 4]
                        total = total + jnp.sum(part, axis=0, keepdims=True)
                    lines.append(total * (1.0 / per))
                out[:, h * half : (h + 1) * half] = jnp.concatenate(lines, axis=0).astype(BF16)
    for c in halos:
        c.wait()
    mask_halos(left_ref, right_ref, me, n)


def exchange_marks(means, v, n):
    d = v.shape[1]
    vm = pl.BlockSpec(memory_space=pltpu.VMEM)
    anyw = pl.BlockSpec(memory_space=pl.ANY)
    return pl.pallas_call(
        functools.partial(marks_kernel, n=n),
        in_specs=[vm, anyw],
        out_specs=[vm] * 4,
        out_shape=[sds((M, d), BF16)] * 2 + [sds((RAD, d), BF16)] * 2,
        scratch_shapes=[
            pltpu.VMEM((16, d // 2), BF16),
            pltpu.VMEM((n, 16, d // 2), BF16),
            pltpu.SemaphoreType.DMA((n,)),
            pltpu.SemaphoreType.DMA((n,)),
            pltpu.SemaphoreType.DMA((4,)),
        ],
        compiler_params=pltpu.CompilerParams(collective_id=1, has_side_effects=True, vmem_limit_bytes=VMEM_LIMIT),
        name="exchange_marks",
    )(means, v)


def sum_kernel(x_ref, *rest, n, with_halo):
    if with_halo:
        body_ref, out_ref, left_ref, right_ref, slots, total, send, recv, send2, recv2, hsem = rest
    else:
        out_ref, slots, total, send, recv, send2, recv2 = rest
    me = lax.axis_index("seq")
    chunk = x_ref.shape[0] // n
    greet_all(me, n)

    def part(ref, i):
        return ref.at[pl.ds(pl.multiple_of(i * chunk, 8), chunk)]

    def first(j, peer):
        return remote(part(x_ref, peer), slots.at[me], send.at[j], recv.at[j], {"seq": peer})

    def second(j, peer):
        return remote(total, part(out_ref, me), send2.at[j], recv2.at[j], {"seq": peer})

    each_peer(me, n, first, lambda c: c.start())
    if with_halo:
        halos = halo_copies(body_ref, left_ref, right_ref, me, n, hsem)
        for c in halos:
            c.start()
    here = pl.ds(pl.multiple_of(me * chunk, 8), chunk)
    slots[pl.ds(me, 1)] = x_ref[here, :][None]
    each_peer(me, n, first, lambda c: c.wait())

    def add(i, acc):
        return acc + slots[i]

    summed = lax.fori_loop(1, n, add, slots[0])
    total[...] = summed
    each_peer(me, n, second, lambda c: c.start())
    out_ref[here, :] = summed
    each_peer(me, n, second, lambda c: c.wait())
    if with_halo:
        for c in halos:
            c.wait()
        mask_halos(left_ref, right_ref, me, n)


def padded_rows(r, n):
    return -(-r // (8 * n)) * 8 * n


def sum_over_seq(x, n, ident, body=None):
    r = x.shape[0]
    vm = pl.BlockSpec(memory_space=pltpu.VMEM)
    anyw = pl.BlockSpec(memory_space=pl.ANY)
    with_halo = body is not None
    out_shape = [sds((r, 128), F32)]
    if with_halo:
        out_shape += [sds((RAD, body.shape[1]), BF16)] * 2
    dma = pltpu.SemaphoreType.DMA
    res = pl.pallas_call(
        functools.partial(sum_kernel, n=n, with_halo=with_halo),
        in_specs=[vm] + [anyw] * with_halo,
        out_specs=[vm] * len(out_shape),
        out_shape=out_shape,
        scratch_shapes=[pltpu.VMEM((n, r // n, 128), F32), pltpu.VMEM((r // n, 128), F32)]
        + [dma((n,))] * 4
        + [dma((4,))] * with_halo,
        compiler_params=pltpu.CompilerParams(collective_id=ident, has_side_effects=True, vmem_limit_bytes=VMEM_LIMIT),
        name="sum_over_seq",
    )(*((x, body) if with_halo else (x,)))
    return res if with_halo else res[0]


def own_kernel(dq_ref, dk_ref, dqa_ref, dka_ref, out_ref, pay, slots, send, recv, *, n):
    me = lax.axis_index("seq")
    rows_dev = max(M // n, 1)
    per_mark = n * rows_dev // M
    dq = dq_ref[...] + dqa_ref[...]
    dk = dk_ref[...] + dka_ref[...]
    if rows_dev < 4:
        pay[...] = jnp.zeros_like(pay)
    for i in range(n):
        at = i * rows_dev // per_mark
        pay[i, 0:rows_dev, :] = dq[at : at + rows_dev]
        pay[i, 4 : 4 + rows_dev, :] = dk[at : at + rows_dev]
    greet_all(me, n)

    def make(j, peer):
        return remote(pay.at[peer], slots.at[me], send.at[j], recv.at[j], {"seq": peer})

    each_peer(me, n, make, lambda c: c.start())
    slots[pl.ds(me, 1)] = pay[pl.ds(me, 1)]
    each_peer(me, n, make, lambda c: c.wait())
    out_ref[...] = lax.fori_loop(1, n, lambda i, acc: acc + slots[i], slots[0])


def own_marks(dq, dk, dqa, dka, n):
    d = dq.shape[1]
    vm = pl.BlockSpec(memory_space=pltpu.VMEM)
    return pl.pallas_call(
        functools.partial(own_kernel, n=n),
        in_specs=[vm] * 4,
        out_specs=vm,
        out_shape=sds((8, d), F32),
        scratch_shapes=[
            pltpu.VMEM((n, 8, d), F32),
            pltpu.VMEM((n, 8, d), F32),
            pltpu.SemaphoreType.DMA((n,)),
            pltpu.SemaphoreType.DMA((n,)),
        ],
        compiler_params=pltpu.CompilerParams(collective_id=4, has_side_effects=True, vmem_limit_bytes=VMEM_LIMIT),
        name="own_marks",
    )(dq, dk, dqa, dka)


RING = 16


def ring_pos(seq):
    x = lax.rem(seq, 2)
    y = lax.rem(lax.div(seq, 2), 2)
    z = lax.div(seq, 4)
    col = x * 3 + y * (1 - 2 * x)
    return col * 4 + z + lax.rem(col, 2) * (3 - 2 * z)


def ring_seq(pos):
    pos = lax.rem(pos + 2 * RING, RING)
    col = lax.div(pos, 4)
    zz = lax.rem(pos, 4)
    z = zz + lax.rem(col, 2) * (3 - 2 * zz)
    x = lax.div(col, 2)
    y = lax.rem(lax.div(col + 1, 2), 2)
    return z * 4 + y * 2 + x


def at(i, size, unit):
    return pl.ds(pl.multiple_of(i * size, unit), size)


def piece(kind, ref, seq, rep):
    if kind == 0:
        half = ref.shape[2] // 2
        return ref.at[:, at(seq, ref.shape[1] // RING, 16), at(rep, half, 128)]
    if kind == 1:
        half = ref.shape[1] // 2
        return ref.at[at(seq, ref.shape[0] // RING, 16), at(rep, half, 128)]
    return ref.at[at(seq * 2 + rep, ref.shape[0] // (2 * RING), 8 if kind == 3 else 16), :]


def gather_kernel(wa, wu, wd, wv, oa, ou, od, ov, sa, su, ca, cu, cd, psem, lsem, send, recv, ssend, srecv):
    seq = lax.axis_index("seq")
    rep = lax.axis_index("rep")
    pos = ring_pos(seq)
    right, left, twin = {"seq": ring_seq(pos + 1)}, {"seq": ring_seq(pos - 1)}, {"rep": 1 - rep}
    greet([right, left, twin])
    ra, ru = wa.shape[1], wu.shape[0]
    ha, hu = wa.shape[2] // 2, wu.shape[1] // 2
    mine_a, mine_u = at(rep, ra, 8), at(rep, ru, 8)
    swap = (
        remote(wa.at[:, :, at(1 - rep, ha, 128)], sa.at[:, mine_a, :], psem.at[0], psem.at[1], twin),
        remote(wu.at[:, at(1 - rep, hu, 128)], su.at[mine_u, :], psem.at[2], psem.at[3], twin),
    )
    for c in swap:
        c.start()
    sa[:, mine_a, :] = wa[:, :, at(rep, ha, 128)]
    su[mine_u, :] = wu[:, at(rep, hu, 128)]
    cd[...] = wd[...].astype(BF16)
    for c in swap:
        c.wait()
    ca[...] = sa[...].astype(BF16)
    cu[...] = su[...].astype(BF16)
    outs = (oa, ou, od, ov)
    own = (ca, cu, cd, wv)
    where = (right, left)
    local = [pltpu.make_async_copy(own[k], piece(k, outs[k], seq, rep), lsem.at[k]) for k in range(4)]

    def origin(way, s):
        return ring_seq(pos - s) if way == 0 else ring_seq(pos + s)

    def hop(way, s, k, src=None):
        block = piece(k, outs[k], origin(way, s), rep)
        return remote(block if src is None else src, block, send.at[way, s, k], recv.at[way, s, k], where[way])

    def share(way, s, k, src=None):
        block = piece(k, outs[k], origin(way, s), rep)
        return remote(block if src is None else src, block, ssend.at[way, s, k], srecv.at[way, s, k], twin)

    def share_in(way, s, k):
        block = piece(k, outs[k], origin(way, s), 1 - rep)
        return remote(block, block, ssend.at[way, s, k], srecv.at[way, s, k], twin)

    for k in range(4):
        hop(0, 0, k, own[k]).start()
        hop(1, 0, k, own[k]).start()
        share(0, 0, k, own[k]).start()
        local[k].start()

    def step(s, _):
        for k in range(4):
            for way in range(2):
                last = 8 if way == 0 else 7

                @pl.when(s <= last)
                def _():
                    block = piece(k, outs[k], origin(way, s), rep)
                    remote(block, block, send.at[way, s - 1, k], recv.at[way, s - 1, k], where[way]).wait_recv()

                    @pl.when(s < last)
                    def _():
                        hop(way, s, k).start()

                    share(way, s, k).start()
        return 0

    lax.fori_loop(1, 9, step, 0)
    for k in range(4):
        local[k].wait()
        hop(0, 0, k, own[k]).wait_send()
        hop(1, 0, k, own[k]).wait_send()
        share(0, 0, k, own[k]).wait_send()
        share_in(0, 0, k).wait_recv()

    def finish(s, _):
        for k in range(4):
            for way in range(2):
                last = 8 if way == 0 else 7

                @pl.when(s <= last)
                def _():
                    @pl.when(s < last)
                    def _():
                        hop(way, s, k).wait_send()

                    share(way, s, k).wait_send()
                    share_in(way, s, k).wait_recv()

        return 0

    lax.fori_loop(1, 9, finish, 0)


def gather_weights(wa, wu, wd, wv):
    d = wa.shape[2]
    ff = wu.shape[1]
    vm = pl.BlockSpec(memory_space=pltpu.VMEM)
    anyw = pl.BlockSpec(memory_space=pl.ANY)
    dma = pltpu.SemaphoreType.DMA
    return pl.pallas_call(
        gather_kernel,
        in_specs=[vm] * 4,
        out_specs=[anyw] * 4,
        out_shape=[sds((4, d, d), BF16), sds((d, ff), BF16), sds((ff, d), BF16), sds((d, 128), F32)],
        scratch_shapes=[
            pltpu.VMEM((4, d // RING, d // 2), F32),
            pltpu.VMEM((d // RING, ff // 2), F32),
            pltpu.VMEM((4, d // RING, d // 2), BF16),
            pltpu.VMEM((d // RING, ff // 2), BF16),
            pltpu.VMEM((ff // (2 * RING), d), BF16),
            dma((4,)),
            dma((4,)),
            dma((2, 9, 4)),
            dma((2, 9, 4)),
            dma((2, 9, 4)),
            dma((2, 9, 4)),
        ],
        compiler_params=pltpu.CompilerParams(collective_id=5, has_side_effects=True, vmem_limit_bytes=VMEM_LIMIT),
        name="gather_weights",
    )(wa, wu, wd, wv)


def adam_refs(grad, w, m, v, wo, mo, vo, rate):
    moment = BETA_ONE * m[...] + (1.0 - BETA_ONE) * grad
    second = BETA_TWO * v[...] + (1.0 - BETA_TWO) * grad * grad
    first_hat = moment * (1.0 / (1.0 - BETA_ONE**STEP))
    second_hat = second * (1.0 / (1.0 - BETA_TWO**STEP))
    wo[...] = w[...] - rate * (first_hat / (jnp.sqrt(second_hat) + ADAM_EPS) + DECAY_RATE * w[...])
    mo[...] = moment
    vo[...] = second


def scatter_kernel(
    ga, gu, gd, gv, *rest
):
    state, rest = rest[:12], rest[12:]
    news, rest = rest[:12], rest[12:]
    mine, rest = rest[:4], rest[4:]
    twins, rest = rest[:4], rest[4:]
    inbox, rest = rest[:4], rest[4:]
    first, rest = rest[:4], rest[4:]
    fa, fu, lsem, tsend, trecv, send, recv, fsem = rest
    grads = (ga, gu, gd, gv)
    seq = lax.axis_index("seq")
    rep = lax.axis_index("rep")
    pos = ring_pos(seq)
    right, left, twin = {"seq": ring_seq(pos + 1)}, {"seq": ring_seq(pos - 1)}, {"rep": 1 - rep}
    where = (left, right)
    greet([right, left, twin])

    def chip(j):
        return ring_seq(pos + 8 - j)

    def load(j, k):
        return pltpu.make_async_copy(piece(k, grads[k], chip(j), rep), mine[k].at[j], lsem.at[j, k])

    def give(j, k):
        return remote(piece(k, grads[k], chip(j), 1 - rep), twins[k].at[j], tsend.at[j, k], trecv.at[j, k], twin)

    def start_all(j, _):
        for k in range(4):
            for jj in (j, 15 - j):
                give(jj, k).start()
                load(jj, k).start()
        return 0

    lax.fori_loop(0, 8, start_all, 0)

    def slot(way, s):
        return lax.rem(17 - s, RING) if way == 0 else s

    def hop(way, s, k, src):
        return remote(src, inbox[k].at[way, s], send.at[way, s, k], recv.at[way, s, k], where[way])

    def ready(j, k):
        load(j, k).wait()
        give(j, k).wait()

    def one(way, s, k):
        j = slot(way, s)
        ready(j, k)
        own = mine[k][pl.ds(j, 1)].astype(F32) + twins[k][pl.ds(j, 1)].astype(F32)

        @pl.when(s == 1)
        def _():
            first[k][pl.ds(way, 1)] = own.astype(first[k].dtype)
            hop(way, 1, k, first[k].at[way]).start()

        @pl.when(s > 1)
        def _():
            hop(way, s - 1, k, first[k].at[way]).wait_recv()
            box = inbox[k].at[way]
            box[pl.ds(s - 1, 1)] = (own + box[pl.ds(s - 1, 1)].astype(F32)).astype(first[k].dtype)
            hop(way, s, k, inbox[k].at[way, s - 1]).start()

    def step(s, _):
        for k in range(4):
            one(0, s, k)

            @pl.when(s < 8)
            def _():
                one(1, s, k)

        return 0

    lax.fori_loop(1, 9, step, 0)
    sums = []
    for k in range(4):
        ready(8, k)
        hop(0, 8, k, first[k].at[0]).wait_recv()
        hop(1, 7, k, first[k].at[1]).wait_recv()
        sums.append(
            (mine[k][8].astype(F32) + twins[k][8].astype(F32))
            + (inbox[k][0, 8].astype(F32) + inbox[k][1, 7].astype(F32))
        )
    w, m, v = state[0::3], state[1::3], state[2::3]
    wo, mo, vo = news[0::3], news[1::3], news[2::3]
    ra, ru = w[0].shape[1], w[1].shape[0]
    ha, hu = w[0].shape[2] // 2, w[1].shape[1] // 2
    fa[0] = sums[0]
    fu[0] = sums[1]
    back = (
        remote(fa.at[0, :, at(1 - rep, ra, 8), :], fa.at[1, :, at(1 - rep, ra, 8), :], fsem.at[0], fsem.at[1], twin),
        remote(fu.at[0, at(1 - rep, ru, 8), :], fu.at[1, at(1 - rep, ru, 8), :], fsem.at[2], fsem.at[3], twin),
    )
    for c in back:
        c.start()
    adam_refs(sums[2], w[2], m[2], v[2], wo[2], mo[2], vo[2], LEARN_RATE)
    adam_refs(sums[3], w[3], m[3], v[3], wo[3], mo[3], vo[3], VECTOR_RATE)
    for c in back:
        c.wait()
    mine_a, mine_u = at(rep, ra, 8), at(rep, ru, 8)
    for side in range(2):
        ca, cu = pl.ds(side * ha, ha), pl.ds(side * hu, hu)
        pick = jnp.where(rep == side, 0, 1)
        for q in range(4):
            adam_refs(fa[pick, q, mine_a, :], *(r.at[q, :, ca] for r in (w[0], m[0], v[0], wo[0], mo[0], vo[0])), LEARN_RATE)
        adam_refs(fu[pick, mine_u, :], *(r.at[:, cu] for r in (w[1], m[1], v[1], wo[1], mo[1], vo[1])), LEARN_RATE)

    def done(s, _):
        for k in range(4):
            hop(0, s, k, first[k].at[0]).wait_send()

            @pl.when(s < 8)
            def _():
                hop(1, s, k, first[k].at[1]).wait_send()

        return 0

    lax.fori_loop(1, 9, done, 0)


def scatter_step(ga, gu, gd, gv, state):
    d = ga.shape[2]
    ff = gu.shape[1]
    vm = pl.BlockSpec(memory_space=pltpu.VMEM)
    anyw = pl.BlockSpec(memory_space=pl.ANY)
    dma = pltpu.SemaphoreType.DMA
    blocks = [((4, d // RING, d // 2), BF16), ((d // RING, ff // 2), BF16), ((ff // (2 * RING), d), BF16), ((d // (2 * RING), 128), F32)]
    return pl.pallas_call(
        scatter_kernel,
        in_specs=[anyw] * 4 + [vm] * 12,
        out_specs=[vm] * 12,
        out_shape=[sds(x.shape, F32) for x in state],
        scratch_shapes=[pltpu.VMEM((RING, *s), t) for s, t in blocks]
        + [pltpu.VMEM((RING, *s), t) for s, t in blocks]
        + [pltpu.VMEM((2, 9, *s), t) for s, t in blocks]
        + [pltpu.VMEM((2, *s), t) for s, t in blocks]
        + [pltpu.VMEM((2, *blocks[0][0]), F32), pltpu.VMEM((2, *blocks[1][0]), F32)]
        + [dma((RING, 4)), dma((RING, 4)), dma((RING, 4)), dma((2, 9, 4)), dma((2, 9, 4)), dma((4,))],
        compiler_params=pltpu.CompilerParams(collective_id=6, has_side_effects=True, vmem_limit_bytes=VMEM_LIMIT),
        name="scatter_step",
    )(ga, gu, gd, gv, *state)


def stack_tall(x):
    return jnp.concatenate([x[:, c : c + 128] for c in range(0, x.shape[1], 128)], axis=0)


def unstack(x, k):
    return jnp.concatenate([x[c * M : (c + 1) * M] for c in range(k)], axis=1)


def pad_rows(x, r):
    return jnp.pad(x, ((0, r - x.shape[0]), (0, 0))) if r > x.shape[0] else x


def adam_step(weight, grad_vec, moment, second, rate_value):
    moment_new = BETA_ONE * moment + (1.0 - BETA_ONE) * grad_vec
    second_new = BETA_TWO * second + (1.0 - BETA_TWO) * grad_vec * grad_vec
    first_hat = moment_new / (1.0 - BETA_ONE**STEP)
    second_hat = second_new / (1.0 - BETA_TWO**STEP)
    weight_new = weight - rate_value * (
        first_hat / (jnp.sqrt(second_hat) + ADAM_EPS) + DECAY_RATE * weight
    )
    return (weight_new, moment_new, second_new)


def per_device(tokens, cotangent, attn_w, w_up, w_down, vectors, attn_m, attn_v, up_m, up_v, down_m, down_v, vec_m, vec_v):
    both = ("seq", "rep")
    x = tokens[0]
    dy = cotangent[0]
    t, d = x.shape
    n = lax.axis_size("seq")
    rows_dev = max(M // n, 1)
    seg_len = t * n // M
    ring = n == RING and lax.axis_size("rep") == 2

    if ring:
        wide = [jnp.pad(a, ((0, 0), (0, 128 - a.shape[1]))) for a in (vectors, vec_m, vec_v)]
        w_attn, up, down, vec = gather_weights(attn_w, w_up, w_down, wide[0])
        vec = vec.astype(BF16)
    else:
        w_attn = lax.all_gather(attn_w.astype(BF16), both, axis=1, tiled=True)
        up = lax.all_gather(w_up.astype(BF16), both, axis=0, tiled=True)
        down = lax.all_gather(w_down.astype(BF16), both, axis=0, tiled=True)
        vec = lax.all_gather(vectors.astype(BF16), both, axis=0, tiled=True)
    vec_t = jnp.transpose(vec.astype(F32))
    gains = jnp.concatenate([vec_t[:2], jnp.zeros((6, d), F32)], axis=0)
    taps = jnp.concatenate([vec_t[2 : 2 + KC], jnp.zeros((7, d), F32)], axis=0)

    h1, q, k, v, means = project(x, w_attn, gains)
    mq, mk, vl, vr = exchange_marks(means, v, n)
    f, e, u, zt = attend(q, k, v, mq, mk)
    a, p, zs, azs, t2s, t3s = pinv(mq, mk)
    r = padded_rows(7 * M, n)
    uz = sum_over_seq(pad_rows(jnp.concatenate([stack_tall(u), zt], axis=0), r), n, 2)
    u, zt = unstack(uz, 6), uz[6 * M : 7 * M]
    out, act, da, h2, mix, dx, dmix, dqf, gw, dkt, dg2 = middle(
        x, dy, f, q, v, vl, vr, w_attn[3], up, down, gains, taps, mk, u, zt, p
    )
    r = padded_rows(6 * M, n)
    gw, gl, gr = sum_over_seq(pad_rows(stack_tall(gw), r), n, 3, dmix)
    gw = unstack(gw, 6)
    dot_xla = functools.partial(jnp.einsum, "ta,tb->ab", preferred_element_type=F32)
    g_down = dot_xla(act, dy).astype(BF16)
    g_up = dot_xla(h2, da).astype(BF16)
    g_o = dot_xla(mix, dx)
    dqt_a, dkt_a = pinv_back(mq, mk, (a, p, zs, azs, t2s, t3s), gw, u, zt, 1.0 / n)
    dv, dkb, dqt, dtap = back(e, k, v, vl, vr, dmix, gl, gr, taps, mq, u, zt, p, gw)
    own = own_marks(dqt, dkt, dqt_a, dkt_a, n)
    dq, dk, ig, dg1 = last(x, dx, dqf, dkb, dv, own, w_attn, gains, seg_len, rows_dev)
    g_q = dot_xla(h1, dq) * QK_SCALE
    g_k = dot_xla(h1, dk) * QK_SCALE
    g_v = dot_xla(h1, dv)
    g_attn = jnp.stack([g_q, g_k, g_v, g_o]).astype(BF16)
    g_vec = jnp.concatenate([dg1[:1], dg2[:1], dtap[:KC]], axis=0)
    if ring:
        g_vec = jnp.transpose(pad_rows(g_vec, 128))
        state = (attn_w, attn_m, attn_v, w_up, up_m, up_v, w_down, down_m, down_v, *wide)
        news = scatter_step(g_attn, g_up, g_down, g_vec, state)
        news = tuple(news[:9]) + tuple(a[:, : vectors.shape[1]] for a in news[9:])
    else:
        red_attn = lax.psum_scatter(g_attn, both, scatter_dimension=1, tiled=True).astype(F32)
        red_up = lax.psum_scatter(g_up, both, scatter_dimension=0, tiled=True).astype(F32)
        red_down = lax.psum_scatter(g_down, both, scatter_dimension=0, tiled=True).astype(F32)
        red_vec = lax.psum_scatter(jnp.transpose(g_vec), both, scatter_dimension=0, tiled=True)
        news = (
            *adam_step(attn_w, red_attn, attn_m, attn_v, LEARN_RATE),
            *adam_step(w_up, red_up, up_m, up_v, LEARN_RATE),
            *adam_step(w_down, red_down, down_m, down_v, LEARN_RATE),
            *adam_step(vectors, red_vec, vec_m, vec_v, VECTOR_RATE),
        )
    return (out[None], ig[None], *news)


def solution(mesh):
    tok = P("rep", "seq", None)
    att = P(None, ("seq", "rep"), None)
    mat = P(("seq", "rep"), None)
    return jax.shard_map(
        per_device,
        mesh=mesh,
        in_specs=(tok, tok, att, mat, mat, mat, att, att, mat, mat, mat, mat, mat, mat),
        out_specs=(tok, tok, att, att, att) + (mat,) * 9,
        check_vma=False,
    )
```

```python
import functools

import jax
import jax.numpy as jnp
from jax import lax
from jax.experimental import pallas as pl
from jax.experimental.pallas import tpu as pltpu
from jax.sharding import PartitionSpec as P

H = 12
HD = 64
M = 64
KC = 33
NSITER = 6
STEP = 10
EPS_NORM = 1e-05
BETA_ONE = 0.9
BETA_TWO = 0.999
ADAM_EPS = 1e-08
LEARN_RATE = 0.03
VECTOR_RATE = 0.15
DECAY_RATE = 0.1

F32 = jnp.float32
BF16 = jnp.bfloat16
GROUP = 256
NG = 3
RAD = 16
QK_SCALE = HD ** (-0.25)
HI = lax.Precision.HIGHEST
VMEM_LIMIT = 58 * 1024 * 1024


def dot(a, b, precision=None):
    return lax.dot_general(a, b, (((1,), (0,)), ((), ())), precision=precision, preferred_element_type=F32)


def dot_nt(a, b, precision=None):
    return lax.dot_general(a, b, (((1,), (1,)), ((), ())), precision=precision, preferred_element_type=F32)


def dot_tn(a, b, precision=None):
    return lax.dot_general(a, b, (((0,), (0,)), ((), ())), precision=precision, preferred_element_type=F32)


def head_mask(shape=(GROUP, GROUP)):
    rows = lax.broadcasted_iota(jnp.int32, shape, 0)
    cols = lax.broadcasted_iota(jnp.int32, shape, 1)
    return lax.shift_right_logical(rows, 6) == lax.shift_right_logical(cols, 6)


def spread(wide):
    tall = jnp.concatenate([wide, wide, wide, wide], axis=0)
    return jnp.where(head_mask(), tall, jnp.zeros_like(tall))


def collect(full):
    kept = jnp.where(head_mask(), full, jnp.zeros_like(full))
    return (kept[0:64] + kept[64:128]) + (kept[128:192] + kept[192:256])


def flip(wide):
    turned = jnp.transpose(spread(wide))
    return (turned[0:64] + turned[64:128]) + (turned[128:192] + turned[192:256])


def gs(g):
    return slice(g * GROUP, (g + 1) * GROUP)


def half_reduce(x, op, init):
    parts = []
    for c in range(x.shape[1] // 128):
        col = x[:, c * 128 : (c + 1) * 128]
        low = lax.broadcasted_iota(jnp.int32, col.shape, 1) < 64
        a = op(jnp.where(low, col, init), axis=1, keepdims=True)
        b = op(jnp.where(low, init, col), axis=1, keepdims=True)
        parts.append(jnp.where(low, a, b))
    return jnp.concatenate(parts, axis=1)


def normalize(x):
    center = x - jnp.mean(x, axis=-1, keepdims=True)
    inv = lax.rsqrt(jnp.mean(center * center, axis=-1, keepdims=True) + EPS_NORM)
    return center * inv, inv


def norm_back(up, normal, inv, gain):
    scaled = up * gain
    centered = scaled - jnp.mean(scaled, axis=-1, keepdims=True)
    return inv * (centered - normal * jnp.mean(scaled * normal, axis=-1, keepdims=True))


def rowsum8(x):
    return jnp.sum(x.reshape(x.shape[0] // 8, 8, x.shape[1]), axis=0)


def gelu_parts(a):
    z = jnp.abs(a)
    t = 1.0 / (1.0 + (0.3275911 * 0.7071067811865476) * z)
    e = jnp.exp(-0.5 * a * a)
    poly = t * (0.127414796 + t * (-0.142248368 + t * (0.7107068705 + t * (-0.7265760135 + t * 0.5307027145))))
    tail = poly * e
    phi = jnp.where(a >= 0, 1.0 - tail, tail)
    return a * phi, phi + a * (e * 0.3989422804014327)


def whole(shape):
    zeros = (0,) * len(shape)
    return pl.BlockSpec(shape, lambda i: zeros, pipeline_mode=pl.Buffered(1))


def rows(tile, width):
    return pl.BlockSpec((tile, width), lambda i: (i, 0))


def sds(shape, dtype):
    return jax.ShapeDtypeStruct(shape, dtype)


def params():
    return pltpu.CompilerParams(dimension_semantics=("arbitrary",), vmem_limit_bytes=VMEM_LIMIT)


def widen(zt, g):
    return jnp.concatenate(
        [jnp.broadcast_to(zt[:, h : h + 1], (M, HD)) for h in range(4 * g, 4 * g + 4)], axis=1
    )


def u_group(ref, g):
    return jnp.concatenate([ref[2 * g * M : (2 * g + 1) * M, :], ref[(2 * g + 1) * M : (2 * g + 2) * M, :]], axis=1)


def zt_group(ref, g):
    return widen(ref[6 * M : 7 * M, :], g)


def put_tall(ref, g, wide):
    ref[2 * g * M : (2 * g + 1) * M, :] = wide[:, :128]
    ref[(2 * g + 1) * M : (2 * g + 2) * M, :] = wide[:, 128:]


def padded_rows(r, n):
    return -(-r // (8 * n)) * 8 * n


MESH = pl.DeviceIdType.MESH
DMA = pltpu.SemaphoreType.DMA
VM = pl.BlockSpec(memory_space=pltpu.VMEM)
ANYW = pl.BlockSpec(memory_space=pl.ANY)


def remote(src, dst, send, recv, where):
    return pltpu.make_async_remote_copy(
        src_ref=src, dst_ref=dst, send_sem=send, recv_sem=recv, device_id=where, device_id_type=MESH
    )


def greet(me, n, others):
    bar = pltpu.get_barrier_semaphore()

    def hello(j, _):
        pl.semaphore_signal(bar, inc=1, device_id={"seq": lax.rem(me + j, n)}, device_id_type=MESH)
        return 0

    lax.fori_loop(1, n, hello, 0)
    for peer in others:
        pl.semaphore_signal(bar, inc=1, device_id=peer, device_id_type=MESH)
    pl.semaphore_wait(bar, n - 1 + len(others))


def each_peer(me, n, make, act):
    def body(j, _):
        act(make(j, lax.rem(me + j, n)))
        return 0

    lax.fori_loop(1, n, body, 0)


def halo_copies(body_ref, left_ref, right_ref, me, n, sems):
    t = body_ref.shape[0]
    right = {"seq": lax.rem(me + 1, n)}
    left = {"seq": lax.rem(me + n - 1, n)}
    return (
        remote(body_ref.at[pl.ds(t - RAD, RAD)], left_ref, sems.at[0], sems.at[1], right),
        remote(body_ref.at[pl.ds(0, RAD)], right_ref, sems.at[2], sems.at[3], left),
    )


def mask_halos(left_ref, right_ref, me, n):
    left_ref[...] = jnp.where(me > 0, left_ref[...], jnp.zeros_like(left_ref))
    right_ref[...] = jnp.where(me < n - 1, right_ref[...], jnp.zeros_like(right_ref))


class SeqSum:
    def __init__(self, me, n, x, out, slots, total, sems):
        self.me, self.n, self.x, self.out, self.slots, self.total, self.sems = me, n, x, out, slots, total, sems
        self.chunk = x.shape[0] // n
        self.here = pl.ds(pl.multiple_of(me * self.chunk, 8), self.chunk)

    def first(self, j, peer):
        src = self.x.at[pl.ds(pl.multiple_of(peer * self.chunk, 8), self.chunk)]
        return remote(src, self.slots.at[self.me], self.sems.at[0, j], self.sems.at[1, j], {"seq": peer})

    def second(self, j, peer):
        return remote(self.total, self.out.at[self.here], self.sems.at[2, j], self.sems.at[3, j], {"seq": peer})

    def start(self):
        each_peer(self.me, self.n, self.first, lambda c: c.start())
        self.slots[pl.ds(self.me, 1)] = self.x[self.here, :][None]

    def turn(self):
        each_peer(self.me, self.n, self.first, lambda c: c.wait())
        summed = lax.fori_loop(1, self.n, lambda i, acc: acc + self.slots[i], self.slots[0])
        self.total[...] = summed
        each_peer(self.me, self.n, self.second, lambda c: c.start())
        self.out[self.here, :] = summed

    def finish(self):
        each_peer(self.me, self.n, self.second, lambda c: c.wait())

    @staticmethod
    def scratch(r, n):
        return [pltpu.VMEM((n, r // n, 128), F32), pltpu.VMEM((r // n, 128), F32), DMA((4, n))]


RING = 16


def ring_pos(seq):
    x = lax.rem(seq, 2)
    y = lax.rem(lax.div(seq, 2), 2)
    z = lax.div(seq, 4)
    col = x * 3 + y * (1 - 2 * x)
    return col * 4 + z + lax.rem(col, 2) * (3 - 2 * z)


def ring_seq(pos):
    pos = lax.rem(pos + 2 * RING, RING)
    col = lax.div(pos, 4)
    zz = lax.rem(pos, 4)
    z = zz + lax.rem(col, 2) * (3 - 2 * zz)
    x = lax.div(col, 2)
    y = lax.rem(lax.div(col + 1, 2), 2)
    return z * 4 + y * 2 + x


def at(i, size, unit):
    return pl.ds(pl.multiple_of(i * size, unit), size)


STACK, HALF, ROWS, LINES = range(4)


def piece(kind, ref, seq, rep):
    if kind == STACK:
        half = ref.shape[2] // 2
        return ref.at[:, at(seq, ref.shape[1] // RING, 16), at(rep, half, 128)]
    if kind == HALF:
        half = ref.shape[1] // 2
        return ref.at[at(seq, ref.shape[0] // RING, 16), at(rep, half, 128)]
    return ref.at[at(seq * 2 + rep, ref.shape[0] // (2 * RING), 8 if kind == LINES else 16), :]


class Place:
    def __init__(self):
        self.seq = lax.axis_index("seq")
        self.rep = lax.axis_index("rep")
        self.pos = ring_pos(self.seq)
        self.right = {"seq": ring_seq(self.pos + 1)}
        self.left = {"seq": ring_seq(self.pos - 1)}
        self.twin = {"rep": 1 - self.rep}


class GatherRing:
    def __init__(self, place, kinds, outs, own, sems):
        self.place, self.kinds, self.outs, self.own = place, kinds, outs, own
        self.send, self.recv, self.ssend, self.srecv = sems
        self.where = (place.right, place.left)

    def block(self, way, s, k, rep):
        p = self.place
        origin = ring_seq(p.pos - s) if way == 0 else ring_seq(p.pos + s)
        return piece(self.kinds[k], self.outs[k], origin, rep)

    def hop(self, way, s, k, src=None):
        b = self.block(way, s, k, self.place.rep)
        return remote(b if src is None else src, b, self.send.at[way, s, k], self.recv.at[way, s, k], self.where[way])

    def arrival(self, way, s, k):
        b = self.block(way, s, k, self.place.rep)
        return remote(b, b, self.send.at[way, s - 1, k], self.recv.at[way, s - 1, k], self.where[way])

    def share(self, way, s, k, src=None):
        b = self.block(way, s, k, self.place.rep)
        return remote(b if src is None else src, b, self.ssend.at[way, s, k], self.srecv.at[way, s, k], self.place.twin)

    def shared(self, way, s, k):
        b = self.block(way, s, k, 1 - self.place.rep)
        return remote(b, b, self.ssend.at[way, s, k], self.srecv.at[way, s, k], self.place.twin)

    def start(self):
        for k in range(len(self.kinds)):
            self.hop(0, 0, k, self.own[k]).start()
            self.hop(1, 0, k, self.own[k]).start()
            self.share(0, 0, k, self.own[k]).start()

    def step(self, s):
        for k in range(len(self.kinds)):
            for way in range(2):
                last = 8 - way

                @pl.when(s <= last)
                def _():
                    self.arrival(way, s, k).wait_recv()

                    @pl.when(s < last)
                    def _():
                        self.hop(way, s, k).start()

                    self.share(way, s, k).start()

    def finish(self):
        for k in range(len(self.kinds)):
            self.hop(0, 0, k, self.own[k]).wait_send()
            self.hop(1, 0, k, self.own[k]).wait_send()
            self.share(0, 0, k, self.own[k]).wait_send()
            self.shared(0, 0, k).wait_recv()

        def body(s, _):
            for k in range(len(self.kinds)):
                for way in range(2):
                    last = 8 - way

                    @pl.when(s <= last)
                    def _():
                        @pl.when(s < last)
                        def _():
                            self.hop(way, s, k).wait_send()

                        self.share(way, s, k).wait_send()
                        self.shared(way, s, k).wait_recv()

            return 0

        lax.fori_loop(1, 9, body, 0)

    @staticmethod
    def scratch(k):
        return [DMA((2, 9, k))] * 4


class ScatterRing:
    def __init__(self, place, kinds, grads, mine, twins, inbox, first, sems):
        self.place, self.kinds, self.grads = place, kinds, grads
        self.mine, self.twins, self.inbox, self.opening = mine, twins, inbox, first
        self.lsem, self.tsend, self.trecv, self.send, self.recv = sems
        self.where = (place.left, place.right)

    def load(self, j, k):
        src = piece(self.kinds[k], self.grads[k], ring_seq(self.place.pos + 8 - j), self.place.rep)
        return pltpu.make_async_copy(src, self.mine[k].at[j], self.lsem.at[j, k])

    def give(self, j, k):
        src = piece(self.kinds[k], self.grads[k], ring_seq(self.place.pos + 8 - j), 1 - self.place.rep)
        return remote(src, self.twins[k].at[j], self.tsend.at[j, k], self.trecv.at[j, k], self.place.twin)

    def hop(self, way, s, k, src):
        return remote(src, self.inbox[k].at[way, s], self.send.at[way, s, k], self.recv.at[way, s, k], self.where[way])

    def start(self):
        def body(j, _):
            for k in range(len(self.kinds)):
                for jj in (j, 15 - j):
                    self.give(jj, k).start()
                    self.load(jj, k).start()
            return 0

        lax.fori_loop(0, 8, body, 0)

    def terms(self, j, k):
        self.load(j, k).wait()
        self.give(j, k).wait()
        return self.mine[k][pl.ds(j, 1)].astype(F32) + self.twins[k][pl.ds(j, 1)].astype(F32)

    def one(self, way, s, k):
        own = self.terms(lax.rem(17 - s, RING) if way == 0 else s, k)
        first = self.opening[k]

        @pl.when(s == 1)
        def _():
            first[pl.ds(way, 1)] = own.astype(first.dtype)
            self.hop(way, 1, k, first.at[way]).start()

        @pl.when(s > 1)
        def _():
            self.hop(way, s - 1, k, first.at[way]).wait_recv()
            box = self.inbox[k].at[way]
            box[pl.ds(s - 1, 1)] = (own + box[pl.ds(s - 1, 1)].astype(F32)).astype(first.dtype)
            self.hop(way, s, k, self.inbox[k].at[way, s - 1]).start()

    def step(self, s):
        for k in range(len(self.kinds)):
            self.one(0, s, k)

            @pl.when(s < 8)
            def _():
                self.one(1, s, k)

    def total(self, k):
        own = self.terms(8, k)[0]
        first = self.opening[k]
        self.hop(0, 8, k, first.at[0]).wait_recv()
        self.hop(1, 7, k, first.at[1]).wait_recv()
        return own + (self.inbox[k][0, 8].astype(F32) + self.inbox[k][1, 7].astype(F32))

    def finish(self):
        def body(s, _):
            for k in range(len(self.kinds)):
                self.hop(0, s, k, self.opening[k].at[0]).wait_send()

                @pl.when(s < 8)
                def _():
                    self.hop(1, s, k, self.opening[k].at[1]).wait_send()

            return 0

        lax.fori_loop(1, 9, body, 0)

    @staticmethod
    def scratch(blocks):
        k = len(blocks)
        return (
            [pltpu.VMEM((RING, *s), t) for s, t in blocks]
            + [pltpu.VMEM((RING, *s), t) for s, t in blocks]
            + [pltpu.VMEM((2, 9, *s), t) for s, t in blocks]
            + [pltpu.VMEM((2, *s), t) for s, t in blocks]
            + [DMA((RING, k))] * 3
            + [DMA((2, 9, k))] * 2
        )


def swap_rows(total, out, place, sems):
    rows_own = total.shape[-2] // 2
    half = total.shape[-1]
    theirs, mine = at(1 - place.rep, rows_own, 8), at(place.rep, rows_own, 8)
    cols = at(place.rep, half, 128)
    if len(total.shape) == 3:
        out[:, :, cols] = total[:, mine, :]
        return remote(total.at[:, theirs, :], out.at[:, :, cols], sems.at[0], sems.at[1], place.twin)
    out[:, cols] = total[mine, :]
    return remote(total.at[theirs, :], out.at[:, cols], sems.at[0], sems.at[1], place.twin)


CHUNK = 64
CTILE = 256


def fill_inner(ext, body_ref, start):
    count = ext.shape[1]
    rows_in = pl.ds(pl.multiple_of(start - RAD, RAD), count)
    for c in range(ext.shape[0]):
        ext[c] = body_ref[rows_in, c * 128 : (c + 1) * 128].astype(F32)


def fill_edge(ext, body_ref, left_ref, right_ref, first):
    tile = ext.shape[1] - 2 * RAD
    t = body_ref.shape[0]
    start = pl.multiple_of(jnp.where(first, 0, t - tile), tile)
    for c in range(ext.shape[0]):
        cols = slice(c * 128, (c + 1) * 128)
        ext[c, RAD : RAD + tile, :] = body_ref[pl.ds(start, tile), cols].astype(F32)
        ext[c, 0:RAD, :] = jnp.where(first, left_ref[:, cols], body_ref[t - tile - RAD : t - tile, cols]).astype(F32)
        ext[c, RAD + tile :, :] = jnp.where(first, body_ref[tile : tile + RAD, cols], right_ref[:, cols]).astype(F32)


def conv_forward(ext, tap_ref, out, row0):
    def step(r, _):
        base = pl.multiple_of(r * CHUNK, CHUNK)
        for c in range(ext.shape[0]):
            cols = slice(c * 128, (c + 1) * 128)
            acc = jnp.zeros((CHUNK, 128), F32)
            for b in range(8):
                reach = 4 if b == 0 else 3
                win = ext[c, pl.ds(base + b, CHUNK + 8 * reach), :]
                for m in range(reach + 1):
                    o = 8 * m + b
                    acc = acc + tap_ref[o : o + 1, cols] * win[8 * m : 8 * m + CHUNK]
            out[pl.ds(pl.multiple_of(row0 + base, CHUNK), CHUNK), cols] = acc.astype(out.dtype)
        return 0

    lax.fori_loop(0, CTILE // CHUNK, step, 0)


def conv_backward(vext, gext, tap_ref, out, tapacc, row0):
    def step(r, _):
        base = pl.multiple_of(r * CHUNK, CHUNK)
        for c in range(vext.shape[0]):
            cols = slice(c * 128, (c + 1) * 128)
            acc = jnp.zeros((CHUNK, 128), F32)
            here = gext[c, pl.ds(base + RAD, CHUNK), :]
            for b in range(8):
                reach = 4 if b == 0 else 3
                win = gext[c, pl.ds(base + b, CHUNK + 8 * reach), :]
                for m in range(reach + 1):
                    o = KC - 1 - (8 * m + b)
                    acc = acc + tap_ref[o : o + 1, cols] * win[8 * m : 8 * m + CHUNK]
                win = vext[c, pl.ds(base + b, CHUNK + 8 * reach), :]
                for m in range(reach + 1):
                    o = 8 * m + b
                    tapacc[o, :, cols] += rowsum8(here * win[8 * m : 8 * m + CHUNK])
            out[pl.ds(pl.multiple_of(row0 + base, CHUNK), CHUNK), cols] = acc
        return 0

    lax.fori_loop(0, CTILE // CHUNK, step, 0)


def wide_eye():
    lane = lax.broadcasted_iota(jnp.int32, (M, GROUP), 1) & 63
    return jnp.where(lane == lax.broadcasted_iota(jnp.int32, (M, GROUP), 0), 1.0, 0.0)


def head_sums(row):
    ones = jnp.where(head_mask(), 1.0, 0.0)
    return dot(jnp.broadcast_to(row, (8, GROUP)), ones, HI)[0:1]


def pinv_begin(mq_ref, mk_ref, a_ref, z_ref):
    for g in range(NG):
        s = dot_nt(mq_ref[:, gs(g)], spread(mk_ref[:, gs(g)]))
        e = jnp.exp(s - half_reduce(s, jnp.max, -jnp.inf))
        a = e / half_reduce(e, jnp.sum, 0.0)
        a_ref[:, gs(g)] = a
        col = jnp.sum(a, axis=0, keepdims=True)
        z_ref[0, :, gs(g)] = flip(a) / jnp.sqrt(head_sums(col * col))


def pinv_step(it, a_ref, z_ref, az_ref, t2_ref, t3_ref):
    eye = wide_eye()
    z = [z_ref[it, :, gs(g)] for g in range(NG)]
    az = [dot(a_ref[:, gs(g)], spread(z[g]), HI) for g in range(NG)]
    t2 = [15.0 * eye - dot(az[g], spread(7.0 * eye - az[g]), HI) for g in range(NG)]
    t3 = [13.0 * eye - dot(az[g], spread(t2[g]), HI) for g in range(NG)]
    for g in range(NG):
        z_ref[it + 1, :, gs(g)] = 0.25 * dot(z[g], spread(t3[g]), HI)
        az_ref[it, :, gs(g)] = az[g]
        t2_ref[it, :, gs(g)] = t2[g]
        t3_ref[it, :, gs(g)] = t3[g]


def pinv_back_step(it, a_ref, z_ref, az_ref, t2_ref, t3_ref, gz_ref, da_ref):
    eye = wide_eye()
    R = range(NG)
    gz = [gz_ref[:, gs(g)] for g in R]
    z = [z_ref[it, :, gs(g)] for g in R]
    az = [az_ref[it, :, gs(g)] for g in R]
    t2 = [t2_ref[it, :, gs(g)] for g in R]
    t3 = [t3_ref[it, :, gs(g)] for g in R]
    bg = [spread(0.25 * gz[g]) for g in R]
    d3 = [dot(0.25 * gz[g], spread(z[g]), HI) for g in R]
    baz = [spread(az[g]) for g in R]
    d2 = [-dot(d3[g], baz[g], HI) for g in R]
    d1 = [-dot(d2[g], baz[g], HI) for g in R]
    daz = [-dot(t2[g], spread(d3[g]), HI) - dot(7.0 * eye - az[g], spread(d2[g]), HI) - d1[g] for g in R]
    for g in R:
        da_ref[:, gs(g)] += dot(z[g], spread(daz[g]), HI)
        gz_ref[:, gs(g)] = dot(t3[g], bg[g], HI) + dot(daz[g], spread(a_ref[:, gs(g)]), HI)


def pinv_back_end(g, a_ref, gz_ref, da_ref):
    a = a_ref[:, gs(g)]
    gz = gz_ref[:, gs(g)]
    col = jnp.sum(a, axis=0, keepdims=True)
    bound = jnp.sqrt(head_sums(col * col))
    tot = head_sums(jnp.sum(gz * a, axis=0, keepdims=True))
    full = flip(da_ref[:, gs(g)]) + gz / bound - (tot / (bound * bound * bound)) * col
    return a * (full - half_reduce(full * a, jnp.sum, 0.0))


def gather_marks(slots, outs, n):
    per = 4 * n // M
    half = slots.shape[2]
    for out, base in zip(outs, (0, 4)):
        if per == 1:
            got = [slots[i].astype(F32) for i in range(n)]
            for h in range(2):
                tall = jnp.concatenate([x[8 * h + base : 8 * h + base + 4] for x in got], axis=0)
                out[:, h * half : (h + 1) * half] = tall.astype(BF16)
        else:
            for h in range(2):
                lines = []
                for m in range(M):
                    total = jnp.zeros((1, half), F32)
                    for s in range(per // 4):
                        part = slots[m * (per // 4) + s].astype(F32)[8 * h + base : 8 * h + base + 4]
                        total = total + jnp.sum(part, axis=0, keepdims=True)
                    lines.append(total * (1.0 / per))
                out[:, h * half : (h + 1) * half] = jnp.concatenate(lines, axis=0).astype(BF16)


class Refs:
    def __init__(self, refs):
        self.it = iter(refs)

    def __call__(self, count):
        return [next(self.it) for _ in range(count)]

    def one(self):
        return next(self.it)


def front_kernel(*refs, n, ring):
    take = Refs(refs)
    x_any = take.one()
    if ring:
        wa, wu, wd, wv = take(4)
        wqkv_o, wo_o, up_o, down_o = take(4)
    else:
        wq, vec = take(2)
    gains, taps = take(2)
    outs = take(7)
    mq, mk, uz, a_ref, z_ref, az_ref, t2_ref, t3_ref, vl, vr = take(10)
    xs = take.one()
    stage = take(7)
    h_s, q_s, k_s, v_s, conv_s, f_s, e_s = stage
    means, pay, slots, ext, bdk, bdq, uacc, zacc, upart = take(9)
    xsem, osem, msem, hsem = take(4)
    sum_bufs = take(3)
    me = lax.axis_index("seq")
    t, d = xs.shape
    half = d // 2
    load_x = pltpu.make_async_copy(x_any, xs, xsem.at[0])
    load_x.start()
    drains = [pltpu.make_async_copy(s, o, osem.at[i]) for i, (s, o) in enumerate(zip(stage, outs))]
    if ring:
        wq, vec, sa, su, so, cu, co, cd, psem, lsem = take(10)
        ring_one, ring_two = take(4), take(4)
        place = Place()
        greet(me, n, [place.twin])
        rep, seq = place.rep, place.seq
        rows_own, ff = d // (2 * RING), wu.shape[1]
        mine = at(rep, rows_own, 8)
        theirs = 1 - rep
        swaps = (
            remote(wa.at[0:3, :, at(theirs, half, 128)], sa.at[:, mine, :], psem.at[0], psem.at[1], place.twin),
            remote(wa.at[3, :, at(theirs, half, 128)], so.at[mine, :], psem.at[2], psem.at[3], place.twin),
            remote(wu.at[:, at(theirs, ff // 2, 128)], su.at[mine, :], psem.at[4], psem.at[5], place.twin),
        )
        for c in swaps:
            c.start()
        sa[:, mine, :] = wa[0:3, :, at(rep, half, 128)]
        so[mine, :] = wa[3, :, at(rep, half, 128)]
        su[mine, :] = wu[:, at(rep, ff // 2, 128)]
        vec[at(seq * 2 + rep, rows_own, 8), :] = wv[...]
        swaps[0].wait()
        wq[:, at(seq, 2 * rows_own, 16), at(rep, half, 128)] = sa[...].astype(BF16)
        first = GatherRing(place, (STACK, LINES), (wq, vec), (None, None), ring_one)
        first.start()
        cd[...] = wd[...].astype(BF16)
        swaps[1].wait()
        swaps[2].wait()
        co[...] = so[...].astype(BF16)
        cu[...] = su[...].astype(BF16)
        rest = GatherRing(place, (HALF, HALF, ROWS), (wo_o, up_o, down_o), (co, cu, cd), ring_two)
        local = [
            pltpu.make_async_copy(src, piece(kind, out, seq, rep), lsem.at[i])
            for i, (src, kind, out) in enumerate(zip(rest.own, rest.kinds, rest.outs))
        ]

        def go(s, _):
            first.step(s)
            return 0

        lax.fori_loop(1, 9, go, 0)
        rest.start()
        for c in local:
            c.start()
        first.finish()
        save_w = pltpu.make_async_copy(wq, wqkv_o, xsem.at[1])
        save_w.start()
    else:
        greet(me, n, [])

    def tick(cond, s):
        if ring:

            @pl.when(cond)
            def _():
                rest.step(s)

    turned = jnp.transpose(vec[...]).astype(BF16).astype(F32)
    gains[...] = turned[0:8]
    taps[...] = turned[2:42]
    load_x.wait()

    def project(i, _):
        here = pl.ds(pl.multiple_of(i * (t // 4), t // 4), t // 4)
        normal, _inv = normalize(xs[here, :].astype(F32))
        h = (normal * gains[0:1, :]).astype(BF16)
        h_s[here, :] = h
        q = (dot(h, wq[0]) * QK_SCALE).astype(BF16)
        q_s[here, :] = q
        means[pl.ds(i, 1), :] = jnp.mean(q.astype(F32), axis=0, keepdims=True)
        k = (dot(h, wq[1]) * QK_SCALE).astype(BF16)
        k_s[here, :] = k
        means[pl.ds(i + 4, 1), :] = jnp.mean(k.astype(F32), axis=0, keepdims=True)
        v_s[here, :] = dot(h, wq[2]).astype(BF16)
        tick((i == 1) | (i == 3), lax.div(i + 1, 2))
        return 0

    lax.fori_loop(0, 4, project, 0)

    pay[...] = jnp.concatenate([means[:, :half], means[:, half:]], axis=0).astype(BF16)

    def mark(j, peer):
        return remote(pay, slots.at[me], msem.at[0, j], msem.at[1, j], {"seq": peer})

    halos = halo_copies(v_s, vl, vr, me, n, hsem)
    for c in halos:
        c.start()
    each_peer(me, n, mark, lambda c: c.start())
    slots[pl.ds(me, 1)] = pay[...][None]
    for c in drains[:4]:
        c.start()

    def inner(i, _):
        fill_inner(ext, v_s, i * CTILE)
        conv_forward(ext, taps, conv_s, i * CTILE)
        tick((i == 3) | (i == 6), 2 + lax.div(i, 3))
        return 0

    lax.fori_loop(1, t // CTILE - 1, inner, 0)
    for c in halos:
        c.wait()
    mask_halos(vl, vr, me, n)

    def edge(i, _):
        fill_edge(ext, v_s, vl, vr, i == 0)
        conv_forward(ext, taps, conv_s, i * (t - CTILE))
        return 0

    lax.fori_loop(0, 2, edge, 0)
    drains[4].start()
    each_peer(me, n, mark, lambda c: c.wait())
    gather_marks(slots, (mq, mk), n)
    for g in range(NG):
        bdk[g] = spread(mk[:, gs(g)])
        bdq[g] = spread(mq[:, gs(g)])
    uacc[...] = jnp.zeros_like(uacc)
    zacc[...] = jnp.zeros_like(zacc)
    ones_bd = jnp.where(head_mask(), 1.0, 0.0).astype(BF16)

    def attend(i, _):
        here = pl.ds(pl.multiple_of(i * (t // 4), t // 4), t // 4)
        for g in range(NG):
            s = dot_nt(q_s[here, gs(g)], bdk[g])
            ex = jnp.exp(s - half_reduce(s, jnp.max, -jnp.inf))
            den = dot(ex.astype(BF16), ones_bd)
            f_s[here, gs(g)] = (ex / den).astype(BF16)
            e = jnp.exp(dot_nt(k_s[here, gs(g)], bdq[g])).astype(BF16)
            e_s[here, gs(g)] = e
            uacc[g] += dot_tn(e, v_s[here, gs(g)])
            zacc[g] += dot_tn(e, jnp.ones((t // 4, 128), BF16))
        tick((i == 1) | (i == 3), 5 + lax.div(i, 2))
        return 0

    lax.fori_loop(0, 4, attend, 0)
    for c in drains[5:]:
        c.start()
    lane = lax.broadcasted_iota(jnp.int32, (M, 128), 1)
    zt = jnp.zeros((M, 128), F32)
    for g in range(NG):
        put_tall(upart, g, collect(uacc[g]))
        for h in range(4):
            zt = zt + jnp.where(lane == 4 * g + h, zacc[g, h * 64 : h * 64 + 64, :], 0.0)
    upart[6 * M : 7 * M, :] = zt
    upart[7 * M :, :] = jnp.zeros((upart.shape[0] - 7 * M, 128), F32)
    summing = SeqSum(me, n, upart, uz, *sum_bufs)
    summing.start()
    pinv_begin(mq, mk, a_ref, z_ref)

    def newton(it, _):
        pinv_step(it, a_ref, z_ref, az_ref, t2_ref, t3_ref)
        return 0

    lax.fori_loop(0, NSITER // 2, newton, 0)
    if ring:
        rest.step(7)
    summing.turn()
    lax.fori_loop(NSITER // 2, NSITER, newton, 0)
    if ring:
        rest.step(8)
    summing.finish()
    for c in drains:
        c.wait()
    if ring:
        for c in local:
            c.wait()
        save_w.wait()
        rest.finish()


def front(x, weights, n, ring):
    t, d = x.shape
    if ring:
        wa, wu, wd, wv = weights
        ff = wu.shape[1]
        extra_out = [sds((3, d, d), BF16), sds((d, d), BF16), sds((d, ff), BF16), sds((ff, d), BF16)]
        rown = d // RING
        extra = [
            pltpu.VMEM((3, d, d), BF16),
            pltpu.VMEM((d, 128), F32),
            pltpu.VMEM((3, rown, d // 2), F32),
            pltpu.VMEM((rown, ff // 2), F32),
            pltpu.VMEM((rown, d // 2), F32),
            pltpu.VMEM((rown, ff // 2), BF16),
            pltpu.VMEM((rown, d // 2), BF16),
            pltpu.VMEM((ff // (2 * RING), d), BF16),
            DMA((6,)),
            DMA((3,)),
        ] + GatherRing.scratch(2) + GatherRing.scratch(3)
    else:
        extra_out, extra = [], []
    r = padded_rows(7 * M, n)
    big = sds((t, d), BF16)
    steps = sds((NSITER, M, d), F32)
    res = pl.pallas_call(
        functools.partial(front_kernel, n=n, ring=ring),
        in_specs=[ANYW] + [VM] * len(weights),
        out_specs=[ANYW] * len(extra_out) + [VM] * 2 + [ANYW] * 7 + [VM] * 10,
        out_shape=extra_out
        + [sds((8, d), F32), sds((40, d), F32)]
        + [big] * 7
        + [sds((M, d), BF16)] * 2
        + [sds((r, 128), F32), sds((M, d), F32), sds((NSITER + 1, M, d), F32), steps, steps, steps]
        + [sds((RAD, d), BF16)] * 2,
        scratch_shapes=[pltpu.VMEM((t, d), BF16)] * 8
        + [
            pltpu.VMEM((8, d), F32),
            pltpu.VMEM((16, d // 2), BF16),
            pltpu.VMEM((n, 16, d // 2), BF16),
            pltpu.VMEM((d // 128, CTILE + 2 * RAD, 128), F32),
            pltpu.VMEM((NG, GROUP, GROUP), BF16),
            pltpu.VMEM((NG, GROUP, GROUP), BF16),
            pltpu.VMEM((NG, GROUP, GROUP), F32),
            pltpu.VMEM((NG, GROUP, 128), F32),
            pltpu.VMEM((r, 128), F32),
            DMA((2,)),
            DMA((7,)),
            DMA((2, n)),
            DMA((4,)),
        ]
        + SeqSum.scratch(r, n)
        + extra,
        compiler_params=pltpu.CompilerParams(collective_id=1, has_side_effects=True, vmem_limit_bytes=VMEM_LIMIT),
        name="front",
    )(x, *weights)
    return res if ring else [None] * 4 + list(res)


FCHUNK = 512


def middle_kernel(
    x_ref, dy_ref, f_ref, q_ref, conv_ref, wo_ref, up_ref, down_ref, gain_ref, mk_ref, uz_ref, z_ref,
    out_ref, act_ref, da_ref, h2_ref, mix_ref, dx_ref, dmix_ref, dqf_ref, gw_ref, dkt_ref, dg_ref,
    wbd, gwacc, dktacc, dgacc, oacc, hacc,
):
    i = pl.program_id(0)
    n = pl.num_programs(0)
    tile = x_ref.shape[0]
    d = x_ref.shape[1]

    @pl.when(i == 0)
    def _():
        gwacc[...] = jnp.zeros_like(gwacc)
        dktacc[...] = jnp.zeros_like(dktacc)
        dgacc[...] = jnp.zeros_like(dgacc)
        for g in range(NG):
            bv = u_group(uz_ref, g) / zt_group(uz_ref, g)
            wbd[g] = spread(dot(z_ref[NSITER, :, gs(g)], spread(bv), HI)).astype(BF16)

    for g in range(NG):
        mix_ref[:, gs(g)] = (dot(f_ref[:, gs(g)], wbd[g]) + conv_ref[:, gs(g)].astype(F32)).astype(BF16)
    x1 = x_ref[...].astype(F32) + dot(mix_ref[...], wo_ref[...])
    normal, inv = normalize(x1)
    gain = gain_ref[1:2, :]
    h2 = (normal * gain).astype(BF16)
    h2_ref[...] = h2
    dy = dy_ref[...]
    ff = up_ref.shape[1]
    for j in range(ff // FCHUNK):
        cols = slice(j * FCHUNK, (j + 1) * FCHUNK)
        a = dot(h2, up_ref[:, cols])
        act, slope = gelu_parts(a)
        act = act.astype(BF16)
        act_ref[:, cols] = act
        da = (dot_nt(dy, down_ref[cols, :]) * slope).astype(BF16)
        da_ref[:, cols] = da
        o = dot(act, down_ref[cols, :])
        h = dot_nt(da, up_ref[:, cols])
        if j == 0:
            oacc[...] = o
            hacc[...] = h
        else:
            oacc[...] += o
            hacc[...] += h
    out_ref[...] = (x1 + oacc[...]).astype(BF16)
    dh2 = hacc[...]
    dgacc[...] += rowsum8(dh2 * normal)
    dx1 = norm_back(dh2, normal, inv, gain) + dy.astype(F32)
    do = dx1.astype(BF16)
    dx_ref[...] = do
    dmix = dot_nt(do, wo_ref[...]).astype(BF16)
    dmix_ref[...] = dmix
    ones_bd = jnp.where(head_mask(), 1.0, 0.0).astype(BF16)
    for g in range(NG):
        dm = dmix[:, gs(g)]
        f = f_ref[:, gs(g)]
        df = dot_nt(dm, wbd[g])
        gwacc[g] += dot_tn(f, dm)
        ff32 = f.astype(F32)
        prod = df * ff32
        hi = prod.astype(BF16)
        lo = (prod - hi.astype(F32)).astype(BF16)
        ds = (ff32 * (df - (dot(hi, ones_bd) + dot(lo, ones_bd)))).astype(BF16)
        dqf_ref[:, gs(g)] = dot(ds, spread(mk_ref[:, gs(g)])).astype(BF16)
        dktacc[g] += dot_tn(ds, q_ref[:, gs(g)])

    @pl.when(i == n - 1)
    def _():
        for g in range(NG):
            put_tall(gw_ref, g, collect(gwacc[g]))
            dkt_ref[:, gs(g)] = collect(dktacc[g])
        if gw_ref.shape[0] > 6 * M:
            gw_ref[6 * M :] = jnp.zeros((gw_ref.shape[0] - 6 * M, 128), F32)
        dg_ref[...] = jnp.broadcast_to(jnp.sum(dgacc[...], axis=0, keepdims=True), (8, d))


def middle(x, dy, f, q, conv, wo, up, down, gains, mk, uz, z, gw_rows):
    t, d = x.shape
    ff = up.shape[1]
    tile = 256
    r = rows(tile, d)
    rf = rows(tile, ff)
    return pl.pallas_call(
        middle_kernel,
        grid=(t // tile,),
        in_specs=[r, r, r, r, r, whole((d, d)), whole(up.shape), whole(down.shape), whole(gains.shape), whole((M, d)),
                  whole(uz.shape), whole(z.shape)],
        out_specs=[r, rf, rf, r, r, r, r, r, whole((gw_rows, 128)), whole((M, d)), whole((8, d))],
        out_shape=[sds((t, d), BF16), sds((t, ff), BF16), sds((t, ff), BF16)] + [sds((t, d), BF16)] * 5
        + [sds((gw_rows, 128), F32), sds((M, d), F32), sds((8, d), F32)],
        scratch_shapes=[
            pltpu.VMEM((NG, GROUP, GROUP), BF16),
            pltpu.VMEM((NG, GROUP, GROUP), F32),
            pltpu.VMEM((NG, GROUP, GROUP), F32),
            pltpu.VMEM((8, d), F32),
            pltpu.VMEM((tile, d), F32),
            pltpu.VMEM((tile, d), F32),
        ],
        compiler_params=params(),
        name="middle",
    )(x, dy, f, q, conv, wo, up, down, gains, mk, uz, z)


def rear_kernel(*refs, n, ring):
    take = Refs(refs)
    bodies = take(4)
    if ring:
        grads = take(3)
    gw_part, uz, a_ref, z_ref, az_ref, t2_ref, t3_ref, mq, mk, vl, vr, taps, dkt_ref = take(13)
    dv_o, dkb_o, dtap, own = take(4)
    if ring:
        r_o, r_up, r_down = take(3)
    v_s, g_s, e_s, k_s = take(4)
    dv_s, dkb_s, dvc, vext, gext, tapacc, gl, gr, gw, gz, da, dubd, rowadd, dqtacc, bdq, pay, slots = take(17)
    isem, osem, hsem, wsem = take(4)
    sum_bufs = take(3)
    me = lax.axis_index("seq")
    t, d = v_s.shape
    loads = [pltpu.make_async_copy(b, s, isem.at[i]) for i, (b, s) in enumerate(zip(bodies, (v_s, g_s, e_s, k_s)))]
    for c in loads:
        c.start()
    if ring:
        mine, twins, inbox, opening = take(3), take(3), take(3), take(3)
        sems = take(5)
        fo, fu, fsem = take(3)
        place = Place()
        greet(me, n, [place.twin])
        ringer = ScatterRing(place, (HALF, HALF, ROWS), grads, mine, twins, inbox, opening, sems)
    else:
        greet(me, n, [])
    summing = SeqSum(me, n, gw_part, gw, *sum_bufs)
    loads[1].wait()
    halos = halo_copies(g_s, gl, gr, me, n, hsem)
    for c in halos:
        c.start()
    summing.start()
    if ring:
        ringer.start()

    def tick(cond, s):
        if ring:

            @pl.when(cond)
            def _():
                ringer.step(s)

    tapacc[...] = jnp.zeros_like(tapacc)
    loads[0].wait()

    def inner(i, _):
        fill_inner(vext, v_s, i * CTILE)
        fill_inner(gext, g_s, i * CTILE)
        conv_backward(vext, gext, taps, dvc, tapacc, i * CTILE)
        tick((i == 2) | (i == 4), lax.div(i, 2))

        @pl.when(i == 4)
        def _():
            summing.turn()

        return 0

    lax.fori_loop(1, t // CTILE - 1, inner, 0)
    tick(True, 3)
    for c in halos:
        c.wait()
    mask_halos(gl, gr, me, n)

    def edge(i, _):
        fill_edge(vext, v_s, vl, vr, i == 0)
        fill_edge(gext, g_s, gl, gr, i == 0)
        conv_backward(vext, gext, taps, dvc, tapacc, i * (t - CTILE))
        return 0

    lax.fori_loop(0, 2, edge, 0)
    dtap[...] = jnp.sum(tapacc[...], axis=1)
    tick(True, 4)
    summing.finish()
    for g in range(NG):
        z = zt_group(uz, g)
        bv = u_group(uz, g) / z
        gwg = u_group(gw, g)
        gz[:, gs(g)] = flip(dot_nt(gwg, spread(bv), HI))
        dbv = dot(flip(z_ref[NSITER, :, gs(g)]), spread(gwg), HI)
        dubd[g] = spread(dbv / z).astype(BF16)
        rowadd[g] = dot_nt(jnp.ones((8, GROUP), F32), spread(dbv * bv / z), HI)
        bdq[g] = spread(mq[:, gs(g)])
    da[...] = jnp.zeros_like(da)

    def newton(j, _):
        pinv_back_step(NSITER - 1 - j, a_ref, z_ref, az_ref, t2_ref, t3_ref, gz, da)
        tick((j == 1) | (j == 3), 5 + lax.div(j, 2))
        return 0

    lax.fori_loop(0, NSITER, newton, 0)
    loads[2].wait()
    loads[3].wait()
    dqtacc[...] = jnp.zeros_like(dqtacc)

    def through(i, _):
        here = pl.ds(pl.multiple_of(i * (t // 4), t // 4), t // 4)
        for g in range(NG):
            e = e_s[here, gs(g)]
            de = dot_nt(v_s[here, gs(g)], dubd[g]) - rowadd[g, 0:1, :]
            ds = (e.astype(F32) * de).astype(BF16)
            dv_s[here, gs(g)] = (dot(e, dubd[g]) + dvc[here, gs(g)]).astype(BF16)
            dkb_s[here, gs(g)] = dot(ds, bdq[g]).astype(BF16)
            dqtacc[g] += dot_tn(ds, k_s[here, gs(g)])
        tick((i == 0) | (i == 3), 7 + lax.div(i, 3))
        return 0

    lax.fori_loop(0, 4, through, 0)
    drains = [
        pltpu.make_async_copy(dv_s, dv_o, osem.at[0]),
        pltpu.make_async_copy(dkb_s, dkb_o, osem.at[1]),
    ]
    for c in drains:
        c.start()

    rows_dev = max(M // n, 1)
    per_mark = n * rows_dev // M
    if rows_dev < 4:
        pay[...] = jnp.zeros_like(pay)
    for g in range(NG):
        ds = pinv_back_end(g, a_ref, gz, da)
        dq = collect(dqtacc[g]) + dot(ds, spread(mk[:, gs(g)].astype(F32)), HI) * (1.0 / n)
        dk = dkt_ref[:, gs(g)] + dot(flip(ds), spread(mq[:, gs(g)].astype(F32)), HI) * (1.0 / n)
        for i in range(n):
            row = i * rows_dev // per_mark
            pay[i, 0:rows_dev, gs(g)] = dq[row : row + rows_dev]
            pay[i, 4 : 4 + rows_dev, gs(g)] = dk[row : row + rows_dev]

    def mark(j, peer):
        return remote(pay.at[peer], slots.at[me], wsem.at[0, j], wsem.at[1, j], {"seq": peer})

    each_peer(me, n, mark, lambda c: c.start())
    slots[pl.ds(me, 1)] = pay[pl.ds(me, 1)]
    if ring:
        fo[...] = ringer.total(0)
        fu[...] = ringer.total(1)
        back = (swap_rows(fo, r_o, place, fsem.at[0]), swap_rows(fu, r_up, place, fsem.at[1]))
        for c in back:
            c.start()
        r_down[...] = ringer.total(2)
    each_peer(me, n, mark, lambda c: c.wait())
    own[...] = lax.fori_loop(1, n, lambda i, acc: acc + slots[i], slots[0])
    for c in drains:
        c.wait()
    if ring:
        for c in back:
            c.wait()
        ringer.finish()


def rear(bodies, grads, gw, uz, a, z, az, t2, t3, mq, mk, vl, vr, taps, dkt, n):
    ring = grads is not None
    t, d = bodies[0].shape
    r = gw.shape[0]
    big = sds((t, d), BF16)
    outs = [big, big, sds((40, d), F32), sds((8, d), F32)]
    extra = []
    if ring:
        ff = grads[1].shape[1]
        own = d // (2 * RING)
        outs += [sds((own, d), F32), sds((own, ff), F32), sds((ff // (2 * RING), d), F32)]
        blocks = [((2 * own, d // 2), BF16), ((2 * own, ff // 2), BF16), ((ff // (2 * RING), d), BF16)]
        extra = ScatterRing.scratch(blocks) + [
            pltpu.VMEM((2 * own, d // 2), F32),
            pltpu.VMEM((2 * own, ff // 2), F32),
            DMA((2, 2)),
        ]
    ext = pltpu.VMEM((d // 128, CTILE + 2 * RAD, 128), F32)
    halo = pltpu.VMEM((RAD, d), BF16)
    small = pltpu.VMEM((M, d), F32)
    return pl.pallas_call(
        functools.partial(rear_kernel, n=n, ring=ring),
        in_specs=[ANYW] * (4 + (3 if ring else 0)) + [VM] * 13,
        out_specs=[ANYW] * 2 + [VM] * (len(outs) - 2),
        out_shape=outs,
        scratch_shapes=[pltpu.VMEM((t, d), BF16)] * 6
        + [
            pltpu.VMEM((t, d), F32),
            ext,
            ext,
            pltpu.VMEM((40, 8, d), F32),
            halo,
            halo,
            pltpu.VMEM((r, 128), F32),
            small,
            small,
            pltpu.VMEM((NG, GROUP, GROUP), BF16),
            pltpu.VMEM((NG, 8, GROUP), F32),
            pltpu.VMEM((NG, GROUP, GROUP), F32),
            pltpu.VMEM((NG, GROUP, GROUP), BF16),
            pltpu.VMEM((n, 8, d), F32),
            pltpu.VMEM((n, 8, d), F32),
            DMA((4,)),
            DMA((2,)),
            DMA((4,)),
            DMA((2, n)),
        ]
        + SeqSum.scratch(r, n)
        + extra,
        compiler_params=pltpu.CompilerParams(collective_id=2, has_side_effects=True, vmem_limit_bytes=VMEM_LIMIT),
        name="rear",
    )(*bodies, *(grads if ring else ()), gw, uz, a, z, az, t2, t3, mq, mk, vl, vr, taps, dkt)


def last_kernel(x_ref, dx_ref, dqf_ref, dkb_ref, dv_ref, own_ref, w_ref, gain_ref, dq_ref, dk_ref, ig_ref, dg_ref, dgacc, *, seg_len, rows_dev):
    i = pl.program_id(0)
    n = pl.num_programs(0)
    tile, d = x_ref.shape

    @pl.when(i == 0)
    def _():
        dgacc[...] = jnp.zeros_like(dgacc)

    at = i * rows_dev // 4
    scale = 1.0 / seg_len
    dq = (dqf_ref[...].astype(F32) + own_ref[pl.ds(at, 1), :] * scale).astype(BF16)
    dk = (dkb_ref[...].astype(F32) + own_ref[pl.ds(at + 4, 1), :] * scale).astype(BF16)
    dq_ref[...] = dq
    dk_ref[...] = dk
    dh = (dot_nt(dq, w_ref[0]) + dot_nt(dk, w_ref[1])) * QK_SCALE + dot_nt(dv_ref[...], w_ref[2])
    normal, inv = normalize(x_ref[...].astype(F32))
    dgacc[...] += rowsum8(dh * normal)
    ig = norm_back(dh, normal, inv, gain_ref[0:1, :]) + dx_ref[...].astype(F32)
    ig_ref[...] = ig.astype(BF16)

    @pl.when(i == n - 1)
    def _():
        dg_ref[...] = jnp.broadcast_to(jnp.sum(dgacc[...], axis=0, keepdims=True), (8, d))


def last(x, dx, dqf, dkb, dv, own, w_attn, gains, seg_len, rows_dev):
    t, d = x.shape
    tile = t // 4
    r = rows(tile, d)
    return pl.pallas_call(
        functools.partial(last_kernel, seg_len=seg_len, rows_dev=rows_dev),
        grid=(4,),
        in_specs=[r, r, r, r, r, whole((8, d)), whole(w_attn.shape), whole(gains.shape)],
        out_specs=[r, r, r, whole((8, d))],
        out_shape=[sds((t, d), BF16)] * 3 + [sds((8, d), F32)],
        scratch_shapes=[pltpu.VMEM((8, d), F32)],
        compiler_params=params(),
        name="last",
    )(x, dx, dqf, dkb, dv, own, w_attn, gains)


def adam_step(weight, grad_vec, moment, second, rate_value):
    moment_new = BETA_ONE * moment + (1.0 - BETA_ONE) * grad_vec
    second_new = BETA_TWO * second + (1.0 - BETA_TWO) * grad_vec * grad_vec
    first_hat = moment_new / (1.0 - BETA_ONE**STEP)
    second_hat = second_new / (1.0 - BETA_TWO**STEP)
    weight_new = weight - rate_value * (
        first_hat / (jnp.sqrt(second_hat) + ADAM_EPS) + DECAY_RATE * weight
    )
    return (weight_new, moment_new, second_new)


def tail_kernel(*refs, n):
    take = Refs(refs)
    grads = take(2)
    r_qkv, r_vec = take(2)
    mine, twins, inbox, opening = take(2), take(2), take(2), take(2)
    sems = take(5)
    fq, fsem = take(2)
    place = Place()
    greet(place.seq, n, [place.twin])
    ringer = ScatterRing(place, (STACK, LINES), grads, mine, twins, inbox, opening, sems)
    ringer.start()

    def go(s, _):
        ringer.step(s)
        return 0

    lax.fori_loop(1, 9, go, 0)
    fq[...] = ringer.total(0)
    back = swap_rows(fq, r_qkv, place, fsem)
    back.start()
    r_vec[...] = ringer.total(1)
    ringer.finish()
    back.wait()


def tail(g_qkv, g_vec, n):
    d = g_qkv.shape[1]
    own = d // (2 * RING)
    blocks = [((3, 2 * own, d // 2), BF16), ((own, 128), F32)]
    return pl.pallas_call(
        functools.partial(tail_kernel, n=n),
        in_specs=[ANYW] * 2,
        out_specs=[VM] * 2,
        out_shape=[sds((3, own, d), F32), sds((own, 128), F32)],
        scratch_shapes=ScatterRing.scratch(blocks) + [pltpu.VMEM(blocks[0][0], F32), DMA((2,))],
        compiler_params=pltpu.CompilerParams(collective_id=3, has_side_effects=True, vmem_limit_bytes=VMEM_LIMIT),
        name="tail",
    )(g_qkv, g_vec)


def per_device(tokens, cotangent, attn_w, w_up, w_down, vectors, attn_m, attn_v, up_m, up_v, down_m, down_v, vec_m, vec_v):
    both = ("seq", "rep")
    x = tokens[0]
    dy = cotangent[0]
    t, d = x.shape
    n = lax.axis_size("seq")
    rows_dev = max(M // n, 1)
    seg_len = t * n // M
    ring = n == RING and lax.axis_size("rep") == 2

    if ring:
        weights = (attn_w, w_up, w_down, jnp.pad(vectors, ((0, 0), (0, 128 - vectors.shape[1]))))
    else:
        w_attn = lax.all_gather(attn_w.astype(BF16), both, axis=1, tiled=True)
        vec = lax.all_gather(vectors.astype(BF16), both, axis=0, tiled=True).astype(F32)
        weights = (w_attn[:3], jnp.pad(vec, ((0, 0), (0, 128 - vec.shape[1]))))
    (w_qkv, wo, up, down, gains, taps, h1, q, k, v, conv, f, e, mq, mk, uz, a, z, az, t2, t3, vl, vr) = front(
        x, weights, n, ring
    )
    if not ring:
        w_qkv, wo = w_attn[:3], w_attn[3]
        up = lax.all_gather(w_up.astype(BF16), both, axis=0, tiled=True)
        down = lax.all_gather(w_down.astype(BF16), both, axis=0, tiled=True)
    out, act, da, h2, mix, dx, dmix, dqf, gw, dkt, dg2 = middle(
        x, dy, f, q, conv, wo, up, down, gains, mk, uz, z, padded_rows(6 * M, n)
    )
    dot_xla = functools.partial(jnp.einsum, "ta,tb->ab", preferred_element_type=F32)
    g_down = dot_xla(act, dy).astype(BF16)
    g_up = dot_xla(h2, da).astype(BF16)
    g_o = dot_xla(mix, dx).astype(BF16)
    res = rear((v, dmix, e, k), (g_o, g_up, g_down) if ring else None, gw, uz, a, z, az, t2, t3, mq, mk, vl, vr, taps, dkt, n)
    dv, dkb, dtap, own = res[:4]
    dq, dk, ig, dg1 = last(x, dx, dqf, dkb, dv, own, w_qkv, gains, seg_len, rows_dev)
    g_q = dot_xla(h1, dq) * QK_SCALE
    g_k = dot_xla(h1, dk) * QK_SCALE
    g_v = dot_xla(h1, dv)
    g_qkv = jnp.stack([g_q, g_k, g_v]).astype(BF16)
    g_vec = jnp.concatenate([dg1[:1], dg2[:1], dtap[:KC]], axis=0)
    if ring:
        g_vec = jnp.transpose(jnp.pad(g_vec, ((0, 128 - g_vec.shape[0]), (0, 0))))
        red_o, red_up, red_down = res[4:]
        red_qkv, red_vec = tail(g_qkv, g_vec, n)
        red_attn = jnp.concatenate([red_qkv, red_o[None]], axis=0)
        red_vec = red_vec[:, : vectors.shape[1]]
    else:
        g_attn = jnp.concatenate([g_qkv, g_o[None]], axis=0)
        red_attn = lax.psum_scatter(g_attn, both, scatter_dimension=1, tiled=True).astype(F32)
        red_up = lax.psum_scatter(g_up, both, scatter_dimension=0, tiled=True).astype(F32)
        red_down = lax.psum_scatter(g_down, both, scatter_dimension=0, tiled=True).astype(F32)
        red_vec = lax.psum_scatter(jnp.transpose(g_vec), both, scatter_dimension=0, tiled=True)
    return (
        out[None],
        ig[None],
        *adam_step(attn_w, red_attn, attn_m, attn_v, LEARN_RATE),
        *adam_step(w_up, red_up, up_m, up_v, LEARN_RATE),
        *adam_step(w_down, red_down, down_m, down_v, LEARN_RATE),
        *adam_step(vectors, red_vec, vec_m, vec_v, VECTOR_RATE),
    )


def solution(mesh):
    tok = P("rep", "seq", None)
    att = P(None, ("seq", "rep"), None)
    mat = P(("seq", "rep"), None)
    return jax.shard_map(
        per_device,
        mesh=mesh,
        in_specs=(tok, tok, att, mat, mat, mat, att, att, mat, mat, mat, mat, mat, mat),
        out_specs=(tok, tok, att, att, att) + (mat,) * 9,
        check_vma=False,
    )
```

```python
import functools

import jax
import jax.numpy as jnp
from jax import lax
from jax.experimental import pallas as pl
from jax.experimental.pallas import tpu as pltpu
from jax.sharding import PartitionSpec as P

H = 12
HD = 64
M = 64
KC = 33
NSITER = 6
STEP = 10
EPS_NORM = 1e-05
BETA_ONE = 0.9
BETA_TWO = 0.999
ADAM_EPS = 1e-08
LEARN_RATE = 0.03
VECTOR_RATE = 0.15
DECAY_RATE = 0.1

F32 = jnp.float32
BF16 = jnp.bfloat16
GROUP = 256
NG = 3
RAD = 16
QK_SCALE = HD ** (-0.25)
HI = lax.Precision.HIGHEST
VMEM_LIMIT = 58 * 1024 * 1024


def dot(a, b, precision=None):
    return lax.dot_general(a, b, (((1,), (0,)), ((), ())), precision=precision, preferred_element_type=F32)


def dot_nt(a, b, precision=None):
    return lax.dot_general(a, b, (((1,), (1,)), ((), ())), precision=precision, preferred_element_type=F32)


def dot_tn(a, b, precision=None):
    return lax.dot_general(a, b, (((0,), (0,)), ((), ())), precision=precision, preferred_element_type=F32)


def head_mask(shape=(GROUP, GROUP)):
    rows = lax.broadcasted_iota(jnp.int32, shape, 0)
    cols = lax.broadcasted_iota(jnp.int32, shape, 1)
    return lax.shift_right_logical(rows, 6) == lax.shift_right_logical(cols, 6)


def spread(wide):
    tall = jnp.concatenate([wide, wide, wide, wide], axis=0)
    return jnp.where(head_mask(), tall, jnp.zeros_like(tall))


def collect(full):
    kept = jnp.where(head_mask(), full, jnp.zeros_like(full))
    return (kept[0:64] + kept[64:128]) + (kept[128:192] + kept[192:256])


def flip(wide):
    turned = jnp.transpose(spread(wide))
    return (turned[0:64] + turned[64:128]) + (turned[128:192] + turned[192:256])


def gs(g):
    return slice(g * GROUP, (g + 1) * GROUP)


def half_reduce(x, op, init):
    parts = []
    for c in range(x.shape[1] // 128):
        col = x[:, c * 128 : (c + 1) * 128]
        low = lax.broadcasted_iota(jnp.int32, col.shape, 1) < 64
        a = op(jnp.where(low, col, init), axis=1, keepdims=True)
        b = op(jnp.where(low, init, col), axis=1, keepdims=True)
        parts.append(jnp.where(low, a, b))
    return jnp.concatenate(parts, axis=1)


def normalize(x):
    center = x - jnp.mean(x, axis=-1, keepdims=True)
    inv = lax.rsqrt(jnp.mean(center * center, axis=-1, keepdims=True) + EPS_NORM)
    return center * inv, inv


def norm_back(up, normal, inv, gain):
    scaled = up * gain
    centered = scaled - jnp.mean(scaled, axis=-1, keepdims=True)
    return inv * (centered - normal * jnp.mean(scaled * normal, axis=-1, keepdims=True))


def rowsum8(x):
    return jnp.sum(x.reshape(x.shape[0] // 8, 8, x.shape[1]), axis=0)


def gelu_parts(a):
    z = jnp.abs(a)
    t = 1.0 / (1.0 + (0.3275911 * 0.7071067811865476) * z)
    e = jnp.exp(-0.5 * a * a)
    poly = t * (0.127414796 + t * (-0.142248368 + t * (0.7107068705 + t * (-0.7265760135 + t * 0.5307027145))))
    tail = poly * e
    phi = jnp.where(a >= 0, 1.0 - tail, tail)
    return a * phi, phi + a * (e * 0.3989422804014327)


def whole(shape):
    zeros = (0,) * len(shape)
    return pl.BlockSpec(shape, lambda i: zeros, pipeline_mode=pl.Buffered(1))


def rows(tile, width):
    return pl.BlockSpec((tile, width), lambda i: (i, 0))


def sds(shape, dtype):
    return jax.ShapeDtypeStruct(shape, dtype)


def params():
    return pltpu.CompilerParams(dimension_semantics=("arbitrary",), vmem_limit_bytes=VMEM_LIMIT)


def widen(zt, g):
    return jnp.concatenate(
        [jnp.broadcast_to(zt[:, h : h + 1], (M, HD)) for h in range(4 * g, 4 * g + 4)], axis=1
    )


def u_group(ref, g):
    return jnp.concatenate([ref[2 * g * M : (2 * g + 1) * M, :], ref[(2 * g + 1) * M : (2 * g + 2) * M, :]], axis=1)


def zt_group(ref, g):
    return widen(ref[6 * M : 7 * M, :], g)


def put_tall(ref, g, wide):
    ref[2 * g * M : (2 * g + 1) * M, :] = wide[:, :128]
    ref[(2 * g + 1) * M : (2 * g + 2) * M, :] = wide[:, 128:]


def padded_rows(r, n):
    return -(-r // (8 * n)) * 8 * n


MESH = pl.DeviceIdType.MESH
DMA = pltpu.SemaphoreType.DMA
VM = pl.BlockSpec(memory_space=pltpu.VMEM)
ANYW = pl.BlockSpec(memory_space=pl.ANY)


def remote(src, dst, send, recv, where):
    return pltpu.make_async_remote_copy(
        src_ref=src, dst_ref=dst, send_sem=send, recv_sem=recv, device_id=where, device_id_type=MESH
    )


def greet(me, n, others):
    bar = pltpu.get_barrier_semaphore()

    def hello(j, _):
        pl.semaphore_signal(bar, inc=1, device_id={"seq": lax.rem(me + j, n)}, device_id_type=MESH)
        return 0

    lax.fori_loop(1, n, hello, 0)
    for peer in others:
        pl.semaphore_signal(bar, inc=1, device_id=peer, device_id_type=MESH)
    pl.semaphore_wait(bar, n - 1 + len(others))


def each_peer(me, n, make, act):
    def body(j, _):
        act(make(j, lax.rem(me + j, n)))
        return 0

    lax.fori_loop(1, n, body, 0)


def halo_copies(body_ref, left_ref, right_ref, me, n, sems):
    t = body_ref.shape[0]
    right = {"seq": lax.rem(me + 1, n)}
    left = {"seq": lax.rem(me + n - 1, n)}
    return (
        remote(body_ref.at[pl.ds(t - RAD, RAD)], left_ref, sems.at[0], sems.at[1], right),
        remote(body_ref.at[pl.ds(0, RAD)], right_ref, sems.at[2], sems.at[3], left),
    )


def mask_halos(left_ref, right_ref, me, n):
    left_ref[...] = jnp.where(me > 0, left_ref[...], jnp.zeros_like(left_ref))
    right_ref[...] = jnp.where(me < n - 1, right_ref[...], jnp.zeros_like(right_ref))


class SeqSum:
    def __init__(self, me, n, x, out, slots, total, sems):
        self.me, self.n, self.x, self.out, self.slots, self.total, self.sems = me, n, x, out, slots, total, sems
        self.chunk = x.shape[0] // n
        self.here = pl.ds(pl.multiple_of(me * self.chunk, 8), self.chunk)

    def first(self, j, peer):
        src = self.x.at[pl.ds(pl.multiple_of(peer * self.chunk, 8), self.chunk)]
        return remote(src, self.slots.at[self.me], self.sems.at[0, j], self.sems.at[1, j], {"seq": peer})

    def second(self, j, peer):
        return remote(self.total, self.out.at[self.here], self.sems.at[2, j], self.sems.at[3, j], {"seq": peer})

    def start(self):
        each_peer(self.me, self.n, self.first, lambda c: c.start())
        self.slots[pl.ds(self.me, 1)] = self.x[self.here, :][None]

    def turn(self):
        each_peer(self.me, self.n, self.first, lambda c: c.wait())
        summed = lax.fori_loop(1, self.n, lambda i, acc: acc + self.slots[i], self.slots[0])
        self.total[...] = summed
        each_peer(self.me, self.n, self.second, lambda c: c.start())
        self.out[self.here, :] = summed

    def finish(self):
        each_peer(self.me, self.n, self.second, lambda c: c.wait())

    @staticmethod
    def scratch(r, n):
        return [pltpu.VMEM((n, r // n, 128), F32), pltpu.VMEM((r // n, 128), F32), DMA((4, n))]


CHIPS = 16
STACK, HALF, ROWS, LINES = range(4)


def at(i, size, unit):
    return pl.ds(pl.multiple_of(i * size, unit), size)


def piece(kind, ref, seq, rep):
    if kind == STACK:
        half = ref.shape[2] // 2
        return ref.at[:, at(seq, ref.shape[1] // CHIPS, 16), at(rep, half, 128)]
    if kind == HALF:
        half = ref.shape[1] // 2
        return ref.at[at(seq, ref.shape[0] // CHIPS, 16), at(rep, half, 128)]
    return ref.at[at(seq * 2 + rep, ref.shape[0] // (2 * CHIPS), 8 if kind == LINES else 16), :]


class Place:
    def __init__(self):
        self.seq = lax.axis_index("seq")
        self.rep = lax.axis_index("rep")
        self.x = lax.rem(self.seq, 2)
        self.y = lax.rem(lax.div(self.seq, 2), 2)
        self.z = lax.div(self.seq, 4)
        self.twin = {"rep": 1 - self.rep}
        self.across = ({"seq": self.chip(4, self.rep)}, {"seq": self.chip(8, self.rep)})

    def chip(self, i, rep):
        j, b, a = lax.rem(i, 4), lax.rem(lax.div(i, 4), 2), lax.div(i, 8)
        z = lax.rem(self.z + 4 - j, 4)
        fx = a + rep * (b - a)
        fy = b + rep * (a - b)
        x = self.x + fx * (1 - 2 * self.x)
        y = self.y + fy * (1 - 2 * self.y)
        return z * 4 + y * 2 + x

    def above(self, j):
        return {"seq": self.chip(4 - j, self.rep)}

    def below(self, j):
        return {"seq": self.chip(j, self.rep)}


class GatherMesh:
    def __init__(self, place, kinds, outs, own, sems):
        self.place, self.kinds, self.outs, self.own = place, kinds, outs, own
        self.zsend, self.send1, self.send2, self.ssend, self.recv, self.srecv = sems

    def block(self, i, k, rep):
        return piece(self.kinds[k], self.outs[k], self.place.chip(i, rep), rep)

    def copy(self, i, k, send, recv, where):
        b = self.block(i, k, self.place.rep)
        src = b if self.own[k] is None or not (isinstance(i, int) and i == 0) else self.own[k]
        return remote(src, b, send, recv, where)

    def to_z(self, j, k):
        return self.copy(0, k, self.zsend.at[j, k], self.recv.at[j, k], self.place.above(j))

    def to_first(self, i, k):
        return self.copy(i, k, self.send1.at[i, k], self.recv.at[i + 4, k], self.place.across[0])

    def to_second(self, i, k):
        return self.copy(i, k, self.send2.at[i, k], self.recv.at[i + 8, k], self.place.across[1])

    def share(self, i, k):
        return self.copy(i, k, self.ssend.at[i, k], self.srecv.at[i, k], self.place.twin)

    def arrival(self, i, k):
        b = self.block(i, k, self.place.rep)
        return remote(b, b, self.ssend.at[i, k], self.recv.at[i, k], self.place.twin)

    def shared(self, i, k):
        b = self.block(i, k, 1 - self.place.rep)
        return remote(b, b, self.ssend.at[i, k], self.srecv.at[i, k], self.place.twin)

    def start_z(self):
        for k in range(len(self.kinds)):
            for j in (1, 2, 3):
                self.to_z(j, k).start()

    def start_across(self):
        for k in range(len(self.kinds)):
            self.to_second(0, k).start()
            self.to_first(0, k).start()
            self.share(0, k).start()

    def steps(self, low, high, which=None):
        which = range(len(self.kinds)) if which is None else which

        def body(i, _):
            for k in which:
                self.arrival(i, k).wait_recv()

                @pl.when(i < 8)
                def _():
                    self.to_second(i, k).start()

                @pl.when(i < 4)
                def _():
                    self.to_first(i, k).start()

                self.share(i, k).start()
            return 0

        lax.fori_loop(low, high, body, 0)

    def finish(self):
        for k in range(len(self.kinds)):
            for j in (1, 2, 3):
                self.to_z(j, k).wait_send()
            self.to_first(0, k).wait_send()
            self.to_second(0, k).wait_send()
            self.share(0, k).wait_send()
            self.shared(0, k).wait_recv()

        def body(i, _):
            for k in range(len(self.kinds)):

                @pl.when(i < 4)
                def _():
                    self.to_first(i, k).wait_send()

                @pl.when(i < 8)
                def _():
                    self.to_second(i, k).wait_send()

                self.share(i, k).wait_send()
                self.shared(i, k).wait_recv()
            return 0

        lax.fori_loop(1, CHIPS, body, 0)

    @staticmethod
    def scratch(k):
        return [DMA((4, k)), DMA((4, k)), DMA((8, k))] + [DMA((CHIPS, k))] * 3


class ScatterMesh:
    def __init__(self, place, kinds, grads, mine, twins, in2, in1, inz, sems):
        self.place, self.kinds, self.grads = place, kinds, grads
        self.mine, self.twins, self.in2, self.in1, self.inz = mine, twins, in2, in1, inz
        self.lsem, self.tsend, self.trecv, self.s2, self.r2, self.s1, self.r1, self.sz, self.rz = sems

    def load(self, i, k):
        src = piece(self.kinds[k], self.grads[k], self.place.chip(i, self.place.rep), self.place.rep)
        return pltpu.make_async_copy(src, self.mine[k].at[i], self.lsem.at[i, k])

    def give(self, i, k):
        other = 1 - self.place.rep
        src = piece(self.kinds[k], self.grads[k], self.place.chip(i, other), other)
        return remote(src, self.twins[k].at[i], self.tsend.at[i, k], self.trecv.at[i, k], self.place.twin)

    def out2(self, i, k):
        return remote(self.mine[k].at[i], self.in2[k].at[i - 8], self.s2.at[i - 8, k], self.r2.at[i - 8, k], self.place.across[1])

    def out1(self, i, k):
        return remote(self.mine[k].at[i], self.in1[k].at[i - 4], self.s1.at[i - 4, k], self.r1.at[i - 4, k], self.place.across[0])

    def outz(self, j, k):
        return remote(self.mine[k].at[j], self.inz[k].at[j], self.sz.at[j, k], self.rz.at[j, k], self.place.below(j))

    def start(self):
        def body(j, _):
            i = CHIPS - 1 - j
            for k in range(len(self.kinds)):
                self.give(i, k).start()
                self.load(i, k).start()
            return 0

        lax.fori_loop(0, CHIPS, body, 0)

    def terms(self, i, k):
        self.load(i, k).wait()
        self.give(i, k).wait()
        return self.mine[k][pl.ds(i, 1)].astype(F32) + self.twins[k][pl.ds(i, 1)].astype(F32)

    def far(self, k):
        def body(j, _):
            i = CHIPS - 1 - j
            self.mine[k][pl.ds(i, 1)] = self.terms(i, k).astype(self.mine[k].dtype)
            self.out2(i, k).start()
            return 0

        lax.fori_loop(0, 8, body, 0)

    def mid(self, k):
        def body(j, _):
            i = 7 - j
            own = self.terms(i, k)
            self.out2(i + 8, k).wait_recv()
            self.mine[k][pl.ds(i, 1)] = (own + self.in2[k][pl.ds(i, 1)].astype(F32)).astype(self.mine[k].dtype)
            self.out1(i, k).start()
            return 0

        lax.fori_loop(0, 4, body, 0)

    def closer(self, i, k):
        own = self.terms(i, k)
        self.out2(i + 8, k).wait_recv()
        self.out1(i + 4, k).wait_recv()
        return own + (self.in2[k][pl.ds(i, 1)].astype(F32) + self.in1[k][pl.ds(i, 1)].astype(F32))

    def near(self, k):
        def body(j, _):
            i = 3 - j
            self.mine[k][pl.ds(i, 1)] = self.closer(i, k).astype(self.mine[k].dtype)
            self.outz(i, k).start()
            return 0

        lax.fori_loop(0, 3, body, 0)

    def total(self, k):
        acc = self.closer(0, k)[0]
        for j in (1, 2, 3):
            self.outz(j, k).wait_recv()
            acc = acc + self.inz[k][j].astype(F32)
        return acc

    def finish(self):
        for k in range(len(self.kinds)):

            def body(i, _):
                @pl.when(i >= 8)
                def _():
                    self.out2(i, k).wait_send()

                @pl.when((i >= 4) & (i < 8))
                def _():
                    self.out1(i, k).wait_send()

                @pl.when(i < 4)
                def _():
                    self.outz(i, k).wait_send()

                return 0

            lax.fori_loop(1, CHIPS, body, 0)

    @staticmethod
    def scratch(blocks):
        k = len(blocks)
        return (
            [pltpu.VMEM((CHIPS, *s), t) for s, t in blocks]
            + [pltpu.VMEM((CHIPS, *s), t) for s, t in blocks]
            + [pltpu.VMEM((8, *s), t) for s, t in blocks]
            + [pltpu.VMEM((4, *s), t) for s, t in blocks]
            + [pltpu.VMEM((4, *s), t) for s, t in blocks]
            + [DMA((CHIPS, k))] * 3
            + [DMA((8, k))] * 2
            + [DMA((4, k))] * 4
        )

    @staticmethod
    def take(take, place, kinds, grads):
        k = len(kinds)
        bufs = [take(k) for _ in range(5)]
        return ScatterMesh(place, kinds, grads, *bufs, take(9))


def swap_rows(total, out, place, sems):
    rows_own = total.shape[-2] // 2
    half = total.shape[-1]
    theirs, mine = at(1 - place.rep, rows_own, 8), at(place.rep, rows_own, 8)
    cols = at(place.rep, half, 128)
    if len(total.shape) == 3:
        out[:, :, cols] = total[:, mine, :]
        return remote(total.at[:, theirs, :], out.at[:, :, cols], sems.at[0], sems.at[1], place.twin)
    out[:, cols] = total[mine, :]
    return remote(total.at[theirs, :], out.at[:, cols], sems.at[0], sems.at[1], place.twin)


CHUNK = 64
CTILE = 256


def fill_inner(ext, body_ref, start):
    count = ext.shape[1]
    rows_in = pl.ds(pl.multiple_of(start - RAD, RAD), count)
    for c in range(ext.shape[0]):
        ext[c] = body_ref[rows_in, c * 128 : (c + 1) * 128].astype(F32)


def fill_edge(ext, body_ref, left_ref, right_ref, first):
    tile = ext.shape[1] - 2 * RAD
    t = body_ref.shape[0]
    start = pl.multiple_of(jnp.where(first, 0, t - tile), tile)
    for c in range(ext.shape[0]):
        cols = slice(c * 128, (c + 1) * 128)
        ext[c, RAD : RAD + tile, :] = body_ref[pl.ds(start, tile), cols].astype(F32)
        ext[c, 0:RAD, :] = jnp.where(first, left_ref[:, cols], body_ref[t - tile - RAD : t - tile, cols]).astype(F32)
        ext[c, RAD + tile :, :] = jnp.where(first, body_ref[tile : tile + RAD, cols], right_ref[:, cols]).astype(F32)


def conv_forward(ext, tap_ref, out, row0):
    def step(r, _):
        base = pl.multiple_of(r * CHUNK, CHUNK)
        for c in range(ext.shape[0]):
            cols = slice(c * 128, (c + 1) * 128)
            acc = jnp.zeros((CHUNK, 128), F32)
            for b in range(8):
                reach = 4 if b == 0 else 3
                win = ext[c, pl.ds(base + b, CHUNK + 8 * reach), :]
                for m in range(reach + 1):
                    o = 8 * m + b
                    acc = acc + tap_ref[o : o + 1, cols] * win[8 * m : 8 * m + CHUNK]
            out[pl.ds(pl.multiple_of(row0 + base, CHUNK), CHUNK), cols] = acc.astype(out.dtype)
        return 0

    lax.fori_loop(0, CTILE // CHUNK, step, 0)


def conv_backward(vext, gext, tap_ref, out, tapacc, row0):
    width = out.shape[1] // 3

    def step(r, _):
        base = pl.multiple_of(r * CHUNK, CHUNK)
        for c in range(vext.shape[0]):
            cols = slice(c * 128, (c + 1) * 128)
            acc = jnp.zeros((CHUNK, 128), F32)
            here = gext[c, pl.ds(base + RAD, CHUNK), :]
            for b in range(8):
                reach = 4 if b == 0 else 3
                win = gext[c, pl.ds(base + b, CHUNK + 8 * reach), :]
                for m in range(reach + 1):
                    o = KC - 1 - (8 * m + b)
                    acc = acc + tap_ref[o : o + 1, cols] * win[8 * m : 8 * m + CHUNK]
                win = vext[c, pl.ds(base + b, CHUNK + 8 * reach), :]
                for m in range(reach + 1):
                    o = 8 * m + b
                    tapacc[o, :, cols] += rowsum8(here * win[8 * m : 8 * m + CHUNK])
            into = slice(2 * width + c * 128, 2 * width + (c + 1) * 128)
            out[pl.ds(pl.multiple_of(row0 + base, CHUNK), CHUNK), into] = acc.astype(out.dtype)
        return 0

    lax.fori_loop(0, CTILE // CHUNK, step, 0)


def wide_eye():
    lane = lax.broadcasted_iota(jnp.int32, (M, GROUP), 1) & 63
    return jnp.where(lane == lax.broadcasted_iota(jnp.int32, (M, GROUP), 0), 1.0, 0.0)


def head_sums(row):
    ones = jnp.where(head_mask(), 1.0, 0.0)
    return dot(jnp.broadcast_to(row, (8, GROUP)), ones, HI)[0:1]


def pinv_begin(mq_ref, mk_ref, a_ref, z_ref):
    for g in range(NG):
        s = dot_nt(mq_ref[:, gs(g)], spread(mk_ref[:, gs(g)]))
        e = jnp.exp(s - half_reduce(s, jnp.max, -jnp.inf))
        a = e / half_reduce(e, jnp.sum, 0.0)
        a_ref[:, gs(g)] = a
        col = jnp.sum(a, axis=0, keepdims=True)
        z_ref[0, :, gs(g)] = flip(a) / jnp.sqrt(head_sums(col * col))


def pinv_step(it, a_ref, z_ref, az_ref, t2_ref, t3_ref):
    eye = wide_eye()
    z = [z_ref[it, :, gs(g)] for g in range(NG)]
    az = [dot(a_ref[:, gs(g)], spread(z[g]), HI) for g in range(NG)]
    t2 = [15.0 * eye - dot(az[g], spread(7.0 * eye - az[g]), HI) for g in range(NG)]
    t3 = [13.0 * eye - dot(az[g], spread(t2[g]), HI) for g in range(NG)]
    for g in range(NG):
        z_ref[it + 1, :, gs(g)] = 0.25 * dot(z[g], spread(t3[g]), HI)
        az_ref[it, :, gs(g)] = az[g]
        t2_ref[it, :, gs(g)] = t2[g]
        t3_ref[it, :, gs(g)] = t3[g]


def pinv_back_step(it, a_ref, z_ref, az_ref, t2_ref, t3_ref, gz_ref, da_ref):
    eye = wide_eye()
    R = range(NG)
    gz = [gz_ref[:, gs(g)] for g in R]
    z = [z_ref[it, :, gs(g)] for g in R]
    az = [az_ref[it, :, gs(g)] for g in R]
    t2 = [t2_ref[it, :, gs(g)] for g in R]
    t3 = [t3_ref[it, :, gs(g)] for g in R]
    bg = [spread(0.25 * gz[g]) for g in R]
    d3 = [dot(0.25 * gz[g], spread(z[g]), HI) for g in R]
    baz = [spread(az[g]) for g in R]
    d2 = [-dot(d3[g], baz[g], HI) for g in R]
    d1 = [-dot(d2[g], baz[g], HI) for g in R]
    daz = [-dot(t2[g], spread(d3[g]), HI) - dot(7.0 * eye - az[g], spread(d2[g]), HI) - d1[g] for g in R]
    for g in R:
        da_ref[:, gs(g)] += dot(z[g], spread(daz[g]), HI)
        gz_ref[:, gs(g)] = dot(t3[g], bg[g], HI) + dot(daz[g], spread(a_ref[:, gs(g)]), HI)


def pinv_back_end(g, a_ref, gz_ref, da_ref):
    a = a_ref[:, gs(g)]
    gz = gz_ref[:, gs(g)]
    col = jnp.sum(a, axis=0, keepdims=True)
    bound = jnp.sqrt(head_sums(col * col))
    tot = head_sums(jnp.sum(gz * a, axis=0, keepdims=True))
    full = flip(da_ref[:, gs(g)]) + gz / bound - (tot / (bound * bound * bound)) * col
    return a * (full - half_reduce(full * a, jnp.sum, 0.0))


def gather_marks(slots, outs, n):
    per = 4 * n // M
    half = slots.shape[2]
    for out, base in zip(outs, (0, 4)):
        if per == 1:
            got = [slots[i].astype(F32) for i in range(n)]
            for h in range(2):
                tall = jnp.concatenate([x[8 * h + base : 8 * h + base + 4] for x in got], axis=0)
                out[:, h * half : (h + 1) * half] = tall.astype(BF16)
        else:
            for h in range(2):
                lines = []
                for m in range(M):
                    total = jnp.zeros((1, half), F32)
                    for s in range(per // 4):
                        part = slots[m * (per // 4) + s].astype(F32)[8 * h + base : 8 * h + base + 4]
                        total = total + jnp.sum(part, axis=0, keepdims=True)
                    lines.append(total * (1.0 / per))
                out[:, h * half : (h + 1) * half] = jnp.concatenate(lines, axis=0).astype(BF16)


class Refs:
    def __init__(self, refs):
        self.it = iter(refs)

    def __call__(self, count):
        return [next(self.it) for _ in range(count)]

    def one(self):
        return next(self.it)


def front_kernel(*refs, n, ring):
    take = Refs(refs)
    x_any = take.one()
    if ring:
        wa, wu, wd, wv = take(4)
        wqkv_o, wo_o, up_o, down_o = take(4)
    else:
        wq, vec = take(2)
    gains, taps = take(2)
    outs = take(7)
    mq, mk, uz, a_ref, z_ref, az_ref, t2_ref, t3_ref, vl, vr = take(10)
    xs = take.one()
    stage = take(7)
    h_s, q_s, k_s, v_s, conv_s, f_s, e_s = stage
    means, pay, slots, ext, bdk, bdq, uacc, zacc, upart = take(9)
    xsem, osem, msem, hsem = take(4)
    sum_bufs = take(3)
    me = lax.axis_index("seq")
    t, d = xs.shape
    half = d // 2
    load_x = pltpu.make_async_copy(x_any, xs, xsem.at[0])
    load_x.start()
    drains = [pltpu.make_async_copy(s, o, osem.at[i]) for i, (s, o) in enumerate(zip(stage, outs))]
    if ring:
        wq, vec, sa, su, so, cu, co, cd, psem, lsem = take(10)
        ring_one, ring_two = take(6), take(6)
        place = Place()
        greet(me, n, [place.twin])
        rep, seq = place.rep, place.seq
        rows_own, ff = d // (2 * CHIPS), wu.shape[1]
        mine = at(rep, rows_own, 8)
        theirs = 1 - rep
        swaps = (
            remote(wa.at[0:3, :, at(theirs, half, 128)], sa.at[:, mine, :], psem.at[0], psem.at[1], place.twin),
            remote(wa.at[3, :, at(theirs, half, 128)], so.at[mine, :], psem.at[2], psem.at[3], place.twin),
            remote(wu.at[:, at(theirs, ff // 2, 128)], su.at[mine, :], psem.at[4], psem.at[5], place.twin),
        )
        for c in swaps:
            c.start()
        sa[:, mine, :] = wa[0:3, :, at(rep, half, 128)]
        so[mine, :] = wa[3, :, at(rep, half, 128)]
        su[mine, :] = wu[:, at(rep, ff // 2, 128)]
        vec[at(seq * 2 + rep, rows_own, 8), :] = wv[...]
        swaps[0].wait()
        wq[:, at(seq, 2 * rows_own, 16), at(rep, half, 128)] = sa[...].astype(BF16)
        first = GatherMesh(place, (STACK, LINES), (wq, vec), (None, None), ring_one)
        first.start_z()
        first.start_across()
        cd[...] = wd[...].astype(BF16)
        swaps[1].wait()
        swaps[2].wait()
        co[...] = so[...].astype(BF16)
        cu[...] = su[...].astype(BF16)
        rest = GatherMesh(place, (HALF, HALF, ROWS), (wo_o, up_o, down_o), (co, cu, cd), ring_two)
        local = [
            pltpu.make_async_copy(src, piece(kind, out, seq, rep), lsem.at[i])
            for i, (src, kind, out) in enumerate(zip(rest.own, rest.kinds, rest.outs))
        ]

        first.steps(1, 8)
        rest.start_z()
        first.steps(8, CHIPS)
        rest.start_across()
        for c in local:
            c.start()
        first.finish()
        save_w = pltpu.make_async_copy(wq, wqkv_o, xsem.at[1])
        save_w.start()
    else:
        greet(me, n, [])

    def tick(cond, low, high, which):
        if ring:

            @pl.when(cond)
            def _():
                rest.steps(low, high, which)

    turned = jnp.transpose(vec[...]).astype(BF16).astype(F32)
    gains[...] = turned[0:8]
    taps[...] = turned[2:42]
    load_x.wait()

    def project(i, _):
        here = pl.ds(pl.multiple_of(i * (t // 4), t // 4), t // 4)
        normal, _inv = normalize(xs[here, :].astype(F32))
        h = (normal * gains[0:1, :]).astype(BF16)
        h_s[here, :] = h
        q = (dot(h, wq[0]) * QK_SCALE).astype(BF16)
        q_s[here, :] = q
        means[pl.ds(i, 1), :] = jnp.mean(q.astype(F32), axis=0, keepdims=True)
        k = (dot(h, wq[1]) * QK_SCALE).astype(BF16)
        k_s[here, :] = k
        means[pl.ds(i + 4, 1), :] = jnp.mean(k.astype(F32), axis=0, keepdims=True)
        v_s[here, :] = dot(h, wq[2]).astype(BF16)
        tick(i == 2, 1, 4, (0, 1))
        tick(i == 3, 1, 4, (2,))
        return 0

    lax.fori_loop(0, 4, project, 0)

    pay[...] = jnp.concatenate([means[:, :half], means[:, half:]], axis=0).astype(BF16)

    def mark(j, peer):
        return remote(pay, slots.at[me], msem.at[0, j], msem.at[1, j], {"seq": peer})

    halos = halo_copies(v_s, vl, vr, me, n, hsem)
    for c in halos:
        c.start()
    each_peer(me, n, mark, lambda c: c.start())
    slots[pl.ds(me, 1)] = pay[...][None]
    for c in drains[:4]:
        c.start()

    def inner(i, _):
        fill_inner(ext, v_s, i * CTILE)
        conv_forward(ext, taps, conv_s, i * CTILE)
        tick(i == 6, 4, 8, (0, 1))
        return 0

    lax.fori_loop(1, t // CTILE - 1, inner, 0)
    for c in halos:
        c.wait()
    mask_halos(vl, vr, me, n)

    def edge(i, _):
        fill_edge(ext, v_s, vl, vr, i == 0)
        conv_forward(ext, taps, conv_s, i * (t - CTILE))
        return 0

    lax.fori_loop(0, 2, edge, 0)
    drains[4].start()
    tick(True, 4, 8, (2,))
    each_peer(me, n, mark, lambda c: c.wait())
    gather_marks(slots, (mq, mk), n)
    for g in range(NG):
        bdk[g] = spread(mk[:, gs(g)])
        bdq[g] = spread(mq[:, gs(g)])
    uacc[...] = jnp.zeros_like(uacc)
    zacc[...] = jnp.zeros_like(zacc)
    ones_bd = jnp.where(head_mask(), 1.0, 0.0).astype(BF16)

    def attend(i, _):
        here = pl.ds(pl.multiple_of(i * (t // 4), t // 4), t // 4)
        for g in range(NG):
            s = dot_nt(q_s[here, gs(g)], bdk[g])
            ex = jnp.exp(s - half_reduce(s, jnp.max, -jnp.inf))
            den = dot(ex.astype(BF16), ones_bd)
            f_s[here, gs(g)] = (ex / den).astype(BF16)
            e = jnp.exp(dot_nt(k_s[here, gs(g)], bdq[g])).astype(BF16)
            e_s[here, gs(g)] = e
            uacc[g] += dot_tn(e, v_s[here, gs(g)])
            zacc[g] += dot_tn(e, jnp.ones((t // 4, 128), BF16))
        tick(i == 3, 8, CHIPS, (0,))
        return 0

    lax.fori_loop(0, 4, attend, 0)
    for c in drains[5:]:
        c.start()
    lane = lax.broadcasted_iota(jnp.int32, (M, 128), 1)
    zt = jnp.zeros((M, 128), F32)
    for g in range(NG):
        put_tall(upart, g, collect(uacc[g]))
        for h in range(4):
            zt = zt + jnp.where(lane == 4 * g + h, zacc[g, h * 64 : h * 64 + 64, :], 0.0)
    upart[6 * M : 7 * M, :] = zt
    upart[7 * M :, :] = jnp.zeros((upart.shape[0] - 7 * M, 128), F32)
    summing = SeqSum(me, n, upart, uz, *sum_bufs)
    summing.start()
    pinv_begin(mq, mk, a_ref, z_ref)

    def newton(it, _):
        pinv_step(it, a_ref, z_ref, az_ref, t2_ref, t3_ref)
        return 0

    lax.fori_loop(0, NSITER // 2, newton, 0)
    tick(True, 8, CHIPS, (1,))
    summing.turn()
    lax.fori_loop(NSITER // 2, NSITER, newton, 0)
    tick(True, 8, CHIPS, (2,))
    summing.finish()
    for c in drains:
        c.wait()
    if ring:
        for c in local:
            c.wait()
        save_w.wait()
        rest.finish()


def front(x, weights, n, ring):
    t, d = x.shape
    if ring:
        wa, wu, wd, wv = weights
        ff = wu.shape[1]
        extra_out = [sds((3, d, d), BF16), sds((d, d), BF16), sds((d, ff), BF16), sds((ff, d), BF16)]
        rown = d // CHIPS
        extra = [
            pltpu.VMEM((3, d, d), BF16),
            pltpu.VMEM((d, 128), F32),
            pltpu.VMEM((3, rown, d // 2), F32),
            pltpu.VMEM((rown, ff // 2), F32),
            pltpu.VMEM((rown, d // 2), F32),
            pltpu.VMEM((rown, ff // 2), BF16),
            pltpu.VMEM((rown, d // 2), BF16),
            pltpu.VMEM((ff // (2 * CHIPS), d), BF16),
            DMA((6,)),
            DMA((3,)),
        ] + GatherMesh.scratch(2) + GatherMesh.scratch(3)
    else:
        extra_out, extra = [], []
    r = padded_rows(7 * M, n)
    big = sds((t, d), BF16)
    steps = sds((NSITER, M, d), F32)
    res = pl.pallas_call(
        functools.partial(front_kernel, n=n, ring=ring),
        in_specs=[ANYW] + [VM] * len(weights),
        out_specs=[ANYW] * len(extra_out) + [VM] * 2 + [ANYW] * 7 + [VM] * 10,
        out_shape=extra_out
        + [sds((8, d), F32), sds((40, d), F32)]
        + [big] * 7
        + [sds((M, d), BF16)] * 2
        + [sds((r, 128), F32), sds((M, d), F32), sds((NSITER + 1, M, d), F32), steps, steps, steps]
        + [sds((RAD, d), BF16)] * 2,
        scratch_shapes=[pltpu.VMEM((t, d), BF16)] * 8
        + [
            pltpu.VMEM((8, d), F32),
            pltpu.VMEM((16, d // 2), BF16),
            pltpu.VMEM((n, 16, d // 2), BF16),
            pltpu.VMEM((d // 128, CTILE + 2 * RAD, 128), F32),
            pltpu.VMEM((NG, GROUP, GROUP), BF16),
            pltpu.VMEM((NG, GROUP, GROUP), BF16),
            pltpu.VMEM((NG, GROUP, GROUP), F32),
            pltpu.VMEM((NG, GROUP, 128), F32),
            pltpu.VMEM((r, 128), F32),
            DMA((2,)),
            DMA((7,)),
            DMA((2, n)),
            DMA((4,)),
        ]
        + SeqSum.scratch(r, n)
        + extra,
        compiler_params=pltpu.CompilerParams(collective_id=1, has_side_effects=True, vmem_limit_bytes=VMEM_LIMIT),
        name="front",
    )(x, *weights)
    return res if ring else [None] * 4 + list(res)


FCHUNK = 512


def middle_kernel(
    x_ref, dy_ref, f_ref, q_ref, conv_ref, wo_ref, up_ref, down_ref, gain_ref, mk_ref, uz_ref, z_ref,
    out_ref, act_ref, da_ref, h2_ref, mix_ref, dx_ref, dmix_ref, dqf_ref, gw_ref, dkt_ref, dg_ref,
    wbd, gwacc, dktacc, dgacc, oacc, hacc,
):
    i = pl.program_id(0)
    n = pl.num_programs(0)
    tile = x_ref.shape[0]
    d = x_ref.shape[1]

    @pl.when(i == 0)
    def _():
        gwacc[...] = jnp.zeros_like(gwacc)
        dktacc[...] = jnp.zeros_like(dktacc)
        dgacc[...] = jnp.zeros_like(dgacc)
        for g in range(NG):
            bv = u_group(uz_ref, g) / zt_group(uz_ref, g)
            wbd[g] = spread(dot(z_ref[NSITER, :, gs(g)], spread(bv), HI)).astype(BF16)

    for g in range(NG):
        mix_ref[:, gs(g)] = (dot(f_ref[:, gs(g)], wbd[g]) + conv_ref[:, gs(g)].astype(F32)).astype(BF16)
    x1 = x_ref[...].astype(F32) + dot(mix_ref[...], wo_ref[...])
    normal, inv = normalize(x1)
    gain = gain_ref[1:2, :]
    h2 = (normal * gain).astype(BF16)
    h2_ref[...] = h2
    dy = dy_ref[...]
    ff = up_ref.shape[1]
    for j in range(ff // FCHUNK):
        cols = slice(j * FCHUNK, (j + 1) * FCHUNK)
        a = dot(h2, up_ref[:, cols])
        act, slope = gelu_parts(a)
        act = act.astype(BF16)
        act_ref[:, cols] = act
        da = (dot_nt(dy, down_ref[cols, :]) * slope).astype(BF16)
        da_ref[:, cols] = da
        o = dot(act, down_ref[cols, :])
        h = dot_nt(da, up_ref[:, cols])
        if j == 0:
            oacc[...] = o
            hacc[...] = h
        else:
            oacc[...] += o
            hacc[...] += h
    out_ref[...] = (x1 + oacc[...]).astype(BF16)
    dh2 = hacc[...]
    dgacc[...] += rowsum8(dh2 * normal)
    dx1 = norm_back(dh2, normal, inv, gain) + dy.astype(F32)
    do = dx1.astype(BF16)
    dx_ref[...] = do
    dmix = dot_nt(do, wo_ref[...]).astype(BF16)
    dmix_ref[...] = dmix
    ones_bd = jnp.where(head_mask(), 1.0, 0.0).astype(BF16)
    for g in range(NG):
        dm = dmix[:, gs(g)]
        f = f_ref[:, gs(g)]
        df = dot_nt(dm, wbd[g])
        gwacc[g] += dot_tn(f, dm)
        ff32 = f.astype(F32)
        prod = df * ff32
        hi = prod.astype(BF16)
        lo = (prod - hi.astype(F32)).astype(BF16)
        ds = (ff32 * (df - (dot(hi, ones_bd) + dot(lo, ones_bd)))).astype(BF16)
        dqf_ref[:, gs(g)] = dot(ds, spread(mk_ref[:, gs(g)])).astype(BF16)
        dktacc[g] += dot_tn(ds, q_ref[:, gs(g)])

    @pl.when(i == n - 1)
    def _():
        for g in range(NG):
            put_tall(gw_ref, g, collect(gwacc[g]))
            dkt_ref[:, gs(g)] = collect(dktacc[g])
        if gw_ref.shape[0] > 6 * M:
            gw_ref[6 * M :] = jnp.zeros((gw_ref.shape[0] - 6 * M, 128), F32)
        dg_ref[...] = jnp.broadcast_to(jnp.sum(dgacc[...], axis=0, keepdims=True), (8, d))


def middle(x, dy, f, q, conv, wo, up, down, gains, mk, uz, z, gw_rows):
    t, d = x.shape
    ff = up.shape[1]
    tile = 256
    r = rows(tile, d)
    rf = rows(tile, ff)
    return pl.pallas_call(
        middle_kernel,
        grid=(t // tile,),
        in_specs=[r, r, r, r, r, whole((d, d)), whole(up.shape), whole(down.shape), whole(gains.shape), whole((M, d)),
                  whole(uz.shape), whole(z.shape)],
        out_specs=[r, rf, rf, r, r, r, r, r, whole((gw_rows, 128)), whole((M, d)), whole((8, d))],
        out_shape=[sds((t, d), BF16), sds((t, ff), BF16), sds((t, ff), BF16)] + [sds((t, d), BF16)] * 5
        + [sds((gw_rows, 128), F32), sds((M, d), F32), sds((8, d), F32)],
        scratch_shapes=[
            pltpu.VMEM((NG, GROUP, GROUP), BF16),
            pltpu.VMEM((NG, GROUP, GROUP), F32),
            pltpu.VMEM((NG, GROUP, GROUP), F32),
            pltpu.VMEM((8, d), F32),
            pltpu.VMEM((tile, d), F32),
            pltpu.VMEM((tile, d), F32),
        ],
        compiler_params=params(),
        name="middle",
    )(x, dy, f, q, conv, wo, up, down, gains, mk, uz, z)


def rear_kernel(*refs, n, ring, seg_len):
    take = Refs(refs)
    bodies = take(5)
    if ring:
        grads = take(3)
    gw_part, uz, a_ref, z_ref, az_ref, t2_ref, t3_ref, mq, mk, vl, vr, taps, dkt_ref, dg2_ref = take(14)
    dqkv_o, gvec_o = take(2)
    if ring:
        r_o, r_up, r_down, r_vec = take(4)
    v_s, g_s, e_s, k_s, dqf_s, dqkv, gvec = take(7)
    vext, gext, tapacc, gl, gr, gw, gz, da, dubd, rowadd, dqtacc, bdq, pay, slots, own = take(15)
    isem, osem, hsem, wsem = take(4)
    sum_bufs = take(3)
    me = lax.axis_index("seq")
    t, d = v_s.shape
    loads = [
        pltpu.make_async_copy(b, s, isem.at[i]) for i, (b, s) in enumerate(zip(bodies, (v_s, g_s, e_s, k_s, dqf_s)))
    ]
    for c in loads:
        c.start()
    if ring:
        place = Place()
        greet(me, n, [place.twin])
        big = ScatterMesh.take(take, place, (HALF, HALF, ROWS), grads)
        vec = ScatterMesh.take(take, place, (LINES,), (gvec,))
        fo, fu, fsem = take(3)
    else:
        greet(me, n, [])
    summing = SeqSum(me, n, gw_part, gw, *sum_bufs)
    loads[1].wait()
    halos = halo_copies(g_s, gl, gr, me, n, hsem)
    for c in halos:
        c.start()
    summing.start()
    if ring:
        big.start()

    def tick(cond, *acts):
        if ring:

            @pl.when(cond)
            def _():
                for act, k in acts:
                    act(k)

    tapacc[...] = jnp.zeros_like(tapacc)
    loads[0].wait()
    if not ring:
        big = vec = None
    far = (lambda k: big.far(k))
    mid = (lambda k: big.mid(k))
    near = (lambda k: big.near(k))

    def inner(i, _):
        fill_inner(vext, v_s, i * CTILE)
        fill_inner(gext, g_s, i * CTILE)
        conv_backward(vext, gext, taps, dqkv, tapacc, i * CTILE)
        tick(i == 1, (far, 0))
        tick(i == 2, (far, 1))
        tick(i == 3, (far, 2))
        tick(i == 5, (mid, 0))

        @pl.when(i == 4)
        def _():
            summing.turn()

        return 0

    lax.fori_loop(1, t // CTILE - 1, inner, 0)
    tick(True, (mid, 1))
    for c in halos:
        c.wait()
    mask_halos(gl, gr, me, n)

    def edge(i, _):
        fill_edge(vext, v_s, vl, vr, i == 0)
        fill_edge(gext, g_s, gl, gr, i == 0)
        conv_backward(vext, gext, taps, dqkv, tapacc, i * (t - CTILE))
        return 0

    lax.fori_loop(0, 2, edge, 0)
    dtap = jnp.sum(tapacc[...], axis=1)
    lines = jnp.concatenate([jnp.zeros((1, d), F32), dg2_ref[0:1, :], dtap, jnp.zeros((128 - 42, d), F32)], axis=0)
    gvec[...] = jnp.transpose(lines)
    if ring:
        vec.start()
    else:
        save_vec = pltpu.make_async_copy(gvec, gvec_o, osem.at[1])
        save_vec.start()
    tick(True, (mid, 2), (near, 0))
    summing.finish()
    for g in range(NG):
        z = zt_group(uz, g)
        bv = u_group(uz, g) / z
        gwg = u_group(gw, g)
        gz[:, gs(g)] = flip(dot_nt(gwg, spread(bv), HI))
        dbv = dot(flip(z_ref[NSITER, :, gs(g)]), spread(gwg), HI)
        dubd[g] = spread(dbv / z).astype(BF16)
        rowadd[g] = dot_nt(jnp.ones((8, GROUP), F32), spread(dbv * bv / z), HI)
        bdq[g] = spread(mq[:, gs(g)])
    da[...] = jnp.zeros_like(da)

    def newton(j, _):
        pinv_back_step(NSITER - 1 - j, a_ref, z_ref, az_ref, t2_ref, t3_ref, gz, da)
        tick(j == 0, (lambda k: vec.far(k), 0))
        tick(j == 1, (near, 1))
        tick(j == 2, (lambda k: vec.mid(k), 0))
        tick(j == 3, (near, 2))
        tick(j == 4, (lambda k: vec.near(k), 0))
        return 0

    lax.fori_loop(0, NSITER, newton, 0)
    loads[2].wait()
    loads[3].wait()
    dqtacc[...] = jnp.zeros_like(dqtacc)

    def cols(part, g):
        return slice(part * d + g * GROUP, part * d + (g + 1) * GROUP)

    def through(i, _):
        here = pl.ds(pl.multiple_of(i * (t // 4), t // 4), t // 4)
        for g in range(NG):
            e = e_s[here, gs(g)]
            de = dot_nt(v_s[here, gs(g)], dubd[g]) - rowadd[g, 0:1, :]
            ds = (e.astype(F32) * de).astype(BF16)
            dqkv[here, cols(2, g)] = (dot(e, dubd[g]) + dqkv[here, cols(2, g)].astype(F32)).astype(BF16)
            dqkv[here, cols(1, g)] = dot(ds, bdq[g]).astype(BF16)
            dqtacc[g] += dot_tn(ds, k_s[here, gs(g)])
        return 0

    lax.fori_loop(0, 4, through, 0)

    rows_dev = max(M // n, 1)
    per_mark = n * rows_dev // M
    if rows_dev < 4:
        pay[...] = jnp.zeros_like(pay)
    for g in range(NG):
        ds = pinv_back_end(g, a_ref, gz, da)
        dq = collect(dqtacc[g]) + dot(ds, spread(mk[:, gs(g)].astype(F32)), HI) * (1.0 / n)
        dk = dkt_ref[:, gs(g)] + dot(flip(ds), spread(mq[:, gs(g)].astype(F32)), HI) * (1.0 / n)
        for i in range(n):
            row = i * rows_dev // per_mark
            pay[i, 0:rows_dev, gs(g)] = dq[row : row + rows_dev]
            pay[i, 4 : 4 + rows_dev, gs(g)] = dk[row : row + rows_dev]

    def mark(j, peer):
        return remote(pay.at[peer], slots.at[me], wsem.at[0, j], wsem.at[1, j], {"seq": peer})

    each_peer(me, n, mark, lambda c: c.start())
    slots[pl.ds(me, 1)] = pay[pl.ds(me, 1)]
    if ring:
        fo[...] = big.total(0)
        fu[...] = big.total(1)
        back = (swap_rows(fo, r_o, place, fsem.at[0]), swap_rows(fu, r_up, place, fsem.at[1]))
        for c in back:
            c.start()
        r_down[...] = big.total(2)
        r_vec[...] = vec.total(0)
    loads[4].wait()
    each_peer(me, n, mark, lambda c: c.wait())
    own[...] = lax.fori_loop(1, n, lambda i, acc: acc + slots[i], slots[0]) * (1.0 / seg_len)

    def landed(i, _):
        here = pl.ds(pl.multiple_of(i * (t // 4), t // 4), t // 4)
        row = lax.div(i * rows_dev, 4)
        dqkv[here, 0:d] = (dqf_s[here, :].astype(F32) + own[pl.ds(row, 1), :]).astype(BF16)
        dqkv[here, d : 2 * d] = (dqkv[here, d : 2 * d].astype(F32) + own[pl.ds(row + 4, 1), :]).astype(BF16)
        pltpu.make_async_copy(dqkv.at[here], dqkv_o.at[here], osem.at[2 + i]).start()
        return 0

    lax.fori_loop(0, 4, landed, 0)
    if ring:
        for c in back:
            c.wait()
        big.finish()
        vec.finish()
        save_vec = pltpu.make_async_copy(gvec, gvec_o, osem.at[1])
        save_vec.start()
    for i in range(4):
        here = pl.ds(i * (t // 4), t // 4)
        pltpu.make_async_copy(dqkv.at[here], dqkv_o.at[here], osem.at[2 + i]).wait()
    save_vec.wait()


def rear(bodies, grads, gw, uz, a, z, az, t2, t3, mq, mk, vl, vr, taps, dkt, dg2, n, seg_len):
    ring = grads is not None
    t, d = bodies[0].shape
    r = gw.shape[0]
    outs = [sds((t, 3 * d), BF16), sds((d, 128), F32)]
    extra = []
    if ring:
        ff = grads[1].shape[1]
        own = d // (2 * CHIPS)
        outs += [sds((own, d), F32), sds((own, ff), F32), sds((ff // (2 * CHIPS), d), F32), sds((own, 128), F32)]
        blocks = [((2 * own, d // 2), BF16), ((2 * own, ff // 2), BF16), ((ff // (2 * CHIPS), d), BF16)]
        extra = ScatterMesh.scratch(blocks) + ScatterMesh.scratch([((own, 128), F32)]) + [
            pltpu.VMEM((2 * own, d // 2), F32),
            pltpu.VMEM((2 * own, ff // 2), F32),
            DMA((2, 2)),
        ]
    ext = pltpu.VMEM((d // 128, CTILE + 2 * RAD, 128), F32)
    halo = pltpu.VMEM((RAD, d), BF16)
    small = pltpu.VMEM((M, d), F32)
    return pl.pallas_call(
        functools.partial(rear_kernel, n=n, ring=ring, seg_len=seg_len),
        in_specs=[ANYW] * (5 + (3 if ring else 0)) + [VM] * 14,
        out_specs=[ANYW] * 2 + [VM] * (len(outs) - 2),
        out_shape=outs,
        scratch_shapes=[pltpu.VMEM((t, d), BF16)] * 5
        + [
            pltpu.VMEM((t, 3 * d), BF16),
            pltpu.VMEM((d, 128), F32),
            ext,
            ext,
            pltpu.VMEM((40, 8, d), F32),
            halo,
            halo,
            pltpu.VMEM((r, 128), F32),
            small,
            small,
            pltpu.VMEM((NG, GROUP, GROUP), BF16),
            pltpu.VMEM((NG, 8, GROUP), F32),
            pltpu.VMEM((NG, GROUP, GROUP), F32),
            pltpu.VMEM((NG, GROUP, GROUP), BF16),
            pltpu.VMEM((n, 8, d), F32),
            pltpu.VMEM((n, 8, d), F32),
            pltpu.VMEM((8, d), F32),
            DMA((5,)),
            DMA((6,)),
            DMA((4,)),
            DMA((2, n)),
        ]
        + SeqSum.scratch(r, n)
        + extra,
        compiler_params=pltpu.CompilerParams(collective_id=2, has_side_effects=True, vmem_limit_bytes=VMEM_LIMIT),
        name="rear",
    )(*bodies, *(grads if ring else ()), gw, uz, a, z, az, t2, t3, mq, mk, vl, vr, taps, dkt, dg2)


def last_kernel(*refs, n, ring):
    take = Refs(refs)
    x_a, dx_a, dqkv_a, w_a = take(4)
    if ring:
        grads = take(1)
    (gains,) = take(1)
    ig_o, dg_o = take(2)
    if ring:
        (r_qkv,) = take(1)
    x_s, dx_s, dqkv_s, w_s, ig_s, part, slots, dgacc, isem, osem, gsem = take(11)
    t, d = x_s.shape
    tile = t // 4
    me = lax.axis_index("seq")

    def here(i):
        return pl.ds(pl.multiple_of(i * tile, tile), tile)

    def loads(i):
        return [
            pltpu.make_async_copy(a.at[here(i)], s.at[here(i)], isem.at[k, i])
            for k, (a, s) in enumerate(((x_a, x_s), (dx_a, dx_s), (dqkv_a, dqkv_s)))
        ]

    load_w = pltpu.make_async_copy(w_a, w_s, isem.at[3, 0])
    load_w.start()
    if ring:
        place = Place()
        greet(me, n, [place.twin])
        scatter = ScatterMesh.take(take, place, (HALF,), grads)
        fq, fsem = take(2)
        scatter.start()
    else:
        greet(me, n, [])
    for i in range(4):
        for c in loads(i):
            c.start()
    if ring:
        scatter.far(0)
    load_w.wait()
    dgacc[...] = jnp.zeros_like(dgacc)

    def body(i, _):
        for c in loads(i):
            c.wait()
        dq, dk, dv = (dqkv_s[here(i), p * d : (p + 1) * d] for p in range(3))
        dh = (dot_nt(dq, w_s[0]) + dot_nt(dk, w_s[1])) * QK_SCALE + dot_nt(dv, w_s[2])
        normal, inv = normalize(x_s[here(i), :].astype(F32))
        dgacc[...] += rowsum8(dh * normal)
        ig = norm_back(dh, normal, inv, gains[0:1, :]) + dx_s[here(i), :].astype(F32)
        ig_s[here(i), :] = ig.astype(BF16)
        pltpu.make_async_copy(ig_s.at[here(i)], ig_o.at[here(i)], osem.at[i]).start()
        if ring:

            @pl.when(i == 2)
            def _():
                scatter.mid(0)

        return 0

    lax.fori_loop(0, 4, body, 0)
    row = jnp.sum(dgacc[...], axis=0, keepdims=True)
    part[...] = jnp.concatenate(
        [row[:, c : c + 128] for c in range(0, d, 128)] + [jnp.zeros((8 - d // 128, 128), F32)], axis=0
    )

    def send(j, peer):
        return remote(part, slots.at[me], gsem.at[0, j], gsem.at[1, j], {"seq": peer})

    each_peer(me, n, send, lambda c: c.start())
    slots[pl.ds(me, 1)] = part[...][None]
    if ring:
        scatter.near(0)
    each_peer(me, n, send, lambda c: c.wait())
    total = lax.fori_loop(1, n, lambda i, acc: acc + slots[i], slots[0])
    if ring:
        twin_sum = remote(dg_o.at[0], dg_o.at[1], gsem.at[0, 0], gsem.at[1, 0], place.twin)
        dg_o[0] = total
        twin_sum.start()
        fq[...] = scatter.total(0)
        back = swap_rows(fq, r_qkv, place, fsem)
        back.start()
        scatter.finish()
        twin_sum.wait()
        back.wait()
    else:
        dg_o[0] = total
        dg_o[1] = jnp.zeros_like(total)
    for i in range(4):
        pltpu.make_async_copy(ig_s.at[here(i)], ig_o.at[here(i)], osem.at[i]).wait()


def last(x, dx, dqkv, w_qkv, gains, g_qkv, n):
    ring = g_qkv is not None
    t, d = x.shape
    outs = [sds((t, d), BF16), sds((2, 8, 128), F32)]
    extra = []
    if ring:
        own = d // (2 * CHIPS)
        wide = g_qkv.shape[1]
        outs += [sds((own, wide), F32)]
        extra = ScatterMesh.scratch([((2 * own, wide // 2), BF16)]) + [pltpu.VMEM((2 * own, wide // 2), F32), DMA((2,))]
    return pl.pallas_call(
        functools.partial(last_kernel, n=n, ring=ring),
        in_specs=[ANYW] * (4 + (1 if ring else 0)) + [VM],
        out_specs=[ANYW] + [VM] * (len(outs) - 1),
        out_shape=outs,
        scratch_shapes=[
            pltpu.VMEM((t, d), BF16),
            pltpu.VMEM((t, d), BF16),
            pltpu.VMEM((t, 3 * d), BF16),
            pltpu.VMEM((3, d, d), BF16),
            pltpu.VMEM((t, d), BF16),
            pltpu.VMEM((8, 128), F32),
            pltpu.VMEM((n, 8, 128), F32),
            pltpu.VMEM((8, d), F32),
            DMA((4, 4)),
            DMA((4,)),
            DMA((2, n)),
        ]
        + extra,
        compiler_params=pltpu.CompilerParams(collective_id=3, has_side_effects=True, vmem_limit_bytes=VMEM_LIMIT),
        name="last",
    )(x, dx, dqkv, w_qkv, *((g_qkv,) if ring else ()), gains)


def adam_step(weight, grad_vec, moment, second, rate_value):
    moment_new = BETA_ONE * moment + (1.0 - BETA_ONE) * grad_vec
    second_new = BETA_TWO * second + (1.0 - BETA_TWO) * grad_vec * grad_vec
    first_hat = moment_new / (1.0 - BETA_ONE**STEP)
    second_hat = second_new / (1.0 - BETA_TWO**STEP)
    weight_new = weight - rate_value * (
        first_hat / (jnp.sqrt(second_hat) + ADAM_EPS) + DECAY_RATE * weight
    )
    return (weight_new, moment_new, second_new)


def per_device(tokens, cotangent, attn_w, w_up, w_down, vectors, attn_m, attn_v, up_m, up_v, down_m, down_v, vec_m, vec_v):
    both = ("seq", "rep")
    x = tokens[0]
    dy = cotangent[0]
    t, d = x.shape
    n = lax.axis_size("seq")
    seg_len = t * n // M
    ring = n == CHIPS and lax.axis_size("rep") == 2

    if ring:
        weights = (attn_w, w_up, w_down, jnp.pad(vectors, ((0, 0), (0, 128 - vectors.shape[1]))))
    else:
        w_attn = lax.all_gather(attn_w.astype(BF16), both, axis=1, tiled=True)
        vec = lax.all_gather(vectors.astype(BF16), both, axis=0, tiled=True).astype(F32)
        weights = (w_attn[:3], jnp.pad(vec, ((0, 0), (0, 128 - vec.shape[1]))))
    (w_qkv, wo, up, down, gains, taps, h1, q, k, v, conv, f, e, mq, mk, uz, a, z, az, t2, t3, vl, vr) = front(
        x, weights, n, ring
    )
    if not ring:
        w_qkv, wo = w_attn[:3], w_attn[3]
        up = lax.all_gather(w_up.astype(BF16), both, axis=0, tiled=True)
        down = lax.all_gather(w_down.astype(BF16), both, axis=0, tiled=True)
    out, act, da, h2, mix, dx, dmix, dqf, gw, dkt, dg2 = middle(
        x, dy, f, q, conv, wo, up, down, gains, mk, uz, z, padded_rows(6 * M, n)
    )
    dot_xla = functools.partial(jnp.einsum, "ta,tb->ab", preferred_element_type=F32)
    g_down = dot_xla(act, dy).astype(BF16)
    g_up = dot_xla(h2, da).astype(BF16)
    g_o = dot_xla(mix, dx).astype(BF16)
    res = rear(
        (v, dmix, e, k, dqf), (g_o, g_up, g_down) if ring else None, gw, uz, a, z, az, t2, t3, mq, mk, vl, vr, taps, dkt, dg2, n, seg_len
    )
    dqkv, g_vec = res[:2]
    column = jnp.concatenate([jnp.full((2 * d,), QK_SCALE, F32), jnp.ones((d,), F32)])
    g_qkv = (dot_xla(h1, dqkv) * column).astype(BF16)
    fin = last(x, dx, dqkv, w_qkv, gains, g_qkv if ring else None, n)
    ig = fin[0]
    dg1 = (fin[1][0] + fin[1][1])[: d // 128].reshape(d)
    if ring:
        red_o, red_up, red_down, red_vec = res[2:]
        own = d // (2 * n)
        red_qkv = jnp.transpose(fin[2].reshape(own, 3, d), (1, 0, 2))
        red_attn = jnp.concatenate([red_qkv, red_o[None]], axis=0)
        start = (lax.axis_index("seq") * 2 + lax.axis_index("rep")) * own
        dg1_own = lax.dynamic_slice_in_dim(dg1, start, own, 0)
        red_vec = jnp.concatenate([dg1_own[:, None], red_vec[:, 1 : vectors.shape[1]]], axis=1)
    else:
        g_attn = jnp.concatenate([jnp.transpose(g_qkv.reshape(d, 3, d), (1, 0, 2)), g_o[None]], axis=0)
        red_attn = lax.psum_scatter(g_attn, both, scatter_dimension=1, tiled=True).astype(F32)
        red_up = lax.psum_scatter(g_up, both, scatter_dimension=0, tiled=True).astype(F32)
        red_down = lax.psum_scatter(g_down, both, scatter_dimension=0, tiled=True).astype(F32)
        g_vec = jnp.concatenate([dg1[:, None] / n, g_vec[:, 1 : vectors.shape[1]]], axis=1)
        red_vec = lax.psum_scatter(g_vec, both, scatter_dimension=0, tiled=True)
    return (
        out[None],
        ig[None],
        *adam_step(attn_w, red_attn, attn_m, attn_v, LEARN_RATE),
        *adam_step(w_up, red_up, up_m, up_v, LEARN_RATE),
        *adam_step(w_down, red_down, down_m, down_v, LEARN_RATE),
        *adam_step(vectors, red_vec, vec_m, vec_v, VECTOR_RATE),
    )


def solution(mesh):
    tok = P("rep", "seq", None)
    att = P(None, ("seq", "rep"), None)
    mat = P(("seq", "rep"), None)
    return jax.shard_map(
        per_device,
        mesh=mesh,
        in_specs=(tok, tok, att, mat, mat, mat, att, att, mat, mat, mat, mat, mat, mat),
        out_specs=(tok, tok, att, att, att) + (mat,) * 9,
        check_vma=False,
    )
```

```python
import functools

import jax
import jax.numpy as jnp
from jax import lax
from jax.experimental import pallas as pl
from jax.experimental.pallas import tpu as pltpu
from jax.sharding import PartitionSpec as P

H = 12
HD = 64
M = 64
KC = 33
NSITER = 6
STEP = 10
EPS_NORM = 1e-05
BETA_ONE = 0.9
BETA_TWO = 0.999
ADAM_EPS = 1e-08
LEARN_RATE = 0.03
VECTOR_RATE = 0.15
DECAY_RATE = 0.1

F32 = jnp.float32
BF16 = jnp.bfloat16
GROUP = 256
NG = 3
RAD = 16
QK_SCALE = HD ** (-0.25)
HI = lax.Precision.HIGHEST
VMEM_LIMIT = 58 * 1024 * 1024


def dot(a, b, precision=None):
    return lax.dot_general(a, b, (((1,), (0,)), ((), ())), precision=precision, preferred_element_type=F32)


def dot_nt(a, b, precision=None):
    return lax.dot_general(a, b, (((1,), (1,)), ((), ())), precision=precision, preferred_element_type=F32)


def dot_tn(a, b, precision=None):
    return lax.dot_general(a, b, (((0,), (0,)), ((), ())), precision=precision, preferred_element_type=F32)


def split(x):
    hi = x.astype(BF16)
    return hi, (x - hi.astype(F32)).astype(BF16)


def dot3(a, b):
    return dot(a[0], b[0]) + (dot(a[0], b[1]) + dot(a[1], b[0]))


def spread2(a):
    return spread(a[0]), spread(a[1])


def head_mask(shape=(GROUP, GROUP)):
    rows = lax.broadcasted_iota(jnp.int32, shape, 0)
    cols = lax.broadcasted_iota(jnp.int32, shape, 1)
    return lax.shift_right_logical(rows, 6) == lax.shift_right_logical(cols, 6)


def spread(wide):
    tall = jnp.concatenate([wide, wide, wide, wide], axis=0)
    return jnp.where(head_mask(), tall, jnp.zeros_like(tall))


def collect(full):
    kept = jnp.where(head_mask(), full, jnp.zeros_like(full))
    return (kept[0:64] + kept[64:128]) + (kept[128:192] + kept[192:256])


def flip(wide):
    turned = jnp.transpose(spread(wide))
    return (turned[0:64] + turned[64:128]) + (turned[128:192] + turned[192:256])


def gs(g):
    return slice(g * GROUP, (g + 1) * GROUP)


def half_reduce(x, op, init):
    parts = []
    for c in range(x.shape[1] // 128):
        col = x[:, c * 128 : (c + 1) * 128]
        low = lax.broadcasted_iota(jnp.int32, col.shape, 1) < 64
        a = op(jnp.where(low, col, init), axis=1, keepdims=True)
        b = op(jnp.where(low, init, col), axis=1, keepdims=True)
        parts.append(jnp.where(low, a, b))
    return jnp.concatenate(parts, axis=1)


def normalize(x):
    center = x - jnp.mean(x, axis=-1, keepdims=True)
    inv = lax.rsqrt(jnp.mean(center * center, axis=-1, keepdims=True) + EPS_NORM)
    return center * inv, inv


def norm_back(up, normal, inv, gain):
    scaled = up * gain
    centered = scaled - jnp.mean(scaled, axis=-1, keepdims=True)
    return inv * (centered - normal * jnp.mean(scaled * normal, axis=-1, keepdims=True))


def rowsum8(x):
    return jnp.sum(x.reshape(x.shape[0] // 8, 8, x.shape[1]), axis=0)


def gelu_parts(a):
    z = jnp.abs(a)
    t = 1.0 / (1.0 + (0.3275911 * 0.7071067811865476) * z)
    e = jnp.exp(-0.5 * a * a)
    poly = t * (0.127414796 + t * (-0.142248368 + t * (0.7107068705 + t * (-0.7265760135 + t * 0.5307027145))))
    tail = poly * e
    phi = jnp.where(a >= 0, 1.0 - tail, tail)
    return a * phi, phi + a * (e * 0.3989422804014327)


def whole(shape):
    zeros = (0,) * len(shape)
    return pl.BlockSpec(shape, lambda i: zeros, pipeline_mode=pl.Buffered(1))


def rows(tile, width):
    return pl.BlockSpec((tile, width), lambda i: (i, 0))


def sds(shape, dtype):
    return jax.ShapeDtypeStruct(shape, dtype)


def params():
    return pltpu.CompilerParams(dimension_semantics=("arbitrary",), vmem_limit_bytes=VMEM_LIMIT)


def widen(zt, g):
    return jnp.concatenate(
        [jnp.broadcast_to(zt[:, h : h + 1], (M, HD)) for h in range(4 * g, 4 * g + 4)], axis=1
    )


def u_group(ref, g):
    return jnp.concatenate([ref[2 * g * M : (2 * g + 1) * M, :], ref[(2 * g + 1) * M : (2 * g + 2) * M, :]], axis=1)


def zt_group(ref, g):
    return widen(ref[6 * M : 7 * M, :], g)


def put_tall(ref, g, wide):
    ref[2 * g * M : (2 * g + 1) * M, :] = wide[:, :128]
    ref[(2 * g + 1) * M : (2 * g + 2) * M, :] = wide[:, 128:]


def padded_rows(r, n):
    return -(-r // (8 * n)) * 8 * n


MESH = pl.DeviceIdType.MESH
DMA = pltpu.SemaphoreType.DMA
VM = pl.BlockSpec(memory_space=pltpu.VMEM)
ANYW = pl.BlockSpec(memory_space=pl.ANY)


def remote(src, dst, send, recv, where):
    return pltpu.make_async_remote_copy(
        src_ref=src, dst_ref=dst, send_sem=send, recv_sem=recv, device_id=where, device_id_type=MESH
    )


def greet(me, n, others):
    bar = pltpu.get_barrier_semaphore()

    def hello(j, _):
        pl.semaphore_signal(bar, inc=1, device_id={"seq": lax.rem(me + j, n)}, device_id_type=MESH)
        return 0

    lax.fori_loop(1, n, hello, 0)
    for peer in others:
        pl.semaphore_signal(bar, inc=1, device_id=peer, device_id_type=MESH)
    pl.semaphore_wait(bar, n - 1 + len(others))


def each_peer(me, n, make, act):
    def body(j, _):
        act(make(j, lax.rem(me + j, n)))
        return 0

    lax.fori_loop(1, n, body, 0)


def halo_copies(body_ref, left_ref, right_ref, me, n, sems):
    t = body_ref.shape[0]
    right = {"seq": lax.rem(me + 1, n)}
    left = {"seq": lax.rem(me + n - 1, n)}
    return (
        remote(body_ref.at[pl.ds(t - RAD, RAD)], left_ref, sems.at[0], sems.at[1], right),
        remote(body_ref.at[pl.ds(0, RAD)], right_ref, sems.at[2], sems.at[3], left),
    )


def mask_halos(left_ref, right_ref, me, n):
    left_ref[...] = jnp.where(me > 0, left_ref[...], jnp.zeros_like(left_ref))
    right_ref[...] = jnp.where(me < n - 1, right_ref[...], jnp.zeros_like(right_ref))


class SeqSum:
    def __init__(self, me, n, x, out, slots, total, sems):
        self.me, self.n, self.x, self.out, self.slots, self.total, self.sems = me, n, x, out, slots, total, sems
        self.chunk = x.shape[0] // n
        self.here = pl.ds(pl.multiple_of(me * self.chunk, 8), self.chunk)

    def first(self, j, peer):
        src = self.x.at[pl.ds(pl.multiple_of(peer * self.chunk, 8), self.chunk)]
        return remote(src, self.slots.at[self.me], self.sems.at[0, j], self.sems.at[1, j], {"seq": peer})

    def second(self, j, peer):
        return remote(self.total, self.out.at[self.here], self.sems.at[2, j], self.sems.at[3, j], {"seq": peer})

    def start(self):
        each_peer(self.me, self.n, self.first, lambda c: c.start())
        self.slots[pl.ds(self.me, 1)] = self.x[self.here, :][None]

    def turn(self):
        each_peer(self.me, self.n, self.first, lambda c: c.wait())
        summed = lax.fori_loop(1, self.n, lambda i, acc: acc + self.slots[i], self.slots[0])
        self.total[...] = summed
        each_peer(self.me, self.n, self.second, lambda c: c.start())
        self.out[self.here, :] = summed

    def finish(self):
        each_peer(self.me, self.n, self.second, lambda c: c.wait())

    @staticmethod
    def scratch(r, n):
        return [pltpu.VMEM((n, r // n, 128), F32), pltpu.VMEM((r // n, 128), F32), DMA((4, n))]


CHIPS = 16
STACK, HALF, ROWS, LINES = range(4)


def at(i, size, unit):
    return pl.ds(pl.multiple_of(i * size, unit), size)


def piece(kind, ref, seq, rep):
    if kind == STACK:
        half = ref.shape[2] // 2
        return ref.at[:, at(seq, ref.shape[1] // CHIPS, 16), at(rep, half, 128)]
    if kind == HALF:
        half = ref.shape[1] // 2
        return ref.at[at(seq, ref.shape[0] // CHIPS, 16), at(rep, half, 128)]
    return ref.at[at(seq * 2 + rep, ref.shape[0] // (2 * CHIPS), 8 if kind == LINES else 16), :]


class Place:
    def __init__(self):
        self.seq = lax.axis_index("seq")
        self.rep = lax.axis_index("rep")
        self.x = lax.rem(self.seq, 2)
        self.y = lax.rem(lax.div(self.seq, 2), 2)
        self.z = lax.div(self.seq, 4)
        self.twin = {"rep": 1 - self.rep}
        self.across = ({"seq": self.chip(4, self.rep)}, {"seq": self.chip(8, self.rep)})

    def chip(self, i, rep):
        j, b, a = lax.rem(i, 4), lax.rem(lax.div(i, 4), 2), lax.div(i, 8)
        z = lax.rem(self.z + 4 - j, 4)
        fx = a + rep * (b - a)
        fy = b + rep * (a - b)
        x = self.x + fx * (1 - 2 * self.x)
        y = self.y + fy * (1 - 2 * self.y)
        return z * 4 + y * 2 + x

    def above(self, j):
        return {"seq": self.chip(4 - j, self.rep)}

    def below(self, j):
        return {"seq": self.chip(j, self.rep)}


class GatherMesh:
    def __init__(self, place, kinds, outs, own, sems):
        self.place, self.kinds, self.outs, self.own = place, kinds, outs, own
        self.zsend, self.send1, self.send2, self.ssend, self.recv, self.srecv = sems

    def block(self, i, k, rep):
        return piece(self.kinds[k], self.outs[k], self.place.chip(i, rep), rep)

    def copy(self, i, k, send, recv, where):
        b = self.block(i, k, self.place.rep)
        src = b if self.own[k] is None or not (isinstance(i, int) and i == 0) else self.own[k]
        return remote(src, b, send, recv, where)

    def to_z(self, j, k):
        return self.copy(0, k, self.zsend.at[j, k], self.recv.at[j, k], self.place.above(j))

    def to_first(self, i, k):
        return self.copy(i, k, self.send1.at[i, k], self.recv.at[i + 4, k], self.place.across[0])

    def to_second(self, i, k):
        return self.copy(i, k, self.send2.at[i, k], self.recv.at[i + 8, k], self.place.across[1])

    def share(self, i, k):
        return self.copy(i, k, self.ssend.at[i, k], self.srecv.at[i, k], self.place.twin)

    def arrival(self, i, k):
        b = self.block(i, k, self.place.rep)
        return remote(b, b, self.ssend.at[i, k], self.recv.at[i, k], self.place.twin)

    def shared(self, i, k):
        b = self.block(i, k, 1 - self.place.rep)
        return remote(b, b, self.ssend.at[i, k], self.srecv.at[i, k], self.place.twin)

    def start_z(self):
        for k in range(len(self.kinds)):
            for j in (1, 2, 3):
                self.to_z(j, k).start()

    def start_across(self):
        for k in range(len(self.kinds)):
            self.to_second(0, k).start()
            self.to_first(0, k).start()
            self.share(0, k).start()

    def each(self, low, high, which, act):
        def body(i, _):
            for k in which:
                act(i, k)
            return 0

        lax.fori_loop(low, high, body, 0)

    def line(self, which):
        def act(i, k):
            self.arrival(i, k).wait_recv()
            self.to_first(i, k).start()
            self.share(i, k).start()

        self.each(1, 4, which, act)

    def line_on(self, which):
        self.each(1, 4, which, lambda i, k: self.to_second(i, k).start())

    def plane(self, which):
        def act(i, k):
            self.arrival(i, k).wait_recv()
            self.to_second(i, k).start()
            self.share(i, k).start()

        self.each(4, 8, which, act)

    def space(self, which):
        def act(i, k):
            self.arrival(i, k).wait_recv()
            self.share(i, k).start()

        self.each(8, CHIPS, which, act)

    def shares_in(self, which):
        self.shared_first(which)
        self.each(1, CHIPS, which, lambda i, k: self.shared(i, k).wait_recv())

    def shared_first(self, which):
        for k in which:
            self.shared(0, k).wait_recv()

    def finish(self):
        which = range(len(self.kinds))
        for k in which:
            for j in (1, 2, 3):
                self.to_z(j, k).wait_send()
            self.to_first(0, k).wait_send()
            self.to_second(0, k).wait_send()
            self.share(0, k).wait_send()

        def act(i, k):
            @pl.when(i < 4)
            def _():
                self.to_first(i, k).wait_send()

            @pl.when(i < 8)
            def _():
                self.to_second(i, k).wait_send()

            self.share(i, k).wait_send()

        self.each(1, CHIPS, which, act)

    @staticmethod
    def scratch(k):
        return [DMA((4, k)), DMA((4, k)), DMA((8, k))] + [DMA((CHIPS, k))] * 3


class ScatterMesh:
    def __init__(self, place, kinds, grads, mine, twins, in2, in1, inz, sems):
        self.place, self.kinds, self.grads = place, kinds, grads
        self.mine, self.twins, self.in2, self.in1, self.inz = mine, twins, in2, in1, inz
        self.lsem, self.tsend, self.trecv, self.s2, self.r2, self.s1, self.r1, self.sz, self.rz = sems

    def load(self, i, k):
        src = piece(self.kinds[k], self.grads[k], self.place.chip(i, self.place.rep), self.place.rep)
        return pltpu.make_async_copy(src, self.mine[k].at[i], self.lsem.at[i, k])

    def give(self, i, k):
        other = 1 - self.place.rep
        src = piece(self.kinds[k], self.grads[k], self.place.chip(i, other), other)
        return remote(src, self.twins[k].at[i], self.tsend.at[i, k], self.trecv.at[i, k], self.place.twin)

    def out2(self, i, k):
        return remote(self.mine[k].at[i], self.in2[k].at[i - 8], self.s2.at[i - 8, k], self.r2.at[i - 8, k], self.place.across[1])

    def out1(self, i, k):
        return remote(self.mine[k].at[i], self.in1[k].at[i - 4], self.s1.at[i - 4, k], self.r1.at[i - 4, k], self.place.across[0])

    def outz(self, j, k):
        return remote(self.mine[k].at[j], self.inz[k].at[j], self.sz.at[j, k], self.rz.at[j, k], self.place.below(j))

    def start(self):
        for low in (8, 0):
            for k in range(len(self.kinds)):

                def body(j, _):
                    self.give(low + 7 - j, k).start()
                    self.load(low + 7 - j, k).start()
                    return 0

                lax.fori_loop(0, 8, body, 0)

    def terms(self, i, k):
        self.load(i, k).wait()
        self.give(i, k).wait()
        return self.mine[k][pl.ds(i, 1)].astype(F32) + self.twins[k][pl.ds(i, 1)].astype(F32)

    def far(self, k):
        def body(j, _):
            i = CHIPS - 1 - j
            self.mine[k][pl.ds(i, 1)] = self.terms(i, k).astype(self.mine[k].dtype)
            self.out2(i, k).start()
            return 0

        lax.fori_loop(0, 8, body, 0)

    def mid(self, k):
        def body(j, _):
            i = 7 - j
            own = self.terms(i, k)
            self.out2(i + 8, k).wait_recv()
            self.mine[k][pl.ds(i, 1)] = (own + self.in2[k][pl.ds(i, 1)].astype(F32)).astype(self.mine[k].dtype)
            self.out1(i, k).start()
            return 0

        lax.fori_loop(0, 4, body, 0)

    def closer(self, i, k):
        own = self.terms(i, k)
        self.out2(i + 8, k).wait_recv()
        self.out1(i + 4, k).wait_recv()
        return own + (self.in2[k][pl.ds(i, 1)].astype(F32) + self.in1[k][pl.ds(i, 1)].astype(F32))

    def near(self, k):
        def body(j, _):
            i = 3 - j
            self.mine[k][pl.ds(i, 1)] = self.closer(i, k).astype(self.mine[k].dtype)
            self.outz(i, k).start()
            return 0

        lax.fori_loop(0, 3, body, 0)

    def total(self, k):
        acc = self.closer(0, k)[0]
        for j in (1, 2, 3):
            self.outz(j, k).wait_recv()
            acc = acc + self.inz[k][j].astype(F32)
        return acc

    def finish(self):
        for k in range(len(self.kinds)):

            def body(i, _):
                @pl.when(i >= 8)
                def _():
                    self.out2(i, k).wait_send()

                @pl.when((i >= 4) & (i < 8))
                def _():
                    self.out1(i, k).wait_send()

                @pl.when(i < 4)
                def _():
                    self.outz(i, k).wait_send()

                return 0

            lax.fori_loop(1, CHIPS, body, 0)

    @staticmethod
    def scratch(blocks):
        k = len(blocks)
        return (
            [pltpu.VMEM((CHIPS, *s), t) for s, t in blocks]
            + [pltpu.VMEM((CHIPS, *s), t) for s, t in blocks]
            + [pltpu.VMEM((8, *s), t) for s, t in blocks]
            + [pltpu.VMEM((4, *s), t) for s, t in blocks]
            + [pltpu.VMEM((4, *s), t) for s, t in blocks]
            + [DMA((CHIPS, k))] * 3
            + [DMA((8, k))] * 2
            + [DMA((4, k))] * 4
        )

    @staticmethod
    def take(take, place, kinds, grads):
        k = len(kinds)
        bufs = [take(k) for _ in range(5)]
        return ScatterMesh(place, kinds, grads, *bufs, take(9))


def swap_rows(total, out, place, sems):
    rows_own = total.shape[-2] // 2
    half = total.shape[-1]
    theirs, mine = at(1 - place.rep, rows_own, 8), at(place.rep, rows_own, 8)
    cols = at(place.rep, half, 128)
    if len(total.shape) == 3:
        out[:, :, cols] = total[:, mine, :]
        return remote(total.at[:, theirs, :], out.at[:, :, cols], sems.at[0], sems.at[1], place.twin)
    out[:, cols] = total[mine, :]
    return remote(total.at[theirs, :], out.at[:, cols], sems.at[0], sems.at[1], place.twin)


CHUNK = 64
CTILE = 256


def fill_inner(ext, body_ref, start):
    count = ext.shape[1]
    rows_in = pl.ds(pl.multiple_of(start - RAD, RAD), count)
    for c in range(ext.shape[0]):
        ext[c] = body_ref[rows_in, c * 128 : (c + 1) * 128].astype(F32)


def fill_edge(ext, body_ref, left_ref, right_ref, first):
    tile = ext.shape[1] - 2 * RAD
    t = body_ref.shape[0]
    start = pl.multiple_of(jnp.where(first, 0, t - tile), tile)
    for c in range(ext.shape[0]):
        cols = slice(c * 128, (c + 1) * 128)
        ext[c, RAD : RAD + tile, :] = body_ref[pl.ds(start, tile), cols].astype(F32)
        ext[c, 0:RAD, :] = jnp.where(first, left_ref[:, cols], body_ref[t - tile - RAD : t - tile, cols]).astype(F32)
        ext[c, RAD + tile :, :] = jnp.where(first, body_ref[tile : tile + RAD, cols], right_ref[:, cols]).astype(F32)


def conv_forward(ext, tap_ref, out, row0):
    def step(r, _):
        base = pl.multiple_of(r * CHUNK, CHUNK)
        for c in range(ext.shape[0]):
            cols = slice(c * 128, (c + 1) * 128)
            acc = jnp.zeros((CHUNK, 128), F32)
            for b in range(8):
                reach = 4 if b == 0 else 3
                win = ext[c, pl.ds(base + b, CHUNK + 8 * reach), :]
                for m in range(reach + 1):
                    o = 8 * m + b
                    acc = acc + tap_ref[o : o + 1, cols] * win[8 * m : 8 * m + CHUNK]
            out[pl.ds(pl.multiple_of(row0 + base, CHUNK), CHUNK), cols] = acc.astype(out.dtype)
        return 0

    lax.fori_loop(0, CTILE // CHUNK, step, 0)


def conv_backward(vext, gext, tap_ref, out, tapacc, row0):
    width = out.shape[1] // 3

    def step(r, _):
        base = pl.multiple_of(r * CHUNK, CHUNK)
        for c in range(vext.shape[0]):
            cols = slice(c * 128, (c + 1) * 128)
            acc = jnp.zeros((CHUNK, 128), F32)
            here = gext[c, pl.ds(base + RAD, CHUNK), :]
            for b in range(8):
                reach = 4 if b == 0 else 3
                win = gext[c, pl.ds(base + b, CHUNK + 8 * reach), :]
                for m in range(reach + 1):
                    o = KC - 1 - (8 * m + b)
                    acc = acc + tap_ref[o : o + 1, cols] * win[8 * m : 8 * m + CHUNK]
                win = vext[c, pl.ds(base + b, CHUNK + 8 * reach), :]
                for m in range(reach + 1):
                    o = 8 * m + b
                    tapacc[o, :, cols] += rowsum8(here * win[8 * m : 8 * m + CHUNK])
            into = slice(2 * width + c * 128, 2 * width + (c + 1) * 128)
            out[pl.ds(pl.multiple_of(row0 + base, CHUNK), CHUNK), into] = acc.astype(out.dtype)
        return 0

    lax.fori_loop(0, CTILE // CHUNK, step, 0)


def wide_eye():
    lane = lax.broadcasted_iota(jnp.int32, (M, GROUP), 1) & 63
    return jnp.where(lane == lax.broadcasted_iota(jnp.int32, (M, GROUP), 0), 1.0, 0.0)


def head_sums(row):
    ones = jnp.where(head_mask(), 1.0, 0.0)
    return dot(jnp.broadcast_to(row, (8, GROUP)), ones, HI)[0:1]


def pinv_begin(mq_ref, mk_ref, a_ref, z_ref):
    for g in range(NG):
        s = dot_nt(mq_ref[:, gs(g)], spread(mk_ref[:, gs(g)]))
        e = jnp.exp(s - half_reduce(s, jnp.max, -jnp.inf))
        a = e / half_reduce(e, jnp.sum, 0.0)
        a_ref[:, gs(g)] = a
        col = jnp.sum(a, axis=0, keepdims=True)
        z_ref[0, :, gs(g)] = flip(a) / jnp.sqrt(head_sums(col * col))


def pinv_step(it, a_ref, z_ref, az_ref, t2_ref, t3_ref):
    eye = wide_eye()
    R = range(NG)
    z = [split(z_ref[it, :, gs(g)]) for g in R]
    az = [dot3(split(a_ref[:, gs(g)]), spread2(z[g])) for g in R]
    azs = [split(az[g]) for g in R]
    t2 = [15.0 * eye - dot3(azs[g], spread2(split(7.0 * eye - az[g]))) for g in R]
    t3 = [13.0 * eye - dot3(azs[g], spread2(split(t2[g]))) for g in R]
    for g in R:
        z_ref[it + 1, :, gs(g)] = 0.25 * dot3(z[g], spread2(split(t3[g])))
        az_ref[it, :, gs(g)] = az[g]
        t2_ref[it, :, gs(g)] = t2[g]
        t3_ref[it, :, gs(g)] = t3[g]


def pinv_back_step(it, a_ref, z_ref, az_ref, t2_ref, t3_ref, gz_ref, da_ref):
    eye = wide_eye()
    R = range(NG)
    az = [az_ref[it, :, gs(g)] for g in R]
    zs = [split(z_ref[it, :, gs(g)]) for g in R]
    gzs = [split(0.25 * gz_ref[:, gs(g)]) for g in R]
    baz = [spread2(split(az[g])) for g in R]
    d3 = [split(dot3(gzs[g], spread2(zs[g]))) for g in R]
    d2 = [split(-dot3(d3[g], baz[g])) for g in R]
    d1 = [-dot3(d2[g], baz[g]) for g in R]
    daz = [
        split(
            -dot3(split(t2_ref[it, :, gs(g)]), spread2(d3[g]))
            - dot3(split(7.0 * eye - az[g]), spread2(d2[g]))
            - d1[g]
        )
        for g in R
    ]
    for g in R:
        da_ref[:, gs(g)] += dot3(zs[g], spread2(daz[g]))
        gz_ref[:, gs(g)] = dot3(split(t3_ref[it, :, gs(g)]), spread2(gzs[g])) + dot3(
            daz[g], spread2(split(a_ref[:, gs(g)]))
        )


def pinv_back_end(g, a_ref, gz_ref, da_ref):
    a = a_ref[:, gs(g)]
    gz = gz_ref[:, gs(g)]
    col = jnp.sum(a, axis=0, keepdims=True)
    bound = jnp.sqrt(head_sums(col * col))
    tot = head_sums(jnp.sum(gz * a, axis=0, keepdims=True))
    full = flip(da_ref[:, gs(g)]) + gz / bound - (tot / (bound * bound * bound)) * col
    return a * (full - half_reduce(full * a, jnp.sum, 0.0))


def gather_marks(slots, outs, n):
    per = 4 * n // M
    half = slots.shape[2]
    for out, base in zip(outs, (0, 4)):
        if per == 1:
            got = [slots[i].astype(F32) for i in range(n)]
            for h in range(2):
                tall = jnp.concatenate([x[8 * h + base : 8 * h + base + 4] for x in got], axis=0)
                out[:, h * half : (h + 1) * half] = tall.astype(BF16)
        else:
            for h in range(2):
                lines = []
                for m in range(M):
                    total = jnp.zeros((1, half), F32)
                    for s in range(per // 4):
                        part = slots[m * (per // 4) + s].astype(F32)[8 * h + base : 8 * h + base + 4]
                        total = total + jnp.sum(part, axis=0, keepdims=True)
                    lines.append(total * (1.0 / per))
                out[:, h * half : (h + 1) * half] = jnp.concatenate(lines, axis=0).astype(BF16)


class Refs:
    def __init__(self, refs):
        self.it = iter(refs)

    def __call__(self, count):
        return [next(self.it) for _ in range(count)]

    def one(self):
        return next(self.it)


def front_kernel(*refs, n, ring):
    take = Refs(refs)
    x_any = take.one()
    if ring:
        wa, wu, wd, wv = take(4)
        wqkv_o, wo_o, up_o, down_o = take(4)
    else:
        wq, vec = take(2)
    gains, taps = take(2)
    outs = take(7)
    mq, mk, uz, a_ref, z_ref, az_ref, t2_ref, t3_ref, vl, vr = take(10)
    xs = take.one()
    stage = take(7)
    h_s, q_s, k_s, v_s, conv_s, f_s, e_s = stage
    means, pay, slots, ext, bdk, bdq, uacc, zacc, upart = take(9)
    xsem, osem, msem, hsem = take(4)
    sum_bufs = take(3)
    me = lax.axis_index("seq")
    t, d = xs.shape
    half = d // 2
    load_x = pltpu.make_async_copy(x_any, xs, xsem.at[0])
    load_x.start()
    drains = [pltpu.make_async_copy(s, o, osem.at[i]) for i, (s, o) in enumerate(zip(stage, outs))]
    if ring:
        wq, vec, sa, su, so, cu, co, cd, psem, lsem = take(10)
        ring_one, ring_two = take(6), take(6)
        place = Place()
        greet(me, n, [place.twin])
        rep, seq = place.rep, place.seq
        rows_own, ff = d // (2 * CHIPS), wu.shape[1]
        mine = at(rep, rows_own, 8)
        theirs = 1 - rep
        swaps = (
            remote(wa.at[0:3, :, at(theirs, half, 128)], sa.at[:, mine, :], psem.at[0], psem.at[1], place.twin),
            remote(wa.at[3, :, at(theirs, half, 128)], so.at[mine, :], psem.at[2], psem.at[3], place.twin),
            remote(wu.at[:, at(theirs, ff // 2, 128)], su.at[mine, :], psem.at[4], psem.at[5], place.twin),
        )
        for c in swaps:
            c.start()
        sa[:, mine, :] = wa[0:3, :, at(rep, half, 128)]
        so[mine, :] = wa[3, :, at(rep, half, 128)]
        su[mine, :] = wu[:, at(rep, ff // 2, 128)]
        vec[at(seq * 2 + rep, rows_own, 8), :] = wv[...]
        swaps[0].wait()
        wq[:, at(seq, 2 * rows_own, 16), at(rep, half, 128)] = sa[...].astype(BF16)
        first = GatherMesh(place, (LINES, HALF, HALF, HALF), (vec, wq.at[2], wq.at[1], wq.at[0]), (None,) * 4, ring_one)
        first.start_z()
        first.start_across()
        cd[...] = wd[...].astype(BF16)
        swaps[1].wait()
        swaps[2].wait()
        co[...] = so[...].astype(BF16)
        cu[...] = su[...].astype(BF16)
        rest = GatherMesh(place, (HALF, ROWS, HALF), (up_o, down_o, wo_o), (cu, cd, co), ring_two)
        local = [
            pltpu.make_async_copy(src, piece(kind, out, seq, rep), lsem.at[i])
            for i, (src, kind, out) in enumerate(zip(rest.own, rest.kinds, rest.outs))
        ]

        rest.start_z()
        for c in local:
            c.start()
        for which in ((0, 1), (2,), (3,)):
            first.line(which)
            first.line_on(which)
            first.plane(which)
        rest.start_across()
        first.space((0,))
        first.shares_in((0,))
        save_w = pltpu.make_async_copy(wq, wqkv_o, xsem.at[1])
    else:
        greet(me, n, [])

    turned = jnp.transpose(vec[...]).astype(BF16).astype(F32)
    gains[...] = turned[0:8]
    taps[...] = turned[2:42]
    load_x.wait()

    def tile(i):
        return pl.ds(pl.multiple_of(i * (t // 4), t // 4), t // 4)

    def norm(i, _):
        normal, _inv = normalize(xs[tile(i), :].astype(F32))
        h_s[tile(i), :] = (normal * gains[0:1, :]).astype(BF16)
        return 0

    def project_v(i, _):
        v_s[tile(i), :] = dot(h_s[tile(i), :], wq[2]).astype(BF16)
        return 0

    def project_k(i, _):
        k = (dot(h_s[tile(i), :], wq[1]) * QK_SCALE).astype(BF16)
        k_s[tile(i), :] = k
        means[pl.ds(i + 4, 1), :] = jnp.mean(k.astype(F32), axis=0, keepdims=True)
        return 0

    def project_q(i, _):
        q = (dot(h_s[tile(i), :], wq[0]) * QK_SCALE).astype(BF16)
        q_s[tile(i), :] = q
        means[pl.ds(i, 1), :] = jnp.mean(q.astype(F32), axis=0, keepdims=True)
        return 0

    lax.fori_loop(0, 4, norm, 0)
    if ring:
        first.space((1,))
        first.shares_in((1,))
    lax.fori_loop(0, 4, project_v, 0)
    if ring:
        rest.line((0,))
        first.space((2,))
        first.shares_in((2,))
    lax.fori_loop(0, 4, project_k, 0)
    if ring:
        first.space((3,))
        first.shares_in((3,))
        save_w.start()
        rest.line_on((0,))
    lax.fori_loop(0, 4, project_q, 0)

    pay[...] = jnp.concatenate([means[:, :half], means[:, half:]], axis=0).astype(BF16)

    def mark(j, peer):
        return remote(pay, slots.at[me], msem.at[0, j], msem.at[1, j], {"seq": peer})

    halos = halo_copies(v_s, vl, vr, me, n, hsem)
    for c in halos:
        c.start()
    each_peer(me, n, mark, lambda c: c.start())
    slots[pl.ds(me, 1)] = pay[...][None]
    for c in drains[:4]:
        c.start()

    def inner(i, _):
        fill_inner(ext, v_s, i * CTILE)
        conv_forward(ext, taps, conv_s, i * CTILE)

        if ring:

            @pl.when(i == 2)
            def _():
                rest.line((1,))
                rest.line_on((1,))

            @pl.when(i == 5)
            def _():
                rest.plane((0,))

        return 0

    lax.fori_loop(1, t // CTILE - 1, inner, 0)
    for c in halos:
        c.wait()
    mask_halos(vl, vr, me, n)

    def edge(i, _):
        fill_edge(ext, v_s, vl, vr, i == 0)
        conv_forward(ext, taps, conv_s, i * (t - CTILE))
        return 0

    lax.fori_loop(0, 2, edge, 0)
    drains[4].start()
    each_peer(me, n, mark, lambda c: c.wait())
    if ring:
        rest.line((2,))
        rest.line_on((2,))
    gather_marks(slots, (mq, mk), n)
    for g in range(NG):
        bdk[g] = spread(mk[:, gs(g)])
        bdq[g] = spread(mq[:, gs(g)])
    uacc[...] = jnp.zeros_like(uacc)
    zacc[...] = jnp.zeros_like(zacc)
    ones_bd = jnp.where(head_mask(), 1.0, 0.0).astype(BF16)

    def attend(i, _):
        here = pl.ds(pl.multiple_of(i * (t // 4), t // 4), t // 4)
        for g in range(NG):
            s = dot_nt(q_s[here, gs(g)], bdk[g])
            ex = jnp.exp(s - half_reduce(s, jnp.max, -jnp.inf))
            den = dot(ex.astype(BF16), ones_bd)
            f_s[here, gs(g)] = (ex / den).astype(BF16)
            e = jnp.exp(dot_nt(k_s[here, gs(g)], bdq[g])).astype(BF16)
            e_s[here, gs(g)] = e
            uacc[g] += dot_tn(e, v_s[here, gs(g)])
            zacc[g] += dot_tn(e, jnp.ones((t // 4, 128), BF16))
        if ring:

            @pl.when(i == 0)
            def _():
                rest.plane((1,))

            @pl.when(i == 1)
            def _():
                rest.plane((2,))

        return 0

    lax.fori_loop(0, 4, attend, 0)
    for c in drains[5:]:
        c.start()
    lane = lax.broadcasted_iota(jnp.int32, (M, 128), 1)
    zt = jnp.zeros((M, 128), F32)
    for g in range(NG):
        put_tall(upart, g, collect(uacc[g]))
        for h in range(4):
            zt = zt + jnp.where(lane == 4 * g + h, zacc[g, h * 64 : h * 64 + 64, :], 0.0)
    upart[6 * M : 7 * M, :] = zt
    upart[7 * M :, :] = jnp.zeros((upart.shape[0] - 7 * M, 128), F32)
    summing = SeqSum(me, n, upart, uz, *sum_bufs)
    summing.start()
    pinv_begin(mq, mk, a_ref, z_ref)

    def newton(it, _):
        pinv_step(it, a_ref, z_ref, az_ref, t2_ref, t3_ref)
        return 0

    lax.fori_loop(0, NSITER // 2, newton, 0)
    summing.turn()
    lax.fori_loop(NSITER // 2, NSITER, newton, 0)
    summing.finish()
    for c in drains:
        c.wait()
    if ring:
        for c in local:
            c.wait()
        save_w.wait()
        rest.space((0, 1, 2))
        rest.shares_in((0, 1, 2))
        first.finish()
        rest.finish()


def front(x, weights, n, ring):
    t, d = x.shape
    if ring:
        wa, wu, wd, wv = weights
        ff = wu.shape[1]
        extra_out = [sds((3, d, d), BF16), sds((d, d), BF16), sds((d, ff), BF16), sds((ff, d), BF16)]
        rown = d // CHIPS
        extra = [
            pltpu.VMEM((3, d, d), BF16),
            pltpu.VMEM((d, 128), F32),
            pltpu.VMEM((3, rown, d // 2), F32),
            pltpu.VMEM((rown, ff // 2), F32),
            pltpu.VMEM((rown, d // 2), F32),
            pltpu.VMEM((rown, ff // 2), BF16),
            pltpu.VMEM((rown, d // 2), BF16),
            pltpu.VMEM((ff // (2 * CHIPS), d), BF16),
            DMA((6,)),
            DMA((3,)),
        ] + GatherMesh.scratch(4) + GatherMesh.scratch(3)
    else:
        extra_out, extra = [], []
    r = padded_rows(7 * M, n)
    big = sds((t, d), BF16)
    steps = sds((NSITER, M, d), F32)
    res = pl.pallas_call(
        functools.partial(front_kernel, n=n, ring=ring),
        in_specs=[ANYW] + [VM] * len(weights),
        out_specs=[ANYW] * len(extra_out) + [VM] * 2 + [ANYW] * 7 + [VM] * 10,
        out_shape=extra_out
        + [sds((8, d), F32), sds((40, d), F32)]
        + [big] * 7
        + [sds((M, d), BF16)] * 2
        + [sds((r, 128), F32), sds((M, d), F32), sds((NSITER + 1, M, d), F32), steps, steps, steps]
        + [sds((RAD, d), BF16)] * 2,
        scratch_shapes=[pltpu.VMEM((t, d), BF16)] * 8
        + [
            pltpu.VMEM((8, d), F32),
            pltpu.VMEM((16, d // 2), BF16),
            pltpu.VMEM((n, 16, d // 2), BF16),
            pltpu.VMEM((d // 128, CTILE + 2 * RAD, 128), F32),
            pltpu.VMEM((NG, GROUP, GROUP), BF16),
            pltpu.VMEM((NG, GROUP, GROUP), BF16),
            pltpu.VMEM((NG, GROUP, GROUP), F32),
            pltpu.VMEM((NG, GROUP, 128), F32),
            pltpu.VMEM((r, 128), F32),
            DMA((2,)),
            DMA((7,)),
            DMA((2, n)),
            DMA((4,)),
        ]
        + SeqSum.scratch(r, n)
        + extra,
        compiler_params=pltpu.CompilerParams(collective_id=1, has_side_effects=True, vmem_limit_bytes=VMEM_LIMIT),
        name="front",
    )(x, *weights)
    return res if ring else [None] * 4 + list(res)


FCHUNK = 512


def middle_kernel(
    x_ref, dy_ref, f_ref, q_ref, conv_ref, wo_ref, up_ref, down_ref, gain_ref, mk_ref, uz_ref, z_ref,
    out_ref, act_ref, da_ref, h2_ref, mix_ref, dx_ref, dmix_ref, dqf_ref, gw_ref, dkt_ref, dg_ref,
    wbd, gwacc, dktacc, dgacc, oacc, hacc,
):
    i = pl.program_id(0)
    n = pl.num_programs(0)
    tile = x_ref.shape[0]
    d = x_ref.shape[1]

    @pl.when(i == 0)
    def _():
        gwacc[...] = jnp.zeros_like(gwacc)
        dktacc[...] = jnp.zeros_like(dktacc)
        dgacc[...] = jnp.zeros_like(dgacc)
        for g in range(NG):
            bv = u_group(uz_ref, g) / zt_group(uz_ref, g)
            wbd[g] = spread(dot(z_ref[NSITER, :, gs(g)], spread(bv), HI)).astype(BF16)

    for g in range(NG):
        mix_ref[:, gs(g)] = (dot(f_ref[:, gs(g)], wbd[g]) + conv_ref[:, gs(g)].astype(F32)).astype(BF16)
    x1 = x_ref[...].astype(F32) + dot(mix_ref[...], wo_ref[...])
    normal, inv = normalize(x1)
    gain = gain_ref[1:2, :]
    h2 = (normal * gain).astype(BF16)
    h2_ref[...] = h2
    dy = dy_ref[...]
    ff = up_ref.shape[1]
    for j in range(ff // FCHUNK):
        cols = slice(j * FCHUNK, (j + 1) * FCHUNK)
        a = dot(h2, up_ref[:, cols])
        act, slope = gelu_parts(a)
        act = act.astype(BF16)
        act_ref[:, cols] = act
        da = (dot_nt(dy, down_ref[cols, :]) * slope).astype(BF16)
        da_ref[:, cols] = da
        o = dot(act, down_ref[cols, :])
        h = dot_nt(da, up_ref[:, cols])
        if j == 0:
            oacc[...] = o
            hacc[...] = h
        else:
            oacc[...] += o
            hacc[...] += h
    out_ref[...] = (x1 + oacc[...]).astype(BF16)
    dh2 = hacc[...]
    dgacc[...] += rowsum8(dh2 * normal)
    dx1 = norm_back(dh2, normal, inv, gain) + dy.astype(F32)
    do = dx1.astype(BF16)
    dx_ref[...] = do
    dmix = dot_nt(do, wo_ref[...]).astype(BF16)
    dmix_ref[...] = dmix
    ones_bd = jnp.where(head_mask(), 1.0, 0.0).astype(BF16)
    for g in range(NG):
        dm = dmix[:, gs(g)]
        f = f_ref[:, gs(g)]
        df = dot_nt(dm, wbd[g])
        gwacc[g] += dot_tn(f, dm)
        ff32 = f.astype(F32)
        prod = df * ff32
        hi = prod.astype(BF16)
        lo = (prod - hi.astype(F32)).astype(BF16)
        ds = (ff32 * (df - (dot(hi, ones_bd) + dot(lo, ones_bd)))).astype(BF16)
        dqf_ref[:, gs(g)] = dot(ds, spread(mk_ref[:, gs(g)])).astype(BF16)
        dktacc[g] += dot_tn(ds, q_ref[:, gs(g)])

    @pl.when(i == n - 1)
    def _():
        for g in range(NG):
            put_tall(gw_ref, g, collect(gwacc[g]))
            dkt_ref[:, gs(g)] = collect(dktacc[g])
        if gw_ref.shape[0] > 6 * M:
            gw_ref[6 * M :] = jnp.zeros((gw_ref.shape[0] - 6 * M, 128), F32)
        dg_ref[...] = jnp.broadcast_to(jnp.sum(dgacc[...], axis=0, keepdims=True), (8, d))


def middle(x, dy, f, q, conv, wo, up, down, gains, mk, uz, z, gw_rows):
    t, d = x.shape
    ff = up.shape[1]
    tile = 512
    r = rows(tile, d)
    rf = rows(tile, ff)
    return pl.pallas_call(
        middle_kernel,
        grid=(t // tile,),
        in_specs=[r, r, r, r, r, whole((d, d)), whole(up.shape), whole(down.shape), whole(gains.shape), whole((M, d)),
                  whole(uz.shape), whole(z.shape)],
        out_specs=[r, rf, rf, r, r, r, r, r, whole((gw_rows, 128)), whole((M, d)), whole((8, d))],
        out_shape=[sds((t, d), BF16), sds((t, ff), BF16), sds((t, ff), BF16)] + [sds((t, d), BF16)] * 5
        + [sds((gw_rows, 128), F32), sds((M, d), F32), sds((8, d), F32)],
        scratch_shapes=[
            pltpu.VMEM((NG, GROUP, GROUP), BF16),
            pltpu.VMEM((NG, GROUP, GROUP), F32),
            pltpu.VMEM((NG, GROUP, GROUP), F32),
            pltpu.VMEM((8, d), F32),
            pltpu.VMEM((tile, d), F32),
            pltpu.VMEM((tile, d), F32),
        ],
        compiler_params=params(),
        name="middle",
    )(x, dy, f, q, conv, wo, up, down, gains, mk, uz, z)


def rear_kernel(*refs, n, ring, seg_len):
    take = Refs(refs)
    bodies = take(5)
    if ring:
        grads = take(3)
    gw_part, uz, a_ref, z_ref, az_ref, t2_ref, t3_ref, mq, mk, vl, vr, taps, dkt_ref, dg2_ref = take(14)
    dqkv_o, gvec_o = take(2)
    if ring:
        r_o, r_up, r_down, r_vec = take(4)
    v_s, g_s, e_s, k_s, dqf_s, dqkv, gvec = take(7)
    vext, gext, tapacc, gl, gr, gw, gz, da, dubd, rowadd, dqtacc, bdq, pay, slots, own = take(15)
    isem, osem, hsem, wsem = take(4)
    sum_bufs = take(3)
    me = lax.axis_index("seq")
    t, d = v_s.shape
    loads = [
        pltpu.make_async_copy(b, s, isem.at[i]) for i, (b, s) in enumerate(zip(bodies, (v_s, g_s, e_s, k_s, dqf_s)))
    ]
    for c in loads:
        c.start()
    if ring:
        place = Place()
        greet(me, n, [place.twin])
        big = ScatterMesh.take(take, place, (ROWS, HALF, HALF), (grads[2], grads[1], grads[0]))
        vec = ScatterMesh.take(take, place, (LINES,), (gvec,))
        fo, fu, fsem = take(3)
    else:
        greet(me, n, [])
    summing = SeqSum(me, n, gw_part, gw, *sum_bufs)
    loads[1].wait()
    halos = halo_copies(g_s, gl, gr, me, n, hsem)
    for c in halos:
        c.start()
    summing.start()
    if ring:
        big.start()

    def tick(cond, *acts):
        if ring:

            @pl.when(cond)
            def _():
                for act, k in acts:
                    act(k)

    tapacc[...] = jnp.zeros_like(tapacc)
    loads[0].wait()
    if not ring:
        big = vec = None
    far = (lambda k: big.far(k))
    mid = (lambda k: big.mid(k))
    near = (lambda k: big.near(k))

    def inner(i, _):
        fill_inner(vext, v_s, i * CTILE)
        fill_inner(gext, g_s, i * CTILE)
        conv_backward(vext, gext, taps, dqkv, tapacc, i * CTILE)

        tick(i == 1, (far, 0))

        @pl.when(i == 2)
        def _():
            summing.turn()

        tick(i == 2, (far, 1))
        tick(i == 3, (far, 2))
        tick(i == 5, (mid, 0))
        return 0

    lax.fori_loop(1, t // CTILE - 1, inner, 0)
    for c in halos:
        c.wait()
    mask_halos(gl, gr, me, n)

    def edge(i, _):
        fill_edge(vext, v_s, vl, vr, i == 0)
        fill_edge(gext, g_s, gl, gr, i == 0)
        conv_backward(vext, gext, taps, dqkv, tapacc, i * (t - CTILE))
        return 0

    lax.fori_loop(0, 2, edge, 0)
    dtap = jnp.sum(tapacc[...], axis=1)
    lines = jnp.concatenate([jnp.zeros((1, d), F32), dg2_ref[0:1, :], dtap, jnp.zeros((128 - 42, d), F32)], axis=0)
    gvec[...] = jnp.transpose(lines)
    if ring:
        vec.start()
    else:
        save_vec = pltpu.make_async_copy(gvec, gvec_o, osem.at[1])
        save_vec.start()
    tick(True, (near, 0))
    summing.finish()
    for g in range(NG):
        z = zt_group(uz, g)
        bv = u_group(uz, g) / z
        gwg = u_group(gw, g)
        gz[:, gs(g)] = flip(dot_nt(gwg, spread(bv), HI))
        dbv = dot(flip(z_ref[NSITER, :, gs(g)]), spread(gwg), HI)
        dubd[g] = spread(dbv / z).astype(BF16)
        rowadd[g] = dot_nt(jnp.ones((8, GROUP), F32), spread(dbv * bv / z), HI)
        bdq[g] = spread(mq[:, gs(g)])
    da[...] = jnp.zeros_like(da)

    def newton(j, _):
        pinv_back_step(NSITER - 1 - j, a_ref, z_ref, az_ref, t2_ref, t3_ref, gz, da)
        tick(j == 0, (mid, 1))
        tick(j == 1, (lambda k: vec.far(k), 0))
        tick(j == 2, (mid, 2))
        tick(j == 3, (near, 1), (lambda k: vec.mid(k), 0))
        tick(j == 4, (near, 2))
        tick(j == 5, (lambda k: vec.near(k), 0))
        return 0

    lax.fori_loop(0, NSITER, newton, 0)
    loads[2].wait()
    loads[3].wait()
    dqtacc[...] = jnp.zeros_like(dqtacc)

    def cols(part, g):
        return slice(part * d + g * GROUP, part * d + (g + 1) * GROUP)

    def through(i, _):
        here = pl.ds(pl.multiple_of(i * (t // 4), t // 4), t // 4)
        for g in range(NG):
            e = e_s[here, gs(g)]
            de = dot_nt(v_s[here, gs(g)], dubd[g]) - rowadd[g, 0:1, :]
            ds = (e.astype(F32) * de).astype(BF16)
            dqkv[here, cols(2, g)] = (dot(e, dubd[g]) + dqkv[here, cols(2, g)].astype(F32)).astype(BF16)
            dqkv[here, cols(1, g)] = dot(ds, bdq[g]).astype(BF16)
            dqtacc[g] += dot_tn(ds, k_s[here, gs(g)])
        return 0

    lax.fori_loop(0, 4, through, 0)

    rows_dev = max(M // n, 1)
    per_mark = n * rows_dev // M
    if rows_dev < 4:
        pay[...] = jnp.zeros_like(pay)
    for g in range(NG):
        ds = pinv_back_end(g, a_ref, gz, da)
        dq = collect(dqtacc[g]) + dot(ds, spread(mk[:, gs(g)].astype(F32)), HI) * (1.0 / n)
        dk = dkt_ref[:, gs(g)] + dot(flip(ds), spread(mq[:, gs(g)].astype(F32)), HI) * (1.0 / n)
        for i in range(n):
            row = i * rows_dev // per_mark
            pay[i, 0:rows_dev, gs(g)] = dq[row : row + rows_dev]
            pay[i, 4 : 4 + rows_dev, gs(g)] = dk[row : row + rows_dev]

    def mark(j, peer):
        return remote(pay.at[peer], slots.at[me], wsem.at[0, j], wsem.at[1, j], {"seq": peer})

    each_peer(me, n, mark, lambda c: c.start())
    slots[pl.ds(me, 1)] = pay[pl.ds(me, 1)]
    if ring:
        fo[...] = big.total(2)
        fu[...] = big.total(1)
        back = (swap_rows(fo, r_o, place, fsem.at[0]), swap_rows(fu, r_up, place, fsem.at[1]))
        for c in back:
            c.start()
        r_down[...] = big.total(0)
        r_vec[...] = vec.total(0)
    loads[4].wait()
    each_peer(me, n, mark, lambda c: c.wait())
    own[...] = lax.fori_loop(1, n, lambda i, acc: acc + slots[i], slots[0]) * (1.0 / seg_len)

    def landed(i, _):
        here = pl.ds(pl.multiple_of(i * (t // 4), t // 4), t // 4)
        row = lax.div(i * rows_dev, 4)
        dqkv[here, 0:d] = (dqf_s[here, :].astype(F32) + own[pl.ds(row, 1), :]).astype(BF16)
        dqkv[here, d : 2 * d] = (dqkv[here, d : 2 * d].astype(F32) + own[pl.ds(row + 4, 1), :]).astype(BF16)
        pltpu.make_async_copy(dqkv.at[here], dqkv_o.at[here], osem.at[2 + i]).start()
        return 0

    lax.fori_loop(0, 4, landed, 0)
    if ring:
        for c in back:
            c.wait()
        big.finish()
        vec.finish()
        save_vec = pltpu.make_async_copy(gvec, gvec_o, osem.at[1])
        save_vec.start()
    for i in range(4):
        here = pl.ds(i * (t // 4), t // 4)
        pltpu.make_async_copy(dqkv.at[here], dqkv_o.at[here], osem.at[2 + i]).wait()
    save_vec.wait()


def rear(bodies, grads, gw, uz, a, z, az, t2, t3, mq, mk, vl, vr, taps, dkt, dg2, n, seg_len):
    ring = grads is not None
    t, d = bodies[0].shape
    r = gw.shape[0]
    outs = [sds((t, 3 * d), BF16), sds((d, 128), F32)]
    extra = []
    if ring:
        ff = grads[1].shape[1]
        own = d // (2 * CHIPS)
        outs += [sds((own, d), F32), sds((own, ff), F32), sds((ff // (2 * CHIPS), d), F32), sds((own, 128), F32)]
        blocks = [((ff // (2 * CHIPS), d), BF16), ((2 * own, ff // 2), BF16), ((2 * own, d // 2), BF16)]
        extra = ScatterMesh.scratch(blocks) + ScatterMesh.scratch([((own, 128), F32)]) + [
            pltpu.VMEM((2 * own, d // 2), F32),
            pltpu.VMEM((2 * own, ff // 2), F32),
            DMA((2, 2)),
        ]
    ext = pltpu.VMEM((d // 128, CTILE + 2 * RAD, 128), F32)
    halo = pltpu.VMEM((RAD, d), BF16)
    small = pltpu.VMEM((M, d), F32)
    return pl.pallas_call(
        functools.partial(rear_kernel, n=n, ring=ring, seg_len=seg_len),
        in_specs=[ANYW] * (5 + (3 if ring else 0)) + [VM] * 14,
        out_specs=[ANYW] * 2 + [VM] * (len(outs) - 2),
        out_shape=outs,
        scratch_shapes=[pltpu.VMEM((t, d), BF16)] * 5
        + [
            pltpu.VMEM((t, 3 * d), BF16),
            pltpu.VMEM((d, 128), F32),
            ext,
            ext,
            pltpu.VMEM((40, 8, d), F32),
            halo,
            halo,
            pltpu.VMEM((r, 128), F32),
            small,
            small,
            pltpu.VMEM((NG, GROUP, GROUP), BF16),
            pltpu.VMEM((NG, 8, GROUP), F32),
            pltpu.VMEM((NG, GROUP, GROUP), F32),
            pltpu.VMEM((NG, GROUP, GROUP), BF16),
            pltpu.VMEM((n, 8, d), F32),
            pltpu.VMEM((n, 8, d), F32),
            pltpu.VMEM((8, d), F32),
            DMA((5,)),
            DMA((6,)),
            DMA((4,)),
            DMA((2, n)),
        ]
        + SeqSum.scratch(r, n)
        + extra,
        compiler_params=pltpu.CompilerParams(collective_id=2, has_side_effects=True, vmem_limit_bytes=VMEM_LIMIT),
        name="rear",
    )(*bodies, *(grads if ring else ()), gw, uz, a, z, az, t2, t3, mq, mk, vl, vr, taps, dkt, dg2)


def last_kernel(*refs, n, ring):
    take = Refs(refs)
    x_a, dx_a, dqkv_a, w_a = take(4)
    if ring:
        grads = take(1)
    (gains,) = take(1)
    ig_o, dg_o = take(2)
    if ring:
        (r_qkv,) = take(1)
    x_s, dx_s, dqkv_s, w_s, ig_s, part, slots, dgacc, isem, osem, gsem = take(11)
    t, d = x_s.shape
    tile = t // 4
    me = lax.axis_index("seq")

    def here(i):
        return pl.ds(pl.multiple_of(i * tile, tile), tile)

    def loads(i):
        return [
            pltpu.make_async_copy(a.at[here(i)], s.at[here(i)], isem.at[k, i])
            for k, (a, s) in enumerate(((x_a, x_s), (dx_a, dx_s), (dqkv_a, dqkv_s)))
        ]

    load_w = pltpu.make_async_copy(w_a, w_s, isem.at[3, 0])
    load_w.start()
    if ring:
        place = Place()
        greet(me, n, [place.twin])
        scatter = ScatterMesh.take(take, place, (HALF,), grads)
        fq, fsem = take(2)
        scatter.start()
    else:
        greet(me, n, [])
    for i in range(4):
        for c in loads(i):
            c.start()
    if ring:
        scatter.far(0)
    load_w.wait()
    dgacc[...] = jnp.zeros_like(dgacc)

    def body(i, _):
        for c in loads(i):
            c.wait()
        dq, dk, dv = (dqkv_s[here(i), p * d : (p + 1) * d] for p in range(3))
        dh = (dot_nt(dq, w_s[0]) + dot_nt(dk, w_s[1])) * QK_SCALE + dot_nt(dv, w_s[2])
        normal, inv = normalize(x_s[here(i), :].astype(F32))
        dgacc[...] += rowsum8(dh * normal)
        ig = norm_back(dh, normal, inv, gains[0:1, :]) + dx_s[here(i), :].astype(F32)
        ig_s[here(i), :] = ig.astype(BF16)
        pltpu.make_async_copy(ig_s.at[here(i)], ig_o.at[here(i)], osem.at[i]).start()
        if ring:

            @pl.when(i == 2)
            def _():
                scatter.mid(0)

        return 0

    lax.fori_loop(0, 4, body, 0)
    row = jnp.sum(dgacc[...], axis=0, keepdims=True)
    part[...] = jnp.concatenate(
        [row[:, c : c + 128] for c in range(0, d, 128)] + [jnp.zeros((8 - d // 128, 128), F32)], axis=0
    )

    def send(j, peer):
        return remote(part, slots.at[me], gsem.at[0, j], gsem.at[1, j], {"seq": peer})

    each_peer(me, n, send, lambda c: c.start())
    slots[pl.ds(me, 1)] = part[...][None]
    if ring:
        scatter.near(0)
    each_peer(me, n, send, lambda c: c.wait())
    total = lax.fori_loop(1, n, lambda i, acc: acc + slots[i], slots[0])
    if ring:
        twin_sum = remote(dg_o.at[0], dg_o.at[1], gsem.at[0, 0], gsem.at[1, 0], place.twin)
        dg_o[0] = total
        twin_sum.start()
        fq[...] = scatter.total(0)
        back = swap_rows(fq, r_qkv, place, fsem)
        back.start()
        scatter.finish()
        twin_sum.wait()
        back.wait()
    else:
        dg_o[0] = total
        dg_o[1] = jnp.zeros_like(total)
    for i in range(4):
        pltpu.make_async_copy(ig_s.at[here(i)], ig_o.at[here(i)], osem.at[i]).wait()


def last(x, dx, dqkv, w_qkv, gains, g_qkv, n):
    ring = g_qkv is not None
    t, d = x.shape
    outs = [sds((t, d), BF16), sds((2, 8, 128), F32)]
    extra = []
    if ring:
        own = d // (2 * CHIPS)
        wide = g_qkv.shape[1]
        outs += [sds((own, wide), F32)]
        extra = ScatterMesh.scratch([((2 * own, wide // 2), BF16)]) + [pltpu.VMEM((2 * own, wide // 2), F32), DMA((2,))]
    return pl.pallas_call(
        functools.partial(last_kernel, n=n, ring=ring),
        in_specs=[ANYW] * (4 + (1 if ring else 0)) + [VM],
        out_specs=[ANYW] + [VM] * (len(outs) - 1),
        out_shape=outs,
        scratch_shapes=[
            pltpu.VMEM((t, d), BF16),
            pltpu.VMEM((t, d), BF16),
            pltpu.VMEM((t, 3 * d), BF16),
            pltpu.VMEM((3, d, d), BF16),
            pltpu.VMEM((t, d), BF16),
            pltpu.VMEM((8, 128), F32),
            pltpu.VMEM((n, 8, 128), F32),
            pltpu.VMEM((8, d), F32),
            DMA((4, 4)),
            DMA((4,)),
            DMA((2, n)),
        ]
        + extra,
        compiler_params=pltpu.CompilerParams(collective_id=3, has_side_effects=True, vmem_limit_bytes=VMEM_LIMIT),
        name="last",
    )(x, dx, dqkv, w_qkv, *((g_qkv,) if ring else ()), gains)


def adam_step(weight, grad_vec, moment, second, rate_value):
    moment_new = BETA_ONE * moment + (1.0 - BETA_ONE) * grad_vec
    second_new = BETA_TWO * second + (1.0 - BETA_TWO) * grad_vec * grad_vec
    first_hat = moment_new / (1.0 - BETA_ONE**STEP)
    second_hat = second_new / (1.0 - BETA_TWO**STEP)
    weight_new = weight - rate_value * (
        first_hat / (jnp.sqrt(second_hat) + ADAM_EPS) + DECAY_RATE * weight
    )
    return (weight_new, moment_new, second_new)


def per_device(tokens, cotangent, attn_w, w_up, w_down, vectors, attn_m, attn_v, up_m, up_v, down_m, down_v, vec_m, vec_v):
    both = ("seq", "rep")
    x = tokens[0]
    dy = cotangent[0]
    t, d = x.shape
    n = lax.axis_size("seq")
    seg_len = t * n // M
    ring = n == CHIPS and lax.axis_size("rep") == 2

    if ring:
        weights = (attn_w, w_up, w_down, jnp.pad(vectors, ((0, 0), (0, 128 - vectors.shape[1]))))
    else:
        w_attn = lax.all_gather(attn_w.astype(BF16), both, axis=1, tiled=True)
        vec = lax.all_gather(vectors.astype(BF16), both, axis=0, tiled=True).astype(F32)
        weights = (w_attn[:3], jnp.pad(vec, ((0, 0), (0, 128 - vec.shape[1]))))
    (w_qkv, wo, up, down, gains, taps, h1, q, k, v, conv, f, e, mq, mk, uz, a, z, az, t2, t3, vl, vr) = front(
        x, weights, n, ring
    )
    if not ring:
        w_qkv, wo = w_attn[:3], w_attn[3]
        up = lax.all_gather(w_up.astype(BF16), both, axis=0, tiled=True)
        down = lax.all_gather(w_down.astype(BF16), both, axis=0, tiled=True)
    out, act, da, h2, mix, dx, dmix, dqf, gw, dkt, dg2 = middle(
        x, dy, f, q, conv, wo, up, down, gains, mk, uz, z, padded_rows(6 * M, n)
    )
    dot_xla = functools.partial(jnp.einsum, "ta,tb->ab", preferred_element_type=F32)
    g_down = dot_xla(act, dy).astype(BF16)
    g_up = dot_xla(h2, da).astype(BF16)
    g_o = dot_xla(mix, dx).astype(BF16)
    res = rear(
        (v, dmix, e, k, dqf), (g_o, g_up, g_down) if ring else None, gw, uz, a, z, az, t2, t3, mq, mk, vl, vr, taps, dkt, dg2, n, seg_len
    )
    dqkv, g_vec = res[:2]
    column = jnp.concatenate([jnp.full((2 * d,), QK_SCALE, F32), jnp.ones((d,), F32)])
    g_qkv = (dot_xla(h1, dqkv) * column).astype(BF16)
    fin = last(x, dx, dqkv, w_qkv, gains, g_qkv if ring else None, n)
    ig = fin[0]
    dg1 = (fin[1][0] + fin[1][1])[: d // 128].reshape(d)
    if ring:
        red_o, red_up, red_down, red_vec = res[2:]
        own = d // (2 * n)
        red_qkv = jnp.transpose(fin[2].reshape(own, 3, d), (1, 0, 2))
        red_attn = jnp.concatenate([red_qkv, red_o[None]], axis=0)
        start = (lax.axis_index("seq") * 2 + lax.axis_index("rep")) * own
        dg1_own = lax.dynamic_slice_in_dim(dg1, start, own, 0)
        red_vec = jnp.concatenate([dg1_own[:, None], red_vec[:, 1 : vectors.shape[1]]], axis=1)
    else:
        g_attn = jnp.concatenate([jnp.transpose(g_qkv.reshape(d, 3, d), (1, 0, 2)), g_o[None]], axis=0)
        red_attn = lax.psum_scatter(g_attn, both, scatter_dimension=1, tiled=True).astype(F32)
        red_up = lax.psum_scatter(g_up, both, scatter_dimension=0, tiled=True).astype(F32)
        red_down = lax.psum_scatter(g_down, both, scatter_dimension=0, tiled=True).astype(F32)
        g_vec = jnp.concatenate([dg1[:, None] / n, g_vec[:, 1 : vectors.shape[1]]], axis=1)
        red_vec = lax.psum_scatter(g_vec, both, scatter_dimension=0, tiled=True)
    return (
        out[None],
        ig[None],
        *adam_step(attn_w, red_attn, attn_m, attn_v, LEARN_RATE),
        *adam_step(w_up, red_up, up_m, up_v, LEARN_RATE),
        *adam_step(w_down, red_down, down_m, down_v, LEARN_RATE),
        *adam_step(vectors, red_vec, vec_m, vec_v, VECTOR_RATE),
    )


def solution(mesh):
    tok = P("rep", "seq", None)
    att = P(None, ("seq", "rep"), None)
    mat = P(("seq", "rep"), None)
    return jax.shard_map(
        per_device,
        mesh=mesh,
        in_specs=(tok, tok, att, mat, mat, mat, att, att, mat, mat, mat, mat, mat, mat),
        out_specs=(tok, tok, att, att, att) + (mat,) * 9,
        check_vma=False,
    )
```

```python
import functools

import jax
import jax.numpy as jnp
from jax import lax
from jax.experimental import pallas as pl
from jax.experimental.pallas import tpu as pltpu
from jax.sharding import PartitionSpec as P

H = 12
HD = 64
M = 64
KC = 33
NSITER = 6
STEP = 10
EPS_NORM = 1e-05
BETA_ONE = 0.9
BETA_TWO = 0.999
ADAM_EPS = 1e-08
LEARN_RATE = 0.03
VECTOR_RATE = 0.15
DECAY_RATE = 0.1

F32 = jnp.float32
BF16 = jnp.bfloat16
GROUP = 256
NG = 3
RAD = 16
QK_SCALE = HD ** (-0.25)
HI = lax.Precision.HIGHEST
VMEM_LIMIT = 58 * 1024 * 1024


def dot(a, b, precision=None):
    return lax.dot_general(a, b, (((1,), (0,)), ((), ())), precision=precision, preferred_element_type=F32)


def dot_nt(a, b, precision=None):
    return lax.dot_general(a, b, (((1,), (1,)), ((), ())), precision=precision, preferred_element_type=F32)


def dot_tn(a, b, precision=None):
    return lax.dot_general(a, b, (((0,), (0,)), ((), ())), precision=precision, preferred_element_type=F32)


def split(x):
    hi = x.astype(BF16)
    return hi, (x - hi.astype(F32)).astype(BF16)


def dot3(a, b):
    return dot(a[0], b[0]) + (dot(a[0], b[1]) + dot(a[1], b[0]))


def spread2(a):
    return spread(a[0]), spread(a[1])


def head_mask(shape=(GROUP, GROUP)):
    rows = lax.broadcasted_iota(jnp.int32, shape, 0)
    cols = lax.broadcasted_iota(jnp.int32, shape, 1)
    return lax.shift_right_logical(rows, 6) == lax.shift_right_logical(cols, 6)


def spread(wide):
    tall = jnp.concatenate([wide, wide, wide, wide], axis=0)
    return jnp.where(head_mask(), tall, jnp.zeros_like(tall))


def collect(full):
    kept = jnp.where(head_mask(), full, jnp.zeros_like(full))
    return (kept[0:64] + kept[64:128]) + (kept[128:192] + kept[192:256])


def flip(wide):
    turned = jnp.transpose(spread(wide))
    return (turned[0:64] + turned[64:128]) + (turned[128:192] + turned[192:256])


def gs(g):
    return slice(g * GROUP, (g + 1) * GROUP)


def half_reduce(x, op, init):
    parts = []
    for c in range(x.shape[1] // 128):
        col = x[:, c * 128 : (c + 1) * 128]
        low = lax.broadcasted_iota(jnp.int32, col.shape, 1) < 64
        a = op(jnp.where(low, col, init), axis=1, keepdims=True)
        b = op(jnp.where(low, init, col), axis=1, keepdims=True)
        parts.append(jnp.where(low, a, b))
    return jnp.concatenate(parts, axis=1)


def normalize(x):
    center = x - jnp.mean(x, axis=-1, keepdims=True)
    inv = lax.rsqrt(jnp.mean(center * center, axis=-1, keepdims=True) + EPS_NORM)
    return center * inv, inv


def norm_back(up, normal, inv, gain):
    scaled = up * gain
    centered = scaled - jnp.mean(scaled, axis=-1, keepdims=True)
    return inv * (centered - normal * jnp.mean(scaled * normal, axis=-1, keepdims=True))


def rowsum8(x):
    return jnp.sum(x.reshape(x.shape[0] // 8, 8, x.shape[1]), axis=0)


def gelu_parts(a):
    z = jnp.abs(a)
    t = 1.0 / (1.0 + (0.3275911 * 0.7071067811865476) * z)
    e = jnp.exp(-0.5 * a * a)
    poly = t * (0.127414796 + t * (-0.142248368 + t * (0.7107068705 + t * (-0.7265760135 + t * 0.5307027145))))
    tail = poly * e
    phi = jnp.where(a >= 0, 1.0 - tail, tail)
    return a * phi, phi + a * (e * 0.3989422804014327)


def whole(shape):
    zeros = (0,) * len(shape)
    return pl.BlockSpec(shape, lambda i: zeros, pipeline_mode=pl.Buffered(1))


def rows(tile, width):
    return pl.BlockSpec((tile, width), lambda i: (i, 0))


def sds(shape, dtype):
    return jax.ShapeDtypeStruct(shape, dtype)


def params():
    return pltpu.CompilerParams(dimension_semantics=("arbitrary",), vmem_limit_bytes=VMEM_LIMIT)


def widen(zt, g):
    return jnp.concatenate(
        [jnp.broadcast_to(zt[:, h : h + 1], (M, HD)) for h in range(4 * g, 4 * g + 4)], axis=1
    )


def u_group(ref, g):
    return jnp.concatenate([ref[2 * g * M : (2 * g + 1) * M, :], ref[(2 * g + 1) * M : (2 * g + 2) * M, :]], axis=1)


def zt_group(ref, g):
    return widen(ref[6 * M : 7 * M, :], g)


def put_tall(ref, g, wide):
    ref[2 * g * M : (2 * g + 1) * M, :] = wide[:, :128]
    ref[(2 * g + 1) * M : (2 * g + 2) * M, :] = wide[:, 128:]


def padded_rows(r, n):
    return -(-r // (8 * n)) * 8 * n


MESH = pl.DeviceIdType.MESH
DMA = pltpu.SemaphoreType.DMA
VM = pl.BlockSpec(memory_space=pltpu.VMEM)
ANYW = pl.BlockSpec(memory_space=pl.ANY)


def remote(src, dst, send, recv, where):
    return pltpu.make_async_remote_copy(
        src_ref=src, dst_ref=dst, send_sem=send, recv_sem=recv, device_id=where, device_id_type=MESH
    )


def greet(me, n, others):
    bar = pltpu.get_barrier_semaphore()

    def hello(j, _):
        pl.semaphore_signal(bar, inc=1, device_id={"seq": lax.rem(me + j, n)}, device_id_type=MESH)
        return 0

    lax.fori_loop(1, n, hello, 0)
    for peer in others:
        pl.semaphore_signal(bar, inc=1, device_id=peer, device_id_type=MESH)
    pl.semaphore_wait(bar, n - 1 + len(others))


def each_peer(me, n, make, act):
    def body(j, _):
        act(make(j, lax.rem(me + j, n)))
        return 0

    lax.fori_loop(1, n, body, 0)


def halo_copies(body_ref, left_ref, right_ref, me, n, sems):
    t = body_ref.shape[0]
    right = {"seq": lax.rem(me + 1, n)}
    left = {"seq": lax.rem(me + n - 1, n)}
    return (
        remote(body_ref.at[pl.ds(t - RAD, RAD)], left_ref, sems.at[0], sems.at[1], right),
        remote(body_ref.at[pl.ds(0, RAD)], right_ref, sems.at[2], sems.at[3], left),
    )


def mask_halos(left_ref, right_ref, me, n):
    left_ref[...] = jnp.where(me > 0, left_ref[...], jnp.zeros_like(left_ref))
    right_ref[...] = jnp.where(me < n - 1, right_ref[...], jnp.zeros_like(right_ref))


class SeqSum:
    def __init__(self, me, n, x, out, slots, total, sems):
        self.me, self.n, self.x, self.out, self.slots, self.total, self.sems = me, n, x, out, slots, total, sems
        self.chunk = x.shape[0] // n
        self.here = pl.ds(pl.multiple_of(me * self.chunk, 8), self.chunk)

    def first(self, j, peer):
        src = self.x.at[pl.ds(pl.multiple_of(peer * self.chunk, 8), self.chunk)]
        return remote(src, self.slots.at[self.me], self.sems.at[0, j], self.sems.at[1, j], {"seq": peer})

    def second(self, j, peer):
        return remote(self.total, self.out.at[self.here], self.sems.at[2, j], self.sems.at[3, j], {"seq": peer})

    def start(self):
        each_peer(self.me, self.n, self.first, lambda c: c.start())
        self.slots[pl.ds(self.me, 1)] = self.x[self.here, :][None]

    def turn(self):
        each_peer(self.me, self.n, self.first, lambda c: c.wait())
        summed = lax.fori_loop(1, self.n, lambda i, acc: acc + self.slots[i], self.slots[0])
        self.total[...] = summed
        each_peer(self.me, self.n, self.second, lambda c: c.start())
        self.out[self.here, :] = summed

    def finish(self):
        each_peer(self.me, self.n, self.second, lambda c: c.wait())

    @staticmethod
    def scratch(r, n):
        return [pltpu.VMEM((n, r // n, 128), F32), pltpu.VMEM((r // n, 128), F32), DMA((4, n))]


CHIPS = 16
STACK, HALF, ROWS, LINES = range(4)


def at(i, size, unit):
    return pl.ds(pl.multiple_of(i * size, unit), size)


def piece(kind, ref, seq, rep):
    if kind == STACK:
        half = ref.shape[2] // 2
        return ref.at[:, at(seq, ref.shape[1] // CHIPS, 16), at(rep, half, 128)]
    if kind == HALF:
        half = ref.shape[1] // 2
        return ref.at[at(seq, ref.shape[0] // CHIPS, 16), at(rep, half, 128)]
    return ref.at[at(seq * 2 + rep, ref.shape[0] // (2 * CHIPS), 8 if kind == LINES else 16), :]


class Place:
    def __init__(self):
        self.seq = lax.axis_index("seq")
        self.rep = lax.axis_index("rep")
        self.x = lax.rem(self.seq, 2)
        self.y = lax.rem(lax.div(self.seq, 2), 2)
        self.z = lax.div(self.seq, 4)
        self.twin = {"rep": 1 - self.rep}
        self.across = ({"seq": self.chip(4, self.rep)}, {"seq": self.chip(8, self.rep)})

    def chip(self, i, rep):
        j, b, a = lax.rem(i, 4), lax.rem(lax.div(i, 4), 2), lax.div(i, 8)
        z = lax.rem(self.z + 4 - j, 4)
        fx = a + rep * (b - a)
        fy = b + rep * (a - b)
        x = self.x + fx * (1 - 2 * self.x)
        y = self.y + fy * (1 - 2 * self.y)
        return z * 4 + y * 2 + x

    def above(self, j):
        return {"seq": self.chip(4 - j, self.rep)}

    def below(self, j):
        return {"seq": self.chip(j, self.rep)}


class GatherMesh:
    def __init__(self, place, kinds, outs, own, sems):
        self.place, self.kinds, self.outs, self.own = place, kinds, outs, own
        self.zsend, self.send1, self.send2, self.ssend, self.recv, self.srecv = sems

    def block(self, i, k, rep):
        return piece(self.kinds[k], self.outs[k], self.place.chip(i, rep), rep)

    def copy(self, i, k, send, recv, where):
        b = self.block(i, k, self.place.rep)
        src = b if self.own[k] is None or not (isinstance(i, int) and i == 0) else self.own[k]
        return remote(src, b, send, recv, where)

    def to_z(self, j, k):
        return self.copy(0, k, self.zsend.at[j, k], self.recv.at[j, k], self.place.above(j))

    def to_first(self, i, k):
        return self.copy(i, k, self.send1.at[i, k], self.recv.at[i + 4, k], self.place.across[0])

    def to_second(self, i, k):
        return self.copy(i, k, self.send2.at[i, k], self.recv.at[i + 8, k], self.place.across[1])

    def share(self, i, k):
        return self.copy(i, k, self.ssend.at[i, k], self.srecv.at[i, k], self.place.twin)

    def arrival(self, i, k):
        b = self.block(i, k, self.place.rep)
        return remote(b, b, self.ssend.at[i, k], self.recv.at[i, k], self.place.twin)

    def shared(self, i, k):
        b = self.block(i, k, 1 - self.place.rep)
        return remote(b, b, self.ssend.at[i, k], self.srecv.at[i, k], self.place.twin)

    def start_z(self):
        for k in range(len(self.kinds)):
            for j in (1, 2, 3):
                self.to_z(j, k).start()

    def start_across(self, which=None):
        for k in range(len(self.kinds)) if which is None else which:
            self.to_second(0, k).start()
            self.to_first(0, k).start()
            self.share(0, k).start()

    def each(self, low, high, which, act):
        def body(i, _):
            for k in which:
                act(i, k)
            return 0

        lax.fori_loop(low, high, body, 0)

    def line(self, which):
        def act(i, k):
            self.arrival(i, k).wait_recv()
            self.to_first(i, k).start()
            self.share(i, k).start()

        self.each(1, 4, which, act)

    def line_on(self, which):
        self.each(1, 4, which, lambda i, k: self.to_second(i, k).start())

    def plane(self, which):
        def act(i, k):
            self.arrival(i, k).wait_recv()
            self.to_second(i, k).start()
            self.share(i, k).start()

        self.each(4, 8, which, act)

    def space(self, which):
        def act(i, k):
            self.arrival(i, k).wait_recv()
            self.share(i, k).start()

        self.each(8, CHIPS, which, act)

    def shares_in(self, which):
        self.shared_first(which)
        self.each(1, CHIPS, which, lambda i, k: self.shared(i, k).wait_recv())

    def shared_first(self, which):
        for k in which:
            self.shared(0, k).wait_recv()

    def finish(self):
        which = range(len(self.kinds))
        for k in which:
            for j in (1, 2, 3):
                self.to_z(j, k).wait_send()
            self.to_first(0, k).wait_send()
            self.to_second(0, k).wait_send()
            self.share(0, k).wait_send()

        def act(i, k):
            @pl.when(i < 4)
            def _():
                self.to_first(i, k).wait_send()

            @pl.when(i < 8)
            def _():
                self.to_second(i, k).wait_send()

            self.share(i, k).wait_send()

        self.each(1, CHIPS, which, act)

    @staticmethod
    def scratch(k):
        return [DMA((4, k)), DMA((4, k)), DMA((8, k))] + [DMA((CHIPS, k))] * 3


class ScatterMesh:
    def __init__(self, place, kinds, grads, mine, twins, in2, in1, inz, sems):
        self.place, self.kinds, self.grads = place, kinds, grads
        self.mine, self.twins, self.in2, self.in1, self.inz = mine, twins, in2, in1, inz
        self.lsem, self.tsend, self.trecv, self.s2, self.r2, self.s1, self.r1, self.sz, self.rz = sems

    def source(self, i, k):
        return piece(self.kinds[k], self.grads[k], self.place.chip(i, self.place.rep), self.place.rep)

    def cell(self, i, k):
        return self.source(i, k) if self.mine is None else self.mine[k].at[i]

    def load(self, i, k):
        return pltpu.make_async_copy(self.source(i, k), self.mine[k].at[i], self.lsem.at[i, k])

    def give(self, i, k):
        other = 1 - self.place.rep
        src = piece(self.kinds[k], self.grads[k], self.place.chip(i, other), other)
        return remote(src, self.twins[k].at[i], self.tsend.at[i, k], self.trecv.at[i, k], self.place.twin)

    def out2(self, i, k):
        return remote(self.cell(i, k), self.in2[k].at[i - 8], self.s2.at[i - 8, k], self.r2.at[i - 8, k], self.place.across[1])

    def out1(self, i, k):
        return remote(self.cell(i, k), self.in1[k].at[i - 4], self.s1.at[i - 4, k], self.r1.at[i - 4, k], self.place.across[0])

    def outz(self, j, k):
        return remote(self.cell(j, k), self.inz[k].at[j], self.sz.at[j, k], self.rz.at[j, k], self.place.below(j))

    def start(self):
        for low in (8, 0):
            for k in range(len(self.kinds)):

                def body(j, _):
                    self.give(low + 7 - j, k).start()
                    if self.mine is not None:
                        self.load(low + 7 - j, k).start()
                    return 0

                lax.fori_loop(0, 8, body, 0)

    def terms(self, i, k):
        if self.mine is not None:
            self.load(i, k).wait()
        self.give(i, k).wait()
        return self.cell(i, k)[...].astype(F32) + self.twins[k].at[i][...].astype(F32)

    def keep(self, i, k, value):
        cell = self.cell(i, k)
        cell[...] = value.astype(cell.dtype)

    def far(self, k):
        def body(j, _):
            i = CHIPS - 1 - j
            self.keep(i, k, self.terms(i, k))
            self.out2(i, k).start()
            return 0

        lax.fori_loop(0, 8, body, 0)

    def mid(self, k):
        def body(j, _):
            i = 7 - j
            own = self.terms(i, k)
            self.out2(i + 8, k).wait_recv()
            self.keep(i, k, own + self.in2[k].at[i][...].astype(F32))
            self.out1(i, k).start()
            return 0

        lax.fori_loop(0, 4, body, 0)

    def closer(self, i, k):
        own = self.terms(i, k)
        self.out2(i + 8, k).wait_recv()
        self.out1(i + 4, k).wait_recv()
        return own + (self.in2[k].at[i][...].astype(F32) + self.in1[k].at[i][...].astype(F32))

    def near(self, k):
        def body(j, _):
            i = 3 - j
            self.keep(i, k, self.closer(i, k))
            self.outz(i, k).start()
            return 0

        lax.fori_loop(0, 3, body, 0)

    def total(self, k):
        acc = self.closer(0, k)
        for j in (1, 2, 3):
            self.outz(j, k).wait_recv()
            acc = acc + self.inz[k][j].astype(F32)
        return acc

    def finish(self):
        for k in range(len(self.kinds)):

            def body(i, _):
                @pl.when(i >= 8)
                def _():
                    self.out2(i, k).wait_send()

                @pl.when((i >= 4) & (i < 8))
                def _():
                    self.out1(i, k).wait_send()

                @pl.when(i < 4)
                def _():
                    self.outz(i, k).wait_send()

                return 0

            lax.fori_loop(1, CHIPS, body, 0)

    @staticmethod
    def scratch(blocks, in_place=False):
        k = len(blocks)
        return (
            ([] if in_place else [pltpu.VMEM((CHIPS, *s), t) for s, t in blocks])
            + [pltpu.VMEM((CHIPS, *s), t) for s, t in blocks]
            + [pltpu.VMEM((8, *s), t) for s, t in blocks]
            + [pltpu.VMEM((4, *s), t) for s, t in blocks]
            + [pltpu.VMEM((4, *s), t) for s, t in blocks]
            + [DMA((CHIPS, k))] * 3
            + [DMA((8, k))] * 2
            + [DMA((4, k))] * 4
        )

    @staticmethod
    def take(take, place, kinds, grads, in_place=False):
        k = len(kinds)
        mine = None if in_place else take(k)
        bufs = [take(k) for _ in range(4)]
        return ScatterMesh(place, kinds, grads, mine, *bufs, take(9))


def swap_rows(total, out, place, sems):
    rows_own = total.shape[-2] // 2
    half = total.shape[-1]
    theirs, mine = at(1 - place.rep, rows_own, 8), at(place.rep, rows_own, 8)
    cols = at(place.rep, half, 128)
    if len(total.shape) == 3:
        out[:, :, cols] = total[:, mine, :]
        return remote(total.at[:, theirs, :], out.at[:, :, cols], sems.at[0], sems.at[1], place.twin)
    out[:, cols] = total[mine, :]
    return remote(total.at[theirs, :], out.at[:, cols], sems.at[0], sems.at[1], place.twin)


CHUNK = 64
CTILE = 256


def fill_inner(ext, body_ref, start):
    count = ext.shape[1]
    rows_in = pl.ds(pl.multiple_of(start - RAD, RAD), count)
    for c in range(ext.shape[0]):
        ext[c] = body_ref[rows_in, c * 128 : (c + 1) * 128].astype(F32)


def fill_edge(ext, body_ref, left_ref, right_ref, first):
    tile = ext.shape[1] - 2 * RAD
    t = body_ref.shape[0]
    start = pl.multiple_of(jnp.where(first, 0, t - tile), tile)
    for c in range(ext.shape[0]):
        cols = slice(c * 128, (c + 1) * 128)
        ext[c, RAD : RAD + tile, :] = body_ref[pl.ds(start, tile), cols].astype(F32)
        ext[c, 0:RAD, :] = jnp.where(first, left_ref[:, cols], body_ref[t - tile - RAD : t - tile, cols]).astype(F32)
        ext[c, RAD + tile :, :] = jnp.where(first, body_ref[tile : tile + RAD, cols], right_ref[:, cols]).astype(F32)


def conv_forward(ext, tap_ref, out, row0):
    def step(r, _):
        base = pl.multiple_of(r * CHUNK, CHUNK)
        for c in range(ext.shape[0]):
            cols = slice(c * 128, (c + 1) * 128)
            acc = jnp.zeros((CHUNK, 128), F32)
            for b in range(8):
                reach = 4 if b == 0 else 3
                win = ext[c, pl.ds(base + b, CHUNK + 8 * reach), :]
                for m in range(reach + 1):
                    o = 8 * m + b
                    acc = acc + tap_ref[o : o + 1, cols] * win[8 * m : 8 * m + CHUNK]
            out[pl.ds(pl.multiple_of(row0 + base, CHUNK), CHUNK), cols] = acc.astype(out.dtype)
        return 0

    lax.fori_loop(0, CTILE // CHUNK, step, 0)


def conv_backward(vext, gext, tap_ref, out, tapacc, row0):
    width = out.shape[1] // 3

    def step(r, _):
        base = pl.multiple_of(r * CHUNK, CHUNK)
        for c in range(vext.shape[0]):
            cols = slice(c * 128, (c + 1) * 128)
            acc = jnp.zeros((CHUNK, 128), F32)
            here = gext[c, pl.ds(base + RAD, CHUNK), :]
            for b in range(8):
                reach = 4 if b == 0 else 3
                win = gext[c, pl.ds(base + b, CHUNK + 8 * reach), :]
                for m in range(reach + 1):
                    o = KC - 1 - (8 * m + b)
                    acc = acc + tap_ref[o : o + 1, cols] * win[8 * m : 8 * m + CHUNK]
                win = vext[c, pl.ds(base + b, CHUNK + 8 * reach), :]
                for m in range(reach + 1):
                    o = 8 * m + b
                    tapacc[o, :, cols] += rowsum8(here * win[8 * m : 8 * m + CHUNK])
            into = slice(2 * width + c * 128, 2 * width + (c + 1) * 128)
            out[pl.ds(pl.multiple_of(row0 + base, CHUNK), CHUNK), into] = acc.astype(out.dtype)
        return 0

    lax.fori_loop(0, CTILE // CHUNK, step, 0)


def wide_eye():
    lane = lax.broadcasted_iota(jnp.int32, (M, GROUP), 1) & 63
    return jnp.where(lane == lax.broadcasted_iota(jnp.int32, (M, GROUP), 0), 1.0, 0.0)


def head_sums(row):
    ones = jnp.where(head_mask(), 1.0, 0.0)
    return dot(jnp.broadcast_to(row, (8, GROUP)), ones, HI)[0:1]


def pinv_begin(mq_ref, mk_ref, a_ref, z_ref):
    for g in range(NG):
        s = dot_nt(mq_ref[:, gs(g)], spread(mk_ref[:, gs(g)]))
        e = jnp.exp(s - half_reduce(s, jnp.max, -jnp.inf))
        a = e / half_reduce(e, jnp.sum, 0.0)
        a_ref[:, gs(g)] = a
        col = jnp.sum(a, axis=0, keepdims=True)
        z_ref[0, :, gs(g)] = flip(a) / jnp.sqrt(head_sums(col * col))


def pinv_step(it, a_ref, z_ref, az_ref, t2_ref, t3_ref):
    eye = wide_eye()
    R = range(NG)
    z = [split(z_ref[it, :, gs(g)]) for g in R]
    az = [dot3(split(a_ref[:, gs(g)]), spread2(z[g])) for g in R]
    azs = [split(az[g]) for g in R]
    t2 = [15.0 * eye - dot3(azs[g], spread2(split(7.0 * eye - az[g]))) for g in R]
    t3 = [13.0 * eye - dot3(azs[g], spread2(split(t2[g]))) for g in R]
    for g in R:
        z_ref[it + 1, :, gs(g)] = 0.25 * dot3(z[g], spread2(split(t3[g])))
        az_ref[it, :, gs(g)] = az[g]
        t2_ref[it, :, gs(g)] = t2[g]
        t3_ref[it, :, gs(g)] = t3[g]


def pinv_back_step(it, a_ref, z_ref, az_ref, t2_ref, t3_ref, gz_ref, da_ref):
    eye = wide_eye()
    R = range(NG)
    az = [az_ref[it, :, gs(g)] for g in R]
    zs = [split(z_ref[it, :, gs(g)]) for g in R]
    gzs = [split(0.25 * gz_ref[:, gs(g)]) for g in R]
    baz = [spread2(split(az[g])) for g in R]
    d3 = [split(dot3(gzs[g], spread2(zs[g]))) for g in R]
    d2 = [split(-dot3(d3[g], baz[g])) for g in R]
    d1 = [-dot3(d2[g], baz[g]) for g in R]
    daz = [
        split(
            -dot3(split(t2_ref[it, :, gs(g)]), spread2(d3[g]))
            - dot3(split(7.0 * eye - az[g]), spread2(d2[g]))
            - d1[g]
        )
        for g in R
    ]
    for g in R:
        da_ref[:, gs(g)] += dot3(zs[g], spread2(daz[g]))
        gz_ref[:, gs(g)] = dot3(split(t3_ref[it, :, gs(g)]), spread2(gzs[g])) + dot3(
            daz[g], spread2(split(a_ref[:, gs(g)]))
        )


def pinv_back_end(g, a_ref, gz_ref, da_ref):
    a = a_ref[:, gs(g)]
    gz = gz_ref[:, gs(g)]
    col = jnp.sum(a, axis=0, keepdims=True)
    bound = jnp.sqrt(head_sums(col * col))
    tot = head_sums(jnp.sum(gz * a, axis=0, keepdims=True))
    full = flip(da_ref[:, gs(g)]) + gz / bound - (tot / (bound * bound * bound)) * col
    return a * (full - half_reduce(full * a, jnp.sum, 0.0))


def gather_marks(slots, outs, n):
    per = 4 * n // M
    half = slots.shape[2]
    for out, base in zip(outs, (0, 4)):
        if per == 1:
            got = [slots[i].astype(F32) for i in range(n)]
            for h in range(2):
                tall = jnp.concatenate([x[8 * h + base : 8 * h + base + 4] for x in got], axis=0)
                out[:, h * half : (h + 1) * half] = tall.astype(BF16)
        else:
            for h in range(2):
                lines = []
                for m in range(M):
                    total = jnp.zeros((1, half), F32)
                    for s in range(per // 4):
                        part = slots[m * (per // 4) + s].astype(F32)[8 * h + base : 8 * h + base + 4]
                        total = total + jnp.sum(part, axis=0, keepdims=True)
                    lines.append(total * (1.0 / per))
                out[:, h * half : (h + 1) * half] = jnp.concatenate(lines, axis=0).astype(BF16)


class Refs:
    def __init__(self, refs):
        self.it = iter(refs)

    def __call__(self, count):
        return [next(self.it) for _ in range(count)]

    def one(self):
        return next(self.it)


def front_kernel(*refs, n, ring):
    take = Refs(refs)
    x_any = take.one()
    if ring:
        wa, wu, wd, wv = take(4)
        wqkv_o, wo_o, ud0_o, ud_own = take(4)
    else:
        wq, vec = take(2)
    gains, taps = take(2)
    outs = take(7)
    mq, mk, uz, a_ref, z_ref, az_ref, t2_ref, t3_ref, vl, vr, p_ref = take(11)
    xs = take.one()
    stage = take(7)
    h_s, q_s, k_s, v_s, conv_s, f_s, e_s = stage
    means, pay, slots, ext, bdk, bdq, uacc, zacc, upart = take(9)
    xsem, osem, msem, hsem = take(4)
    sum_bufs = take(3)
    me = lax.axis_index("seq")
    t, d = xs.shape
    half = d // 2
    load_x = pltpu.make_async_copy(x_any, xs, xsem.at[0])
    load_x.start()
    drains = [pltpu.make_async_copy(s, o, osem.at[i]) for i, (s, o) in enumerate(zip(stage, outs))]
    if ring:
        wq, vec, sa, su, sd, so, co, psem, lsem = take(9)
        ring_one, ring_two = take(6), take(6)
        place = Place()
        greet(me, n, [place.twin])
        rep, seq = place.rep, place.seq
        rows_own = d // (2 * CHIPS)
        mine = at(rep, rows_own, 8)
        theirs = 1 - rep
        swaps = (
            remote(wa.at[0:3, :, at(theirs, half, 128)], sa.at[:, mine, :], psem.at[0], psem.at[1], place.twin),
            remote(wa.at[3, :, at(theirs, half, 128)], so.at[mine, :], psem.at[2], psem.at[3], place.twin),
            remote(wu.at[:, :, at(theirs, half, 128)], su.at[:, mine, :], psem.at[4], psem.at[5], place.twin),
            remote(wd.at[:, :, at(theirs, half, 128)], sd.at[pl.ds(2 * rep, 2)], psem.at[6], psem.at[7], place.twin),
        )
        for c in swaps:
            c.start()
        sa[:, mine, :] = wa[0:3, :, at(rep, half, 128)]
        so[mine, :] = wa[3, :, at(rep, half, 128)]
        su[:, mine, :] = wu[:, :, at(rep, half, 128)]
        sd[pl.ds(2 * rep, 2)] = wd[:, :, at(rep, half, 128)]
        vec[at(seq * 2 + rep, rows_own, 8), :] = wv[...]
        swaps[0].wait()
        wq[:, at(seq, 2 * rows_own, 16), at(rep, half, 128)] = sa[...].astype(BF16)
        first = GatherMesh(place, (LINES, HALF, HALF, HALF), (vec, wq.at[2], wq.at[1], wq.at[0]), (None,) * 4, ring_one)
        first.start_z()
        first.start_across((0, 1))
        for c in swaps[1:]:
            c.wait()
        co[...] = so[...].astype(BF16)
        ud_own[:, 0] = su[...].astype(BF16)
        ud_own[:, 1] = sd[...].astype(BF16)
        rest = GatherMesh(place, (STACK, HALF), (ud0_o, wo_o), (ud_own.at[0], co), ring_two)
        local = [
            pltpu.make_async_copy(src, piece(kind, out, seq, rep), lsem.at[i])
            for i, (src, kind, out) in enumerate(zip(rest.own, rest.kinds, rest.outs))
        ]

        rest.start_z()
        for c in local:
            c.start()
        first.line((0, 1))
        first.line_on((0, 1))
        first.start_across((2, 3))
        first.plane((0, 1))
        for which in ((2,), (3,)):
            first.line(which)
            first.line_on(which)
        first.space((0,))
        first.shares_in((0,))
        save_w = pltpu.make_async_copy(wq, wqkv_o, xsem.at[1])
    else:
        greet(me, n, [])

    turned = jnp.transpose(vec[...]).astype(BF16).astype(F32)
    gains[...] = turned[0:8]
    taps[...] = turned[2:42]
    load_x.wait()

    def tile(i):
        return pl.ds(pl.multiple_of(i * (t // 4), t // 4), t // 4)

    def norm(i, _):
        normal, _inv = normalize(xs[tile(i), :].astype(F32))
        h_s[tile(i), :] = (normal * gains[0:1, :]).astype(BF16)
        return 0

    def project_v(i, _):
        v_s[tile(i), :] = dot(h_s[tile(i), :], wq[2]).astype(BF16)
        return 0

    def project_k(i, _):
        k = (dot(h_s[tile(i), :], wq[1]) * QK_SCALE).astype(BF16)
        k_s[tile(i), :] = k
        means[pl.ds(i + 4, 1), :] = jnp.mean(k.astype(F32), axis=0, keepdims=True)
        return 0

    def project_q(i, _):
        q = (dot(h_s[tile(i), :], wq[0]) * QK_SCALE).astype(BF16)
        q_s[tile(i), :] = q
        means[pl.ds(i, 1), :] = jnp.mean(q.astype(F32), axis=0, keepdims=True)
        return 0

    def inner(i, _):
        fill_inner(ext, v_s, i * CTILE)
        conv_forward(ext, taps, conv_s, i * CTILE)
        if ring:

            @pl.when(i == 4)
            def _():
                rest.line_on((0,))

            @pl.when(i == 5)
            def _():
                rest.line((1,))
                rest.line_on((1,))

        return 0

    tiles = t // CTILE
    lax.fori_loop(0, 4, norm, 0)
    if ring:
        first.plane((2,))
        first.space((1,))
        first.shares_in((1,))
    lax.fori_loop(0, 4, project_v, 0)
    halos = halo_copies(v_s, vl, vr, me, n, hsem)
    for c in halos:
        c.start()
    if ring:
        first.plane((3,))
        rest.start_across()
    lax.fori_loop(1, tiles // 2, inner, 0)
    if ring:
        first.space((2,))
        first.shares_in((2,))
    lax.fori_loop(0, 4, project_k, 0)
    if ring:
        first.space((3,))
        first.shares_in((3,))
        save_w.start()
        rest.line((0,))
    lax.fori_loop(0, 4, project_q, 0)

    pay[...] = jnp.concatenate([means[:, :half], means[:, half:]], axis=0).astype(BF16)

    def mark(j, peer):
        return remote(pay, slots.at[me], msem.at[0, j], msem.at[1, j], {"seq": peer})

    each_peer(me, n, mark, lambda c: c.start())
    slots[pl.ds(me, 1)] = pay[...][None]
    for c in drains[:4]:
        c.start()

    lax.fori_loop(tiles // 2, tiles - 1, inner, 0)
    for c in halos:
        c.wait()
    mask_halos(vl, vr, me, n)

    def edge(i, _):
        fill_edge(ext, v_s, vl, vr, i == 0)
        conv_forward(ext, taps, conv_s, i * (t - CTILE))
        return 0

    lax.fori_loop(0, 2, edge, 0)
    drains[4].start()
    each_peer(me, n, mark, lambda c: c.wait())
    gather_marks(slots, (mq, mk), n)
    for g in range(NG):
        bdk[g] = spread(mk[:, gs(g)])
        bdq[g] = spread(mq[:, gs(g)])
    uacc[...] = jnp.zeros_like(uacc)
    zacc[...] = jnp.zeros_like(zacc)
    ones_bd = jnp.where(head_mask(), 1.0, 0.0).astype(BF16)

    def attend(i, _):
        here = pl.ds(pl.multiple_of(i * (t // 4), t // 4), t // 4)
        for g in range(NG):
            s = dot_nt(q_s[here, gs(g)], bdk[g])
            ex = jnp.exp(s - half_reduce(s, jnp.max, -jnp.inf))
            den = dot(ex.astype(BF16), ones_bd)
            f_s[here, gs(g)] = (ex / den).astype(BF16)
            e = jnp.exp(dot_nt(k_s[here, gs(g)], bdq[g])).astype(BF16)
            e_s[here, gs(g)] = e
            uacc[g] += dot_tn(e, v_s[here, gs(g)])
            zacc[g] += dot_tn(e, jnp.ones((t // 4, 128), BF16))
        if ring:

            @pl.when(i == 0)
            def _():
                rest.plane((0,))

            @pl.when(i == 1)
            def _():
                rest.plane((1,))

        return 0

    lax.fori_loop(0, 4, attend, 0)
    for c in drains[5:]:
        c.start()
    lane = lax.broadcasted_iota(jnp.int32, (M, 128), 1)
    zt = jnp.zeros((M, 128), F32)
    for g in range(NG):
        put_tall(upart, g, collect(uacc[g]))
        for h in range(4):
            zt = zt + jnp.where(lane == 4 * g + h, zacc[g, h * 64 : h * 64 + 64, :], 0.0)
    upart[6 * M : 7 * M, :] = zt
    upart[7 * M :, :] = jnp.zeros((upart.shape[0] - 7 * M, 128), F32)
    summing = SeqSum(me, n, upart, uz, *sum_bufs)
    summing.start()
    pinv_begin(mq, mk, a_ref, z_ref)

    def newton(it, _):
        pinv_step(it, a_ref, z_ref, az_ref, t2_ref, t3_ref)
        return 0

    lax.fori_loop(0, NSITER // 2, newton, 0)
    summing.turn()
    lax.fori_loop(NSITER // 2, NSITER, newton, 0)
    summing.finish()
    p_ref[...] = z_ref[NSITER]
    for c in drains:
        c.wait()
    if ring:
        for c in local:
            c.wait()
        save_w.wait()
        rest.space((0, 1))
        rest.shares_in((0, 1))
        first.finish()
        rest.finish()


def front(x, weights, n, ring):
    t, d = x.shape
    if ring:
        rown = d // CHIPS
        own4 = (4, rown, d // 2)
        extra_out = [sds((3, d, d), BF16), sds((d, d), BF16), sds((2, d, d), BF16), sds((4, 2, rown, d // 2), BF16)]
        extra = [
            pltpu.VMEM((3, d, d), BF16),
            pltpu.VMEM((d, 128), F32),
            pltpu.VMEM((3, rown, d // 2), F32),
            pltpu.VMEM(own4, F32),
            pltpu.VMEM(own4, F32),
            pltpu.VMEM((rown, d // 2), F32),
            pltpu.VMEM((rown, d // 2), BF16),
            DMA((8,)),
            DMA((2,)),
        ] + GatherMesh.scratch(4) + GatherMesh.scratch(2)
    else:
        extra_out, extra = [], []
    r = padded_rows(7 * M, n)
    big = sds((t, d), BF16)
    steps = sds((NSITER, M, d), F32)
    res = pl.pallas_call(
        functools.partial(front_kernel, n=n, ring=ring),
        in_specs=[ANYW] + [VM] * len(weights),
        out_specs=([ANYW] * 3 + [VM] if ring else []) + [VM] * 2 + [ANYW] * 7 + [VM] * 11,
        out_shape=extra_out
        + [sds((8, d), F32), sds((40, d), F32)]
        + [big] * 7
        + [sds((M, d), BF16)] * 2
        + [sds((r, 128), F32), sds((M, d), F32), sds((NSITER + 1, M, d), F32), steps, steps, steps]
        + [sds((RAD, d), BF16)] * 2
        + [sds((M, d), F32)],
        scratch_shapes=[pltpu.VMEM((t, d), BF16)] * 8
        + [
            pltpu.VMEM((8, d), F32),
            pltpu.VMEM((16, d // 2), BF16),
            pltpu.VMEM((n, 16, d // 2), BF16),
            pltpu.VMEM((d // 128, CTILE + 2 * RAD, 128), F32),
            pltpu.VMEM((NG, GROUP, GROUP), BF16),
            pltpu.VMEM((NG, GROUP, GROUP), BF16),
            pltpu.VMEM((NG, GROUP, GROUP), F32),
            pltpu.VMEM((NG, GROUP, 128), F32),
            pltpu.VMEM((r, 128), F32),
            DMA((2,)),
            DMA((7,)),
            DMA((2, n)),
            DMA((4,)),
        ]
        + SeqSum.scratch(r, n)
        + extra,
        compiler_params=pltpu.CompilerParams(collective_id=1, has_side_effects=True, vmem_limit_bytes=VMEM_LIMIT),
        name="front",
    )(x, *weights)
    return res if ring else [None] * 4 + list(res)


PARTS = 4
HALF_D = 384
PART = 768


def middle_kernel(*refs, n, ring):
    take = Refs(refs)
    x_a, dy_a, f_a, q_a, conv_a, wo_a, ud_a = take(7)
    if ring:
        ud_own = take.one()
    gains, mk, uz, p_ref = take(4)
    out_o, dx_o, dmix_o, dqf_o, g_o = take(5)
    gw_ref, dkt_ref, dg_ref = take(3)
    if ring:
        t_ud = take.one()
    x_s, dy_s, f_s, mix_s, h2_s, da_s, x1_s, wo_s, ud = take(9)
    oacc, hacc, wbd, bdk, gwacc, dktacc, dgacc = take(7)
    isem, osem = take(2)
    t, d = x_s.shape
    tile = t // 4
    act_s, q_s = x_s, x_s
    seq = lax.axis_index("seq")
    parts_in = 1 if ring else PARTS
    gain = gains[1:2, :]

    def here(i):
        return pl.ds(pl.multiple_of(i * tile, tile), tile)

    load_q = pltpu.make_async_copy(q_a, q_s, isem.at[7])
    loads = [
        pltpu.make_async_copy(a, b, isem.at[i])
        for i, (a, b) in enumerate(
            ((f_a, f_s), (conv_a, mix_s), (x_a, x_s), (wo_a, wo_s), (ud_a, ud.at[pl.ds(0, parts_in)]), (dy_a, dy_s))
        )
    ]
    for c in loads:
        c.start()
    if ring:
        place = Place()
        gathers = [None] + [
            GatherMesh(place, (STACK,), (ud.at[p],), (ud_own.at[p],), take(6)) for p in range(1, PARTS)
        ]
        scatters = [
            ScatterMesh.take(take, place, (STACK,), (ud.at[p],), in_place=True) for p in range(PARTS - 1)
        ]
        greet(seq, n, [place.twin])
        for g in gathers[1:]:
            g.start_z()
        for p in range(1, PARTS):
            gathers[p].start_across()
            ud[p, :, at(seq, d // CHIPS, 16), at(place.rep, d // 2, 128)] = ud_own[p]

    def tick(cond, *acts):
        if ring and acts:

            @pl.when(cond)
            def _():
                for act in acts:
                    act()

    K = (0,)

    def move(p, *names):
        return [functools.partial(getattr(gathers[p], name), K) for name in names] if ring else []

    def send(p, *names):
        return [functools.partial(getattr(scatters[p], name), 0) for name in names] if ring else []

    gwacc[...] = jnp.zeros_like(gwacc)
    dktacc[...] = jnp.zeros_like(dktacc)
    dgacc[...] = jnp.zeros_like(dgacc)
    for g in range(NG):
        bv = u_group(uz, g) / zt_group(uz, g)
        wbd[g] = spread(dot(p_ref[:, gs(g)], spread(bv), HI)).astype(BF16)
        bdk[g] = spread(mk[:, gs(g)])
    for c in loads[:4]:
        c.wait()

    def before(i, _):
        r = here(i)
        for g in range(NG):
            mix_s[r, gs(g)] = (dot(f_s[r, gs(g)], wbd[g]) + mix_s[r, gs(g)].astype(F32)).astype(BF16)
        x1 = x_s[r, :].astype(F32) + dot(mix_s[r, :], wo_s[...])
        oacc[r, :] = x1
        x1_s[r, :] = x1.astype(BF16)
        normal, _inv = normalize(x1)
        h2_s[r, :] = (normal * gain).astype(BF16)
        tick(i == 1, *move(1, "line", "line_on"))
        tick(i == 3, *move(1, "plane"))
        return 0

    lax.fori_loop(0, 4, before, 0)
    loads[4].wait()
    loads[5].wait()
    plan = {
        (0, 0): move(2, "line", "line_on"),
        (0, 2): move(1, "space") + move(2, "plane"),
        (0, 3): move(3, "line", "line_on"),
        (1, 0): move(3, "plane") + send(0, "far"),
        (1, 1): move(2, "space"),
        (1, 2): send(0, "mid"),
        (1, 3): move(3, "space"),
        (2, 0): send(0, "near") + send(1, "far"),
        (2, 2): send(1, "mid"),
        (3, 0): send(1, "near") + send(2, "far"),
        (3, 2): send(2, "mid"),
    }
    for p in range(PARTS):
        if ring and p > 0:
            gathers[p].shares_in(K)
        u, dn = ud.at[p, 0], ud.at[p, 1]

        def through(i, _):
            r = here(i)
            h2 = h2_s[r, :]
            dy = dy_s[r, :]
            o = h = None
            for c in range(0, d, PART):
                cols = slice(c, c + PART)
                act, slope = gelu_parts(dot(h2, u[:, cols]))
                act = act.astype(BF16)
                act_s[r, cols] = act
                da = (dot_nt(dy, dn[cols, :]) * slope).astype(BF16)
                da_s[r, cols] = da
                oc, hc = dot(act, dn[cols, :]), dot_nt(da, u[:, cols])
                o, h = (oc, hc) if o is None else (o + oc, h + hc)
            oacc[r, :] += o
            hacc[r, :] = h if p == 0 else hacc[r, :] + h
            for j in range(4):
                tick(i == j, *plan.get((p, j), []))
            return 0

        lax.fori_loop(0, 4, through, 0)
        if ring and p > 0:
            gathers[p].finish()

        def grads(j, _):
            cols = pl.ds(pl.multiple_of(j * HALF_D, HALF_D), HALF_D)
            ud[p, 0, cols, :] = dot_tn(h2_s[:, cols], da_s[...]).astype(BF16)
            ud[p, 1, cols, :] = dot_tn(act_s[:, cols], dy_s[...]).astype(BF16)
            return 0

        lax.fori_loop(0, d // HALF_D, grads, 0)
        if ring and p < PARTS - 1:
            scatters[p].start()
        if ring and p == 2:
            t_ud[0] = scatters[0].total(0)
    load_q.start()
    first_out = PARTS - 1 if ring else 0
    stored = [
        pltpu.make_async_copy(ud.at[p], g_o.at[pl.ds(2 * (p - first_out), 2)], osem.at[16 + p])
        for p in range(first_out, PARTS)
    ]
    for c in stored:
        c.start()
    tick(True, *send(2, "near"))
    if ring:
        t_ud[1] = scatters[1].total(0)
    load_q.wait()

    def after(i, _):
        r = here(i)
        normal, inv = normalize(x1_s[r, :].astype(F32))
        x1_s[r, :] = oacc[r, :].astype(BF16)
        pltpu.make_async_copy(x1_s.at[r], out_o.at[r], osem.at[i]).start()
        dh2 = hacc[r, :]
        dgacc[...] += rowsum8(dh2 * normal)
        dx = (norm_back(dh2, normal, inv, gain) + dy_s[r, :].astype(F32)).astype(BF16)
        dy_s[r, :] = dx
        pltpu.make_async_copy(dy_s.at[r], dx_o.at[r], osem.at[4 + i]).start()
        dmix = dot_nt(dx, wo_s[...]).astype(BF16)
        h2_s[r, :] = dmix
        pltpu.make_async_copy(h2_s.at[r], dmix_o.at[r], osem.at[8 + i]).start()
        ones_bd = jnp.where(head_mask(), 1.0, 0.0).astype(BF16)
        for g in range(NG):
            dm = dmix[:, gs(g)]
            f = f_s[r, gs(g)]
            df = dot_nt(dm, wbd[g])
            gwacc[g] += dot_tn(f, dm)
            ff32 = f.astype(F32)
            prod = df * ff32
            hi, lo = split(prod)
            ds = (ff32 * (df - (dot(hi, ones_bd) + dot(lo, ones_bd)))).astype(BF16)
            da_s[r, gs(g)] = dot(ds, bdk[g]).astype(BF16)
            dktacc[g] += dot_tn(ds, q_s[r, gs(g)])
        pltpu.make_async_copy(da_s.at[r], dqf_o.at[r], osem.at[12 + i]).start()
        return 0

    lax.fori_loop(0, 4, after, 0)

    def grad_o(j, _):
        cols = pl.ds(pl.multiple_of(j * HALF_D, HALF_D), HALF_D)
        wo_s[cols, :] = dot_tn(mix_s[:, cols], dy_s[...]).astype(BF16)
        return 0

    lax.fori_loop(0, d // HALF_D, grad_o, 0)
    stored.append(pltpu.make_async_copy(wo_s, g_o.at[2 * (PARTS - first_out)], osem.at[20]))
    stored[-1].start()
    for g in range(NG):
        put_tall(gw_ref, g, collect(gwacc[g]))
        dkt_ref[:, gs(g)] = collect(dktacc[g])
    if gw_ref.shape[0] > 6 * M:
        gw_ref[6 * M :] = jnp.zeros((gw_ref.shape[0] - 6 * M, 128), F32)
    dg_ref[...] = jnp.broadcast_to(jnp.sum(dgacc[...], axis=0, keepdims=True), dg_ref.shape)
    if ring:
        t_ud[2] = scatters[2].total(0)
        for sc in scatters:
            sc.finish()
    for i in range(4):
        for b, src, dst in ((0, x1_s, out_o), (4, dy_s, dx_o), (8, h2_s, dmix_o), (12, da_s, dqf_o)):
            pltpu.make_async_copy(src.at[here(i)], dst.at[here(i)], osem.at[b + i]).wait()
    for c in stored:
        c.wait()


def middle(x, dy, f, q, conv, wo, ud, ud_own, gains, mk, uz, p, gw_rows, n):
    ring = ud_own is not None
    t, d = x.shape
    big = sds((t, d), BF16)
    outs = [big] * 4 + [sds((3 if ring else 2 * PARTS + 1, d, d), BF16)]
    outs += [sds((gw_rows, 128), F32), sds((M, d), F32), sds((8, d), F32)]
    extra = []
    if ring:
        cell = (2, d // CHIPS, d // 2)
        outs += [sds((PARTS - 1, *cell), F32)]
        extra = GatherMesh.scratch(1) * (PARTS - 1) + ScatterMesh.scratch([(cell, BF16)], True) * (PARTS - 1)
    square = pltpu.VMEM((NG, GROUP, GROUP), BF16)
    square_f = pltpu.VMEM((NG, GROUP, GROUP), F32)
    return pl.pallas_call(
        functools.partial(middle_kernel, n=n, ring=ring),
        in_specs=[ANYW] * 7 + [VM] * (5 if ring else 4),
        out_specs=[ANYW] * 5 + [VM] * (len(outs) - 5),
        out_shape=outs,
        scratch_shapes=[pltpu.VMEM((t, d), BF16)] * 7
        + [
            pltpu.VMEM((d, d), BF16),
            pltpu.VMEM((PARTS, 2, d, d), BF16),
            pltpu.VMEM((t, d), F32),
            pltpu.VMEM((t, d), F32),
            square,
            square,
            square_f,
            square_f,
            pltpu.VMEM((8, d), F32),
            DMA((8,)),
            DMA((21,)),
        ]
        + extra,
        compiler_params=pltpu.CompilerParams(
            collective_id=4 if ring else None, has_side_effects=True, vmem_limit_bytes=61 * 1024 * 1024
        ),
        name="middle",
    )(x, dy, f, q, conv, wo, ud, *((ud_own,) if ring else ()), gains, mk, uz, p)


def rear_kernel(*refs, n, ring, seg_len):
    take = Refs(refs)
    bodies = take(5)
    if ring:
        grads = take(1)
    gw_part, uz, a_ref, z_ref, az_ref, t2_ref, t3_ref, mq, mk, vl, vr, taps, dkt_ref, dg2_ref = take(14)
    if ring:
        t_ud = take.one()
    dqkv_o, gvec_o = take(2)
    if ring:
        r_uo, r_down, r_vec = take(3)
    v_s, g_s, e_s, k_s, dqf_s, dqkv, gvec = take(7)
    vext, gext, tapacc, gl, gr, gw, gz, da, dubd, rowadd, dqtacc, bdq, pay, slots, own = take(15)
    isem, osem, hsem, wsem = take(4)
    sum_bufs = take(3)
    me = lax.axis_index("seq")
    t, d = v_s.shape
    loads = [
        pltpu.make_async_copy(b, s, isem.at[i]) for i, (b, s) in enumerate(zip(bodies, (v_s, g_s, e_s, k_s, dqf_s)))
    ]
    for c in loads:
        c.start()
    if ring:
        place = Place()
        greet(me, n, [place.twin])
        big = ScatterMesh.take(take, place, (STACK,), grads)
        vec = ScatterMesh.take(take, place, (LINES,), (gvec,))
        fuo, fd, fsem = take(3)
    else:
        greet(me, n, [])
    summing = SeqSum(me, n, gw_part, gw, *sum_bufs)
    loads[1].wait()
    halos = halo_copies(g_s, gl, gr, me, n, hsem)
    for c in halos:
        c.start()
    summing.start()
    if ring:
        big.start()

    def tick(cond, *acts):
        if ring:

            @pl.when(cond)
            def _():
                for act, k in acts:
                    act(k)

    tapacc[...] = jnp.zeros_like(tapacc)
    loads[0].wait()
    if not ring:
        big = vec = None
    far = (lambda k: big.far(k))
    mid = (lambda k: big.mid(k))
    near = (lambda k: big.near(k))

    def inner(i, _):
        fill_inner(vext, v_s, i * CTILE)
        fill_inner(gext, g_s, i * CTILE)
        conv_backward(vext, gext, taps, dqkv, tapacc, i * CTILE)


        @pl.when(i == 2)
        def _():
            summing.turn()

        tick(i == 2, (far, 0))
        tick(i == 6, (mid, 0))
        return 0

    lax.fori_loop(1, t // CTILE - 1, inner, 0)
    for c in halos:
        c.wait()
    mask_halos(gl, gr, me, n)

    def edge(i, _):
        fill_edge(vext, v_s, vl, vr, i == 0)
        fill_edge(gext, g_s, gl, gr, i == 0)
        conv_backward(vext, gext, taps, dqkv, tapacc, i * (t - CTILE))
        return 0

    lax.fori_loop(0, 2, edge, 0)
    dtap = jnp.sum(tapacc[...], axis=1)
    lines = jnp.concatenate([jnp.zeros((1, d), F32), dg2_ref[0:1, :], dtap, jnp.zeros((128 - 42, d), F32)], axis=0)
    gvec[...] = jnp.transpose(lines)
    if ring:
        vec.start()
    else:
        save_vec = pltpu.make_async_copy(gvec, gvec_o, osem.at[1])
        save_vec.start()
    tick(True, (near, 0))
    summing.finish()
    for g in range(NG):
        z = zt_group(uz, g)
        bv = u_group(uz, g) / z
        gwg = u_group(gw, g)
        gz[:, gs(g)] = flip(dot_nt(gwg, spread(bv), HI))
        dbv = dot(flip(z_ref[NSITER, :, gs(g)]), spread(gwg), HI)
        dubd[g] = spread(dbv / z).astype(BF16)
        rowadd[g] = dot_nt(jnp.ones((8, GROUP), F32), spread(dbv * bv / z), HI)
        bdq[g] = spread(mq[:, gs(g)])
    da[...] = jnp.zeros_like(da)

    def newton(j, _):
        pinv_back_step(NSITER - 1 - j, a_ref, z_ref, az_ref, t2_ref, t3_ref, gz, da)
        tick(j == 1, (lambda k: vec.far(k), 0))
        tick(j == 3, (lambda k: vec.mid(k), 0))
        tick(j == 5, (lambda k: vec.near(k), 0))
        return 0

    lax.fori_loop(0, NSITER, newton, 0)
    loads[2].wait()
    loads[3].wait()
    dqtacc[...] = jnp.zeros_like(dqtacc)

    def cols(part, g):
        return slice(part * d + g * GROUP, part * d + (g + 1) * GROUP)

    def through(i, _):
        here = pl.ds(pl.multiple_of(i * (t // 4), t // 4), t // 4)
        for g in range(NG):
            e = e_s[here, gs(g)]
            de = dot_nt(v_s[here, gs(g)], dubd[g]) - rowadd[g, 0:1, :]
            ds = (e.astype(F32) * de).astype(BF16)
            dqkv[here, cols(2, g)] = (dot(e, dubd[g]) + dqkv[here, cols(2, g)].astype(F32)).astype(BF16)
            dqkv[here, cols(1, g)] = dot(ds, bdq[g]).astype(BF16)
            dqtacc[g] += dot_tn(ds, k_s[here, gs(g)])
        return 0

    lax.fori_loop(0, 4, through, 0)

    rows_dev = max(M // n, 1)
    per_mark = n * rows_dev // M
    if rows_dev < 4:
        pay[...] = jnp.zeros_like(pay)
    for g in range(NG):
        ds = pinv_back_end(g, a_ref, gz, da)
        dq = collect(dqtacc[g]) + dot(ds, spread(mk[:, gs(g)].astype(F32)), HI) * (1.0 / n)
        dk = dkt_ref[:, gs(g)] + dot(flip(ds), spread(mq[:, gs(g)].astype(F32)), HI) * (1.0 / n)
        for i in range(n):
            row = i * rows_dev // per_mark
            pay[i, 0:rows_dev, gs(g)] = dq[row : row + rows_dev]
            pay[i, 4 : 4 + rows_dev, gs(g)] = dk[row : row + rows_dev]

    def mark(j, peer):
        return remote(pay.at[peer], slots.at[me], wsem.at[0, j], wsem.at[1, j], {"seq": peer})

    each_peer(me, n, mark, lambda c: c.start())
    slots[pl.ds(me, 1)] = pay[pl.ds(me, 1)]
    if ring:
        last_ud = big.total(0)
        for p in range(PARTS - 1):
            fuo[p] = t_ud[p, 0]
            fd[p] = t_ud[p, 1]
        fuo[PARTS - 1] = last_ud[0]
        fd[PARTS - 1] = last_ud[1]
        fuo[PARTS] = last_ud[2]
        cols = at(place.rep, d // 2, 128)
        back = [swap_rows(fuo, r_uo, place, fsem.at[0])]
        for j in range(2):
            r_down[j, :, cols] = fd[2 * place.rep + j]
            src = fd.at[2 * (1 - place.rep) + j]
            back.append(remote(src, r_down.at[j, :, cols], fsem.at[1 + j, 0], fsem.at[1 + j, 1], place.twin))
        for c in back:
            c.start()
        r_vec[...] = vec.total(0)
    loads[4].wait()
    each_peer(me, n, mark, lambda c: c.wait())
    own[...] = lax.fori_loop(1, n, lambda i, acc: acc + slots[i], slots[0]) * (1.0 / seg_len)

    def landed(i, _):
        here = pl.ds(pl.multiple_of(i * (t // 4), t // 4), t // 4)
        row = lax.div(i * rows_dev, 4)
        dqkv[here, 0:d] = (dqf_s[here, :].astype(F32) + own[pl.ds(row, 1), :]).astype(BF16)
        dqkv[here, d : 2 * d] = (dqkv[here, d : 2 * d].astype(F32) + own[pl.ds(row + 4, 1), :]).astype(BF16)
        pltpu.make_async_copy(dqkv.at[here], dqkv_o.at[here], osem.at[2 + i]).start()
        return 0

    lax.fori_loop(0, 4, landed, 0)
    if ring:
        for c in back:
            c.wait()
        big.finish()
        vec.finish()
        save_vec = pltpu.make_async_copy(gvec, gvec_o, osem.at[1])
        save_vec.start()
    for i in range(4):
        here = pl.ds(i * (t // 4), t // 4)
        pltpu.make_async_copy(dqkv.at[here], dqkv_o.at[here], osem.at[2 + i]).wait()
    save_vec.wait()


def rear(bodies, grads, gw, uz, a, z, az, t2, t3, mq, mk, vl, vr, taps, dkt, dg2, t_ud, n, seg_len):
    ring = grads is not None
    t, d = bodies[0].shape
    r = gw.shape[0]
    outs = [sds((t, 3 * d), BF16), sds((d, 128), F32)]
    extra = []
    if ring:
        own = d // (2 * CHIPS)
        outs += [sds((PARTS + 1, own, d), F32), sds((2, 2 * own, d), F32), sds((own, 128), F32)]
        extra = ScatterMesh.scratch([((3, 2 * own, d // 2), BF16)]) + ScatterMesh.scratch([((own, 128), F32)]) + [
            pltpu.VMEM((PARTS + 1, 2 * own, d // 2), F32),
            pltpu.VMEM((PARTS, 2 * own, d // 2), F32),
            DMA((3, 2)),
        ]
    ext = pltpu.VMEM((d // 128, CTILE + 2 * RAD, 128), F32)
    halo = pltpu.VMEM((RAD, d), BF16)
    small = pltpu.VMEM((M, d), F32)
    return pl.pallas_call(
        functools.partial(rear_kernel, n=n, ring=ring, seg_len=seg_len),
        in_specs=[ANYW] * (5 + (1 if ring else 0)) + [VM] * (14 + (1 if ring else 0)),
        out_specs=[ANYW] * 2 + [VM] * (len(outs) - 2),
        out_shape=outs,
        scratch_shapes=[pltpu.VMEM((t, d), BF16)] * 5
        + [
            pltpu.VMEM((t, 3 * d), BF16),
            pltpu.VMEM((d, 128), F32),
            ext,
            ext,
            pltpu.VMEM((40, 8, d), F32),
            halo,
            halo,
            pltpu.VMEM((r, 128), F32),
            small,
            small,
            pltpu.VMEM((NG, GROUP, GROUP), BF16),
            pltpu.VMEM((NG, 8, GROUP), F32),
            pltpu.VMEM((NG, GROUP, GROUP), F32),
            pltpu.VMEM((NG, GROUP, GROUP), BF16),
            pltpu.VMEM((n, 8, d), F32),
            pltpu.VMEM((n, 8, d), F32),
            pltpu.VMEM((8, d), F32),
            DMA((5,)),
            DMA((6,)),
            DMA((4,)),
            DMA((2, n)),
        ]
        + SeqSum.scratch(r, n)
        + extra,
        compiler_params=pltpu.CompilerParams(collective_id=2, has_side_effects=True, vmem_limit_bytes=VMEM_LIMIT),
        name="rear",
    )(*bodies, *(grads if ring else ()), gw, uz, a, z, az, t2, t3, mq, mk, vl, vr, taps, dkt, dg2, *((t_ud,) if ring else ()))


def last_kernel(*refs, n, ring):
    take = Refs(refs)
    x_a, dx_a, dqkv_a, w_a = take(4)
    if ring:
        grads = take(1)
    (gains,) = take(1)
    ig_o, dg_o = take(2)
    if ring:
        (r_qkv,) = take(1)
    x_s, dx_s, dqkv_s, w_s, ig_s, part, slots, dgacc, isem, osem, gsem = take(11)
    t, d = x_s.shape
    tile = t // 4
    me = lax.axis_index("seq")

    def here(i):
        return pl.ds(pl.multiple_of(i * tile, tile), tile)

    def loads(i):
        return [
            pltpu.make_async_copy(a.at[here(i)], s.at[here(i)], isem.at[k, i])
            for k, (a, s) in enumerate(((x_a, x_s), (dx_a, dx_s), (dqkv_a, dqkv_s)))
        ]

    load_w = pltpu.make_async_copy(w_a, w_s, isem.at[3, 0])
    load_w.start()
    if ring:
        place = Place()
        greet(me, n, [place.twin])
        scatter = ScatterMesh.take(take, place, (HALF,), grads)
        fq, fsem = take(2)
        scatter.start()
    else:
        greet(me, n, [])
    for i in range(4):
        for c in loads(i):
            c.start()
    if ring:
        scatter.far(0)
    load_w.wait()
    dgacc[...] = jnp.zeros_like(dgacc)

    def body(i, _):
        for c in loads(i):
            c.wait()
        dq, dk, dv = (dqkv_s[here(i), p * d : (p + 1) * d] for p in range(3))
        dh = (dot_nt(dq, w_s[0]) + dot_nt(dk, w_s[1])) * QK_SCALE + dot_nt(dv, w_s[2])
        normal, inv = normalize(x_s[here(i), :].astype(F32))
        dgacc[...] += rowsum8(dh * normal)
        ig = norm_back(dh, normal, inv, gains[0:1, :]) + dx_s[here(i), :].astype(F32)
        ig_s[here(i), :] = ig.astype(BF16)
        pltpu.make_async_copy(ig_s.at[here(i)], ig_o.at[here(i)], osem.at[i]).start()
        if ring:

            @pl.when(i == 2)
            def _():
                scatter.mid(0)

        return 0

    lax.fori_loop(0, 4, body, 0)
    row = jnp.sum(dgacc[...], axis=0, keepdims=True)
    part[...] = jnp.concatenate(
        [row[:, c : c + 128] for c in range(0, d, 128)] + [jnp.zeros((8 - d // 128, 128), F32)], axis=0
    )

    def send(j, peer):
        return remote(part, slots.at[me], gsem.at[0, j], gsem.at[1, j], {"seq": peer})

    each_peer(me, n, send, lambda c: c.start())
    slots[pl.ds(me, 1)] = part[...][None]
    if ring:
        scatter.near(0)
    each_peer(me, n, send, lambda c: c.wait())
    total = lax.fori_loop(1, n, lambda i, acc: acc + slots[i], slots[0])
    if ring:
        twin_sum = remote(dg_o.at[0], dg_o.at[1], gsem.at[0, 0], gsem.at[1, 0], place.twin)
        dg_o[0] = total
        twin_sum.start()
        fq[...] = scatter.total(0)
        back = swap_rows(fq, r_qkv, place, fsem)
        back.start()
        scatter.finish()
        twin_sum.wait()
        back.wait()
    else:
        dg_o[0] = total
        dg_o[1] = jnp.zeros_like(total)
    for i in range(4):
        pltpu.make_async_copy(ig_s.at[here(i)], ig_o.at[here(i)], osem.at[i]).wait()


def last(x, dx, dqkv, w_qkv, gains, g_qkv, n):
    ring = g_qkv is not None
    t, d = x.shape
    outs = [sds((t, d), BF16), sds((2, 8, 128), F32)]
    extra = []
    if ring:
        own = d // (2 * CHIPS)
        wide = g_qkv.shape[1]
        outs += [sds((own, wide), F32)]
        extra = ScatterMesh.scratch([((2 * own, wide // 2), BF16)]) + [pltpu.VMEM((2 * own, wide // 2), F32), DMA((2,))]
    return pl.pallas_call(
        functools.partial(last_kernel, n=n, ring=ring),
        in_specs=[ANYW] * (4 + (1 if ring else 0)) + [VM],
        out_specs=[ANYW] + [VM] * (len(outs) - 1),
        out_shape=outs,
        scratch_shapes=[
            pltpu.VMEM((t, d), BF16),
            pltpu.VMEM((t, d), BF16),
            pltpu.VMEM((t, 3 * d), BF16),
            pltpu.VMEM((3, d, d), BF16),
            pltpu.VMEM((t, d), BF16),
            pltpu.VMEM((8, 128), F32),
            pltpu.VMEM((n, 8, 128), F32),
            pltpu.VMEM((8, d), F32),
            DMA((4, 4)),
            DMA((4,)),
            DMA((2, n)),
        ]
        + extra,
        compiler_params=pltpu.CompilerParams(collective_id=3, has_side_effects=True, vmem_limit_bytes=VMEM_LIMIT),
        name="last",
    )(x, dx, dqkv, w_qkv, *((g_qkv,) if ring else ()), gains)


def adam_step(weight, grad_vec, moment, second, rate_value):
    moment_new = BETA_ONE * moment + (1.0 - BETA_ONE) * grad_vec
    second_new = BETA_TWO * second + (1.0 - BETA_TWO) * grad_vec * grad_vec
    first_hat = moment_new / (1.0 - BETA_ONE**STEP)
    second_hat = second_new / (1.0 - BETA_TWO**STEP)
    weight_new = weight - rate_value * (
        first_hat / (jnp.sqrt(second_hat) + ADAM_EPS) + DECAY_RATE * weight
    )
    return (weight_new, moment_new, second_new)


def per_device(tokens, cotangent, attn_w, w_up, w_down, vectors, attn_m, attn_v, up_m, up_v, down_m, down_v, vec_m, vec_v):
    both = ("seq", "rep")
    x = tokens[0]
    dy = cotangent[0]
    t, d = x.shape
    n = lax.axis_size("seq")
    seg_len = t * n // M
    ring = n == CHIPS and lax.axis_size("rep") == 2

    rown = d // n
    if ring:
        ups = jnp.transpose(w_up.reshape(rown // 2, n, PARTS, rown), (2, 0, 1, 3)).reshape(PARTS, rown // 2, d)
        weights = (attn_w, ups, w_down.reshape(2, rown, d), jnp.pad(vectors, ((0, 0), (0, 128 - vectors.shape[1]))))
    else:
        w_attn = lax.all_gather(attn_w.astype(BF16), both, axis=1, tiled=True)
        vec = lax.all_gather(vectors.astype(BF16), both, axis=0, tiled=True).astype(F32)
        weights = (w_attn[:3], jnp.pad(vec, ((0, 0), (0, 128 - vec.shape[1]))))
    (w_qkv, wo, ud, ud_own, gains, taps, h1, q, k, v, conv, f, e, mq, mk, uz, a, z, az, t2, t3, vl, vr, pinverse) = front(
        x, weights, n, ring
    )
    if not ring:
        w_qkv, wo = w_attn[:3], w_attn[3]
        up = lax.all_gather(w_up.astype(BF16), both, axis=0, tiled=True)
        down = lax.all_gather(w_down.astype(BF16), both, axis=0, tiled=True)
        ud = jnp.stack([jnp.transpose(up.reshape(d, PARTS, d), (1, 0, 2)), down.reshape(PARTS, d, d)], axis=1)
    else:
        ud = ud[None]
    res = middle(x, dy, f, q, conv, wo, ud, ud_own, gains, mk, uz, pinverse, padded_rows(6 * M, n), n)
    out, dx, dmix, dqf, g_last, gw, dkt, dg2 = res[:8]
    dot_xla = functools.partial(jnp.einsum, "ta,tb->ab", preferred_element_type=F32)
    res = rear(
        (v, dmix, e, k, dqf),
        (g_last,) if ring else None,
        gw, uz, a, z, az, t2, t3, mq, mk, vl, vr, taps, dkt, dg2,
        res[8] if ring else None,
        n, seg_len,
    )
    dqkv, g_vec = res[:2]
    column = jnp.concatenate([jnp.full((2 * d,), QK_SCALE, F32), jnp.ones((d,), F32)])
    g_qkv = (dot_xla(h1, dqkv) * column).astype(BF16)
    fin = last(x, dx, dqkv, w_qkv, gains, g_qkv if ring else None, n)
    ig = fin[0]
    dg1 = (fin[1][0] + fin[1][1])[: d // 128].reshape(d)
    if ring:
        r_uo, r_down, red_vec = res[2:]
        red_o = r_uo[PARTS]
        red_up = jnp.transpose(r_uo[:PARTS].reshape(PARTS, rown // 2, n, rown), (1, 2, 0, 3)).reshape(w_up.shape)
        red_down = r_down.reshape(w_down.shape)
        own = d // (2 * n)
        red_qkv = jnp.transpose(fin[2].reshape(own, 3, d), (1, 0, 2))
        red_attn = jnp.concatenate([red_qkv, red_o[None]], axis=0)
        start = (lax.axis_index("seq") * 2 + lax.axis_index("rep")) * own
        dg1_own = lax.dynamic_slice_in_dim(dg1, start, own, 0)
        red_vec = jnp.concatenate([dg1_own[:, None], red_vec[:, 1 : vectors.shape[1]]], axis=1)
    else:
        g_attn = jnp.concatenate([jnp.transpose(g_qkv.reshape(d, 3, d), (1, 0, 2)), g_last[2 * PARTS :]], axis=0)
        g_pairs = g_last[: 2 * PARTS].reshape(PARTS, 2, d, d)
        g_up = jnp.transpose(g_pairs[:, 0], (1, 0, 2)).reshape(d, PARTS * d)
        g_down = g_pairs[:, 1].reshape(PARTS * d, d)
        red_attn = lax.psum_scatter(g_attn, both, scatter_dimension=1, tiled=True).astype(F32)
        red_up = lax.psum_scatter(g_up, both, scatter_dimension=0, tiled=True).astype(F32)
        red_down = lax.psum_scatter(g_down, both, scatter_dimension=0, tiled=True).astype(F32)
        g_vec = jnp.concatenate([dg1[:, None] / n, g_vec[:, 1 : vectors.shape[1]]], axis=1)
        red_vec = lax.psum_scatter(g_vec, both, scatter_dimension=0, tiled=True)
    return (
        out[None],
        ig[None],
        *adam_step(attn_w, red_attn, attn_m, attn_v, LEARN_RATE),
        *adam_step(w_up, red_up, up_m, up_v, LEARN_RATE),
        *adam_step(w_down, red_down, down_m, down_v, LEARN_RATE),
        *adam_step(vectors, red_vec, vec_m, vec_v, VECTOR_RATE),
    )


def solution(mesh):
    tok = P("rep", "seq", None)
    att = P(None, ("seq", "rep"), None)
    mat = P(("seq", "rep"), None)
    return jax.shard_map(
        per_device,
        mesh=mesh,
        in_specs=(tok, tok, att, mat, mat, mat, att, att, mat, mat, mat, mat, mat, mat),
        out_specs=(tok, tok, att, att, att) + (mat,) * 9,
        check_vma=False,
    )
```

```python
import functools

import jax
import jax.numpy as jnp
from jax import lax
from jax.experimental import pallas as pl
from jax.experimental.pallas import tpu as pltpu
from jax.sharding import PartitionSpec as P

H = 12
HD = 64
M = 64
KC = 33
NSITER = 6
STEP = 10
EPS_NORM = 1e-05
BETA_ONE = 0.9
BETA_TWO = 0.999
ADAM_EPS = 1e-08
LEARN_RATE = 0.03
VECTOR_RATE = 0.15
DECAY_RATE = 0.1

F32 = jnp.float32
BF16 = jnp.bfloat16
GROUP = 256
NG = 3
RAD = 16
QK_SCALE = HD ** (-0.25)
HI = lax.Precision.HIGHEST
VMEM_LIMIT = 58 * 1024 * 1024


def dot(a, b, precision=None):
    return lax.dot_general(a, b, (((1,), (0,)), ((), ())), precision=precision, preferred_element_type=F32)


def dot_nt(a, b, precision=None):
    return lax.dot_general(a, b, (((1,), (1,)), ((), ())), precision=precision, preferred_element_type=F32)


def dot_tn(a, b, precision=None):
    return lax.dot_general(a, b, (((0,), (0,)), ((), ())), precision=precision, preferred_element_type=F32)


def split(x):
    hi = x.astype(BF16)
    return hi, (x - hi.astype(F32)).astype(BF16)


def dot3(a, b):
    return dot(a[0], b[0]) + (dot(a[0], b[1]) + dot(a[1], b[0]))


def spread2(a):
    return spread(a[0]), spread(a[1])


def head_mask(shape=(GROUP, GROUP)):
    rows = lax.broadcasted_iota(jnp.int32, shape, 0)
    cols = lax.broadcasted_iota(jnp.int32, shape, 1)
    return lax.shift_right_logical(rows, 6) == lax.shift_right_logical(cols, 6)


def spread(wide):
    tall = jnp.concatenate([wide, wide, wide, wide], axis=0)
    return jnp.where(head_mask(), tall, jnp.zeros_like(tall))


def collect(full):
    kept = jnp.where(head_mask(), full, jnp.zeros_like(full))
    return (kept[0:64] + kept[64:128]) + (kept[128:192] + kept[192:256])


def flip(wide):
    turned = jnp.transpose(spread(wide))
    return (turned[0:64] + turned[64:128]) + (turned[128:192] + turned[192:256])


def gs(g):
    return slice(g * GROUP, (g + 1) * GROUP)


def half_reduce(x, op, init):
    parts = []
    for c in range(x.shape[1] // 128):
        col = x[:, c * 128 : (c + 1) * 128]
        low = lax.broadcasted_iota(jnp.int32, col.shape, 1) < 64
        a = op(jnp.where(low, col, init), axis=1, keepdims=True)
        b = op(jnp.where(low, init, col), axis=1, keepdims=True)
        parts.append(jnp.where(low, a, b))
    return jnp.concatenate(parts, axis=1)


def normalize(x):
    center = x - jnp.mean(x, axis=-1, keepdims=True)
    inv = lax.rsqrt(jnp.mean(center * center, axis=-1, keepdims=True) + EPS_NORM)
    return center * inv, inv


def norm_back(up, normal, inv, gain):
    scaled = up * gain
    centered = scaled - jnp.mean(scaled, axis=-1, keepdims=True)
    return inv * (centered - normal * jnp.mean(scaled * normal, axis=-1, keepdims=True))


def rowsum8(x):
    return jnp.sum(x.reshape(x.shape[0] // 8, 8, x.shape[1]), axis=0)


def gelu_parts(a):
    z = jnp.abs(a)
    t = 1.0 / (1.0 + (0.3275911 * 0.7071067811865476) * z)
    e = jnp.exp(-0.5 * a * a)
    poly = t * (0.127414796 + t * (-0.142248368 + t * (0.7107068705 + t * (-0.7265760135 + t * 0.5307027145))))
    tail = poly * e
    phi = jnp.where(a >= 0, 1.0 - tail, tail)
    return a * phi, phi + a * (e * 0.3989422804014327)


def whole(shape):
    zeros = (0,) * len(shape)
    return pl.BlockSpec(shape, lambda i: zeros, pipeline_mode=pl.Buffered(1))


def rows(tile, width):
    return pl.BlockSpec((tile, width), lambda i: (i, 0))


def sds(shape, dtype):
    return jax.ShapeDtypeStruct(shape, dtype)


def params():
    return pltpu.CompilerParams(dimension_semantics=("arbitrary",), vmem_limit_bytes=VMEM_LIMIT)


def widen(zt, g):
    return jnp.concatenate(
        [jnp.broadcast_to(zt[:, h : h + 1], (M, HD)) for h in range(4 * g, 4 * g + 4)], axis=1
    )


def u_group(ref, g):
    return jnp.concatenate([ref[2 * g * M : (2 * g + 1) * M, :], ref[(2 * g + 1) * M : (2 * g + 2) * M, :]], axis=1)


def zt_group(ref, g):
    return widen(ref[6 * M : 7 * M, :], g)


def put_tall(ref, g, wide):
    ref[2 * g * M : (2 * g + 1) * M, :] = wide[:, :128]
    ref[(2 * g + 1) * M : (2 * g + 2) * M, :] = wide[:, 128:]


def padded_rows(r, n):
    return -(-r // (8 * n)) * 8 * n


MESH = pl.DeviceIdType.MESH
DMA = pltpu.SemaphoreType.DMA
VM = pl.BlockSpec(memory_space=pltpu.VMEM)
ANYW = pl.BlockSpec(memory_space=pl.ANY)


def remote(src, dst, send, recv, where):
    return pltpu.make_async_remote_copy(
        src_ref=src, dst_ref=dst, send_sem=send, recv_sem=recv, device_id=where, device_id_type=MESH
    )


def greet(me, n, others):
    bar = pltpu.get_barrier_semaphore()

    def hello(j, _):
        pl.semaphore_signal(bar, inc=1, device_id={"seq": lax.rem(me + j, n)}, device_id_type=MESH)
        return 0

    lax.fori_loop(1, n, hello, 0)
    for peer in others:
        pl.semaphore_signal(bar, inc=1, device_id=peer, device_id_type=MESH)
    pl.semaphore_wait(bar, n - 1 + len(others))


def each_peer(me, n, make, act):
    def body(j, _):
        act(make(j, lax.rem(me + j, n)))
        return 0

    lax.fori_loop(1, n, body, 0)


def halo_copies(body_ref, left_ref, right_ref, me, n, sems):
    t = body_ref.shape[0]
    right = {"seq": lax.rem(me + 1, n)}
    left = {"seq": lax.rem(me + n - 1, n)}
    return (
        remote(body_ref.at[pl.ds(t - RAD, RAD)], left_ref, sems.at[0], sems.at[1], right),
        remote(body_ref.at[pl.ds(0, RAD)], right_ref, sems.at[2], sems.at[3], left),
    )


def mask_halos(left_ref, right_ref, me, n):
    left_ref[...] = jnp.where(me > 0, left_ref[...], jnp.zeros_like(left_ref))
    right_ref[...] = jnp.where(me < n - 1, right_ref[...], jnp.zeros_like(right_ref))


class SeqSum:
    def __init__(self, me, n, x, out, slots, total, sems):
        self.me, self.n, self.x, self.out, self.slots, self.total, self.sems = me, n, x, out, slots, total, sems
        self.chunk = x.shape[0] // n
        self.here = pl.ds(pl.multiple_of(me * self.chunk, 8), self.chunk)

    def first(self, j, peer):
        src = self.x.at[pl.ds(pl.multiple_of(peer * self.chunk, 8), self.chunk)]
        return remote(src, self.slots.at[self.me], self.sems.at[0, j], self.sems.at[1, j], {"seq": peer})

    def second(self, j, peer):
        return remote(self.total, self.out.at[self.here], self.sems.at[2, j], self.sems.at[3, j], {"seq": peer})

    def start(self):
        each_peer(self.me, self.n, self.first, lambda c: c.start())
        self.slots[pl.ds(self.me, 1)] = self.x[self.here, :][None]

    def turn(self):
        each_peer(self.me, self.n, self.first, lambda c: c.wait())
        summed = lax.fori_loop(1, self.n, lambda i, acc: acc + self.slots[i], self.slots[0])
        self.total[...] = summed
        each_peer(self.me, self.n, self.second, lambda c: c.start())
        self.out[self.here, :] = summed

    def finish(self):
        each_peer(self.me, self.n, self.second, lambda c: c.wait())

    @staticmethod
    def scratch(r, n):
        return [pltpu.VMEM((n, r // n, 128), F32), pltpu.VMEM((r // n, 128), F32), DMA((4, n))]


CHIPS = 16
STACK, HALF, ROWS, LINES = range(4)


def at(i, size, unit):
    return pl.ds(pl.multiple_of(i * size, unit), size)


def piece(kind, ref, seq, rep):
    if kind == STACK:
        half = ref.shape[2] // 2
        return ref.at[:, at(seq, ref.shape[1] // CHIPS, 16), at(rep, half, 128)]
    if kind == HALF:
        half = ref.shape[1] // 2
        return ref.at[at(seq, ref.shape[0] // CHIPS, 16), at(rep, half, 128)]
    return ref.at[at(seq * 2 + rep, ref.shape[0] // (2 * CHIPS), 8 if kind == LINES else 16), :]


class Place:
    def __init__(self):
        self.seq = lax.axis_index("seq")
        self.rep = lax.axis_index("rep")
        self.x = lax.rem(self.seq, 2)
        self.y = lax.rem(lax.div(self.seq, 2), 2)
        self.z = lax.div(self.seq, 4)
        self.twin = {"rep": 1 - self.rep}
        self.across = ({"seq": self.chip(4, self.rep)}, {"seq": self.chip(8, self.rep)})

    def chip(self, i, rep):
        j, b, a = lax.rem(i, 4), lax.rem(lax.div(i, 4), 2), lax.div(i, 8)
        z = lax.rem(self.z + 4 - j, 4)
        fx = a + rep * (b - a)
        fy = b + rep * (a - b)
        x = self.x + fx * (1 - 2 * self.x)
        y = self.y + fy * (1 - 2 * self.y)
        return z * 4 + y * 2 + x

    def above(self, j):
        return {"seq": self.chip(4 - j, self.rep)}

    def below(self, j):
        return {"seq": self.chip(j, self.rep)}


class GatherMesh:
    def __init__(self, place, kinds, outs, own, sems):
        self.place, self.kinds, self.outs, self.own = place, kinds, outs, own
        self.zsend, self.send1, self.send2, self.ssend, self.recv, self.srecv = sems

    def block(self, i, k, rep):
        return piece(self.kinds[k], self.outs[k], self.place.chip(i, rep), rep)

    def copy(self, i, k, send, recv, where):
        b = self.block(i, k, self.place.rep)
        src = b if self.own[k] is None or not (isinstance(i, int) and i == 0) else self.own[k]
        return remote(src, b, send, recv, where)

    def to_z(self, j, k):
        return self.copy(0, k, self.zsend.at[j, k], self.recv.at[j, k], self.place.above(j))

    def to_first(self, i, k):
        return self.copy(i, k, self.send1.at[i, k], self.recv.at[i + 4, k], self.place.across[0])

    def to_second(self, i, k):
        return self.copy(i, k, self.send2.at[i, k], self.recv.at[i + 8, k], self.place.across[1])

    def share(self, i, k):
        return self.copy(i, k, self.ssend.at[i, k], self.srecv.at[i, k], self.place.twin)

    def arrival(self, i, k):
        b = self.block(i, k, self.place.rep)
        return remote(b, b, self.ssend.at[i, k], self.recv.at[i, k], self.place.twin)

    def shared(self, i, k):
        b = self.block(i, k, 1 - self.place.rep)
        return remote(b, b, self.ssend.at[i, k], self.srecv.at[i, k], self.place.twin)

    def start_z(self):
        for k in range(len(self.kinds)):
            for j in (1, 2, 3):
                self.to_z(j, k).start()

    def start_across(self, which=None):
        for k in range(len(self.kinds)) if which is None else which:
            self.to_second(0, k).start()
            self.to_first(0, k).start()
            self.share(0, k).start()

    def each(self, low, high, which, act):
        def body(i, _):
            for k in which:
                act(i, k)
            return 0

        lax.fori_loop(low, high, body, 0)

    def line(self, which):
        def act(i, k):
            self.arrival(i, k).wait_recv()
            self.to_first(i, k).start()
            self.share(i, k).start()

        self.each(1, 4, which, act)

    def line_on(self, which):
        self.each(1, 4, which, lambda i, k: self.to_second(i, k).start())

    def plane(self, which):
        def act(i, k):
            self.arrival(i, k).wait_recv()
            self.to_second(i, k).start()
            self.share(i, k).start()

        self.each(4, 8, which, act)

    def space(self, which):
        def act(i, k):
            self.arrival(i, k).wait_recv()
            self.share(i, k).start()

        self.each(8, CHIPS, which, act)

    def shares_in(self, which):
        self.shared_first(which)
        self.each(1, CHIPS, which, lambda i, k: self.shared(i, k).wait_recv())

    def shared_first(self, which):
        for k in which:
            self.shared(0, k).wait_recv()

    def finish(self):
        which = range(len(self.kinds))
        for k in which:
            for j in (1, 2, 3):
                self.to_z(j, k).wait_send()
            self.to_first(0, k).wait_send()
            self.to_second(0, k).wait_send()
            self.share(0, k).wait_send()

        def act(i, k):
            @pl.when(i < 4)
            def _():
                self.to_first(i, k).wait_send()

            @pl.when(i < 8)
            def _():
                self.to_second(i, k).wait_send()

            self.share(i, k).wait_send()

        self.each(1, CHIPS, which, act)

    @staticmethod
    def scratch(k):
        return [DMA((4, k)), DMA((4, k)), DMA((8, k))] + [DMA((CHIPS, k))] * 3


class ScatterMesh:
    def __init__(self, place, kinds, grads, mine, twins, in2, in1, inz, sems):
        self.place, self.kinds, self.grads = place, kinds, grads
        self.mine, self.twins, self.in2, self.in1, self.inz = mine, twins, in2, in1, inz
        self.lsem, self.tsend, self.trecv, self.s2, self.r2, self.s1, self.r1, self.sz, self.rz = sems

    def source(self, i, k):
        return piece(self.kinds[k], self.grads[k], self.place.chip(i, self.place.rep), self.place.rep)

    def cell(self, i, k):
        return self.source(i, k) if self.mine is None else self.mine[k].at[i]

    def load(self, i, k):
        return pltpu.make_async_copy(self.source(i, k), self.mine[k].at[i], self.lsem.at[i, k])

    def give(self, i, k):
        other = 1 - self.place.rep
        src = piece(self.kinds[k], self.grads[k], self.place.chip(i, other), other)
        return remote(src, self.twins[k].at[i], self.tsend.at[i, k], self.trecv.at[i, k], self.place.twin)

    def out2(self, i, k):
        return remote(self.cell(i, k), self.in2[k].at[i - 8], self.s2.at[i - 8, k], self.r2.at[i - 8, k], self.place.across[1])

    def out1(self, i, k):
        return remote(self.cell(i, k), self.in1[k].at[i - 4], self.s1.at[i - 4, k], self.r1.at[i - 4, k], self.place.across[0])

    def outz(self, j, k):
        return remote(self.cell(j, k), self.inz[k].at[j], self.sz.at[j, k], self.rz.at[j, k], self.place.below(j))

    def start(self, which=None):
        for low in (8, 0):
            for k in range(len(self.kinds)) if which is None else which:

                def body(j, _):
                    self.give(low + 7 - j, k).start()
                    if self.mine is not None:
                        self.load(low + 7 - j, k).start()
                    return 0

                lax.fori_loop(0, 8, body, 0)

    def terms(self, i, k):
        if self.mine is not None:
            self.load(i, k).wait()
        self.give(i, k).wait()
        return self.cell(i, k)[...].astype(F32) + self.twins[k].at[i][...].astype(F32)

    def keep(self, i, k, value):
        cell = self.cell(i, k)
        cell[...] = value.astype(cell.dtype)

    def far(self, k):
        def body(j, _):
            i = CHIPS - 1 - j
            self.keep(i, k, self.terms(i, k))
            self.out2(i, k).start()
            return 0

        lax.fori_loop(0, 8, body, 0)

    def mid(self, k):
        def body(j, _):
            i = 7 - j
            own = self.terms(i, k)
            self.out2(i + 8, k).wait_recv()
            self.keep(i, k, own + self.in2[k].at[i][...].astype(F32))
            self.out1(i, k).start()
            return 0

        lax.fori_loop(0, 4, body, 0)

    def closer(self, i, k):
        own = self.terms(i, k)
        self.out2(i + 8, k).wait_recv()
        self.out1(i + 4, k).wait_recv()
        return own + (self.in2[k].at[i][...].astype(F32) + self.in1[k].at[i][...].astype(F32))

    def near(self, k):
        def body(j, _):
            i = 3 - j
            self.keep(i, k, self.closer(i, k))
            self.outz(i, k).start()
            return 0

        lax.fori_loop(0, 3, body, 0)

    def total(self, k):
        acc = self.closer(0, k)
        for j in (1, 2, 3):
            self.outz(j, k).wait_recv()
            acc = acc + self.inz[k][j].astype(F32)
        return acc

    def finish(self):
        for k in range(len(self.kinds)):

            def body(i, _):
                @pl.when(i >= 8)
                def _():
                    self.out2(i, k).wait_send()

                @pl.when((i >= 4) & (i < 8))
                def _():
                    self.out1(i, k).wait_send()

                @pl.when(i < 4)
                def _():
                    self.outz(i, k).wait_send()

                return 0

            lax.fori_loop(1, CHIPS, body, 0)

    @staticmethod
    def scratch(blocks, in_place=False):
        k = len(blocks)
        return (
            ([] if in_place else [pltpu.VMEM((CHIPS, *s), t) for s, t in blocks])
            + [pltpu.VMEM((CHIPS, *s), t) for s, t in blocks]
            + [pltpu.VMEM((8, *s), t) for s, t in blocks]
            + [pltpu.VMEM((4, *s), t) for s, t in blocks]
            + [pltpu.VMEM((4, *s), t) for s, t in blocks]
            + [DMA((CHIPS, k))] * 3
            + [DMA((8, k))] * 2
            + [DMA((4, k))] * 4
        )

    @staticmethod
    def take(take, place, kinds, grads, in_place=False):
        k = len(kinds)
        mine = None if in_place else take(k)
        bufs = [take(k) for _ in range(4)]
        return ScatterMesh(place, kinds, grads, mine, *bufs, take(9))


def swap_rows(total, out, place, sems):
    rows_own = total.shape[-2] // 2
    half = total.shape[-1]
    theirs, mine = at(1 - place.rep, rows_own, 8), at(place.rep, rows_own, 8)
    cols = at(place.rep, half, 128)
    if len(total.shape) == 3:
        out[:, :, cols] = total[:, mine, :]
        return remote(total.at[:, theirs, :], out.at[:, :, cols], sems.at[0], sems.at[1], place.twin)
    out[:, cols] = total[mine, :]
    return remote(total.at[theirs, :], out.at[:, cols], sems.at[0], sems.at[1], place.twin)


CHUNK = 64
CTILE = 256


def fill_inner(ext, body_ref, start):
    count = ext.shape[1]
    rows_in = pl.ds(pl.multiple_of(start - RAD, RAD), count)
    for c in range(ext.shape[0]):
        ext[c] = body_ref[rows_in, c * 128 : (c + 1) * 128].astype(F32)


def fill_edge(ext, body_ref, left_ref, right_ref, first):
    tile = ext.shape[1] - 2 * RAD
    t = body_ref.shape[0]
    start = pl.multiple_of(jnp.where(first, 0, t - tile), tile)
    for c in range(ext.shape[0]):
        cols = slice(c * 128, (c + 1) * 128)
        ext[c, RAD : RAD + tile, :] = body_ref[pl.ds(start, tile), cols].astype(F32)
        ext[c, 0:RAD, :] = jnp.where(first, left_ref[:, cols], body_ref[t - tile - RAD : t - tile, cols]).astype(F32)
        ext[c, RAD + tile :, :] = jnp.where(first, body_ref[tile : tile + RAD, cols], right_ref[:, cols]).astype(F32)


def conv_forward(ext, tap_ref, out, row0):
    def step(r, _):
        base = pl.multiple_of(r * CHUNK, CHUNK)
        for c in range(ext.shape[0]):
            cols = slice(c * 128, (c + 1) * 128)
            acc = jnp.zeros((CHUNK, 128), F32)
            for b in range(8):
                reach = 4 if b == 0 else 3
                win = ext[c, pl.ds(base + b, CHUNK + 8 * reach), :]
                for m in range(reach + 1):
                    o = 8 * m + b
                    acc = acc + tap_ref[o : o + 1, cols] * win[8 * m : 8 * m + CHUNK]
            out[pl.ds(pl.multiple_of(row0 + base, CHUNK), CHUNK), cols] = acc.astype(out.dtype)
        return 0

    lax.fori_loop(0, CTILE // CHUNK, step, 0)


def conv_backward(vext, gext, tap_ref, out, tapacc, row0):
    width = out.shape[1] // 3

    def step(r, _):
        base = pl.multiple_of(r * CHUNK, CHUNK)
        for c in range(vext.shape[0]):
            cols = slice(c * 128, (c + 1) * 128)
            acc = jnp.zeros((CHUNK, 128), F32)
            here = gext[c, pl.ds(base + RAD, CHUNK), :]
            for b in range(8):
                reach = 4 if b == 0 else 3
                win = gext[c, pl.ds(base + b, CHUNK + 8 * reach), :]
                for m in range(reach + 1):
                    o = KC - 1 - (8 * m + b)
                    acc = acc + tap_ref[o : o + 1, cols] * win[8 * m : 8 * m + CHUNK]
                win = vext[c, pl.ds(base + b, CHUNK + 8 * reach), :]
                for m in range(reach + 1):
                    o = 8 * m + b
                    tapacc[o, :, cols] += rowsum8(here * win[8 * m : 8 * m + CHUNK])
            into = slice(2 * width + c * 128, 2 * width + (c + 1) * 128)
            out[pl.ds(pl.multiple_of(row0 + base, CHUNK), CHUNK), into] = acc.astype(out.dtype)
        return 0

    lax.fori_loop(0, CTILE // CHUNK, step, 0)


def wide_eye():
    lane = lax.broadcasted_iota(jnp.int32, (M, GROUP), 1) & 63
    return jnp.where(lane == lax.broadcasted_iota(jnp.int32, (M, GROUP), 0), 1.0, 0.0)


def head_sums(row):
    ones = jnp.where(head_mask(), 1.0, 0.0)
    return dot(jnp.broadcast_to(row, (8, GROUP)), ones, HI)[0:1]


def pinv_begin(mq_ref, mk_ref, a_ref, z_ref):
    for g in range(NG):
        s = dot_nt(mq_ref[:, gs(g)], spread(mk_ref[:, gs(g)]))
        e = jnp.exp(s - half_reduce(s, jnp.max, -jnp.inf))
        a = e / half_reduce(e, jnp.sum, 0.0)
        a_ref[:, gs(g)] = a
        col = jnp.sum(a, axis=0, keepdims=True)
        z_ref[0, :, gs(g)] = flip(a) / jnp.sqrt(head_sums(col * col))


def pinv_step(it, a_ref, z_ref, az_ref, t2_ref, t3_ref):
    eye = wide_eye()
    R = range(NG)
    z = [split(z_ref[it, :, gs(g)]) for g in R]
    az = [dot3(split(a_ref[:, gs(g)]), spread2(z[g])) for g in R]
    azs = [split(az[g]) for g in R]
    t2 = [15.0 * eye - dot3(azs[g], spread2(split(7.0 * eye - az[g]))) for g in R]
    t3 = [13.0 * eye - dot3(azs[g], spread2(split(t2[g]))) for g in R]
    for g in R:
        z_ref[it + 1, :, gs(g)] = 0.25 * dot3(z[g], spread2(split(t3[g])))
        az_ref[it, :, gs(g)] = az[g]
        t2_ref[it, :, gs(g)] = t2[g]
        t3_ref[it, :, gs(g)] = t3[g]


def pinv_back_step(it, a_ref, z_ref, az_ref, t2_ref, t3_ref, gz_ref, da_ref):
    eye = wide_eye()
    R = range(NG)
    az = [az_ref[it, :, gs(g)] for g in R]
    zs = [split(z_ref[it, :, gs(g)]) for g in R]
    gzs = [split(0.25 * gz_ref[:, gs(g)]) for g in R]
    baz = [spread2(split(az[g])) for g in R]
    d3 = [split(dot3(gzs[g], spread2(zs[g]))) for g in R]
    d2 = [split(-dot3(d3[g], baz[g])) for g in R]
    d1 = [-dot3(d2[g], baz[g]) for g in R]
    daz = [
        split(
            -dot3(split(t2_ref[it, :, gs(g)]), spread2(d3[g]))
            - dot3(split(7.0 * eye - az[g]), spread2(d2[g]))
            - d1[g]
        )
        for g in R
    ]
    for g in R:
        da_ref[:, gs(g)] += dot3(zs[g], spread2(daz[g]))
        gz_ref[:, gs(g)] = dot3(split(t3_ref[it, :, gs(g)]), spread2(gzs[g])) + dot3(
            daz[g], spread2(split(a_ref[:, gs(g)]))
        )


def pinv_back_end(g, a_ref, gz_ref, da_ref):
    a = a_ref[:, gs(g)]
    gz = gz_ref[:, gs(g)]
    col = jnp.sum(a, axis=0, keepdims=True)
    bound = jnp.sqrt(head_sums(col * col))
    tot = head_sums(jnp.sum(gz * a, axis=0, keepdims=True))
    full = flip(da_ref[:, gs(g)]) + gz / bound - (tot / (bound * bound * bound)) * col
    return a * (full - half_reduce(full * a, jnp.sum, 0.0))


def gather_marks(slots, outs, n):
    per = 4 * n // M
    half = slots.shape[2]
    for out, base in zip(outs, (0, 4)):
        if per == 1:
            got = [slots[i].astype(F32) for i in range(n)]
            for h in range(2):
                tall = jnp.concatenate([x[8 * h + base : 8 * h + base + 4] for x in got], axis=0)
                out[:, h * half : (h + 1) * half] = tall.astype(BF16)
        else:
            for h in range(2):
                lines = []
                for m in range(M):
                    total = jnp.zeros((1, half), F32)
                    for s in range(per // 4):
                        part = slots[m * (per // 4) + s].astype(F32)[8 * h + base : 8 * h + base + 4]
                        total = total + jnp.sum(part, axis=0, keepdims=True)
                    lines.append(total * (1.0 / per))
                out[:, h * half : (h + 1) * half] = jnp.concatenate(lines, axis=0).astype(BF16)


class Refs:
    def __init__(self, refs):
        self.it = iter(refs)

    def __call__(self, count):
        return [next(self.it) for _ in range(count)]

    def one(self):
        return next(self.it)


def front_kernel(*refs, n, ring):
    take = Refs(refs)
    x_any = take.one()
    if ring:
        wa, wu, wd, wv = take(4)
        wqkv_o, wo_o, ud0_o, ud_own = take(4)
    else:
        wq, vec = take(2)
    gains, taps = take(2)
    outs = take(7)
    mq, mk, uz, a_ref, z_ref, az_ref, t2_ref, t3_ref, vl, vr, p_ref = take(11)
    xs = take.one()
    stage = take(7)
    h_s, q_s, k_s, v_s, conv_s, f_s, e_s = stage
    means, pay, slots, ext, bdk, bdq, uacc, zacc, upart = take(9)
    xsem, osem, msem, hsem = take(4)
    sum_bufs = take(3)
    me = lax.axis_index("seq")
    t, d = xs.shape
    half = d // 2
    load_x = pltpu.make_async_copy(x_any, xs, xsem.at[0])
    load_x.start()
    drains = [pltpu.make_async_copy(s, o, osem.at[i]) for i, (s, o) in enumerate(zip(stage, outs))]
    if ring:
        wq, vec, sa, su, sd, so, co, wperm, psem, lsem = take(10)
        ring_one, ring_two = take(6), take(6)
        place = Place()
        greet(me, n, [place.twin])
        rep, seq = place.rep, place.seq
        rows_own = d // (2 * CHIPS)
        mine = at(rep, rows_own, 8)
        theirs = 1 - rep
        swaps = [
            remote(wa.at[0:3, :, at(theirs, half, 128)], sa.at[:, mine, :], psem.at[0], psem.at[1], place.twin),
            remote(wa.at[3, :, at(theirs, half, 128)], so.at[mine, :], psem.at[2], psem.at[3], place.twin),
            remote(wd.at[:, :, at(theirs, half, 128)], sd.at[pl.ds(2 * rep, 2)], psem.at[6], psem.at[7], place.twin),
        ]
        for c in swaps:
            c.start()
        sa[:, mine, :] = wa[0:3, :, at(rep, half, 128)]
        so[mine, :] = wa[3, :, at(rep, half, 128)]
        sd[pl.ds(2 * rep, 2)] = wd[:, :, at(rep, half, 128)]
        vec[at(seq * 2 + rep, rows_own, 8), :] = jnp.zeros((rows_own, 128), F32)
        vec[at(seq * 2 + rep, rows_own, 8), 0 : wv.shape[1]] = wv[...]
        swaps[0].wait()
        wq[:, at(seq, 2 * rows_own, 16), at(rep, half, 128)] = sa[...].astype(BF16)
        first = GatherMesh(place, (LINES, HALF, HALF, HALF), (vec, wq.at[2], wq.at[1], wq.at[0]), (None,) * 4, ring_one)
        first.start_z()
        first.start_across((0, 1))
        rows_chip = 2 * rows_own
        for p in range(PARTS):
            for c in range(0, CHIPS, 8):
                got = [
                    wu[:, (PARTS * (c + h) + p) * rows_chip : (PARTS * (c + h) + p + 1) * rows_chip] for h in range(8)
                ]
                wperm[p, :, c * rows_chip : (c + 8) * rows_chip] = jnp.concatenate(got, axis=1)
        swaps.append(
            remote(wperm.at[:, :, at(theirs, half, 128)], su.at[:, mine, :], psem.at[4], psem.at[5], place.twin)
        )
        swaps[-1].start()
        su[:, mine, :] = wperm[:, :, at(rep, half, 128)]
        for c in swaps[1:]:
            c.wait()
        co[...] = so[...].astype(BF16)
        ud_own[:, 0] = su[...].astype(BF16)
        ud_own[:, 1] = sd[...].astype(BF16)
        rest = GatherMesh(place, (STACK, HALF), (ud0_o, wo_o), (ud_own.at[0], co), ring_two)
        local = [
            pltpu.make_async_copy(src, piece(kind, out, seq, rep), lsem.at[i])
            for i, (src, kind, out) in enumerate(zip(rest.own, rest.kinds, rest.outs))
        ]

        rest.start_z()
        for c in local:
            c.start()
        first.line((0, 1))
        first.line_on((0, 1))
        first.start_across((2, 3))
        first.plane((0, 1))
        for which in ((2,), (3,)):
            first.line(which)
            first.line_on(which)
        first.space((0,))
        first.shares_in((0,))
        save_w = pltpu.make_async_copy(wq, wqkv_o, xsem.at[1])
    else:
        greet(me, n, [])

    turned = jnp.transpose(vec[...]).astype(BF16).astype(F32)
    gains[...] = turned[0:8]
    taps[...] = turned[2:42]
    load_x.wait()

    def tile(i):
        return pl.ds(pl.multiple_of(i * (t // 4), t // 4), t // 4)

    def norm(i, _):
        normal, _inv = normalize(xs[tile(i), :].astype(F32))
        h_s[tile(i), :] = (normal * gains[0:1, :]).astype(BF16)
        return 0

    def project_v(i, _):
        v_s[tile(i), :] = dot(h_s[tile(i), :], wq[2]).astype(BF16)
        return 0

    def project_k(i, _):
        k = (dot(h_s[tile(i), :], wq[1]) * QK_SCALE).astype(BF16)
        k_s[tile(i), :] = k
        means[pl.ds(i + 4, 1), :] = jnp.mean(k.astype(F32), axis=0, keepdims=True)
        return 0

    def project_q(i, _):
        q = (dot(h_s[tile(i), :], wq[0]) * QK_SCALE).astype(BF16)
        q_s[tile(i), :] = q
        means[pl.ds(i, 1), :] = jnp.mean(q.astype(F32), axis=0, keepdims=True)
        return 0

    def inner(i, _):
        fill_inner(ext, v_s, i * CTILE)
        conv_forward(ext, taps, conv_s, i * CTILE)
        if ring:

            @pl.when(i == 4)
            def _():
                rest.line_on((0,))

            @pl.when(i == 5)
            def _():
                rest.line((1,))
                rest.line_on((1,))

        return 0

    tiles = t // CTILE
    lax.fori_loop(0, 4, norm, 0)
    if ring:
        first.plane((2,))
        first.space((1,))
        first.shares_in((1,))
    lax.fori_loop(0, 4, project_v, 0)
    halos = halo_copies(v_s, vl, vr, me, n, hsem)
    for c in halos:
        c.start()
    if ring:
        first.plane((3,))
        rest.start_across()
    lax.fori_loop(1, tiles // 2, inner, 0)
    if ring:
        first.space((2,))
        first.shares_in((2,))
    lax.fori_loop(0, 4, project_k, 0)
    if ring:
        first.space((3,))
        first.shares_in((3,))
        save_w.start()
        rest.line((0,))
    lax.fori_loop(0, 4, project_q, 0)

    pay[...] = jnp.concatenate([means[:, :half], means[:, half:]], axis=0).astype(BF16)

    def mark(j, peer):
        return remote(pay, slots.at[me], msem.at[0, j], msem.at[1, j], {"seq": peer})

    each_peer(me, n, mark, lambda c: c.start())
    slots[pl.ds(me, 1)] = pay[...][None]
    for c in drains[:4]:
        c.start()

    lax.fori_loop(tiles // 2, tiles - 1, inner, 0)
    for c in halos:
        c.wait()
    mask_halos(vl, vr, me, n)

    def edge(i, _):
        fill_edge(ext, v_s, vl, vr, i == 0)
        conv_forward(ext, taps, conv_s, i * (t - CTILE))
        return 0

    lax.fori_loop(0, 2, edge, 0)
    drains[4].start()
    each_peer(me, n, mark, lambda c: c.wait())
    gather_marks(slots, (mq, mk), n)
    for g in range(NG):
        bdk[g] = spread(mk[:, gs(g)])
        bdq[g] = spread(mq[:, gs(g)])
    uacc[...] = jnp.zeros_like(uacc)
    zacc[...] = jnp.zeros_like(zacc)
    ones_bd = jnp.where(head_mask(), 1.0, 0.0).astype(BF16)

    def attend(i, _):
        here = pl.ds(pl.multiple_of(i * (t // 4), t // 4), t // 4)
        for g in range(NG):
            s = dot_nt(q_s[here, gs(g)], bdk[g])
            ex = jnp.exp(s - half_reduce(s, jnp.max, -jnp.inf))
            den = dot(ex.astype(BF16), ones_bd)
            f_s[here, gs(g)] = (ex / den).astype(BF16)
            e = jnp.exp(dot_nt(k_s[here, gs(g)], bdq[g])).astype(BF16)
            e_s[here, gs(g)] = e
            uacc[g] += dot_tn(e, v_s[here, gs(g)])
            zacc[g] += dot_tn(e, jnp.ones((t // 4, 128), BF16))
        if ring:

            @pl.when(i == 0)
            def _():
                rest.plane((0,))

            @pl.when(i == 1)
            def _():
                rest.plane((1,))

        return 0

    lax.fori_loop(0, 4, attend, 0)
    for c in drains[5:]:
        c.start()
    lane = lax.broadcasted_iota(jnp.int32, (M, 128), 1)
    zt = jnp.zeros((M, 128), F32)
    for g in range(NG):
        put_tall(upart, g, collect(uacc[g]))
        for h in range(4):
            zt = zt + jnp.where(lane == 4 * g + h, zacc[g, h * 64 : h * 64 + 64, :], 0.0)
    upart[6 * M : 7 * M, :] = zt
    upart[7 * M :, :] = jnp.zeros((upart.shape[0] - 7 * M, 128), F32)
    summing = SeqSum(me, n, upart, uz, *sum_bufs)
    summing.start()
    pinv_begin(mq, mk, a_ref, z_ref)

    def newton(it, _):
        pinv_step(it, a_ref, z_ref, az_ref, t2_ref, t3_ref)
        return 0

    lax.fori_loop(0, NSITER // 2, newton, 0)
    summing.turn()
    lax.fori_loop(NSITER // 2, NSITER, newton, 0)
    summing.finish()
    p_ref[...] = z_ref[NSITER]
    for c in drains:
        c.wait()
    if ring:
        for c in local:
            c.wait()
        save_w.wait()
        rest.space((0, 1))
        rest.shares_in((0, 1))
        first.finish()
        rest.finish()


def front(x, weights, n, ring):
    t, d = x.shape
    if ring:
        rown = d // CHIPS
        own4 = (4, rown, d // 2)
        extra_out = [sds((3, d, d), BF16), sds((d, d), BF16), sds((2, d, d), BF16), sds((4, 2, rown, d // 2), BF16)]
        extra = [
            pltpu.VMEM((3, d, d), BF16),
            pltpu.VMEM((d, 128), F32),
            pltpu.VMEM((3, rown, d // 2), F32),
            pltpu.VMEM(own4, F32),
            pltpu.VMEM(own4, F32),
            pltpu.VMEM((rown, d // 2), F32),
            pltpu.VMEM((rown, d // 2), BF16),
            pltpu.VMEM((PARTS, rown // 2, d), F32),
            DMA((8,)),
            DMA((2,)),
        ] + GatherMesh.scratch(4) + GatherMesh.scratch(2)
    else:
        extra_out, extra = [], []
    r = padded_rows(7 * M, n)
    big = sds((t, d), BF16)
    steps = sds((NSITER, M, d), F32)
    res = pl.pallas_call(
        functools.partial(front_kernel, n=n, ring=ring),
        in_specs=[ANYW] + [VM] * len(weights),
        out_specs=([ANYW] * 3 + [VM] if ring else []) + [VM] * 2 + [ANYW] * 7 + [VM] * 11,
        out_shape=extra_out
        + [sds((8, d), F32), sds((40, d), F32)]
        + [big] * 7
        + [sds((M, d), BF16)] * 2
        + [sds((r, 128), F32), sds((M, d), F32), sds((NSITER + 1, M, d), F32), steps, steps, steps]
        + [sds((RAD, d), BF16)] * 2
        + [sds((M, d), F32)],
        scratch_shapes=[pltpu.VMEM((t, d), BF16)] * 8
        + [
            pltpu.VMEM((8, d), F32),
            pltpu.VMEM((16, d // 2), BF16),
            pltpu.VMEM((n, 16, d // 2), BF16),
            pltpu.VMEM((d // 128, CTILE + 2 * RAD, 128), F32),
            pltpu.VMEM((NG, GROUP, GROUP), BF16),
            pltpu.VMEM((NG, GROUP, GROUP), BF16),
            pltpu.VMEM((NG, GROUP, GROUP), F32),
            pltpu.VMEM((NG, GROUP, 128), F32),
            pltpu.VMEM((r, 128), F32),
            DMA((2,)),
            DMA((7,)),
            DMA((2, n)),
            DMA((4,)),
        ]
        + SeqSum.scratch(r, n)
        + extra,
        compiler_params=pltpu.CompilerParams(collective_id=1, has_side_effects=True, vmem_limit_bytes=VMEM_LIMIT),
        name="front",
    )(x, *weights)
    return res if ring else [None] * 4 + list(res)


PARTS = 4
HALF_D = 384
PART = 768


def middle_kernel(*refs, n, ring):
    take = Refs(refs)
    x_a, dy_a, f_a, q_a, conv_a, wo_a, ud_a = take(7)
    if ring:
        ud_own = take.one()
    gains, mk, uz, p_ref = take(4)
    out_o, dx_o, dmix_o, dqf_o, g_o = take(5)
    gw_ref, dkt_ref, dg_ref = take(3)
    if ring:
        t_ud = take.one()
    x_s, dy_s, f_s, mix_s, h2_s, da_s, x1_s, wo_s, ud = take(9)
    oacc, hacc, wbd, bdk, gwacc, dktacc, dgacc = take(7)
    isem, osem = take(2)
    t, d = x_s.shape
    tile = t // 4
    act_s, q_s = x_s, x_s
    seq = lax.axis_index("seq")
    parts_in = 1 if ring else PARTS
    gain = gains[1:2, :]

    def here(i):
        return pl.ds(pl.multiple_of(i * tile, tile), tile)

    load_q = pltpu.make_async_copy(q_a, q_s, isem.at[7])
    loads = [
        pltpu.make_async_copy(a, b, isem.at[i])
        for i, (a, b) in enumerate(
            ((f_a, f_s), (conv_a, mix_s), (x_a, x_s), (wo_a, wo_s), (ud_a, ud.at[pl.ds(0, parts_in)]), (dy_a, dy_s))
        )
    ]
    for c in loads:
        c.start()
    if ring:
        place = Place()
        gathers = [None] + [
            GatherMesh(place, (STACK,), (ud.at[p],), (ud_own.at[p],), take(6)) for p in range(1, PARTS)
        ]
        scatters = [
            ScatterMesh.take(take, place, (STACK,), (ud.at[p],), in_place=True) for p in range(PARTS - 1)
        ]
        greet(seq, n, [place.twin])
        for g in gathers[1:]:
            g.start_z()
        for p in range(1, PARTS):
            gathers[p].start_across()
            ud[p, :, at(seq, d // CHIPS, 16), at(place.rep, d // 2, 128)] = ud_own[p]

    def tick(cond, *acts):
        if ring and acts:

            @pl.when(cond)
            def _():
                for act in acts:
                    act()

    K = (0,)

    def move(p, *names):
        return [functools.partial(getattr(gathers[p], name), K) for name in names] if ring else []

    def send(p, *names):
        return [functools.partial(getattr(scatters[p], name), 0) for name in names] if ring else []

    gwacc[...] = jnp.zeros_like(gwacc)
    dktacc[...] = jnp.zeros_like(dktacc)
    dgacc[...] = jnp.zeros_like(dgacc)
    for g in range(NG):
        bv = u_group(uz, g) / zt_group(uz, g)
        wbd[g] = spread(dot(p_ref[:, gs(g)], spread(bv), HI)).astype(BF16)
        bdk[g] = spread(mk[:, gs(g)])
    for c in loads[:4]:
        c.wait()

    def before(i, _):
        r = here(i)
        for g in range(NG):
            mix_s[r, gs(g)] = (dot(f_s[r, gs(g)], wbd[g]) + mix_s[r, gs(g)].astype(F32)).astype(BF16)
        x1 = x_s[r, :].astype(F32) + dot(mix_s[r, :], wo_s[...])
        oacc[r, :] = x1
        x1_s[r, :] = x1.astype(BF16)
        normal, _inv = normalize(x1)
        h2_s[r, :] = (normal * gain).astype(BF16)
        tick(i == 1, *move(1, "line", "line_on"))
        tick(i == 3, *move(1, "plane"))
        return 0

    lax.fori_loop(0, 4, before, 0)
    loads[4].wait()
    loads[5].wait()
    plan = {
        (0, 0): move(2, "line", "line_on"),
        (0, 2): move(1, "space") + move(2, "plane"),
        (0, 3): move(3, "line", "line_on"),
        (1, 0): move(3, "plane") + send(0, "far"),
        (1, 1): move(2, "space"),
        (1, 2): send(0, "mid"),
        (1, 3): move(3, "space"),
        (2, 0): send(0, "near") + send(1, "far"),
        (2, 2): send(1, "mid"),
        (3, 0): send(1, "near") + send(2, "far"),
        (3, 2): send(2, "mid"),
    }
    for p in range(PARTS):
        if ring and p > 0:
            gathers[p].shares_in(K)
        u, dn = ud.at[p, 0], ud.at[p, 1]

        def through(i, _):
            r = here(i)
            h2 = h2_s[r, :]
            dy = dy_s[r, :]
            o = h = None
            for c in range(0, d, PART):
                cols = slice(c, c + PART)
                act, slope = gelu_parts(dot(h2, u[:, cols]))
                act = act.astype(BF16)
                act_s[r, cols] = act
                da = (dot_nt(dy, dn[cols, :]) * slope).astype(BF16)
                da_s[r, cols] = da
                oc, hc = dot(act, dn[cols, :]), dot_nt(da, u[:, cols])
                o, h = (oc, hc) if o is None else (o + oc, h + hc)
            oacc[r, :] += o
            hacc[r, :] = h if p == 0 else hacc[r, :] + h
            for j in range(4):
                tick(i == j, *plan.get((p, j), []))
            return 0

        lax.fori_loop(0, 4, through, 0)
        if ring and p > 0:
            gathers[p].finish()

        def grads(j, _):
            cols = pl.ds(pl.multiple_of(j * HALF_D, HALF_D), HALF_D)
            ud[p, 0, cols, :] = dot_tn(h2_s[:, cols], da_s[...]).astype(BF16)
            ud[p, 1, cols, :] = dot_tn(act_s[:, cols], dy_s[...]).astype(BF16)
            return 0

        lax.fori_loop(0, d // HALF_D, grads, 0)
        if ring and p < PARTS - 1:
            scatters[p].start()
        if ring and p == 2:
            t_ud[0] = scatters[0].total(0)
    load_q.start()
    first_out = PARTS - 1 if ring else 0
    stored = [
        pltpu.make_async_copy(ud.at[p], g_o.at[pl.ds(2 * (p - first_out), 2)], osem.at[16 + p])
        for p in range(first_out, PARTS)
    ]
    for c in stored:
        c.start()
    tick(True, *send(2, "near"))
    if ring:
        t_ud[1] = scatters[1].total(0)
    load_q.wait()

    def after(i, _):
        r = here(i)
        normal, inv = normalize(x1_s[r, :].astype(F32))
        x1_s[r, :] = oacc[r, :].astype(BF16)
        pltpu.make_async_copy(x1_s.at[r], out_o.at[r], osem.at[i]).start()
        dh2 = hacc[r, :]
        dgacc[...] += rowsum8(dh2 * normal)
        dx = (norm_back(dh2, normal, inv, gain) + dy_s[r, :].astype(F32)).astype(BF16)
        dy_s[r, :] = dx
        pltpu.make_async_copy(dy_s.at[r], dx_o.at[r], osem.at[4 + i]).start()
        dmix = dot_nt(dx, wo_s[...]).astype(BF16)
        h2_s[r, :] = dmix
        pltpu.make_async_copy(h2_s.at[r], dmix_o.at[r], osem.at[8 + i]).start()
        ones_bd = jnp.where(head_mask(), 1.0, 0.0).astype(BF16)
        for g in range(NG):
            dm = dmix[:, gs(g)]
            f = f_s[r, gs(g)]
            df = dot_nt(dm, wbd[g])
            gwacc[g] += dot_tn(f, dm)
            ff32 = f.astype(F32)
            prod = df * ff32
            hi, lo = split(prod)
            ds = (ff32 * (df - (dot(hi, ones_bd) + dot(lo, ones_bd)))).astype(BF16)
            da_s[r, gs(g)] = dot(ds, bdk[g]).astype(BF16)
            dktacc[g] += dot_tn(ds, q_s[r, gs(g)])
        pltpu.make_async_copy(da_s.at[r], dqf_o.at[r], osem.at[12 + i]).start()
        return 0

    lax.fori_loop(0, 4, after, 0)

    def grad_o(j, _):
        cols = pl.ds(pl.multiple_of(j * HALF_D, HALF_D), HALF_D)
        wo_s[cols, :] = dot_tn(mix_s[:, cols], dy_s[...]).astype(BF16)
        return 0

    lax.fori_loop(0, d // HALF_D, grad_o, 0)
    stored.append(pltpu.make_async_copy(wo_s, g_o.at[2 * (PARTS - first_out)], osem.at[20]))
    stored[-1].start()
    for g in range(NG):
        put_tall(gw_ref, g, collect(gwacc[g]))
        dkt_ref[:, gs(g)] = collect(dktacc[g])
    if gw_ref.shape[0] > 6 * M:
        gw_ref[6 * M :] = jnp.zeros((gw_ref.shape[0] - 6 * M, 128), F32)
    dg_ref[...] = jnp.broadcast_to(jnp.sum(dgacc[...], axis=0, keepdims=True), dg_ref.shape)
    if ring:
        t_ud[2] = scatters[2].total(0)
        for sc in scatters:
            sc.finish()
    for i in range(4):
        for b, src, dst in ((0, x1_s, out_o), (4, dy_s, dx_o), (8, h2_s, dmix_o), (12, da_s, dqf_o)):
            pltpu.make_async_copy(src.at[here(i)], dst.at[here(i)], osem.at[b + i]).wait()
    for c in stored:
        c.wait()


def middle(x, dy, f, q, conv, wo, ud, ud_own, gains, mk, uz, p, gw_rows, n):
    ring = ud_own is not None
    t, d = x.shape
    big = sds((t, d), BF16)
    outs = [big] * 4 + [sds((3 if ring else 2 * PARTS + 1, d, d), BF16)]
    outs += [sds((gw_rows, 128), F32), sds((M, d), F32), sds((8, d), F32)]
    extra = []
    if ring:
        cell = (2, d // CHIPS, d // 2)
        outs += [sds((PARTS - 1, *cell), F32)]
        extra = GatherMesh.scratch(1) * (PARTS - 1) + ScatterMesh.scratch([(cell, BF16)], True) * (PARTS - 1)
    square = pltpu.VMEM((NG, GROUP, GROUP), BF16)
    square_f = pltpu.VMEM((NG, GROUP, GROUP), F32)
    return pl.pallas_call(
        functools.partial(middle_kernel, n=n, ring=ring),
        in_specs=[ANYW] * 7 + [VM] * (5 if ring else 4),
        out_specs=[ANYW] * 5 + [VM] * (len(outs) - 5),
        out_shape=outs,
        scratch_shapes=[pltpu.VMEM((t, d), BF16)] * 7
        + [
            pltpu.VMEM((d, d), BF16),
            pltpu.VMEM((PARTS, 2, d, d), BF16),
            pltpu.VMEM((t, d), F32),
            pltpu.VMEM((t, d), F32),
            square,
            square,
            square_f,
            square_f,
            pltpu.VMEM((8, d), F32),
            DMA((8,)),
            DMA((21,)),
        ]
        + extra,
        compiler_params=pltpu.CompilerParams(
            collective_id=4 if ring else None, has_side_effects=True, vmem_limit_bytes=61 * 1024 * 1024
        ),
        name="middle",
    )(x, dy, f, q, conv, wo, ud, *((ud_own,) if ring else ()), gains, mk, uz, p)


def rear_kernel(*refs, n, ring, seg_len):
    take = Refs(refs)
    bodies = take(5)
    x_a, dx_a, h1_a, w_a = take(4)
    if ring:
        grads = take(1)
    gw_part, uz, a_ref, z_ref, az_ref, t2_ref, t3_ref, mq, mk, vl, vr, taps, dkt_ref, dg2_ref, gains = take(15)
    if ring:
        t_ud = take.one()
    ig_o, gvec_o, gqkv_o, dg_o = take(4)
    if ring:
        r_uo, r_down, r_vec, r_qkv = take(4)
    v_s, g_s, e_s, k_s, dqf_s, dqkv, gvec = take(7)
    vext, gext, tapacc, gl, gr, gw, gz, da, dubd, rowadd, dqtacc, bdq, pay, slots, own = take(15)
    w_s, gqkv, part, dslots, dgacc, gsem = take(6)
    isem, osem, hsem, wsem = take(4)
    sum_bufs = take(3)
    me = lax.axis_index("seq")
    t, d = v_s.shape
    loads = [
        pltpu.make_async_copy(b, s, isem.at[i]) for i, (b, s) in enumerate(zip(bodies, (v_s, g_s, e_s, k_s, dqf_s)))
    ]
    for c in loads:
        c.start()
    load_x = pltpu.make_async_copy(x_a, v_s, isem.at[5])
    load_dx = pltpu.make_async_copy(dx_a, g_s, isem.at[6])
    load_h1 = pltpu.make_async_copy(h1_a, e_s, isem.at[7])
    load_w = pltpu.make_async_copy(w_a, w_s, isem.at[8])
    load_w.start()
    if ring:
        place = Place()
        greet(me, n, [place.twin])
        big = ScatterMesh.take(take, place, (STACK,), grads)
        vec = ScatterMesh.take(take, place, (LINES,), (gvec,))
        late = ScatterMesh.take(take, place, (HALF,) * 3, [gqkv.at[i] for i in range(3)], in_place=True)
        fuo, fd, fq, fsem = take(4)
    else:
        greet(me, n, [])
    summing = SeqSum(me, n, gw_part, gw, *sum_bufs)
    loads[1].wait()
    halos = halo_copies(g_s, gl, gr, me, n, hsem)
    for c in halos:
        c.start()
    summing.start()
    if ring:
        big.start()

    def tick(cond, *acts):
        if ring:

            @pl.when(cond)
            def _():
                for act, k in acts:
                    act(k)

    tapacc[...] = jnp.zeros_like(tapacc)
    loads[0].wait()
    if not ring:
        big = vec = None
    far = (lambda k: big.far(k))
    mid = (lambda k: big.mid(k))
    near = (lambda k: big.near(k))

    def inner(i, _):
        fill_inner(vext, v_s, i * CTILE)
        fill_inner(gext, g_s, i * CTILE)
        conv_backward(vext, gext, taps, dqkv, tapacc, i * CTILE)


        @pl.when(i == 2)
        def _():
            summing.turn()

        tick(i == 2, (far, 0))
        tick(i == 6, (mid, 0))
        return 0

    lax.fori_loop(1, t // CTILE - 1, inner, 0)
    for c in halos:
        c.wait()
    mask_halos(gl, gr, me, n)

    def edge(i, _):
        fill_edge(vext, v_s, vl, vr, i == 0)
        fill_edge(gext, g_s, gl, gr, i == 0)
        conv_backward(vext, gext, taps, dqkv, tapacc, i * (t - CTILE))
        return 0

    lax.fori_loop(0, 2, edge, 0)
    load_dx.start()
    dtap = jnp.sum(tapacc[...], axis=1)
    lines = jnp.concatenate([jnp.zeros((1, d), F32), dg2_ref[0:1, :], dtap, jnp.zeros((128 - 42, d), F32)], axis=0)
    gvec[...] = jnp.transpose(lines)
    if ring:
        vec.start()
    else:
        save_vec = pltpu.make_async_copy(gvec, gvec_o, osem.at[1])
        save_vec.start()
    tick(True, (near, 0))
    summing.finish()
    for g in range(NG):
        z = zt_group(uz, g)
        bv = u_group(uz, g) / z
        gwg = u_group(gw, g)
        gz[:, gs(g)] = flip(dot_nt(gwg, spread(bv), HI))
        dbv = dot(flip(z_ref[NSITER, :, gs(g)]), spread(gwg), HI)
        dubd[g] = spread(dbv / z).astype(BF16)
        rowadd[g] = dot_nt(jnp.ones((8, GROUP), F32), spread(dbv * bv / z), HI)
        bdq[g] = spread(mq[:, gs(g)])
    da[...] = jnp.zeros_like(da)

    def newton(j, _):
        pinv_back_step(NSITER - 1 - j, a_ref, z_ref, az_ref, t2_ref, t3_ref, gz, da)
        tick(j == 1, (lambda k: vec.far(k), 0))
        tick(j == 3, (lambda k: vec.mid(k), 0))
        tick(j == 5, (lambda k: vec.near(k), 0))
        return 0

    lax.fori_loop(0, NSITER, newton, 0)
    loads[2].wait()
    loads[3].wait()
    dqtacc[...] = jnp.zeros_like(dqtacc)

    def cols(part, g):
        return slice(part * d + g * GROUP, part * d + (g + 1) * GROUP)

    def through(i, _):
        here = pl.ds(pl.multiple_of(i * (t // 4), t // 4), t // 4)
        for g in range(NG):
            e = e_s[here, gs(g)]
            de = dot_nt(v_s[here, gs(g)], dubd[g]) - rowadd[g, 0:1, :]
            ds = (e.astype(F32) * de).astype(BF16)
            dqkv[here, cols(2, g)] = (dot(e, dubd[g]) + dqkv[here, cols(2, g)].astype(F32)).astype(BF16)
            dqkv[here, cols(1, g)] = dot(ds, bdq[g]).astype(BF16)
            dqtacc[g] += dot_tn(ds, k_s[here, gs(g)])
        return 0

    lax.fori_loop(0, 4, through, 0)
    load_x.start()
    load_h1.start()

    rows_dev = max(M // n, 1)
    per_mark = n * rows_dev // M
    if rows_dev < 4:
        pay[...] = jnp.zeros_like(pay)
    for g in range(NG):
        ds = pinv_back_end(g, a_ref, gz, da)
        dq = collect(dqtacc[g]) + dot(ds, spread(mk[:, gs(g)].astype(F32)), HI) * (1.0 / n)
        dk = dkt_ref[:, gs(g)] + dot(flip(ds), spread(mq[:, gs(g)].astype(F32)), HI) * (1.0 / n)
        for i in range(n):
            row = i * rows_dev // per_mark
            pay[i, 0:rows_dev, gs(g)] = dq[row : row + rows_dev]
            pay[i, 4 : 4 + rows_dev, gs(g)] = dk[row : row + rows_dev]

    def mark(j, peer):
        return remote(pay.at[peer], slots.at[me], wsem.at[0, j], wsem.at[1, j], {"seq": peer})

    each_peer(me, n, mark, lambda c: c.start())
    slots[pl.ds(me, 1)] = pay[pl.ds(me, 1)]

    def project_back(p, scale):
        def body(j, _):
            cols = pl.ds(pl.multiple_of(j * HALF_D, HALF_D), HALF_D)
            gqkv[p, cols, :] = (dot_tn(e_s[:, cols], dqkv[:, p * d : (p + 1) * d]) * scale).astype(BF16)
            return 0

        lax.fori_loop(0, d // HALF_D, body, 0)
        if ring:
            late.start((p,))

    load_h1.wait()
    project_back(2, 1.0)
    if ring:
        last_ud = big.total(0)
        for p in range(PARTS - 1):
            fuo[p] = t_ud[p, 0]
            fd[p] = t_ud[p, 1]
        fuo[PARTS - 1] = last_ud[0]
        fd[PARTS - 1] = last_ud[1]
        fuo[PARTS] = last_ud[2]
        cols = at(place.rep, d // 2, 128)
        back = [swap_rows(fuo, r_uo, place, fsem.at[0])]
        for j in range(2):
            r_down[j, :, cols] = fd[2 * place.rep + j]
            src = fd.at[2 * (1 - place.rep) + j]
            back.append(remote(src, r_down.at[j, :, cols], fsem.at[1 + j, 0], fsem.at[1 + j, 1], place.twin))
        for c in back:
            c.start()
        r_vec[...] = vec.total(0)
        late.far(2)
    loads[4].wait()
    each_peer(me, n, mark, lambda c: c.wait())
    own[...] = lax.fori_loop(1, n, lambda i, acc: acc + slots[i], slots[0]) * (1.0 / seg_len)

    def landed(i, _):
        here = pl.ds(pl.multiple_of(i * (t // 4), t // 4), t // 4)
        row = lax.div(i * rows_dev, 4)
        dqkv[here, 0:d] = (dqf_s[here, :].astype(F32) + own[pl.ds(row, 1), :]).astype(BF16)
        dqkv[here, d : 2 * d] = (dqkv[here, d : 2 * d].astype(F32) + own[pl.ds(row + 4, 1), :]).astype(BF16)
        return 0

    lax.fori_loop(0, 4, landed, 0)
    project_back(1, QK_SCALE)
    project_back(0, QK_SCALE)
    tick(True, (lambda k: late.far(k), 1), (lambda k: late.far(k), 0), (lambda k: late.mid(k), 2))
    for c in (load_w, load_x, load_dx):
        c.wait()
    dgacc[...] = jnp.zeros_like(dgacc)

    def back_through(i, _):
        here = pl.ds(pl.multiple_of(i * (t // 4), t // 4), t // 4)
        dq, dk, dv = (dqkv[here, p * d : (p + 1) * d] for p in range(3))
        dh = (dot_nt(dq, w_s[0]) + dot_nt(dk, w_s[1])) * QK_SCALE + dot_nt(dv, w_s[2])
        normal, inv = normalize(v_s[here, :].astype(F32))
        dgacc[...] += rowsum8(dh * normal)
        ig = norm_back(dh, normal, inv, gains[0:1, :]) + g_s[here, :].astype(F32)
        v_s[here, :] = ig.astype(BF16)
        pltpu.make_async_copy(v_s.at[here], ig_o.at[here], osem.at[2 + i]).start()
        tick(i == 1, (lambda k: late.near(k), 2), (lambda k: late.mid(k), 1))
        tick(i == 2, (lambda k: late.mid(k), 0))
        return 0

    lax.fori_loop(0, 4, back_through, 0)
    row = jnp.sum(dgacc[...], axis=0, keepdims=True)
    part[...] = jnp.concatenate(
        [row[:, c : c + 128] for c in range(0, d, 128)] + [jnp.zeros((8 - d // 128, 128), F32)], axis=0
    )

    def send(j, peer):
        return remote(part, dslots.at[me], gsem.at[0, j], gsem.at[1, j], {"seq": peer})

    each_peer(me, n, send, lambda c: c.start())
    dslots[pl.ds(me, 1)] = part[...][None]
    tick(True, (lambda k: late.near(k), 1), (lambda k: late.near(k), 0))
    each_peer(me, n, send, lambda c: c.wait())
    total = lax.fori_loop(1, n, lambda i, acc: acc + dslots[i], dslots[0])
    dg_o[0] = total
    if ring:
        twin_sum = remote(dg_o.at[0], dg_o.at[1], gsem.at[0, 0], gsem.at[1, 0], place.twin)
        twin_sum.start()
        for p in (2, 1, 0):
            fq[p] = late.total(p)
        back.append(swap_rows(fq, r_qkv, place, fsem.at[3]))
        back[-1].start()
        twin_sum.wait()
        big.finish()
        vec.finish()
        late.finish()
        for c in back:
            c.wait()
    else:
        dg_o[1] = jnp.zeros_like(total)
        save_vec.wait()
        save_g = pltpu.make_async_copy(gqkv, gqkv_o, osem.at[0])
        save_g.start()
        save_g.wait()
    for i in range(4):
        here = pl.ds(i * (t // 4), t // 4)
        pltpu.make_async_copy(v_s.at[here], ig_o.at[here], osem.at[2 + i]).wait()


def rear(bodies, more, grads, gw, uz, a, z, az, t2, t3, mq, mk, vl, vr, taps, dkt, dg2, gains, t_ud, n, seg_len):
    ring = grads is not None
    t, d = bodies[0].shape
    r = gw.shape[0]
    outs = [sds((t, d), BF16), sds((d, 128), F32), sds((3, d, d), BF16), sds((2, 8, 128), F32)]
    extra = []
    if ring:
        own = d // (2 * CHIPS)
        outs += [sds((PARTS + 1, own, d), F32), sds((2, 2 * own, d), F32), sds((own, 128), F32), sds((3, own, d), F32)]
        extra = ScatterMesh.scratch([((3, 2 * own, d // 2), BF16)]) + ScatterMesh.scratch([((own, 128), F32)])
        extra += ScatterMesh.scratch([((2 * own, d // 2), BF16)] * 3, True) + [
            pltpu.VMEM((PARTS + 1, 2 * own, d // 2), F32),
            pltpu.VMEM((PARTS, 2 * own, d // 2), F32),
            pltpu.VMEM((3, 2 * own, d // 2), F32),
            DMA((4, 2)),
        ]
    ext = pltpu.VMEM((d // 128, CTILE + 2 * RAD, 128), F32)
    halo = pltpu.VMEM((RAD, d), BF16)
    small = pltpu.VMEM((M, d), F32)
    return pl.pallas_call(
        functools.partial(rear_kernel, n=n, ring=ring, seg_len=seg_len),
        in_specs=[ANYW] * (9 + (1 if ring else 0)) + [VM] * (15 + (1 if ring else 0)),
        out_specs=[ANYW] * 3 + [VM] * (len(outs) - 3),
        out_shape=outs,
        scratch_shapes=[pltpu.VMEM((t, d), BF16)] * 5
        + [
            pltpu.VMEM((t, 3 * d), BF16),
            pltpu.VMEM((d, 128), F32),
            ext,
            ext,
            pltpu.VMEM((40, 8, d), F32),
            halo,
            halo,
            pltpu.VMEM((r, 128), F32),
            small,
            small,
            pltpu.VMEM((NG, GROUP, GROUP), BF16),
            pltpu.VMEM((NG, 8, GROUP), F32),
            pltpu.VMEM((NG, GROUP, GROUP), F32),
            pltpu.VMEM((NG, GROUP, GROUP), BF16),
            pltpu.VMEM((n, 8, d), F32),
            pltpu.VMEM((n, 8, d), F32),
            pltpu.VMEM((8, d), F32),
            pltpu.VMEM((3, d, d), BF16),
            pltpu.VMEM((3, d, d), BF16),
            pltpu.VMEM((8, 128), F32),
            pltpu.VMEM((n, 8, 128), F32),
            pltpu.VMEM((8, d), F32),
            DMA((2, n)),
            DMA((9,)),
            DMA((6,)),
            DMA((4,)),
            DMA((2, n)),
        ]
        + SeqSum.scratch(r, n)
        + extra,
        compiler_params=pltpu.CompilerParams(
            collective_id=2, has_side_effects=True, vmem_limit_bytes=61 * 1024 * 1024
        ),
        name="rear",
    )(*bodies, *more, *(grads if ring else ()), gw, uz, a, z, az, t2, t3, mq, mk, vl, vr, taps, dkt, dg2, gains, *((t_ud,) if ring else ()))


def adam_into(grad, at_in, at_out, rate):
    w, m, v = at_in
    moment = BETA_ONE * m[...] + (1.0 - BETA_ONE) * grad
    second = BETA_TWO * v[...] + (1.0 - BETA_TWO) * grad * grad
    first_hat = moment * (1.0 / (1.0 - BETA_ONE**STEP))
    second_hat = second * (1.0 / (1.0 - BETA_TWO**STEP))
    at_out[0][...] = w[...] - rate * (first_hat / (jnp.sqrt(second_hat) + ADAM_EPS) + DECAY_RATE * w[...])
    at_out[1][...] = moment
    at_out[2][...] = second


def adam_kernel(*refs):
    take = Refs(refs)
    r_qkv, r_uo, r_down = take(3)
    attn, up, down = take(3), take(3), take(3)
    attn_n, up_n, down_n = take(3), take(3), take(3)
    for i in range(4):
        grad = r_qkv[i] if i < 3 else r_uo[PARTS]
        adam_into(grad, [r.at[i] for r in attn], [r.at[i] for r in attn_n], LEARN_RATE)
    rows_chip = r_down.shape[1]
    wide = PARTS * rows_chip
    for c in range(0, up[0].shape[1], 2 * wide):
        got = [r_uo[p, :, (c + h * wide) // PARTS : (c + h * wide) // PARTS + rows_chip] for h in range(2) for p in range(PARTS)]
        cols = slice(c, c + 2 * wide)
        adam_into(jnp.concatenate(got, axis=1), [r.at[:, cols] for r in up], [r.at[:, cols] for r in up_n], LEARN_RATE)
    for j in range(2):
        rows_j = slice(j * rows_chip, (j + 1) * rows_chip)
        adam_into(r_down[j], [r.at[rows_j, :] for r in down], [r.at[rows_j, :] for r in down_n], LEARN_RATE)


def adam_all(r_qkv, r_uo, r_down, state):
    return pl.pallas_call(
        adam_kernel,
        in_specs=[VM] * 12,
        out_specs=[VM] * 9,
        out_shape=[sds(x.shape, F32) for x in state],
        compiler_params=pltpu.CompilerParams(vmem_limit_bytes=VMEM_LIMIT),
        name="adam_all",
    )(r_qkv, r_uo, r_down, *state)


def adam_step(weight, grad_vec, moment, second, rate_value):
    moment_new = BETA_ONE * moment + (1.0 - BETA_ONE) * grad_vec
    second_new = BETA_TWO * second + (1.0 - BETA_TWO) * grad_vec * grad_vec
    first_hat = moment_new / (1.0 - BETA_ONE**STEP)
    second_hat = second_new / (1.0 - BETA_TWO**STEP)
    weight_new = weight - rate_value * (
        first_hat / (jnp.sqrt(second_hat) + ADAM_EPS) + DECAY_RATE * weight
    )
    return (weight_new, moment_new, second_new)


def per_device(tokens, cotangent, attn_w, w_up, w_down, vectors, attn_m, attn_v, up_m, up_v, down_m, down_v, vec_m, vec_v):
    both = ("seq", "rep")
    x = tokens[0]
    dy = cotangent[0]
    t, d = x.shape
    n = lax.axis_size("seq")
    seg_len = t * n // M
    ring = n == CHIPS and lax.axis_size("rep") == 2

    rown = d // n
    if ring:
        weights = (attn_w, w_up, w_down.reshape(2, rown, d), vectors)
    else:
        w_attn = lax.all_gather(attn_w.astype(BF16), both, axis=1, tiled=True)
        vec = lax.all_gather(vectors.astype(BF16), both, axis=0, tiled=True).astype(F32)
        weights = (w_attn[:3], jnp.pad(vec, ((0, 0), (0, 128 - vec.shape[1]))))
    (w_qkv, wo, ud, ud_own, gains, taps, h1, q, k, v, conv, f, e, mq, mk, uz, a, z, az, t2, t3, vl, vr, pinverse) = front(
        x, weights, n, ring
    )
    if not ring:
        w_qkv, wo = w_attn[:3], w_attn[3]
        up = lax.all_gather(w_up.astype(BF16), both, axis=0, tiled=True)
        down = lax.all_gather(w_down.astype(BF16), both, axis=0, tiled=True)
        ud = jnp.stack([jnp.transpose(up.reshape(d, PARTS, d), (1, 0, 2)), down.reshape(PARTS, d, d)], axis=1)
    else:
        ud = ud[None]
    res = middle(x, dy, f, q, conv, wo, ud, ud_own, gains, mk, uz, pinverse, padded_rows(6 * M, n), n)
    out, dx, dmix, dqf, g_last, gw, dkt, dg2 = res[:8]
    res = rear(
        (v, dmix, e, k, dqf),
        (x, dx, h1, w_qkv),
        (g_last,) if ring else None,
        gw, uz, a, z, az, t2, t3, mq, mk, vl, vr, taps, dkt, dg2, gains,
        res[8] if ring else None,
        n, seg_len,
    )
    ig, g_vec, g_qkv, dg = res[:4]
    dg1 = (dg[0] + dg[1])[: d // 128].reshape(d)
    if ring:
        r_uo, r_down, red_vec, r_qkv = res[4:]
        own = d // (2 * n)
        start = (lax.axis_index("seq") * 2 + lax.axis_index("rep")) * own
        dg1_own = lax.dynamic_slice_in_dim(dg1, start, own, 0)
        red_vec = jnp.concatenate([dg1_own[:, None], red_vec[:, 1 : vectors.shape[1]]], axis=1)
        state = (attn_w, attn_m, attn_v, w_up, up_m, up_v, w_down, down_m, down_v)
        news = adam_all(r_qkv, r_uo, r_down, state)
    else:
        g_attn = jnp.concatenate([g_qkv, g_last[2 * PARTS :]], axis=0)
        g_pairs = g_last[: 2 * PARTS].reshape(PARTS, 2, d, d)
        g_up = jnp.transpose(g_pairs[:, 0], (1, 0, 2)).reshape(d, PARTS * d)
        g_down = g_pairs[:, 1].reshape(PARTS * d, d)
        red_attn = lax.psum_scatter(g_attn, both, scatter_dimension=1, tiled=True).astype(F32)
        red_up = lax.psum_scatter(g_up, both, scatter_dimension=0, tiled=True).astype(F32)
        red_down = lax.psum_scatter(g_down, both, scatter_dimension=0, tiled=True).astype(F32)
        g_vec = jnp.concatenate([dg1[:, None] / n, g_vec[:, 1 : vectors.shape[1]]], axis=1)
        red_vec = lax.psum_scatter(g_vec, both, scatter_dimension=0, tiled=True)
        news = (
            *adam_step(attn_w, red_attn, attn_m, attn_v, LEARN_RATE),
            *adam_step(w_up, red_up, up_m, up_v, LEARN_RATE),
            *adam_step(w_down, red_down, down_m, down_v, LEARN_RATE),
        )
    return (out[None], ig[None], *news, *adam_step(vectors, red_vec, vec_m, vec_v, VECTOR_RATE))


def solution(mesh):
    tok = P("rep", "seq", None)
    att = P(None, ("seq", "rep"), None)
    mat = P(("seq", "rep"), None)
    return jax.shard_map(
        per_device,
        mesh=mesh,
        in_specs=(tok, tok, att, mat, mat, mat, att, att, mat, mat, mat, mat, mat, mat),
        out_specs=(tok, tok, att, att, att) + (mat,) * 9,
        check_vma=False,
    )
```

```python
import functools

import jax
import jax.numpy as jnp
from jax import lax
from jax.experimental import pallas as pl
from jax.experimental.pallas import tpu as pltpu
from jax.sharding import PartitionSpec as P

H = 12
HD = 64
M = 64
KC = 33
NSITER = 6
STEP = 10
EPS_NORM = 1e-05
BETA_ONE = 0.9
BETA_TWO = 0.999
ADAM_EPS = 1e-08
LEARN_RATE = 0.03
VECTOR_RATE = 0.15
DECAY_RATE = 0.1

F32 = jnp.float32
BF16 = jnp.bfloat16
GROUP = 256
NG = 3
RAD = 16
QK_SCALE = HD ** (-0.25)
HI = lax.Precision.HIGHEST
VMEM_LIMIT = 58 * 1024 * 1024


def dot(a, b, precision=None):
    return lax.dot_general(a, b, (((1,), (0,)), ((), ())), precision=precision, preferred_element_type=F32)


def dot_nt(a, b, precision=None):
    return lax.dot_general(a, b, (((1,), (1,)), ((), ())), precision=precision, preferred_element_type=F32)


def dot_tn(a, b, precision=None):
    return lax.dot_general(a, b, (((0,), (0,)), ((), ())), precision=precision, preferred_element_type=F32)


def split(x):
    hi = x.astype(BF16)
    return hi, (x - hi.astype(F32)).astype(BF16)


def dot3(a, b):
    return dot(a[0], b[0]) + (dot(a[0], b[1]) + dot(a[1], b[0]))


def spread2(a):
    return spread(a[0]), spread(a[1])


def head_mask(shape=(GROUP, GROUP)):
    rows = lax.broadcasted_iota(jnp.int32, shape, 0)
    cols = lax.broadcasted_iota(jnp.int32, shape, 1)
    return lax.shift_right_logical(rows, 6) == lax.shift_right_logical(cols, 6)


def spread(wide):
    tall = jnp.concatenate([wide, wide, wide, wide], axis=0)
    return jnp.where(head_mask(), tall, jnp.zeros_like(tall))


def collect(full):
    kept = jnp.where(head_mask(), full, jnp.zeros_like(full))
    return (kept[0:64] + kept[64:128]) + (kept[128:192] + kept[192:256])


def flip(wide):
    turned = jnp.transpose(spread(wide))
    return (turned[0:64] + turned[64:128]) + (turned[128:192] + turned[192:256])


def gs(g):
    return slice(g * GROUP, (g + 1) * GROUP)


def half_reduce(x, op, init):
    parts = []
    for c in range(x.shape[1] // 128):
        col = x[:, c * 128 : (c + 1) * 128]
        low = lax.broadcasted_iota(jnp.int32, col.shape, 1) < 64
        a = op(jnp.where(low, col, init), axis=1, keepdims=True)
        b = op(jnp.where(low, init, col), axis=1, keepdims=True)
        parts.append(jnp.where(low, a, b))
    return jnp.concatenate(parts, axis=1)


def normalize(x):
    center = x - jnp.mean(x, axis=-1, keepdims=True)
    inv = lax.rsqrt(jnp.mean(center * center, axis=-1, keepdims=True) + EPS_NORM)
    return center * inv, inv


def norm_back(up, normal, inv, gain):
    scaled = up * gain
    centered = scaled - jnp.mean(scaled, axis=-1, keepdims=True)
    return inv * (centered - normal * jnp.mean(scaled * normal, axis=-1, keepdims=True))


def rowsum8(x):
    return jnp.sum(x.reshape(x.shape[0] // 8, 8, x.shape[1]), axis=0)


def gelu_parts(a):
    z = jnp.abs(a)
    t = 1.0 / (1.0 + (0.3275911 * 0.7071067811865476) * z)
    e = jnp.exp(-0.5 * a * a)
    poly = t * (0.127414796 + t * (-0.142248368 + t * (0.7107068705 + t * (-0.7265760135 + t * 0.5307027145))))
    tail = poly * e
    phi = jnp.where(a >= 0, 1.0 - tail, tail)
    return a * phi, phi + a * (e * 0.3989422804014327)


def whole(shape):
    zeros = (0,) * len(shape)
    return pl.BlockSpec(shape, lambda i: zeros, pipeline_mode=pl.Buffered(1))


def rows(tile, width):
    return pl.BlockSpec((tile, width), lambda i: (i, 0))


def sds(shape, dtype):
    return jax.ShapeDtypeStruct(shape, dtype)


def params():
    return pltpu.CompilerParams(dimension_semantics=("arbitrary",), vmem_limit_bytes=VMEM_LIMIT)


def widen(zt, g):
    return jnp.concatenate(
        [jnp.broadcast_to(zt[:, h : h + 1], (M, HD)) for h in range(4 * g, 4 * g + 4)], axis=1
    )


def u_group(ref, g):
    return jnp.concatenate([ref[2 * g * M : (2 * g + 1) * M, :], ref[(2 * g + 1) * M : (2 * g + 2) * M, :]], axis=1)


def zt_group(ref, g):
    return widen(ref[6 * M : 7 * M, :], g)


def put_tall(ref, g, wide):
    ref[2 * g * M : (2 * g + 1) * M, :] = wide[:, :128]
    ref[(2 * g + 1) * M : (2 * g + 2) * M, :] = wide[:, 128:]


def padded_rows(r, n):
    return -(-r // (8 * n)) * 8 * n


MESH = pl.DeviceIdType.MESH
DMA = pltpu.SemaphoreType.DMA
VM = pl.BlockSpec(memory_space=pltpu.VMEM)
ANYW = pl.BlockSpec(memory_space=pl.ANY)


def remote(src, dst, send, recv, where):
    return pltpu.make_async_remote_copy(
        src_ref=src, dst_ref=dst, send_sem=send, recv_sem=recv, device_id=where, device_id_type=MESH
    )


def greet(me, n, others):
    bar = pltpu.get_barrier_semaphore()

    def hello(j, _):
        pl.semaphore_signal(bar, inc=1, device_id={"seq": lax.rem(me + j, n)}, device_id_type=MESH)
        return 0

    lax.fori_loop(1, n, hello, 0)
    for peer in others:
        pl.semaphore_signal(bar, inc=1, device_id=peer, device_id_type=MESH)
    pl.semaphore_wait(bar, n - 1 + len(others))


def each_peer(me, n, make, act):
    def body(j, _):
        act(make(j, lax.rem(me + j, n)))
        return 0

    lax.fori_loop(1, n, body, 0)


def halo_copies(body_ref, left_ref, right_ref, me, n, sems):
    t = body_ref.shape[0]
    right = {"seq": lax.rem(me + 1, n)}
    left = {"seq": lax.rem(me + n - 1, n)}
    return (
        remote(body_ref.at[pl.ds(t - RAD, RAD)], left_ref, sems.at[0], sems.at[1], right),
        remote(body_ref.at[pl.ds(0, RAD)], right_ref, sems.at[2], sems.at[3], left),
    )


def mask_halos(left_ref, right_ref, me, n):
    left_ref[...] = jnp.where(me > 0, left_ref[...], jnp.zeros_like(left_ref))
    right_ref[...] = jnp.where(me < n - 1, right_ref[...], jnp.zeros_like(right_ref))


class SeqSum:
    def __init__(self, me, n, x, out, slots, total, sems):
        self.me, self.n, self.x, self.out, self.slots, self.total, self.sems = me, n, x, out, slots, total, sems
        self.chunk = x.shape[0] // n
        self.here = pl.ds(pl.multiple_of(me * self.chunk, 8), self.chunk)

    def first(self, j, peer):
        src = self.x.at[pl.ds(pl.multiple_of(peer * self.chunk, 8), self.chunk)]
        return remote(src, self.slots.at[self.me], self.sems.at[0, j], self.sems.at[1, j], {"seq": peer})

    def second(self, j, peer):
        return remote(self.total, self.out.at[self.here], self.sems.at[2, j], self.sems.at[3, j], {"seq": peer})

    def start(self):
        each_peer(self.me, self.n, self.first, lambda c: c.start())
        self.slots[pl.ds(self.me, 1)] = self.x[self.here, :][None]

    def turn(self):
        each_peer(self.me, self.n, self.first, lambda c: c.wait())
        summed = lax.fori_loop(1, self.n, lambda i, acc: acc + self.slots[i], self.slots[0])
        self.total[...] = summed
        each_peer(self.me, self.n, self.second, lambda c: c.start())
        self.out[self.here, :] = summed

    def finish(self):
        each_peer(self.me, self.n, self.second, lambda c: c.wait())

    @staticmethod
    def scratch(r, n):
        return [pltpu.VMEM((n, r // n, 128), F32), pltpu.VMEM((r // n, 128), F32), DMA((4, n))]


CHIPS = 16
STACK, HALF, ROWS, LINES = range(4)


def at(i, size, unit):
    return pl.ds(pl.multiple_of(i * size, unit), size)


def piece(kind, ref, seq, rep):
    if kind == STACK:
        half = ref.shape[2] // 2
        return ref.at[:, at(seq, ref.shape[1] // CHIPS, 16), at(rep, half, 128)]
    if kind == HALF:
        half = ref.shape[1] // 2
        return ref.at[at(seq, ref.shape[0] // CHIPS, 16), at(rep, half, 128)]
    return ref.at[at(seq * 2 + rep, ref.shape[0] // (2 * CHIPS), 8 if kind == LINES else 16), :]


class Place:
    def __init__(self):
        self.seq = lax.axis_index("seq")
        self.rep = lax.axis_index("rep")
        self.x = lax.rem(self.seq, 2)
        self.y = lax.rem(lax.div(self.seq, 2), 2)
        self.z = lax.div(self.seq, 4)
        self.twin = {"rep": 1 - self.rep}
        self.across = ({"seq": self.chip(4, self.rep)}, {"seq": self.chip(8, self.rep)})

    def chip(self, i, rep):
        j, b, a = lax.rem(i, 4), lax.rem(lax.div(i, 4), 2), lax.div(i, 8)
        z = lax.rem(self.z + 4 - j, 4)
        fx = a + rep * (b - a)
        fy = b + rep * (a - b)
        x = self.x + fx * (1 - 2 * self.x)
        y = self.y + fy * (1 - 2 * self.y)
        return z * 4 + y * 2 + x

    def above(self, j):
        return {"seq": self.chip(4 - j, self.rep)}

    def below(self, j):
        return {"seq": self.chip(j, self.rep)}


class GatherMesh:
    def __init__(self, place, kinds, outs, own, sems):
        self.place, self.kinds, self.outs, self.own = place, kinds, outs, own
        self.zsend, self.send1, self.send2, self.ssend, self.recv, self.srecv = sems

    def block(self, i, k, rep):
        return piece(self.kinds[k], self.outs[k], self.place.chip(i, rep), rep)

    def copy(self, i, k, send, recv, where):
        b = self.block(i, k, self.place.rep)
        src = b if self.own[k] is None or not (isinstance(i, int) and i == 0) else self.own[k]
        return remote(src, b, send, recv, where)

    def to_z(self, j, k):
        return self.copy(0, k, self.zsend.at[j, k], self.recv.at[j, k], self.place.above(j))

    def to_first(self, i, k):
        return self.copy(i, k, self.send1.at[i, k], self.recv.at[i + 4, k], self.place.across[0])

    def to_second(self, i, k):
        return self.copy(i, k, self.send2.at[i, k], self.recv.at[i + 8, k], self.place.across[1])

    def share(self, i, k):
        return self.copy(i, k, self.ssend.at[i, k], self.srecv.at[i, k], self.place.twin)

    def arrival(self, i, k):
        b = self.block(i, k, self.place.rep)
        return remote(b, b, self.ssend.at[i, k], self.recv.at[i, k], self.place.twin)

    def shared(self, i, k):
        b = self.block(i, k, 1 - self.place.rep)
        return remote(b, b, self.ssend.at[i, k], self.srecv.at[i, k], self.place.twin)

    def start_z(self):
        for k in range(len(self.kinds)):
            for j in (1, 2, 3):
                self.to_z(j, k).start()

    def start_across(self, which=None):
        for k in range(len(self.kinds)) if which is None else which:
            self.to_second(0, k).start()
            self.to_first(0, k).start()
            self.share(0, k).start()

    def each(self, low, high, which, act):
        def body(i, _):
            for k in which:
                act(i, k)
            return 0

        lax.fori_loop(low, high, body, 0)

    def line(self, which):
        def act(i, k):
            self.arrival(i, k).wait_recv()
            self.to_first(i, k).start()
            self.share(i, k).start()

        self.each(1, 4, which, act)

    def line_on(self, which):
        self.each(1, 4, which, lambda i, k: self.to_second(i, k).start())

    def plane(self, which):
        def act(i, k):
            self.arrival(i, k).wait_recv()
            self.to_second(i, k).start()
            self.share(i, k).start()

        self.each(4, 8, which, act)

    def space(self, which):
        def act(i, k):
            self.arrival(i, k).wait_recv()
            self.share(i, k).start()

        self.each(8, CHIPS, which, act)

    def shares_in(self, which):
        self.shared_first(which)
        self.each(1, CHIPS, which, lambda i, k: self.shared(i, k).wait_recv())

    def shared_first(self, which):
        for k in which:
            self.shared(0, k).wait_recv()

    def finish(self):
        which = range(len(self.kinds))
        for k in which:
            for j in (1, 2, 3):
                self.to_z(j, k).wait_send()
            self.to_first(0, k).wait_send()
            self.to_second(0, k).wait_send()
            self.share(0, k).wait_send()

        def act(i, k):
            @pl.when(i < 4)
            def _():
                self.to_first(i, k).wait_send()

            @pl.when(i < 8)
            def _():
                self.to_second(i, k).wait_send()

            self.share(i, k).wait_send()

        self.each(1, CHIPS, which, act)

    @staticmethod
    def scratch(k):
        return [DMA((4, k)), DMA((4, k)), DMA((8, k))] + [DMA((CHIPS, k))] * 3


class ScatterMesh:
    def __init__(self, place, kinds, grads, mine, twins, in2, in1, inz, sems):
        self.place, self.kinds, self.grads = place, kinds, grads
        self.mine, self.twins, self.in2, self.in1, self.inz = mine, twins, in2, in1, inz
        self.lsem, self.tsend, self.trecv, self.s2, self.r2, self.s1, self.r1, self.sz, self.rz = sems

    def source(self, i, k):
        return piece(self.kinds[k], self.grads[k], self.place.chip(i, self.place.rep), self.place.rep)

    def cell(self, i, k):
        return self.source(i, k) if self.mine is None else self.mine[k].at[i]

    def load(self, i, k):
        return pltpu.make_async_copy(self.source(i, k), self.mine[k].at[i], self.lsem.at[i, k])

    def give(self, i, k):
        other = 1 - self.place.rep
        src = piece(self.kinds[k], self.grads[k], self.place.chip(i, other), other)
        return remote(src, self.twins[k].at[i], self.tsend.at[i, k], self.trecv.at[i, k], self.place.twin)

    def out2(self, i, k):
        return remote(self.cell(i, k), self.in2[k].at[i - 8], self.s2.at[i - 8, k], self.r2.at[i - 8, k], self.place.across[1])

    def out1(self, i, k):
        return remote(self.cell(i, k), self.in1[k].at[i - 4], self.s1.at[i - 4, k], self.r1.at[i - 4, k], self.place.across[0])

    def outz(self, j, k):
        return remote(self.cell(j, k), self.inz[k].at[j], self.sz.at[j, k], self.rz.at[j, k], self.place.below(j))

    def start(self, which=None):
        for low in (8, 0):
            for k in range(len(self.kinds)) if which is None else which:

                def body(j, _):
                    self.give(low + 7 - j, k).start()
                    if self.mine is not None:
                        self.load(low + 7 - j, k).start()
                    return 0

                lax.fori_loop(0, 8, body, 0)

    def terms(self, i, k):
        if self.mine is not None:
            self.load(i, k).wait()
        self.give(i, k).wait()
        return self.cell(i, k)[...].astype(F32) + self.twins[k].at[i][...].astype(F32)

    def keep(self, i, k, value):
        cell = self.cell(i, k)
        cell[...] = value.astype(cell.dtype)

    def far(self, k):
        def body(j, _):
            i = CHIPS - 1 - j
            self.keep(i, k, self.terms(i, k))
            self.out2(i, k).start()
            return 0

        lax.fori_loop(0, 8, body, 0)

    def mid(self, k):
        def body(j, _):
            i = 7 - j
            own = self.terms(i, k)
            self.out2(i + 8, k).wait_recv()
            self.keep(i, k, own + self.in2[k].at[i][...].astype(F32))
            self.out1(i, k).start()
            return 0

        lax.fori_loop(0, 4, body, 0)

    def closer(self, i, k):
        own = self.terms(i, k)
        self.out2(i + 8, k).wait_recv()
        self.out1(i + 4, k).wait_recv()
        return own + (self.in2[k].at[i][...].astype(F32) + self.in1[k].at[i][...].astype(F32))

    def near(self, k):
        def body(j, _):
            i = 3 - j
            self.keep(i, k, self.closer(i, k))
            self.outz(i, k).start()
            return 0

        lax.fori_loop(0, 3, body, 0)

    def total(self, k):
        acc = self.closer(0, k)
        for j in (1, 2, 3):
            self.outz(j, k).wait_recv()
            acc = acc + self.inz[k][j].astype(F32)
        return acc

    def finish(self):
        for k in range(len(self.kinds)):

            def body(i, _):
                @pl.when(i >= 8)
                def _():
                    self.out2(i, k).wait_send()

                @pl.when((i >= 4) & (i < 8))
                def _():
                    self.out1(i, k).wait_send()

                @pl.when(i < 4)
                def _():
                    self.outz(i, k).wait_send()

                return 0

            lax.fori_loop(1, CHIPS, body, 0)

    @staticmethod
    def scratch(blocks, in_place=False):
        k = len(blocks)
        return (
            ([] if in_place else [pltpu.VMEM((CHIPS, *s), t) for s, t in blocks])
            + [pltpu.VMEM((CHIPS, *s), t) for s, t in blocks]
            + [pltpu.VMEM((8, *s), t) for s, t in blocks]
            + [pltpu.VMEM((4, *s), t) for s, t in blocks]
            + [pltpu.VMEM((4, *s), t) for s, t in blocks]
            + [DMA((CHIPS, k))] * 3
            + [DMA((8, k))] * 2
            + [DMA((4, k))] * 4
        )

    @staticmethod
    def take(take, place, kinds, grads, in_place=False):
        k = len(kinds)
        mine = None if in_place else take(k)
        bufs = [take(k) for _ in range(4)]
        return ScatterMesh(place, kinds, grads, mine, *bufs, take(9))


def swap_rows(total, out, place, sems):
    rows_own = total.shape[-2] // 2
    half = total.shape[-1]
    theirs, mine = at(1 - place.rep, rows_own, 8), at(place.rep, rows_own, 8)
    cols = at(place.rep, half, 128)
    if len(total.shape) == 3:
        out[:, :, cols] = total[:, mine, :]
        return remote(total.at[:, theirs, :], out.at[:, :, cols], sems.at[0], sems.at[1], place.twin)
    out[:, cols] = total[mine, :]
    return remote(total.at[theirs, :], out.at[:, cols], sems.at[0], sems.at[1], place.twin)


CHUNK = 64
CTILE = 256


def fill_inner(ext, body_ref, start):
    count = ext.shape[1]
    rows_in = pl.ds(pl.multiple_of(start - RAD, RAD), count)
    for c in range(ext.shape[0]):
        ext[c] = body_ref[rows_in, c * 128 : (c + 1) * 128].astype(F32)


def fill_edge(ext, body_ref, left_ref, right_ref, first):
    tile = ext.shape[1] - 2 * RAD
    t = body_ref.shape[0]
    start = pl.multiple_of(jnp.where(first, 0, t - tile), tile)
    for c in range(ext.shape[0]):
        cols = slice(c * 128, (c + 1) * 128)
        ext[c, RAD : RAD + tile, :] = body_ref[pl.ds(start, tile), cols].astype(F32)
        ext[c, 0:RAD, :] = jnp.where(first, left_ref[:, cols], body_ref[t - tile - RAD : t - tile, cols]).astype(F32)
        ext[c, RAD + tile :, :] = jnp.where(first, body_ref[tile : tile + RAD, cols], right_ref[:, cols]).astype(F32)


def conv_forward(ext, tap_ref, out, row0):
    def step(r, _):
        base = pl.multiple_of(r * CHUNK, CHUNK)
        for c in range(ext.shape[0]):
            cols = slice(c * 128, (c + 1) * 128)
            acc = jnp.zeros((CHUNK, 128), F32)
            for b in range(8):
                reach = 4 if b == 0 else 3
                win = ext[c, pl.ds(base + b, CHUNK + 8 * reach), :]
                for m in range(reach + 1):
                    o = 8 * m + b
                    acc = acc + tap_ref[o : o + 1, cols] * win[8 * m : 8 * m + CHUNK]
            out[pl.ds(pl.multiple_of(row0 + base, CHUNK), CHUNK), cols] = acc.astype(out.dtype)
        return 0

    lax.fori_loop(0, CTILE // CHUNK, step, 0)


def conv_back_chunk(vext, gext, tap_ref, out, tapacc, row0, base):
    width = out.shape[1] // 3
    for c in range(vext.shape[0]):
        cols = slice(c * 128, (c + 1) * 128)
        acc = jnp.zeros((CHUNK, 128), F32)
        here = gext[c, pl.ds(base + RAD, CHUNK), :]
        for b in range(8):
            reach = 4 if b == 0 else 3
            win = gext[c, pl.ds(base + b, CHUNK + 8 * reach), :]
            for m in range(reach + 1):
                o = KC - 1 - (8 * m + b)
                acc = acc + tap_ref[o : o + 1, cols] * win[8 * m : 8 * m + CHUNK]
            win = vext[c, pl.ds(base + b, CHUNK + 8 * reach), :]
            for m in range(reach + 1):
                o = 8 * m + b
                tapacc[o, :, cols] += rowsum8(here * win[8 * m : 8 * m + CHUNK])
        into = slice(2 * width + c * 128, 2 * width + (c + 1) * 128)
        out[pl.ds(pl.multiple_of(row0 + base, CHUNK), CHUNK), into] = acc.astype(out.dtype)


def conv_backward(vext, gext, tap_ref, out, tapacc, row0):
    def step(r, _):
        conv_back_chunk(vext, gext, tap_ref, out, tapacc, row0, pl.multiple_of(r * CHUNK, CHUNK))
        return 0

    lax.fori_loop(0, CTILE // CHUNK, step, 0)


def wide_eye():
    lane = lax.broadcasted_iota(jnp.int32, (M, GROUP), 1) & 63
    return jnp.where(lane == lax.broadcasted_iota(jnp.int32, (M, GROUP), 0), 1.0, 0.0)


def head_sums(row):
    ones = jnp.where(head_mask(), 1.0, 0.0)
    return dot(jnp.broadcast_to(row, (8, GROUP)), ones, HI)[0:1]


def pinv_begin(mq_ref, mk_ref, a_ref, z_ref):
    for g in range(NG):
        s = dot_nt(mq_ref[:, gs(g)], spread(mk_ref[:, gs(g)]))
        e = jnp.exp(s - half_reduce(s, jnp.max, -jnp.inf))
        a = e / half_reduce(e, jnp.sum, 0.0)
        a_ref[:, gs(g)] = a
        col = jnp.sum(a, axis=0, keepdims=True)
        z_ref[0, :, gs(g)] = flip(a) / jnp.sqrt(head_sums(col * col))


def pinv_step(it, a_ref, z_ref, az_ref, t2_ref, t3_ref):
    eye = wide_eye()
    R = range(NG)
    z = [split(z_ref[it, :, gs(g)]) for g in R]
    az = [dot3(split(a_ref[:, gs(g)]), spread2(z[g])) for g in R]
    azs = [split(az[g]) for g in R]
    t2 = [15.0 * eye - dot3(azs[g], spread2(split(7.0 * eye - az[g]))) for g in R]
    t3 = [13.0 * eye - dot3(azs[g], spread2(split(t2[g]))) for g in R]
    for g in R:
        z_ref[it + 1, :, gs(g)] = 0.25 * dot3(z[g], spread2(split(t3[g])))
        az_ref[it, :, gs(g)] = az[g]
        t2_ref[it, :, gs(g)] = t2[g]
        t3_ref[it, :, gs(g)] = t3[g]


def pinv_back_step(it, a_ref, z_ref, az_ref, t2_ref, t3_ref, gz_ref, da_ref):
    eye = wide_eye()
    R = range(NG)
    az = [az_ref[it, :, gs(g)] for g in R]
    zs = [split(z_ref[it, :, gs(g)]) for g in R]
    gzs = [split(0.25 * gz_ref[:, gs(g)]) for g in R]
    baz = [spread2(split(az[g])) for g in R]
    d3 = [split(dot3(gzs[g], spread2(zs[g]))) for g in R]
    d2 = [split(-dot3(d3[g], baz[g])) for g in R]
    d1 = [-dot3(d2[g], baz[g]) for g in R]
    daz = [
        split(
            -dot3(split(t2_ref[it, :, gs(g)]), spread2(d3[g]))
            - dot3(split(7.0 * eye - az[g]), spread2(d2[g]))
            - d1[g]
        )
        for g in R
    ]
    for g in R:
        da_ref[:, gs(g)] += dot3(zs[g], spread2(daz[g]))
        gz_ref[:, gs(g)] = dot3(split(t3_ref[it, :, gs(g)]), spread2(gzs[g])) + dot3(
            daz[g], spread2(split(a_ref[:, gs(g)]))
        )


def pinv_back_end(g, a_ref, gz_ref, da_ref):
    a = a_ref[:, gs(g)]
    gz = gz_ref[:, gs(g)]
    col = jnp.sum(a, axis=0, keepdims=True)
    bound = jnp.sqrt(head_sums(col * col))
    tot = head_sums(jnp.sum(gz * a, axis=0, keepdims=True))
    full = flip(da_ref[:, gs(g)]) + gz / bound - (tot / (bound * bound * bound)) * col
    return a * (full - half_reduce(full * a, jnp.sum, 0.0))


def gather_marks(slots, outs, n):
    per = 4 * n // M
    half = slots.shape[2]
    for out, base in zip(outs, (0, 4)):
        if per == 1:
            got = [slots[i].astype(F32) for i in range(n)]
            for h in range(2):
                tall = jnp.concatenate([x[8 * h + base : 8 * h + base + 4] for x in got], axis=0)
                out[:, h * half : (h + 1) * half] = tall.astype(BF16)
        else:
            for h in range(2):
                lines = []
                for m in range(M):
                    total = jnp.zeros((1, half), F32)
                    for s in range(per // 4):
                        part = slots[m * (per // 4) + s].astype(F32)[8 * h + base : 8 * h + base + 4]
                        total = total + jnp.sum(part, axis=0, keepdims=True)
                    lines.append(total * (1.0 / per))
                out[:, h * half : (h + 1) * half] = jnp.concatenate(lines, axis=0).astype(BF16)


class Refs:
    def __init__(self, refs):
        self.it = iter(refs)

    def __call__(self, count):
        return [next(self.it) for _ in range(count)]

    def one(self):
        return next(self.it)


def front_kernel(*refs, n, ring):
    take = Refs(refs)
    x_any = take.one()
    if ring:
        wa, wu, wd, wv = take(4)
        wqkv_o, wo_o, ud0_o, ud_own = take(4)
    else:
        wq, vec = take(2)
    gains, taps = take(2)
    outs = take(7)
    mq, mk, uz, a_ref, z_ref, az_ref, t2_ref, t3_ref, vl, vr, p_ref = take(11)
    xs = take.one()
    stage = take(7)
    h_s, q_s, k_s, v_s, conv_s, f_s, e_s = stage
    means, pay, slots, ext, bdk, bdq, uacc, zacc, upart = take(9)
    xsem, osem, msem, hsem = take(4)
    sum_bufs = take(3)
    me = lax.axis_index("seq")
    t, d = xs.shape
    half = d // 2
    load_x = pltpu.make_async_copy(x_any, xs, xsem.at[0])
    load_x.start()
    drains = [pltpu.make_async_copy(s, o, osem.at[i]) for i, (s, o) in enumerate(zip(stage, outs))]
    if ring:
        wq, vec, sa, su, sd, so, co, wperm, psem, lsem = take(10)
        ring_one, ring_two = take(6), take(6)
        place = Place()
        greet(me, n, [place.twin])
        rep, seq = place.rep, place.seq
        rows_own = d // (2 * CHIPS)
        mine = at(rep, rows_own, 8)
        theirs = 1 - rep
        swaps = [
            remote(wa.at[0:3, :, at(theirs, half, 128)], sa.at[:, mine, :], psem.at[0], psem.at[1], place.twin),
            remote(wa.at[3, :, at(theirs, half, 128)], so.at[mine, :], psem.at[2], psem.at[3], place.twin),
            remote(wd.at[:, :, at(theirs, half, 128)], sd.at[pl.ds(2 * rep, 2)], psem.at[6], psem.at[7], place.twin),
        ]
        for c in swaps:
            c.start()
        sa[:, mine, :] = wa[0:3, :, at(rep, half, 128)]
        so[mine, :] = wa[3, :, at(rep, half, 128)]
        sd[pl.ds(2 * rep, 2)] = wd[:, :, at(rep, half, 128)]
        vec[at(seq * 2 + rep, rows_own, 8), :] = jnp.zeros((rows_own, 128), F32)
        vec[at(seq * 2 + rep, rows_own, 8), 0 : wv.shape[1]] = wv[...]
        swaps[0].wait()
        wq[:, at(seq, 2 * rows_own, 16), at(rep, half, 128)] = sa[...].astype(BF16)
        first = GatherMesh(place, (LINES, HALF, HALF, HALF), (vec, wq.at[2], wq.at[1], wq.at[0]), (None,) * 4, ring_one)
        first.start_z()
        first.start_across((0, 1))
        rows_chip = 2 * rows_own
        for p in range(PARTS):
            for c in range(0, CHIPS, 8):
                got = [
                    wu[:, (PARTS * (c + h) + p) * rows_chip : (PARTS * (c + h) + p + 1) * rows_chip] for h in range(8)
                ]
                wperm[p, :, c * rows_chip : (c + 8) * rows_chip] = jnp.concatenate(got, axis=1)
        swaps.append(
            remote(wperm.at[:, :, at(theirs, half, 128)], su.at[:, mine, :], psem.at[4], psem.at[5], place.twin)
        )
        swaps[-1].start()
        su[:, mine, :] = wperm[:, :, at(rep, half, 128)]
        for c in swaps[1:]:
            c.wait()
        co[...] = so[...].astype(BF16)
        ud_own[:, 0] = su[...].astype(BF16)
        ud_own[:, 1] = sd[...].astype(BF16)
        rest = GatherMesh(place, (STACK, HALF), (ud0_o, wo_o), (ud_own.at[0], co), ring_two)
        local = [
            pltpu.make_async_copy(src, piece(kind, out, seq, rep), lsem.at[i])
            for i, (src, kind, out) in enumerate(zip(rest.own, rest.kinds, rest.outs))
        ]

        rest.start_z()
        for c in local:
            c.start()
        first.line((0, 1))
        first.line_on((0, 1))
        first.start_across((2, 3))
        first.plane((0, 1))
        for which in ((2,), (3,)):
            first.line(which)
            first.line_on(which)
        first.space((0,))
        first.shares_in((0,))
        save_w = pltpu.make_async_copy(wq, wqkv_o, xsem.at[1])
    else:
        greet(me, n, [])

    turned = jnp.transpose(vec[...]).astype(BF16).astype(F32)
    gains[...] = turned[0:8]
    taps[...] = turned[2:42]
    load_x.wait()

    def tile(i):
        return pl.ds(pl.multiple_of(i * (t // 4), t // 4), t // 4)

    def norm(i, _):
        normal, _inv = normalize(xs[tile(i), :].astype(F32))
        h_s[tile(i), :] = (normal * gains[0:1, :]).astype(BF16)
        return 0

    def project_v(i, _):
        v_s[tile(i), :] = dot(h_s[tile(i), :], wq[2]).astype(BF16)
        return 0

    def project_k(i, _):
        k = (dot(h_s[tile(i), :], wq[1]) * QK_SCALE).astype(BF16)
        k_s[tile(i), :] = k
        means[pl.ds(i + 4, 1), :] = jnp.mean(k.astype(F32), axis=0, keepdims=True)
        return 0

    def project_q(i, _):
        q = (dot(h_s[tile(i), :], wq[0]) * QK_SCALE).astype(BF16)
        q_s[tile(i), :] = q
        means[pl.ds(i, 1), :] = jnp.mean(q.astype(F32), axis=0, keepdims=True)
        return 0

    def inner(i, _):
        fill_inner(ext, v_s, i * CTILE)
        conv_forward(ext, taps, conv_s, i * CTILE)
        if ring:

            @pl.when(i == 4)
            def _():
                rest.line_on((0,))

            @pl.when(i == 5)
            def _():
                rest.line((1,))
                rest.line_on((1,))

        return 0

    tiles = t // CTILE
    lax.fori_loop(0, 4, norm, 0)
    if ring:
        first.plane((2,))
        first.space((1,))
        first.shares_in((1,))
    lax.fori_loop(0, 4, project_v, 0)
    halos = halo_copies(v_s, vl, vr, me, n, hsem)
    for c in halos:
        c.start()
    if ring:
        first.plane((3,))
        rest.start_across()
    lax.fori_loop(1, tiles // 2, inner, 0)
    if ring:
        first.space((2,))
        first.shares_in((2,))
    lax.fori_loop(0, 4, project_k, 0)
    if ring:
        first.space((3,))
        first.shares_in((3,))
        save_w.start()
        rest.line((0,))
    lax.fori_loop(0, 4, project_q, 0)

    pay[...] = jnp.concatenate([means[:, :half], means[:, half:]], axis=0).astype(BF16)

    def mark(j, peer):
        return remote(pay, slots.at[me], msem.at[0, j], msem.at[1, j], {"seq": peer})

    each_peer(me, n, mark, lambda c: c.start())
    slots[pl.ds(me, 1)] = pay[...][None]
    for c in drains[:4]:
        c.start()

    lax.fori_loop(tiles // 2, tiles - 1, inner, 0)
    for c in halos:
        c.wait()
    mask_halos(vl, vr, me, n)

    def edge(i, _):
        fill_edge(ext, v_s, vl, vr, i == 0)
        conv_forward(ext, taps, conv_s, i * (t - CTILE))
        return 0

    lax.fori_loop(0, 2, edge, 0)
    drains[4].start()
    each_peer(me, n, mark, lambda c: c.wait())
    gather_marks(slots, (mq, mk), n)
    for g in range(NG):
        bdk[g] = spread(mk[:, gs(g)])
        bdq[g] = spread(mq[:, gs(g)])
    uacc[...] = jnp.zeros_like(uacc)
    zacc[...] = jnp.zeros_like(zacc)
    ones_bd = jnp.where(head_mask(), 1.0, 0.0).astype(BF16)

    def expand(i, _):
        for g in range(NG):
            e = jnp.exp(dot_nt(k_s[tile(i), gs(g)], bdq[g])).astype(BF16)
            e_s[tile(i), gs(g)] = e
            uacc[g] += dot_tn(e, v_s[tile(i), gs(g)])
            zacc[g] += dot_tn(e, jnp.ones((t // 4, 128), BF16))
        if ring:

            @pl.when(i == 0)
            def _():
                rest.plane((0,))

            @pl.when(i == 1)
            def _():
                rest.plane((1,))

        return 0

    def attend(i, _):
        for g in range(NG):
            s = dot_nt(q_s[tile(i), gs(g)], bdk[g])
            ex = jnp.exp(s - half_reduce(s, jnp.max, -jnp.inf))
            den = dot(ex.astype(BF16), ones_bd)
            f_s[tile(i), gs(g)] = (ex / den).astype(BF16)
        return 0

    lax.fori_loop(0, 4, expand, 0)
    lane = lax.broadcasted_iota(jnp.int32, (M, 128), 1)
    zt = jnp.zeros((M, 128), F32)
    for g in range(NG):
        put_tall(upart, g, collect(uacc[g]))
        for h in range(4):
            zt = zt + jnp.where(lane == 4 * g + h, zacc[g, h * 64 : h * 64 + 64, :], 0.0)
    upart[6 * M : 7 * M, :] = zt
    upart[7 * M :, :] = jnp.zeros((upart.shape[0] - 7 * M, 128), F32)
    summing = SeqSum(me, n, upart, uz, *sum_bufs)
    summing.start()
    pinv_begin(mq, mk, a_ref, z_ref)

    def newton(it, _):
        pinv_step(it, a_ref, z_ref, az_ref, t2_ref, t3_ref)
        return 0

    lax.fori_loop(0, 4, attend, 0)
    for c in drains[5:]:
        c.start()
    summing.turn()
    lax.fori_loop(0, NSITER, newton, 0)
    summing.finish()
    p_ref[...] = z_ref[NSITER]
    for c in drains:
        c.wait()
    if ring:
        for c in local:
            c.wait()
        save_w.wait()
        rest.space((0, 1))
        rest.shares_in((0, 1))
        first.finish()
        rest.finish()


def front(x, weights, n, ring):
    t, d = x.shape
    if ring:
        rown = d // CHIPS
        own4 = (4, rown, d // 2)
        extra_out = [sds((3, d, d), BF16), sds((d, d), BF16), sds((2, d, d), BF16), sds((4, 2, rown, d // 2), BF16)]
        extra = [
            pltpu.VMEM((3, d, d), BF16),
            pltpu.VMEM((d, 128), F32),
            pltpu.VMEM((3, rown, d // 2), F32),
            pltpu.VMEM(own4, F32),
            pltpu.VMEM(own4, F32),
            pltpu.VMEM((rown, d // 2), F32),
            pltpu.VMEM((rown, d // 2), BF16),
            pltpu.VMEM((PARTS, rown // 2, d), F32),
            DMA((8,)),
            DMA((2,)),
        ] + GatherMesh.scratch(4) + GatherMesh.scratch(2)
    else:
        extra_out, extra = [], []
    r = padded_rows(7 * M, n)
    big = sds((t, d), BF16)
    steps = sds((NSITER, M, d), F32)
    res = pl.pallas_call(
        functools.partial(front_kernel, n=n, ring=ring),
        in_specs=[ANYW] + [VM] * len(weights),
        out_specs=([ANYW] * 3 + [VM] if ring else []) + [VM] * 2 + [ANYW] * 7 + [VM] * 11,
        out_shape=extra_out
        + [sds((8, d), F32), sds((40, d), F32)]
        + [big] * 7
        + [sds((M, d), BF16)] * 2
        + [sds((r, 128), F32), sds((M, d), F32), sds((NSITER + 1, M, d), F32), steps, steps, steps]
        + [sds((RAD, d), BF16)] * 2
        + [sds((M, d), F32)],
        scratch_shapes=[pltpu.VMEM((t, d), BF16)] * 8
        + [
            pltpu.VMEM((8, d), F32),
            pltpu.VMEM((16, d // 2), BF16),
            pltpu.VMEM((n, 16, d // 2), BF16),
            pltpu.VMEM((d // 128, CTILE + 2 * RAD, 128), F32),
            pltpu.VMEM((NG, GROUP, GROUP), BF16),
            pltpu.VMEM((NG, GROUP, GROUP), BF16),
            pltpu.VMEM((NG, GROUP, GROUP), F32),
            pltpu.VMEM((NG, GROUP, 128), F32),
            pltpu.VMEM((r, 128), F32),
            DMA((2,)),
            DMA((7,)),
            DMA((2, n)),
            DMA((4,)),
        ]
        + SeqSum.scratch(r, n)
        + extra,
        compiler_params=pltpu.CompilerParams(collective_id=1, has_side_effects=True, vmem_limit_bytes=VMEM_LIMIT),
        name="front",
    )(x, *weights)
    return res if ring else [None] * 4 + list(res)


PARTS = 4
HALF_D = 384
PART = 768


def middle_kernel(*refs, n, ring):
    take = Refs(refs)
    x_a, dy_a, f_a, q_a, conv_a, wo_a, ud_a = take(7)
    if ring:
        ud_own = take.one()
    gains, mk, uz, p_ref = take(4)
    out_o, dx_o, dmix_o, dqf_o, g_o = take(5)
    gw_ref, dkt_ref, dg_ref = take(3)
    if ring:
        t_ud = take.one()
    x_s, dy_s, f_s, mix_s, h2_s, da_s, x1_s, wo_s, ud = take(9)
    oacc, hacc, wbd, bdk, gwacc, dktacc, dgacc = take(7)
    isem, osem = take(2)
    t, d = x_s.shape
    tile = t // 4
    act_s, q_s = x_s, x_s
    seq = lax.axis_index("seq")
    parts_in = 1 if ring else PARTS
    gain = gains[1:2, :]

    def here(i):
        return pl.ds(pl.multiple_of(i * tile, tile), tile)

    load_q = pltpu.make_async_copy(q_a, q_s, isem.at[7])
    loads = [
        pltpu.make_async_copy(a, b, isem.at[i])
        for i, (a, b) in enumerate(
            ((f_a, f_s), (conv_a, mix_s), (x_a, x_s), (wo_a, wo_s), (ud_a, ud.at[pl.ds(0, parts_in)]), (dy_a, dy_s))
        )
    ]
    for c in loads:
        c.start()
    if ring:
        place = Place()
        gathers = [None] + [
            GatherMesh(place, (STACK,), (ud.at[p],), (ud_own.at[p],), take(6)) for p in range(1, PARTS)
        ]
        scatters = [
            ScatterMesh.take(take, place, (STACK,), (ud.at[p],), in_place=True) for p in range(PARTS - 1)
        ]
        greet(seq, n, [place.twin])
        for g in gathers[1:]:
            g.start_z()
        for p in range(1, PARTS):
            gathers[p].start_across()
            ud[p, :, at(seq, d // CHIPS, 16), at(place.rep, d // 2, 128)] = ud_own[p]

    def tick(cond, *acts):
        if ring and acts:

            @pl.when(cond)
            def _():
                for act in acts:
                    act()

    K = (0,)

    def move(p, *names):
        return [functools.partial(getattr(gathers[p], name), K) for name in names] if ring else []

    def send(p, *names):
        return [functools.partial(getattr(scatters[p], name), 0) for name in names] if ring else []

    gwacc[...] = jnp.zeros_like(gwacc)
    dktacc[...] = jnp.zeros_like(dktacc)
    dgacc[...] = jnp.zeros_like(dgacc)
    for g in range(NG):
        bv = u_group(uz, g) / zt_group(uz, g)
        wbd[g] = spread(dot(p_ref[:, gs(g)], spread(bv), HI)).astype(BF16)
        bdk[g] = spread(mk[:, gs(g)])
    for c in loads[:4]:
        c.wait()

    def before(i, _):
        r = here(i)
        for g in range(NG):
            mix_s[r, gs(g)] = (dot(f_s[r, gs(g)], wbd[g]) + mix_s[r, gs(g)].astype(F32)).astype(BF16)
        x1 = x_s[r, :].astype(F32) + dot(mix_s[r, :], wo_s[...])
        oacc[r, :] = x1
        x1_s[r, :] = x1.astype(BF16)
        normal, _inv = normalize(x1)
        h2_s[r, :] = (normal * gain).astype(BF16)
        tick(i == 1, *move(1, "line", "line_on"))
        tick(i == 3, *move(1, "plane"))
        return 0

    lax.fori_loop(0, 4, before, 0)
    loads[4].wait()
    loads[5].wait()
    plan = {
        (0, 0): move(2, "line", "line_on"),
        (0, 2): move(1, "space") + move(2, "plane"),
        (0, 3): move(3, "line", "line_on"),
        (1, 0): move(3, "plane") + send(0, "far"),
        (1, 1): move(2, "space"),
        (1, 3): send(0, "mid") + move(3, "space"),
        (2, 0): send(1, "far"),
        (2, 1): send(0, "near"),
        (2, 3): send(1, "mid"),
        (3, 0): send(2, "far"),
        (3, 1): send(1, "near"),
        (3, 3): send(2, "mid"),
    }
    for p in range(PARTS):
        if ring and p > 0:
            gathers[p].shares_in(K)
        u, dn = ud.at[p, 0], ud.at[p, 1]

        def through(i, _):
            r = here(i)
            h2 = h2_s[r, :]
            dy = dy_s[r, :]
            o = h = None
            for c in range(0, d, PART):
                cols = slice(c, c + PART)
                act, slope = gelu_parts(dot(h2, u[:, cols]))
                act = act.astype(BF16)
                act_s[r, cols] = act
                da = (dot_nt(dy, dn[cols, :]) * slope).astype(BF16)
                da_s[r, cols] = da
                oc, hc = dot(act, dn[cols, :]), dot_nt(da, u[:, cols])
                o, h = (oc, hc) if o is None else (o + oc, h + hc)
            oacc[r, :] += o
            hacc[r, :] = h if p == 0 else hacc[r, :] + h
            for j in range(4):
                tick(i == j, *plan.get((p, j), []))
            return 0

        lax.fori_loop(0, 4, through, 0)
        if ring and p > 0:
            gathers[p].finish()

        def grads(j, _):
            cols = pl.ds(pl.multiple_of(j * HALF_D, HALF_D), HALF_D)
            ud[p, 0, cols, :] = dot_tn(h2_s[:, cols], da_s[...]).astype(BF16)
            ud[p, 1, cols, :] = dot_tn(act_s[:, cols], dy_s[...]).astype(BF16)
            return 0

        lax.fori_loop(0, d // HALF_D, grads, 0)
        if ring and p < PARTS - 1:
            scatters[p].start()
        if ring and p == 3:
            t_ud[0] = scatters[0].total(0)
    load_q.start()
    first_out = PARTS - 1 if ring else 0
    stored = [
        pltpu.make_async_copy(ud.at[p], g_o.at[pl.ds(2 * (p - first_out), 2)], osem.at[16 + p])
        for p in range(first_out, PARTS)
    ]
    for c in stored:
        c.start()
    tick(True, *send(2, "near"))
    if ring:
        t_ud[1] = scatters[1].total(0)
    load_q.wait()

    def after(i, _):
        r = here(i)
        normal, inv = normalize(x1_s[r, :].astype(F32))
        x1_s[r, :] = oacc[r, :].astype(BF16)
        pltpu.make_async_copy(x1_s.at[r], out_o.at[r], osem.at[i]).start()
        dh2 = hacc[r, :]
        dgacc[...] += rowsum8(dh2 * normal)
        dx = (norm_back(dh2, normal, inv, gain) + dy_s[r, :].astype(F32)).astype(BF16)
        dy_s[r, :] = dx
        pltpu.make_async_copy(dy_s.at[r], dx_o.at[r], osem.at[4 + i]).start()
        dmix = dot_nt(dx, wo_s[...]).astype(BF16)
        h2_s[r, :] = dmix
        pltpu.make_async_copy(h2_s.at[r], dmix_o.at[r], osem.at[8 + i]).start()
        ones_bd = jnp.where(head_mask(), 1.0, 0.0).astype(BF16)
        for g in range(NG):
            dm = dmix[:, gs(g)]
            f = f_s[r, gs(g)]
            df = dot_nt(dm, wbd[g])
            gwacc[g] += dot_tn(f, dm)
            ff32 = f.astype(F32)
            prod = df * ff32
            hi, lo = split(prod)
            ds = (ff32 * (df - (dot(hi, ones_bd) + dot(lo, ones_bd)))).astype(BF16)
            da_s[r, gs(g)] = dot(ds, bdk[g]).astype(BF16)
            dktacc[g] += dot_tn(ds, q_s[r, gs(g)])
        pltpu.make_async_copy(da_s.at[r], dqf_o.at[r], osem.at[12 + i]).start()
        return 0

    lax.fori_loop(0, 4, after, 0)

    def grad_o(j, _):
        cols = pl.ds(pl.multiple_of(j * HALF_D, HALF_D), HALF_D)
        wo_s[cols, :] = dot_tn(mix_s[:, cols], dy_s[...]).astype(BF16)
        return 0

    lax.fori_loop(0, d // HALF_D, grad_o, 0)
    stored.append(pltpu.make_async_copy(wo_s, g_o.at[2 * (PARTS - first_out)], osem.at[20]))
    stored[-1].start()
    for g in range(NG):
        put_tall(gw_ref, g, collect(gwacc[g]))
        dkt_ref[:, gs(g)] = collect(dktacc[g])
    if gw_ref.shape[0] > 6 * M:
        gw_ref[6 * M :] = jnp.zeros((gw_ref.shape[0] - 6 * M, 128), F32)
    dg_ref[...] = jnp.broadcast_to(jnp.sum(dgacc[...], axis=0, keepdims=True), dg_ref.shape)
    if ring:
        t_ud[2] = scatters[2].total(0)
        for sc in scatters:
            sc.finish()
    for i in range(4):
        for b, src, dst in ((0, x1_s, out_o), (4, dy_s, dx_o), (8, h2_s, dmix_o), (12, da_s, dqf_o)):
            pltpu.make_async_copy(src.at[here(i)], dst.at[here(i)], osem.at[b + i]).wait()
    for c in stored:
        c.wait()


def middle(x, dy, f, q, conv, wo, ud, ud_own, gains, mk, uz, p, gw_rows, n):
    ring = ud_own is not None
    t, d = x.shape
    big = sds((t, d), BF16)
    outs = [big] * 4 + [sds((3 if ring else 2 * PARTS + 1, d, d), BF16)]
    outs += [sds((gw_rows, 128), F32), sds((M, d), F32), sds((8, d), F32)]
    extra = []
    if ring:
        cell = (2, d // CHIPS, d // 2)
        outs += [sds((PARTS - 1, *cell), F32)]
        extra = GatherMesh.scratch(1) * (PARTS - 1) + ScatterMesh.scratch([(cell, BF16)], True) * (PARTS - 1)
    square = pltpu.VMEM((NG, GROUP, GROUP), BF16)
    square_f = pltpu.VMEM((NG, GROUP, GROUP), F32)
    return pl.pallas_call(
        functools.partial(middle_kernel, n=n, ring=ring),
        in_specs=[ANYW] * 7 + [VM] * (5 if ring else 4),
        out_specs=[ANYW] * 5 + [VM] * (len(outs) - 5),
        out_shape=outs,
        scratch_shapes=[pltpu.VMEM((t, d), BF16)] * 7
        + [
            pltpu.VMEM((d, d), BF16),
            pltpu.VMEM((PARTS, 2, d, d), BF16),
            pltpu.VMEM((t, d), F32),
            pltpu.VMEM((t, d), F32),
            square,
            square,
            square_f,
            square_f,
            pltpu.VMEM((8, d), F32),
            DMA((8,)),
            DMA((21,)),
        ]
        + extra,
        compiler_params=pltpu.CompilerParams(
            collective_id=4 if ring else None, has_side_effects=True, vmem_limit_bytes=61 * 1024 * 1024
        ),
        name="middle",
    )(x, dy, f, q, conv, wo, ud, *((ud_own,) if ring else ()), gains, mk, uz, p)


def rear_kernel(*refs, n, ring, seg_len):
    take = Refs(refs)
    bodies = take(5)
    x_a, dx_a, h1_a, w_a = take(4)
    if ring:
        grads = take(1)
    gw_part, uz, a_ref, z_ref, az_ref, t2_ref, t3_ref, mq, mk, vl, vr, taps, dkt_ref, dg2_ref, gains = take(15)
    if ring:
        t_ud = take.one()
    ig_o, gvec_o, gqkv_o, dg_o = take(4)
    if ring:
        r_uo, r_down, r_vec, r_qkv = take(4)
    v_s, g_s, e_s, k_s, dqf_s, dqkv, gvec = take(7)
    vext, gext, tapacc, gl, gr, gw, gz, da, dubd, rowadd, dqtacc, bdq, pay, slots, own = take(15)
    w_s, gqkv, part, dslots, dgacc, gsem = take(6)
    isem, osem, hsem, wsem = take(4)
    sum_bufs = take(3)
    me = lax.axis_index("seq")
    t, d = v_s.shape
    loads = [
        pltpu.make_async_copy(b, s, isem.at[i]) for i, (b, s) in enumerate(zip(bodies, (v_s, g_s, e_s, k_s, dqf_s)))
    ]
    for c in loads:
        c.start()
    load_x = pltpu.make_async_copy(x_a, v_s, isem.at[5])
    load_dx = pltpu.make_async_copy(dx_a, g_s, isem.at[6])
    load_h1 = pltpu.make_async_copy(h1_a, e_s, isem.at[7])
    load_w = pltpu.make_async_copy(w_a, w_s, isem.at[8])
    load_w.start()
    if ring:
        place = Place()
        greet(me, n, [place.twin])
        big = ScatterMesh.take(take, place, (STACK,), grads)
        vec = ScatterMesh.take(take, place, (LINES,), (gvec,))
        late = ScatterMesh.take(take, place, (HALF,) * 3, [gqkv.at[i] for i in range(3)], in_place=True)
        fuo, fd, fq, fsem = take(4)
    else:
        greet(me, n, [])
    summing = SeqSum(me, n, gw_part, gw, *sum_bufs)
    loads[1].wait()
    halos = halo_copies(g_s, gl, gr, me, n, hsem)
    for c in halos:
        c.start()
    summing.start()
    if ring:
        big.start()

    def tick(cond, *acts):
        if ring:

            @pl.when(cond)
            def _():
                for act, k in acts:
                    act(k)

    tapacc[...] = jnp.zeros_like(tapacc)
    loads[0].wait()
    if not ring:
        big = vec = None
    far = (lambda k: big.far(k))
    mid = (lambda k: big.mid(k))
    near = (lambda k: big.near(k))

    def inner(i, _):
        fill_inner(vext, v_s, i * CTILE)
        fill_inner(gext, g_s, i * CTILE)
        conv_backward(vext, gext, taps, dqkv, tapacc, i * CTILE)


        @pl.when(i == 2)
        def _():
            summing.turn()

        tick(i == 2, (far, 0))
        return 0

    beside = NSITER // 2
    split_at = t // CTILE - 1 - beside
    lax.fori_loop(1, split_at, inner, 0)
    for c in halos:
        c.wait()
    mask_halos(gl, gr, me, n)

    def edge(i, _):
        fill_edge(vext, v_s, vl, vr, i == 0)
        fill_edge(gext, g_s, gl, gr, i == 0)
        conv_backward(vext, gext, taps, dqkv, tapacc, i * (t - CTILE))
        return 0

    lax.fori_loop(0, 2, edge, 0)
    summing.finish()
    for g in range(NG):
        z = zt_group(uz, g)
        bv = u_group(uz, g) / z
        gwg = u_group(gw, g)
        gz[:, gs(g)] = flip(dot_nt(gwg, spread(bv), HI))
        dbv = dot(flip(z_ref[NSITER, :, gs(g)]), spread(gwg), HI)
        dubd[g] = spread(dbv / z).astype(BF16)
        rowadd[g] = dot_nt(jnp.ones((8, GROUP), F32), spread(dbv * bv / z), HI)
        bdq[g] = spread(mq[:, gs(g)])
    da[...] = jnp.zeros_like(da)

    def newton(j, _):
        row0 = pl.multiple_of((split_at + lax.div(j, 2)) * CTILE, CTILE)

        @pl.when(lax.rem(j, 2) == 0)
        def _():
            fill_inner(vext, v_s, row0)
            fill_inner(gext, g_s, row0)

        base = lax.rem(j, 2) * (CTILE // 2)
        for h in range(2):
            conv_back_chunk(vext, gext, taps, dqkv, tapacc, row0, pl.multiple_of(base + h * CHUNK, CHUNK))
        pinv_back_step(NSITER - 1 - j, a_ref, z_ref, az_ref, t2_ref, t3_ref, gz, da)
        tick(j == 0, (mid, 0))
        tick(j == 3, (near, 0))
        return 0

    lax.fori_loop(0, NSITER, newton, 0)
    load_dx.start()
    dtap = jnp.sum(tapacc[...], axis=1)
    lines = jnp.concatenate([jnp.zeros((1, d), F32), dg2_ref[0:1, :], dtap, jnp.zeros((128 - 42, d), F32)], axis=0)
    gvec[...] = jnp.transpose(lines)
    if ring:
        vec.start()
    else:
        save_vec = pltpu.make_async_copy(gvec, gvec_o, osem.at[1])
        save_vec.start()
    loads[2].wait()
    loads[3].wait()
    dqtacc[...] = jnp.zeros_like(dqtacc)

    def cols(part, g):
        return slice(part * d + g * GROUP, part * d + (g + 1) * GROUP)

    def through(i, _):
        here = pl.ds(pl.multiple_of(i * (t // 4), t // 4), t // 4)
        for g in range(NG):
            e = e_s[here, gs(g)]
            de = dot_nt(v_s[here, gs(g)], dubd[g]) - rowadd[g, 0:1, :]
            ds = (e.astype(F32) * de).astype(BF16)
            dqkv[here, cols(2, g)] = (dot(e, dubd[g]) + dqkv[here, cols(2, g)].astype(F32)).astype(BF16)
            dqkv[here, cols(1, g)] = dot(ds, bdq[g]).astype(BF16)
            dqtacc[g] += dot_tn(ds, k_s[here, gs(g)])
        tick(i == 0, (lambda k: vec.far(k), 0))
        tick(i == 2, (lambda k: vec.mid(k), 0))
        return 0

    lax.fori_loop(0, 4, through, 0)
    load_x.start()
    load_h1.start()

    rows_dev = max(M // n, 1)
    per_mark = n * rows_dev // M
    if rows_dev < 4:
        pay[...] = jnp.zeros_like(pay)
    for g in range(NG):
        ds = pinv_back_end(g, a_ref, gz, da)
        dq = collect(dqtacc[g]) + dot(ds, spread(mk[:, gs(g)].astype(F32)), HI) * (1.0 / n)
        dk = dkt_ref[:, gs(g)] + dot(flip(ds), spread(mq[:, gs(g)].astype(F32)), HI) * (1.0 / n)
        for i in range(n):
            row = i * rows_dev // per_mark
            pay[i, 0:rows_dev, gs(g)] = dq[row : row + rows_dev]
            pay[i, 4 : 4 + rows_dev, gs(g)] = dk[row : row + rows_dev]

    def mark(j, peer):
        return remote(pay.at[peer], slots.at[me], wsem.at[0, j], wsem.at[1, j], {"seq": peer})

    each_peer(me, n, mark, lambda c: c.start())
    slots[pl.ds(me, 1)] = pay[pl.ds(me, 1)]

    def project_back(p, scale):
        def body(j, _):
            cols = pl.ds(pl.multiple_of(j * HALF_D, HALF_D), HALF_D)
            gqkv[p, cols, :] = (dot_tn(e_s[:, cols], dqkv[:, p * d : (p + 1) * d]) * scale).astype(BF16)
            return 0

        lax.fori_loop(0, d // HALF_D, body, 0)
        if ring:
            late.start((p,))

    load_h1.wait()
    project_back(2, 1.0)
    if ring:
        last_ud = big.total(0)
        for p in range(PARTS - 1):
            fuo[p] = t_ud[p, 0]
            fd[p] = t_ud[p, 1]
        fuo[PARTS - 1] = last_ud[0]
        fd[PARTS - 1] = last_ud[1]
        fuo[PARTS] = last_ud[2]
        cols = at(place.rep, d // 2, 128)
        back = [swap_rows(fuo, r_uo, place, fsem.at[0])]
        for j in range(2):
            r_down[j, :, cols] = fd[2 * place.rep + j]
            src = fd.at[2 * (1 - place.rep) + j]
            back.append(remote(src, r_down.at[j, :, cols], fsem.at[1 + j, 0], fsem.at[1 + j, 1], place.twin))
        for c in back:
            c.start()
        vec.near(0)
        late.far(2)
    loads[4].wait()
    each_peer(me, n, mark, lambda c: c.wait())
    own[...] = lax.fori_loop(1, n, lambda i, acc: acc + slots[i], slots[0]) * (1.0 / seg_len)

    def landed(i, _):
        here = pl.ds(pl.multiple_of(i * (t // 4), t // 4), t // 4)
        row = lax.div(i * rows_dev, 4)
        dqkv[here, 0:d] = (dqf_s[here, :].astype(F32) + own[pl.ds(row, 1), :]).astype(BF16)
        dqkv[here, d : 2 * d] = (dqkv[here, d : 2 * d].astype(F32) + own[pl.ds(row + 4, 1), :]).astype(BF16)
        return 0

    lax.fori_loop(0, 4, landed, 0)
    project_back(1, QK_SCALE)
    project_back(0, QK_SCALE)
    tick(True, (lambda k: late.far(k), 1), (lambda k: late.far(k), 0), (lambda k: late.mid(k), 2))
    for c in (load_w, load_x, load_dx):
        c.wait()
    dgacc[...] = jnp.zeros_like(dgacc)

    def back_through(i, _):
        here = pl.ds(pl.multiple_of(i * (t // 4), t // 4), t // 4)
        dq, dk, dv = (dqkv[here, p * d : (p + 1) * d] for p in range(3))
        dh = (dot_nt(dq, w_s[0]) + dot_nt(dk, w_s[1])) * QK_SCALE + dot_nt(dv, w_s[2])
        normal, inv = normalize(v_s[here, :].astype(F32))
        dgacc[...] += rowsum8(dh * normal)
        ig = norm_back(dh, normal, inv, gains[0:1, :]) + g_s[here, :].astype(F32)
        v_s[here, :] = ig.astype(BF16)
        pltpu.make_async_copy(v_s.at[here], ig_o.at[here], osem.at[2 + i]).start()
        tick(i == 1, (lambda k: late.near(k), 2), (lambda k: late.mid(k), 1))
        tick(i == 2, (lambda k: late.mid(k), 0))
        return 0

    lax.fori_loop(0, 4, back_through, 0)
    row = jnp.sum(dgacc[...], axis=0, keepdims=True)
    part[...] = jnp.concatenate(
        [row[:, c : c + 128] for c in range(0, d, 128)] + [jnp.zeros((8 - d // 128, 128), F32)], axis=0
    )

    def send(j, peer):
        return remote(part, dslots.at[me], gsem.at[0, j], gsem.at[1, j], {"seq": peer})

    each_peer(me, n, send, lambda c: c.start())
    dslots[pl.ds(me, 1)] = part[...][None]
    tick(True, (lambda k: late.near(k), 1), (lambda k: late.near(k), 0))
    each_peer(me, n, send, lambda c: c.wait())
    total = lax.fori_loop(1, n, lambda i, acc: acc + dslots[i], dslots[0])
    dg_o[0] = total
    if ring:
        twin_sum = remote(dg_o.at[0], dg_o.at[1], gsem.at[0, 0], gsem.at[1, 0], place.twin)
        twin_sum.start()
        r_vec[...] = vec.total(0)
        for p in (2, 1, 0):
            fq[p] = late.total(p)
        back.append(swap_rows(fq, r_qkv, place, fsem.at[3]))
        back[-1].start()
        twin_sum.wait()
        big.finish()
        vec.finish()
        late.finish()
        for c in back:
            c.wait()
    else:
        dg_o[1] = jnp.zeros_like(total)
        save_vec.wait()
        save_g = pltpu.make_async_copy(gqkv, gqkv_o, osem.at[0])
        save_g.start()
        save_g.wait()
    for i in range(4):
        here = pl.ds(i * (t // 4), t // 4)
        pltpu.make_async_copy(v_s.at[here], ig_o.at[here], osem.at[2 + i]).wait()


def rear(bodies, more, grads, gw, uz, a, z, az, t2, t3, mq, mk, vl, vr, taps, dkt, dg2, gains, t_ud, n, seg_len):
    ring = grads is not None
    t, d = bodies[0].shape
    r = gw.shape[0]
    outs = [sds((t, d), BF16), sds((d, 128), F32), sds((3, d, d), BF16), sds((2, 8, 128), F32)]
    extra = []
    if ring:
        own = d // (2 * CHIPS)
        outs += [sds((PARTS + 1, own, d), F32), sds((2, 2 * own, d), F32), sds((own, 128), F32), sds((3, own, d), F32)]
        extra = ScatterMesh.scratch([((3, 2 * own, d // 2), BF16)]) + ScatterMesh.scratch([((own, 128), F32)])
        extra += ScatterMesh.scratch([((2 * own, d // 2), BF16)] * 3, True) + [
            pltpu.VMEM((PARTS + 1, 2 * own, d // 2), F32),
            pltpu.VMEM((PARTS, 2 * own, d // 2), F32),
            pltpu.VMEM((3, 2 * own, d // 2), F32),
            DMA((4, 2)),
        ]
    ext = pltpu.VMEM((d // 128, CTILE + 2 * RAD, 128), F32)
    halo = pltpu.VMEM((RAD, d), BF16)
    small = pltpu.VMEM((M, d), F32)
    return pl.pallas_call(
        functools.partial(rear_kernel, n=n, ring=ring, seg_len=seg_len),
        in_specs=[ANYW] * (9 + (1 if ring else 0)) + [VM] * (15 + (1 if ring else 0)),
        out_specs=[ANYW] * 3 + [VM] * (len(outs) - 3),
        out_shape=outs,
        scratch_shapes=[pltpu.VMEM((t, d), BF16)] * 5
        + [
            pltpu.VMEM((t, 3 * d), BF16),
            pltpu.VMEM((d, 128), F32),
            ext,
            ext,
            pltpu.VMEM((40, 8, d), F32),
            halo,
            halo,
            pltpu.VMEM((r, 128), F32),
            small,
            small,
            pltpu.VMEM((NG, GROUP, GROUP), BF16),
            pltpu.VMEM((NG, 8, GROUP), F32),
            pltpu.VMEM((NG, GROUP, GROUP), F32),
            pltpu.VMEM((NG, GROUP, GROUP), BF16),
            pltpu.VMEM((n, 8, d), F32),
            pltpu.VMEM((n, 8, d), F32),
            pltpu.VMEM((8, d), F32),
            pltpu.VMEM((3, d, d), BF16),
            pltpu.VMEM((3, d, d), BF16),
            pltpu.VMEM((8, 128), F32),
            pltpu.VMEM((n, 8, 128), F32),
            pltpu.VMEM((8, d), F32),
            DMA((2, n)),
            DMA((9,)),
            DMA((6,)),
            DMA((4,)),
            DMA((2, n)),
        ]
        + SeqSum.scratch(r, n)
        + extra,
        compiler_params=pltpu.CompilerParams(
            collective_id=2, has_side_effects=True, vmem_limit_bytes=61 * 1024 * 1024
        ),
        name="rear",
    )(*bodies, *more, *(grads if ring else ()), gw, uz, a, z, az, t2, t3, mq, mk, vl, vr, taps, dkt, dg2, gains, *((t_ud,) if ring else ()))


def adam_into(grad, at_in, at_out, rate):
    w, m, v = at_in
    moment = BETA_ONE * m[...] + (1.0 - BETA_ONE) * grad
    second = BETA_TWO * v[...] + (1.0 - BETA_TWO) * grad * grad
    first_hat = moment * (1.0 / (1.0 - BETA_ONE**STEP))
    second_hat = second * (1.0 / (1.0 - BETA_TWO**STEP))
    at_out[0][...] = w[...] - rate * (first_hat / (jnp.sqrt(second_hat) + ADAM_EPS) + DECAY_RATE * w[...])
    at_out[1][...] = moment
    at_out[2][...] = second


def adam_kernel(*refs):
    take = Refs(refs)
    held = take(2)
    r_qkv, r_uo, r_down = take(3)
    attn, up, down = take(3), take(3), take(3)
    given = take(2)
    attn_n, up_n, down_n = take(3), take(3), take(3)
    sem = take.one()
    block = held[0].shape[0] // 4
    moves = []
    for j, (a, b) in enumerate(zip(held, given)):
        for i in range(4):
            part = pl.ds(i * block, block)
            moves.append(pltpu.make_async_copy(a.at[part], b.at[part], sem.at[j, i]))
    for c in moves:
        c.start()
    for i in range(4):
        grad = r_qkv[i] if i < 3 else r_uo[PARTS]
        adam_into(grad, [r.at[i] for r in attn], [r.at[i] for r in attn_n], LEARN_RATE)
    rows_chip = r_down.shape[1]
    wide = PARTS * rows_chip
    for c in range(0, up[0].shape[1], 2 * wide):
        got = [r_uo[p, :, (c + h * wide) // PARTS : (c + h * wide) // PARTS + rows_chip] for h in range(2) for p in range(PARTS)]
        cols = slice(c, c + 2 * wide)
        adam_into(jnp.concatenate(got, axis=1), [r.at[:, cols] for r in up], [r.at[:, cols] for r in up_n], LEARN_RATE)
    for j in range(2):
        rows_j = slice(j * rows_chip, (j + 1) * rows_chip)
        adam_into(r_down[j], [r.at[rows_j, :] for r in down], [r.at[rows_j, :] for r in down_n], LEARN_RATE)
    for c in moves:
        c.wait()


def adam_all(out, ig, r_qkv, r_uo, r_down, state):
    return pl.pallas_call(
        adam_kernel,
        in_specs=[ANYW] * 2 + [VM] * 12,
        out_specs=[ANYW] * 2 + [VM] * 9,
        out_shape=[sds(out.shape, BF16)] * 2 + [sds(x.shape, F32) for x in state],
        scratch_shapes=[DMA((2, 4))],
        compiler_params=pltpu.CompilerParams(vmem_limit_bytes=VMEM_LIMIT),
        name="adam_all",
    )(out, ig, r_qkv, r_uo, r_down, *state)


def adam_step(weight, grad_vec, moment, second, rate_value):
    moment_new = BETA_ONE * moment + (1.0 - BETA_ONE) * grad_vec
    second_new = BETA_TWO * second + (1.0 - BETA_TWO) * grad_vec * grad_vec
    first_hat = moment_new / (1.0 - BETA_ONE**STEP)
    second_hat = second_new / (1.0 - BETA_TWO**STEP)
    weight_new = weight - rate_value * (
        first_hat / (jnp.sqrt(second_hat) + ADAM_EPS) + DECAY_RATE * weight
    )
    return (weight_new, moment_new, second_new)


def per_device(tokens, cotangent, attn_w, w_up, w_down, vectors, attn_m, attn_v, up_m, up_v, down_m, down_v, vec_m, vec_v):
    both = ("seq", "rep")
    x = tokens[0]
    dy = cotangent[0]
    t, d = x.shape
    n = lax.axis_size("seq")
    seg_len = t * n // M
    ring = n == CHIPS and lax.axis_size("rep") == 2

    rown = d // n
    if ring:
        weights = (attn_w, w_up, w_down.reshape(2, rown, d), vectors)
    else:
        w_attn = lax.all_gather(attn_w.astype(BF16), both, axis=1, tiled=True)
        vec = lax.all_gather(vectors.astype(BF16), both, axis=0, tiled=True).astype(F32)
        weights = (w_attn[:3], jnp.pad(vec, ((0, 0), (0, 128 - vec.shape[1]))))
    (w_qkv, wo, ud, ud_own, gains, taps, h1, q, k, v, conv, f, e, mq, mk, uz, a, z, az, t2, t3, vl, vr, pinverse) = front(
        x, weights, n, ring
    )
    if not ring:
        w_qkv, wo = w_attn[:3], w_attn[3]
        up = lax.all_gather(w_up.astype(BF16), both, axis=0, tiled=True)
        down = lax.all_gather(w_down.astype(BF16), both, axis=0, tiled=True)
        ud = jnp.stack([jnp.transpose(up.reshape(d, PARTS, d), (1, 0, 2)), down.reshape(PARTS, d, d)], axis=1)
    else:
        ud = ud[None]
    res = middle(x, dy, f, q, conv, wo, ud, ud_own, gains, mk, uz, pinverse, padded_rows(6 * M, n), n)
    out, dx, dmix, dqf, g_last, gw, dkt, dg2 = res[:8]
    res = rear(
        (v, dmix, e, k, dqf),
        (x, dx, h1, w_qkv),
        (g_last,) if ring else None,
        gw, uz, a, z, az, t2, t3, mq, mk, vl, vr, taps, dkt, dg2, gains,
        res[8] if ring else None,
        n, seg_len,
    )
    ig, g_vec, g_qkv, dg = res[:4]
    dg1 = (dg[0] + dg[1])[: d // 128].reshape(d)
    if ring:
        r_uo, r_down, red_vec, r_qkv = res[4:]
        own = d // (2 * n)
        start = (lax.axis_index("seq") * 2 + lax.axis_index("rep")) * own
        dg1_own = lax.dynamic_slice_in_dim(dg1, start, own, 0)
        red_vec = jnp.concatenate([dg1_own[:, None], red_vec[:, 1 : vectors.shape[1]]], axis=1)
        state = (attn_w, attn_m, attn_v, w_up, up_m, up_v, w_down, down_m, down_v)
        out, ig, *news = adam_all(out, ig, r_qkv, r_uo, r_down, state)
    else:
        g_attn = jnp.concatenate([g_qkv, g_last[2 * PARTS :]], axis=0)
        g_pairs = g_last[: 2 * PARTS].reshape(PARTS, 2, d, d)
        g_up = jnp.transpose(g_pairs[:, 0], (1, 0, 2)).reshape(d, PARTS * d)
        g_down = g_pairs[:, 1].reshape(PARTS * d, d)
        red_attn = lax.psum_scatter(g_attn, both, scatter_dimension=1, tiled=True).astype(F32)
        red_up = lax.psum_scatter(g_up, both, scatter_dimension=0, tiled=True).astype(F32)
        red_down = lax.psum_scatter(g_down, both, scatter_dimension=0, tiled=True).astype(F32)
        g_vec = jnp.concatenate([dg1[:, None] / n, g_vec[:, 1 : vectors.shape[1]]], axis=1)
        red_vec = lax.psum_scatter(g_vec, both, scatter_dimension=0, tiled=True)
        news = (
            *adam_step(attn_w, red_attn, attn_m, attn_v, LEARN_RATE),
            *adam_step(w_up, red_up, up_m, up_v, LEARN_RATE),
            *adam_step(w_down, red_down, down_m, down_v, LEARN_RATE),
        )
    return (out[None], ig[None], *news, *adam_step(vectors, red_vec, vec_m, vec_v, VECTOR_RATE))


def solution(mesh):
    tok = P("rep", "seq", None)
    att = P(None, ("seq", "rep"), None)
    mat = P(("seq", "rep"), None)
    return jax.shard_map(
        per_device,
        mesh=mesh,
        in_specs=(tok, tok, att, mat, mat, mat, att, att, mat, mat, mat, mat, mat, mat),
        out_specs=(tok, tok, att, att, att) + (mat,) * 9,
        check_vma=False,
    )
```

```python
import functools

import jax
import jax.numpy as jnp
from jax import lax
from jax.experimental import pallas as pl
from jax.experimental.pallas import tpu as pltpu
from jax.sharding import PartitionSpec as P

H = 12
HD = 64
M = 64
KC = 33
NSITER = 6
STEP = 10
EPS_NORM = 1e-05
BETA_ONE = 0.9
BETA_TWO = 0.999
ADAM_EPS = 1e-08
LEARN_RATE = 0.03
VECTOR_RATE = 0.15
DECAY_RATE = 0.1

F32 = jnp.float32
BF16 = jnp.bfloat16
GROUP = 256
NG = 3
RAD = 16
QK_SCALE = HD ** (-0.25)
HI = lax.Precision.HIGHEST
VMEM_LIMIT = 58 * 1024 * 1024


def dot(a, b, precision=None):
    return lax.dot_general(a, b, (((1,), (0,)), ((), ())), precision=precision, preferred_element_type=F32)


def dot_nt(a, b, precision=None):
    return lax.dot_general(a, b, (((1,), (1,)), ((), ())), precision=precision, preferred_element_type=F32)


def dot_tn(a, b, precision=None):
    return lax.dot_general(a, b, (((0,), (0,)), ((), ())), precision=precision, preferred_element_type=F32)


def split(x):
    hi = x.astype(BF16)
    return hi, (x - hi.astype(F32)).astype(BF16)


def dot3(a, b):
    return dot(a[0], b[0]) + (dot(a[0], b[1]) + dot(a[1], b[0]))


def spread2(a):
    return spread(a[0]), spread(a[1])


def head_mask(shape=(GROUP, GROUP)):
    rows = lax.broadcasted_iota(jnp.int32, shape, 0)
    cols = lax.broadcasted_iota(jnp.int32, shape, 1)
    return lax.shift_right_logical(rows, 6) == lax.shift_right_logical(cols, 6)


def spread(wide):
    tall = jnp.concatenate([wide, wide, wide, wide], axis=0)
    return jnp.where(head_mask(), tall, jnp.zeros_like(tall))


def collect(full):
    kept = jnp.where(head_mask(), full, jnp.zeros_like(full))
    return (kept[0:64] + kept[64:128]) + (kept[128:192] + kept[192:256])


def flip(wide):
    turned = jnp.transpose(spread(wide))
    return (turned[0:64] + turned[64:128]) + (turned[128:192] + turned[192:256])


def gs(g):
    return slice(g * GROUP, (g + 1) * GROUP)


def half_reduce(x, op, init):
    parts = []
    for c in range(x.shape[1] // 128):
        col = x[:, c * 128 : (c + 1) * 128]
        low = lax.broadcasted_iota(jnp.int32, col.shape, 1) < 64
        a = op(jnp.where(low, col, init), axis=1, keepdims=True)
        b = op(jnp.where(low, init, col), axis=1, keepdims=True)
        parts.append(jnp.where(low, a, b))
    return jnp.concatenate(parts, axis=1)


def normalize(x):
    center = x - jnp.mean(x, axis=-1, keepdims=True)
    inv = lax.rsqrt(jnp.mean(center * center, axis=-1, keepdims=True) + EPS_NORM)
    return center * inv, inv


def norm_back(up, normal, inv, gain):
    scaled = up * gain
    centered = scaled - jnp.mean(scaled, axis=-1, keepdims=True)
    return inv * (centered - normal * jnp.mean(scaled * normal, axis=-1, keepdims=True))


def rowsum8(x):
    return jnp.sum(x.reshape(x.shape[0] // 8, 8, x.shape[1]), axis=0)


def gelu_parts(a):
    z = jnp.abs(a)
    t = 1.0 / (1.0 + (0.3275911 * 0.7071067811865476) * z)
    e = jnp.exp(-0.5 * a * a)
    poly = t * (0.127414796 + t * (-0.142248368 + t * (0.7107068705 + t * (-0.7265760135 + t * 0.5307027145))))
    tail = poly * e
    phi = jnp.where(a >= 0, 1.0 - tail, tail)
    return a * phi, phi + a * (e * 0.3989422804014327)


def whole(shape):
    zeros = (0,) * len(shape)
    return pl.BlockSpec(shape, lambda i: zeros, pipeline_mode=pl.Buffered(1))


def rows(tile, width):
    return pl.BlockSpec((tile, width), lambda i: (i, 0))


def sds(shape, dtype):
    return jax.ShapeDtypeStruct(shape, dtype)


def params():
    return pltpu.CompilerParams(dimension_semantics=("arbitrary",), vmem_limit_bytes=VMEM_LIMIT)


def widen(zt, g):
    return jnp.concatenate(
        [jnp.broadcast_to(zt[:, h : h + 1], (M, HD)) for h in range(4 * g, 4 * g + 4)], axis=1
    )


def u_group(ref, g):
    return jnp.concatenate([ref[2 * g * M : (2 * g + 1) * M, :], ref[(2 * g + 1) * M : (2 * g + 2) * M, :]], axis=1)


def zt_group(ref, g):
    return widen(ref[6 * M : 7 * M, :], g)


def put_tall(ref, g, wide):
    ref[2 * g * M : (2 * g + 1) * M, :] = wide[:, :128]
    ref[(2 * g + 1) * M : (2 * g + 2) * M, :] = wide[:, 128:]


def padded_rows(r, n):
    return -(-r // (8 * n)) * 8 * n


MESH = pl.DeviceIdType.MESH
DMA = pltpu.SemaphoreType.DMA
VM = pl.BlockSpec(memory_space=pltpu.VMEM)
ANYW = pl.BlockSpec(memory_space=pl.ANY)


def remote(src, dst, send, recv, where):
    return pltpu.make_async_remote_copy(
        src_ref=src, dst_ref=dst, send_sem=send, recv_sem=recv, device_id=where, device_id_type=MESH
    )


def greet(me, n, others):
    bar = pltpu.get_barrier_semaphore()

    def hello(j, _):
        pl.semaphore_signal(bar, inc=1, device_id={"seq": lax.rem(me + j, n)}, device_id_type=MESH)
        return 0

    lax.fori_loop(1, n, hello, 0)
    for peer in others:
        pl.semaphore_signal(bar, inc=1, device_id=peer, device_id_type=MESH)
    pl.semaphore_wait(bar, n - 1 + len(others))


def each_peer(me, n, make, act):
    def body(j, _):
        act(make(j, lax.rem(me + j, n)))
        return 0

    lax.fori_loop(1, n, body, 0)


def halo_copies(body_ref, left_ref, right_ref, me, n, sems):
    t = body_ref.shape[0]
    right = {"seq": lax.rem(me + 1, n)}
    left = {"seq": lax.rem(me + n - 1, n)}
    return (
        remote(body_ref.at[pl.ds(t - RAD, RAD)], left_ref, sems.at[0], sems.at[1], right),
        remote(body_ref.at[pl.ds(0, RAD)], right_ref, sems.at[2], sems.at[3], left),
    )


def mask_halos(left_ref, right_ref, me, n):
    left_ref[...] = jnp.where(me > 0, left_ref[...], jnp.zeros_like(left_ref))
    right_ref[...] = jnp.where(me < n - 1, right_ref[...], jnp.zeros_like(right_ref))


class SeqSum:
    def __init__(self, me, n, x, out, slots, total, sems):
        self.me, self.n, self.x, self.out, self.slots, self.total, self.sems = me, n, x, out, slots, total, sems
        self.chunk = x.shape[0] // n
        self.here = pl.ds(pl.multiple_of(me * self.chunk, 8), self.chunk)

    def first(self, j, peer):
        src = self.x.at[pl.ds(pl.multiple_of(peer * self.chunk, 8), self.chunk)]
        return remote(src, self.slots.at[self.me], self.sems.at[0, j], self.sems.at[1, j], {"seq": peer})

    def second(self, j, peer):
        return remote(self.total, self.out.at[self.here], self.sems.at[2, j], self.sems.at[3, j], {"seq": peer})

    def start(self):
        each_peer(self.me, self.n, self.first, lambda c: c.start())
        self.slots[pl.ds(self.me, 1)] = self.x[self.here, :][None]

    def turn(self):
        each_peer(self.me, self.n, self.first, lambda c: c.wait())
        summed = lax.fori_loop(1, self.n, lambda i, acc: acc + self.slots[i], self.slots[0])
        self.total[...] = summed
        each_peer(self.me, self.n, self.second, lambda c: c.start())
        self.out[self.here, :] = summed

    def finish(self):
        each_peer(self.me, self.n, self.second, lambda c: c.wait())

    @staticmethod
    def scratch(r, n):
        return [pltpu.VMEM((n, r // n, 128), F32), pltpu.VMEM((r // n, 128), F32), DMA((4, n))]


CHIPS = 16
STACK, HALF, ROWS, LINES = range(4)


def at(i, size, unit):
    return pl.ds(pl.multiple_of(i * size, unit), size)


def piece(kind, ref, seq, rep):
    if kind == STACK:
        half = ref.shape[2] // 2
        return ref.at[:, at(seq, ref.shape[1] // CHIPS, 16), at(rep, half, 128)]
    if kind == HALF:
        half = ref.shape[1] // 2
        return ref.at[at(seq, ref.shape[0] // CHIPS, 16), at(rep, half, 128)]
    return ref.at[at(seq * 2 + rep, ref.shape[0] // (2 * CHIPS), 8 if kind == LINES else 16), :]


class Place:
    def __init__(self):
        self.seq = lax.axis_index("seq")
        self.rep = lax.axis_index("rep")
        self.x = lax.rem(self.seq, 2)
        self.y = lax.rem(lax.div(self.seq, 2), 2)
        self.z = lax.div(self.seq, 4)
        self.twin = {"rep": 1 - self.rep}
        self.across = ({"seq": self.chip(4, self.rep)}, {"seq": self.chip(8, self.rep)})

    def chip(self, i, rep):
        j, b, a = lax.rem(i, 4), lax.rem(lax.div(i, 4), 2), lax.div(i, 8)
        z = lax.rem(self.z + 4 - j, 4)
        fx = a + rep * (b - a)
        fy = b + rep * (a - b)
        x = self.x + fx * (1 - 2 * self.x)
        y = self.y + fy * (1 - 2 * self.y)
        return z * 4 + y * 2 + x

    def above(self, j):
        return {"seq": self.chip(4 - j, self.rep)}

    def below(self, j):
        return {"seq": self.chip(j, self.rep)}


class GatherMesh:
    def __init__(self, place, kinds, outs, own, sems):
        self.place, self.kinds, self.outs, self.own = place, kinds, outs, own
        self.zsend, self.send1, self.send2, self.ssend, self.recv, self.srecv = sems

    def block(self, i, k, rep):
        return piece(self.kinds[k], self.outs[k], self.place.chip(i, rep), rep)

    def copy(self, i, k, send, recv, where):
        b = self.block(i, k, self.place.rep)
        src = b if self.own[k] is None or not (isinstance(i, int) and i == 0) else self.own[k]
        return remote(src, b, send, recv, where)

    def to_z(self, j, k):
        return self.copy(0, k, self.zsend.at[j, k], self.recv.at[j, k], self.place.above(j))

    def to_first(self, i, k):
        return self.copy(i, k, self.send1.at[i, k], self.recv.at[i + 4, k], self.place.across[0])

    def to_second(self, i, k):
        return self.copy(i, k, self.send2.at[i, k], self.recv.at[i + 8, k], self.place.across[1])

    def share(self, i, k):
        return self.copy(i, k, self.ssend.at[i, k], self.srecv.at[i, k], self.place.twin)

    def arrival(self, i, k):
        b = self.block(i, k, self.place.rep)
        return remote(b, b, self.ssend.at[i, k], self.recv.at[i, k], self.place.twin)

    def shared(self, i, k):
        b = self.block(i, k, 1 - self.place.rep)
        return remote(b, b, self.ssend.at[i, k], self.srecv.at[i, k], self.place.twin)

    def start_z(self):
        for k in range(len(self.kinds)):
            for j in (1, 2, 3):
                self.to_z(j, k).start()

    def start_across(self, which=None):
        for k in range(len(self.kinds)) if which is None else which:
            self.to_second(0, k).start()
            self.to_first(0, k).start()
            self.share(0, k).start()

    def each(self, low, high, which, act):
        def body(i, _):
            for k in which:
                act(i, k)
            return 0

        lax.fori_loop(low, high, body, 0)

    def line(self, which):
        def act(i, k):
            self.arrival(i, k).wait_recv()
            self.to_first(i, k).start()
            self.share(i, k).start()

        self.each(1, 4, which, act)

    def line_on(self, which):
        self.each(1, 4, which, lambda i, k: self.to_second(i, k).start())

    def plane(self, which):
        def act(i, k):
            self.arrival(i, k).wait_recv()
            self.to_second(i, k).start()
            self.share(i, k).start()

        self.each(4, 8, which, act)

    def space(self, which):
        def act(i, k):
            self.arrival(i, k).wait_recv()
            self.share(i, k).start()

        self.each(8, CHIPS, which, act)

    def shares_in(self, which):
        self.shared_first(which)
        self.each(1, CHIPS, which, lambda i, k: self.shared(i, k).wait_recv())

    def shared_first(self, which):
        for k in which:
            self.shared(0, k).wait_recv()

    def finish(self):
        which = range(len(self.kinds))
        for k in which:
            for j in (1, 2, 3):
                self.to_z(j, k).wait_send()
            self.to_first(0, k).wait_send()
            self.to_second(0, k).wait_send()
            self.share(0, k).wait_send()

        def act(i, k):
            @pl.when(i < 4)
            def _():
                self.to_first(i, k).wait_send()

            @pl.when(i < 8)
            def _():
                self.to_second(i, k).wait_send()

            self.share(i, k).wait_send()

        self.each(1, CHIPS, which, act)

    @staticmethod
    def scratch(k):
        return [DMA((4, k)), DMA((4, k)), DMA((8, k))] + [DMA((CHIPS, k))] * 3


class ScatterMesh:
    def __init__(self, place, kinds, grads, mine, twins, in2, in1, inz, sems):
        self.place, self.kinds, self.grads = place, kinds, grads
        self.mine, self.twins, self.in2, self.in1, self.inz = mine, twins, in2, in1, inz
        self.lsem, self.tsend, self.trecv, self.s2, self.r2, self.s1, self.r1, self.sz, self.rz = sems

    def source(self, i, k):
        return piece(self.kinds[k], self.grads[k], self.place.chip(i, self.place.rep), self.place.rep)

    def cell(self, i, k):
        return self.source(i, k) if self.mine is None else self.mine[k].at[i]

    def load(self, i, k):
        return pltpu.make_async_copy(self.source(i, k), self.mine[k].at[i], self.lsem.at[i, k])

    def give(self, i, k):
        other = 1 - self.place.rep
        src = piece(self.kinds[k], self.grads[k], self.place.chip(i, other), other)
        return remote(src, self.twins[k].at[i], self.tsend.at[i, k], self.trecv.at[i, k], self.place.twin)

    def out2(self, i, k):
        return remote(self.cell(i, k), self.in2[k].at[i - 8], self.s2.at[i - 8, k], self.r2.at[i - 8, k], self.place.across[1])

    def out1(self, i, k):
        return remote(self.cell(i, k), self.in1[k].at[i - 4], self.s1.at[i - 4, k], self.r1.at[i - 4, k], self.place.across[0])

    def outz(self, j, k):
        return remote(self.cell(j, k), self.inz[k].at[j], self.sz.at[j, k], self.rz.at[j, k], self.place.below(j))

    def start(self, which=None):
        for low in (8, 0):
            for k in range(len(self.kinds)) if which is None else which:

                def body(j, _):
                    self.give(low + 7 - j, k).start()
                    if self.mine is not None:
                        self.load(low + 7 - j, k).start()
                    return 0

                lax.fori_loop(0, 8, body, 0)

    def terms(self, i, k):
        if self.mine is not None:
            self.load(i, k).wait()
        self.give(i, k).wait()
        return self.cell(i, k)[...].astype(F32) + self.twins[k].at[i][...].astype(F32)

    def keep(self, i, k, value):
        cell = self.cell(i, k)
        cell[...] = value.astype(cell.dtype)

    def far(self, k):
        def body(j, _):
            i = CHIPS - 1 - j
            self.keep(i, k, self.terms(i, k))
            self.out2(i, k).start()
            return 0

        lax.fori_loop(0, 8, body, 0)

    def mid(self, k):
        def body(j, _):
            i = 7 - j
            own = self.terms(i, k)
            self.out2(i + 8, k).wait_recv()
            self.keep(i, k, own + self.in2[k].at[i][...].astype(F32))
            self.out1(i, k).start()
            return 0

        lax.fori_loop(0, 4, body, 0)

    def closer(self, i, k):
        own = self.terms(i, k)
        self.out2(i + 8, k).wait_recv()
        self.out1(i + 4, k).wait_recv()
        return own + (self.in2[k].at[i][...].astype(F32) + self.in1[k].at[i][...].astype(F32))

    def near(self, k):
        def body(j, _):
            i = 3 - j
            self.keep(i, k, self.closer(i, k))
            self.outz(i, k).start()
            return 0

        lax.fori_loop(0, 3, body, 0)

    def total(self, k):
        acc = self.closer(0, k)
        for j in (1, 2, 3):
            self.outz(j, k).wait_recv()
            acc = acc + self.inz[k][j].astype(F32)
        return acc

    def finish(self):
        for k in range(len(self.kinds)):

            def body(i, _):
                @pl.when(i >= 8)
                def _():
                    self.out2(i, k).wait_send()

                @pl.when((i >= 4) & (i < 8))
                def _():
                    self.out1(i, k).wait_send()

                @pl.when(i < 4)
                def _():
                    self.outz(i, k).wait_send()

                return 0

            lax.fori_loop(1, CHIPS, body, 0)

    @staticmethod
    def scratch(blocks, in_place=False):
        k = len(blocks)
        return (
            ([] if in_place else [pltpu.VMEM((CHIPS, *s), t) for s, t in blocks])
            + [pltpu.VMEM((CHIPS, *s), t) for s, t in blocks]
            + [pltpu.VMEM((8, *s), t) for s, t in blocks]
            + [pltpu.VMEM((4, *s), t) for s, t in blocks]
            + [pltpu.VMEM((4, *s), t) for s, t in blocks]
            + [DMA((CHIPS, k))] * 3
            + [DMA((8, k))] * 2
            + [DMA((4, k))] * 4
        )

    @staticmethod
    def take(take, place, kinds, grads, in_place=False):
        k = len(kinds)
        mine = None if in_place else take(k)
        bufs = [take(k) for _ in range(4)]
        return ScatterMesh(place, kinds, grads, mine, *bufs, take(9))


def swap_rows(total, out, place, sems):
    rows_own = total.shape[-2] // 2
    half = total.shape[-1]
    theirs, mine = at(1 - place.rep, rows_own, 8), at(place.rep, rows_own, 8)
    cols = at(place.rep, half, 128)
    if len(total.shape) == 3:
        out[:, :, cols] = total[:, mine, :]
        return remote(total.at[:, theirs, :], out.at[:, :, cols], sems.at[0], sems.at[1], place.twin)
    out[:, cols] = total[mine, :]
    return remote(total.at[theirs, :], out.at[:, cols], sems.at[0], sems.at[1], place.twin)


CHUNK = 64
CTILE = 256


def fill_inner(ext, body_ref, start):
    count = ext.shape[1]
    rows_in = pl.ds(pl.multiple_of(start - RAD, RAD), count)
    for c in range(ext.shape[0]):
        ext[c] = body_ref[rows_in, c * 128 : (c + 1) * 128].astype(F32)


def fill_edge(ext, body_ref, left_ref, right_ref, first):
    tile = ext.shape[1] - 2 * RAD
    t = body_ref.shape[0]
    start = pl.multiple_of(jnp.where(first, 0, t - tile), tile)
    for c in range(ext.shape[0]):
        cols = slice(c * 128, (c + 1) * 128)
        ext[c, RAD : RAD + tile, :] = body_ref[pl.ds(start, tile), cols].astype(F32)
        ext[c, 0:RAD, :] = jnp.where(first, left_ref[:, cols], body_ref[t - tile - RAD : t - tile, cols]).astype(F32)
        ext[c, RAD + tile :, :] = jnp.where(first, body_ref[tile : tile + RAD, cols], right_ref[:, cols]).astype(F32)


def conv_forward(ext, tap_ref, out, row0):
    def step(r, _):
        base = pl.multiple_of(r * CHUNK, CHUNK)
        for c in range(ext.shape[0]):
            cols = slice(c * 128, (c + 1) * 128)
            acc = jnp.zeros((CHUNK, 128), F32)
            for b in range(8):
                reach = 4 if b == 0 else 3
                win = ext[c, pl.ds(base + b, CHUNK + 8 * reach), :]
                for m in range(reach + 1):
                    o = 8 * m + b
                    acc = acc + tap_ref[o : o + 1, cols] * win[8 * m : 8 * m + CHUNK]
            out[pl.ds(pl.multiple_of(row0 + base, CHUNK), CHUNK), cols] = acc.astype(out.dtype)
        return 0

    lax.fori_loop(0, CTILE // CHUNK, step, 0)


def conv_back_chunk(vext, gext, tap_ref, out, tapacc, row0, base):
    width = out.shape[1] // 3
    for c in range(vext.shape[0]):
        cols = slice(c * 128, (c + 1) * 128)
        acc = jnp.zeros((CHUNK, 128), F32)
        here = gext[c, pl.ds(base + RAD, CHUNK), :]
        for b in range(8):
            reach = 4 if b == 0 else 3
            win = gext[c, pl.ds(base + b, CHUNK + 8 * reach), :]
            for m in range(reach + 1):
                o = KC - 1 - (8 * m + b)
                acc = acc + tap_ref[o : o + 1, cols] * win[8 * m : 8 * m + CHUNK]
            win = vext[c, pl.ds(base + b, CHUNK + 8 * reach), :]
            for m in range(reach + 1):
                o = 8 * m + b
                tapacc[o, :, cols] += rowsum8(here * win[8 * m : 8 * m + CHUNK])
        into = slice(2 * width + c * 128, 2 * width + (c + 1) * 128)
        out[pl.ds(pl.multiple_of(row0 + base, CHUNK), CHUNK), into] = acc.astype(out.dtype)


def conv_backward(vext, gext, tap_ref, out, tapacc, row0):
    def step(r, _):
        conv_back_chunk(vext, gext, tap_ref, out, tapacc, row0, pl.multiple_of(r * CHUNK, CHUNK))
        return 0

    lax.fori_loop(0, CTILE // CHUNK, step, 0)


def wide_eye():
    lane = lax.broadcasted_iota(jnp.int32, (M, GROUP), 1) & 63
    return jnp.where(lane == lax.broadcasted_iota(jnp.int32, (M, GROUP), 0), 1.0, 0.0)


def head_sums(row):
    ones = jnp.where(head_mask(), 1.0, 0.0)
    return dot(jnp.broadcast_to(row, (8, GROUP)), ones, HI)[0:1]


def pinv_begin(mq_ref, mk_ref, a_ref, z_ref):
    for g in range(NG):
        s = dot_nt(mq_ref[:, gs(g)], spread(mk_ref[:, gs(g)]))
        e = jnp.exp(s - half_reduce(s, jnp.max, -jnp.inf))
        a = e / half_reduce(e, jnp.sum, 0.0)
        a_ref[:, gs(g)] = a
        col = jnp.sum(a, axis=0, keepdims=True)
        z_ref[0, :, gs(g)] = flip(a) / jnp.sqrt(head_sums(col * col))


def pinv_step(it, a_ref, z_ref, az_ref, t2_ref, t3_ref):
    eye = wide_eye()
    R = range(NG)
    z = [split(z_ref[it, :, gs(g)]) for g in R]
    az = [dot3(split(a_ref[:, gs(g)]), spread2(z[g])) for g in R]
    azs = [split(az[g]) for g in R]
    t2 = [15.0 * eye - dot3(azs[g], spread2(split(7.0 * eye - az[g]))) for g in R]
    t3 = [13.0 * eye - dot3(azs[g], spread2(split(t2[g]))) for g in R]
    for g in R:
        z_ref[it + 1, :, gs(g)] = 0.25 * dot3(z[g], spread2(split(t3[g])))
        az_ref[it, :, gs(g)] = az[g]
        t2_ref[it, :, gs(g)] = t2[g]
        t3_ref[it, :, gs(g)] = t3[g]


def pinv_back_step(it, a_ref, z_ref, az_ref, t2_ref, t3_ref, gz_ref, da_ref):
    eye = wide_eye()
    R = range(NG)
    az = [az_ref[it, :, gs(g)] for g in R]
    zs = [split(z_ref[it, :, gs(g)]) for g in R]
    gzs = [split(0.25 * gz_ref[:, gs(g)]) for g in R]
    baz = [spread2(split(az[g])) for g in R]
    d3 = [split(dot3(gzs[g], spread2(zs[g]))) for g in R]
    d2 = [split(-dot3(d3[g], baz[g])) for g in R]
    d1 = [-dot3(d2[g], baz[g]) for g in R]
    daz = [
        split(
            -dot3(split(t2_ref[it, :, gs(g)]), spread2(d3[g]))
            - dot3(split(7.0 * eye - az[g]), spread2(d2[g]))
            - d1[g]
        )
        for g in R
    ]
    for g in R:
        da_ref[:, gs(g)] += dot3(zs[g], spread2(daz[g]))
        gz_ref[:, gs(g)] = dot3(split(t3_ref[it, :, gs(g)]), spread2(gzs[g])) + dot3(
            daz[g], spread2(split(a_ref[:, gs(g)]))
        )


def pinv_back_end(g, a_ref, gz_ref, da_ref):
    a = a_ref[:, gs(g)]
    gz = gz_ref[:, gs(g)]
    col = jnp.sum(a, axis=0, keepdims=True)
    bound = jnp.sqrt(head_sums(col * col))
    tot = head_sums(jnp.sum(gz * a, axis=0, keepdims=True))
    full = flip(da_ref[:, gs(g)]) + gz / bound - (tot / (bound * bound * bound)) * col
    return a * (full - half_reduce(full * a, jnp.sum, 0.0))


def gather_marks(slots, outs, n):
    per = 4 * n // M
    half = slots.shape[2]
    for out, base in zip(outs, (0, 4)):
        if per == 1:
            got = [slots[i].astype(F32) for i in range(n)]
            for h in range(2):
                tall = jnp.concatenate([x[8 * h + base : 8 * h + base + 4] for x in got], axis=0)
                out[:, h * half : (h + 1) * half] = tall.astype(BF16)
        else:
            for h in range(2):
                lines = []
                for m in range(M):
                    total = jnp.zeros((1, half), F32)
                    for s in range(per // 4):
                        part = slots[m * (per // 4) + s].astype(F32)[8 * h + base : 8 * h + base + 4]
                        total = total + jnp.sum(part, axis=0, keepdims=True)
                    lines.append(total * (1.0 / per))
                out[:, h * half : (h + 1) * half] = jnp.concatenate(lines, axis=0).astype(BF16)


class Refs:
    def __init__(self, refs):
        self.it = iter(refs)

    def __call__(self, count):
        return [next(self.it) for _ in range(count)]

    def one(self):
        return next(self.it)


def front_kernel(*refs, n, ring):
    take = Refs(refs)
    x_any = take.one()
    if ring:
        wa, wu, wd, wv = take(4)
        wqkv_o, wo_o, ud0_o, ud_own = take(4)
    else:
        wq, vec = take(2)
    gains, taps = take(2)
    outs = take(7)
    mq, mk, uz, a_ref, z_ref, az_ref, t2_ref, t3_ref, vl, vr, p_ref = take(11)
    xs = take.one()
    stage = take(7)
    h_s, q_s, k_s, v_s, conv_s, f_s, e_s = stage
    means, pay, slots, ext, bdk, bdq, uacc, zacc, upart = take(9)
    xsem, osem, msem, hsem = take(4)
    sum_bufs = take(3)
    me = lax.axis_index("seq")
    t, d = xs.shape
    half = d // 2
    load_x = pltpu.make_async_copy(x_any, xs, xsem.at[0])
    load_x.start()
    drains = [pltpu.make_async_copy(s, o, osem.at[i]) for i, (s, o) in enumerate(zip(stage, outs))]
    if ring:
        wq, vec, sa, su, sd, so, co, wperm, psem, lsem = take(10)
        ring_one, ring_two = take(6), take(6)
        place = Place()
        greet(me, n, [place.twin])
        rep, seq = place.rep, place.seq
        rows_own = d // (2 * CHIPS)
        mine = at(rep, rows_own, 8)
        theirs = 1 - rep
        swaps = [
            remote(wa.at[0:3, :, at(theirs, half, 128)], sa.at[:, mine, :], psem.at[0], psem.at[1], place.twin),
            remote(wa.at[3, :, at(theirs, half, 128)], so.at[mine, :], psem.at[2], psem.at[3], place.twin),
            remote(wd.at[:, :, at(theirs, half, 128)], sd.at[pl.ds(2 * rep, 2)], psem.at[6], psem.at[7], place.twin),
        ]
        for c in swaps:
            c.start()
        sa[:, mine, :] = wa[0:3, :, at(rep, half, 128)]
        so[mine, :] = wa[3, :, at(rep, half, 128)]
        sd[pl.ds(2 * rep, 2)] = wd[:, :, at(rep, half, 128)]
        vec[at(seq * 2 + rep, rows_own, 8), :] = jnp.zeros((rows_own, 128), F32)
        vec[at(seq * 2 + rep, rows_own, 8), 0 : wv.shape[1]] = wv[...]
        swaps[0].wait()
        wq[:, at(seq, 2 * rows_own, 16), at(rep, half, 128)] = sa[...].astype(BF16)
        first = GatherMesh(place, (LINES, HALF, HALF, HALF), (vec, wq.at[2], wq.at[1], wq.at[0]), (None,) * 4, ring_one)
        first.start_z()
        first.start_across((0, 1))
        rows_chip = 2 * rows_own
        for p in range(PARTS):
            for c in range(0, CHIPS, 8):
                got = [
                    wu[:, (PARTS * (c + h) + p) * rows_chip : (PARTS * (c + h) + p + 1) * rows_chip] for h in range(8)
                ]
                wperm[p, :, c * rows_chip : (c + 8) * rows_chip] = jnp.concatenate(got, axis=1)
        swaps.append(
            remote(wperm.at[:, :, at(theirs, half, 128)], su.at[:, mine, :], psem.at[4], psem.at[5], place.twin)
        )
        swaps[-1].start()
        su[:, mine, :] = wperm[:, :, at(rep, half, 128)]
        for c in swaps[1:]:
            c.wait()
        co[...] = so[...].astype(BF16)
        ud_own[:, 0] = su[...].astype(BF16)
        ud_own[:, 1] = sd[...].astype(BF16)
        rest = GatherMesh(place, (STACK, HALF), (ud0_o, wo_o), (ud_own.at[0], co), ring_two)
        local = [
            pltpu.make_async_copy(src, piece(kind, out, seq, rep), lsem.at[i])
            for i, (src, kind, out) in enumerate(zip(rest.own, rest.kinds, rest.outs))
        ]

        rest.start_z()
        for c in local:
            c.start()
        first.line((0, 1))
        first.line_on((0, 1))
        first.start_across((2, 3))
        first.plane((0, 1))
        for which in ((2,), (3,)):
            first.line(which)
            first.line_on(which)
        first.space((0,))
        first.shares_in((0,))
        save_w = pltpu.make_async_copy(wq, wqkv_o, xsem.at[1])
    else:
        greet(me, n, [])

    turned = jnp.transpose(vec[...]).astype(BF16).astype(F32)
    gains[...] = turned[0:8]
    taps[...] = turned[2:42]
    load_x.wait()

    def tile(i):
        return pl.ds(pl.multiple_of(i * (t // 4), t // 4), t // 4)

    def norm(i, _):
        normal, _inv = normalize(xs[tile(i), :].astype(F32))
        h_s[tile(i), :] = (normal * gains[0:1, :]).astype(BF16)
        return 0

    def project_v(i, _):
        v_s[tile(i), :] = dot(h_s[tile(i), :], wq[2]).astype(BF16)
        return 0

    def project_k(i, _):
        k = (dot(h_s[tile(i), :], wq[1]) * QK_SCALE).astype(BF16)
        k_s[tile(i), :] = k
        means[pl.ds(i + 4, 1), :] = jnp.mean(k.astype(F32), axis=0, keepdims=True)
        return 0

    def project_q(i, _):
        q = (dot(h_s[tile(i), :], wq[0]) * QK_SCALE).astype(BF16)
        q_s[tile(i), :] = q
        means[pl.ds(i, 1), :] = jnp.mean(q.astype(F32), axis=0, keepdims=True)
        return 0

    def inner(i, _):
        fill_inner(ext, v_s, i * CTILE)
        conv_forward(ext, taps, conv_s, i * CTILE)
        if ring:

            @pl.when(i == 4)
            def _():
                rest.line_on((0,))

            @pl.when(i == 5)
            def _():
                rest.line((1,))
                rest.line_on((1,))

        return 0

    tiles = t // CTILE
    lax.fori_loop(0, 4, norm, 0)
    if ring:
        first.plane((2,))
        first.space((1,))
        first.shares_in((1,))
    lax.fori_loop(0, 4, project_v, 0)
    halos = halo_copies(v_s, vl, vr, me, n, hsem)
    for c in halos:
        c.start()
    if ring:
        first.plane((3,))
        rest.start_across()
    lax.fori_loop(1, tiles // 2, inner, 0)
    if ring:
        first.space((2,))
        first.shares_in((2,))
    lax.fori_loop(0, 4, project_k, 0)
    if ring:
        first.space((3,))
        first.shares_in((3,))
        save_w.start()
        rest.line((0,))
    lax.fori_loop(0, 4, project_q, 0)

    pay[...] = jnp.concatenate([means[:, :half], means[:, half:]], axis=0).astype(BF16)

    def mark(j, peer):
        return remote(pay, slots.at[me], msem.at[0, j], msem.at[1, j], {"seq": peer})

    each_peer(me, n, mark, lambda c: c.start())
    slots[pl.ds(me, 1)] = pay[...][None]
    for c in drains[:4]:
        c.start()

    lax.fori_loop(tiles // 2, tiles - 1, inner, 0)
    for c in halos:
        c.wait()
    mask_halos(vl, vr, me, n)

    def edge(i, _):
        fill_edge(ext, v_s, vl, vr, i == 0)
        conv_forward(ext, taps, conv_s, i * (t - CTILE))
        return 0

    lax.fori_loop(0, 2, edge, 0)
    drains[4].start()
    each_peer(me, n, mark, lambda c: c.wait())
    gather_marks(slots, (mq, mk), n)
    for g in range(NG):
        bdk[g] = spread(mk[:, gs(g)])
        bdq[g] = spread(mq[:, gs(g)])
    uacc[...] = jnp.zeros_like(uacc)
    zacc[...] = jnp.zeros_like(zacc)
    ones_bd = jnp.where(head_mask(), 1.0, 0.0).astype(BF16)

    def expand(i, _):
        for g in range(NG):
            e = jnp.exp(dot_nt(k_s[tile(i), gs(g)], bdq[g])).astype(BF16)
            e_s[tile(i), gs(g)] = e
            uacc[g] += dot_tn(e, v_s[tile(i), gs(g)])
            zacc[g] += dot_tn(e, jnp.ones((t // 4, 128), BF16))
        if ring:

            @pl.when(i == 0)
            def _():
                rest.plane((0,))

            @pl.when(i == 1)
            def _():
                rest.plane((1,))

        return 0

    def attend(i, _):
        for g in range(NG):
            s = dot_nt(q_s[tile(i), gs(g)], bdk[g])
            ex = jnp.exp(s - half_reduce(s, jnp.max, -jnp.inf))
            den = dot(ex.astype(BF16), ones_bd)
            f_s[tile(i), gs(g)] = (ex / den).astype(BF16)
        return 0

    lax.fori_loop(0, 4, expand, 0)
    lane = lax.broadcasted_iota(jnp.int32, (M, 128), 1)
    zt = jnp.zeros((M, 128), F32)
    for g in range(NG):
        put_tall(upart, g, collect(uacc[g]))
        for h in range(4):
            zt = zt + jnp.where(lane == 4 * g + h, zacc[g, h * 64 : h * 64 + 64, :], 0.0)
    upart[6 * M : 7 * M, :] = zt
    upart[7 * M :, :] = jnp.zeros((upart.shape[0] - 7 * M, 128), F32)
    summing = SeqSum(me, n, upart, uz, *sum_bufs)
    summing.start()
    pinv_begin(mq, mk, a_ref, z_ref)

    def newton(it, _):
        pinv_step(it, a_ref, z_ref, az_ref, t2_ref, t3_ref)
        return 0

    lax.fori_loop(0, 4, attend, 0)
    for c in drains[5:]:
        c.start()
    summing.turn()
    lax.fori_loop(0, NSITER, newton, 0)
    summing.finish()
    p_ref[...] = z_ref[NSITER]
    for c in drains:
        c.wait()
    if ring:
        for c in local:
            c.wait()
        save_w.wait()
        rest.space((0, 1))
        rest.shares_in((0, 1))
        first.finish()
        rest.finish()


def front(x, weights, n, ring):
    t, d = x.shape
    if ring:
        rown = d // CHIPS
        own4 = (4, rown, d // 2)
        extra_out = [sds((3, d, d), BF16), sds((d, d), BF16), sds((2, d, d), BF16), sds((4, 2, rown, d // 2), BF16)]
        extra = [
            pltpu.VMEM((3, d, d), BF16),
            pltpu.VMEM((d, 128), F32),
            pltpu.VMEM((3, rown, d // 2), F32),
            pltpu.VMEM(own4, F32),
            pltpu.VMEM(own4, F32),
            pltpu.VMEM((rown, d // 2), F32),
            pltpu.VMEM((rown, d // 2), BF16),
            pltpu.VMEM((PARTS, rown // 2, d), F32),
            DMA((8,)),
            DMA((2,)),
        ] + GatherMesh.scratch(4) + GatherMesh.scratch(2)
    else:
        extra_out, extra = [], []
    r = padded_rows(7 * M, n)
    big = sds((t, d), BF16)
    steps = sds((NSITER, M, d), F32)
    res = pl.pallas_call(
        functools.partial(front_kernel, n=n, ring=ring),
        in_specs=[ANYW] + [VM] * len(weights),
        out_specs=([ANYW] * 3 + [VM] if ring else []) + [VM] * 2 + [ANYW] * 7 + [VM] * 11,
        out_shape=extra_out
        + [sds((8, d), F32), sds((40, d), F32)]
        + [big] * 7
        + [sds((M, d), BF16)] * 2
        + [sds((r, 128), F32), sds((M, d), F32), sds((NSITER + 1, M, d), F32), steps, steps, steps]
        + [sds((RAD, d), BF16)] * 2
        + [sds((M, d), F32)],
        scratch_shapes=[pltpu.VMEM((t, d), BF16)] * 8
        + [
            pltpu.VMEM((8, d), F32),
            pltpu.VMEM((16, d // 2), BF16),
            pltpu.VMEM((n, 16, d // 2), BF16),
            pltpu.VMEM((d // 128, CTILE + 2 * RAD, 128), F32),
            pltpu.VMEM((NG, GROUP, GROUP), BF16),
            pltpu.VMEM((NG, GROUP, GROUP), BF16),
            pltpu.VMEM((NG, GROUP, GROUP), F32),
            pltpu.VMEM((NG, GROUP, 128), F32),
            pltpu.VMEM((r, 128), F32),
            DMA((2,)),
            DMA((7,)),
            DMA((2, n)),
            DMA((4,)),
        ]
        + SeqSum.scratch(r, n)
        + extra,
        compiler_params=pltpu.CompilerParams(collective_id=1, has_side_effects=True, vmem_limit_bytes=VMEM_LIMIT),
        name="front",
    )(x, *weights)
    return res if ring else [None] * 4 + list(res)


PARTS = 4
HALF_D = 384
PART = 768


def middle_kernel(*refs, n, ring):
    take = Refs(refs)
    x_a, dy_a, f_a, q_a, conv_a, wo_a, ud_a = take(7)
    if ring:
        ud_own = take.one()
    gains, mk, uz, p_ref = take(4)
    out_o, dx_o, dmix_o, dqf_o, g_o = take(5)
    gw_ref, dkt_ref, dg_ref = take(3)
    if ring:
        t_ud = take.one()
    x_s, dy_s, f_s, mix_s, h2_s, da_s, x1_s, wo_s, ud = take(9)
    oacc, hacc, wbd, bdk, gwacc, dktacc, dgacc = take(7)
    isem, osem = take(2)
    t, d = x_s.shape
    tile = t // 4
    act_s, q_s = x_s, x_s
    seq = lax.axis_index("seq")
    parts_in = 1 if ring else PARTS
    gain = gains[1:2, :]

    def here(i):
        return pl.ds(pl.multiple_of(i * tile, tile), tile)

    load_q = pltpu.make_async_copy(q_a, q_s, isem.at[7])
    loads = [
        pltpu.make_async_copy(a, b, isem.at[i])
        for i, (a, b) in enumerate(
            ((f_a, f_s), (conv_a, mix_s), (x_a, x_s), (wo_a, wo_s), (ud_a, ud.at[pl.ds(0, parts_in)]), (dy_a, dy_s))
        )
    ]
    for c in loads:
        c.start()
    if ring:
        place = Place()
        gathers = [None] + [
            GatherMesh(place, (STACK,), (ud.at[p],), (ud_own.at[p],), take(6)) for p in range(1, PARTS)
        ]
        scatters = [
            ScatterMesh.take(take, place, (STACK,), (ud.at[p],), in_place=True) for p in range(PARTS - 1)
        ]
        greet(seq, n, [place.twin])
        for g in gathers[1:]:
            g.start_z()
        for p in range(1, PARTS):
            gathers[p].start_across()
            ud[p, :, at(seq, d // CHIPS, 16), at(place.rep, d // 2, 128)] = ud_own[p]

    def tick(cond, *acts):
        if ring and acts:

            @pl.when(cond)
            def _():
                for act in acts:
                    act()

    K = (0,)

    def move(p, *names):
        return [functools.partial(getattr(gathers[p], name), K) for name in names] if ring else []

    def send(p, *names):
        return [functools.partial(getattr(scatters[p], name), 0) for name in names] if ring else []

    gwacc[...] = jnp.zeros_like(gwacc)
    dktacc[...] = jnp.zeros_like(dktacc)
    dgacc[...] = jnp.zeros_like(dgacc)
    for g in range(NG):
        bv = u_group(uz, g) / zt_group(uz, g)
        wbd[g] = spread(dot(p_ref[:, gs(g)], spread(bv), HI)).astype(BF16)
        bdk[g] = spread(mk[:, gs(g)])
    for c in loads[:4]:
        c.wait()

    def before(i, _):
        r = here(i)
        for g in range(NG):
            mix_s[r, gs(g)] = (dot(f_s[r, gs(g)], wbd[g]) + mix_s[r, gs(g)].astype(F32)).astype(BF16)
        x1 = x_s[r, :].astype(F32) + dot(mix_s[r, :], wo_s[...])
        oacc[r, :] = x1
        x1_s[r, :] = x1.astype(BF16)
        normal, _inv = normalize(x1)
        h2_s[r, :] = (normal * gain).astype(BF16)
        tick(i == 1, *move(1, "line", "line_on"))
        tick(i == 3, *move(1, "plane"))
        return 0

    lax.fori_loop(0, 4, before, 0)
    loads[4].wait()
    loads[5].wait()
    plan = {
        (0, 0): move(2, "line", "line_on"),
        (0, 2): move(1, "space") + move(2, "plane"),
        (0, 3): move(3, "line", "line_on"),
        (1, 0): move(3, "plane") + send(0, "far"),
        (1, 1): move(2, "space"),
        (1, 3): send(0, "mid") + move(3, "space"),
        (2, 0): send(1, "far"),
        (2, 1): send(0, "near"),
        (2, 3): send(1, "mid"),
        (3, 0): send(2, "far"),
        (3, 1): send(1, "near"),
        (3, 3): send(2, "mid"),
    }
    for p in range(PARTS):
        if ring and p > 0:
            gathers[p].shares_in(K)
        u, dn = ud.at[p, 0], ud.at[p, 1]

        def through(i, _):
            r = here(i)
            h2 = h2_s[r, :]
            dy = dy_s[r, :]
            o = h = None
            for c in range(0, d, PART):
                cols = slice(c, c + PART)
                act, slope = gelu_parts(dot(h2, u[:, cols]))
                act = act.astype(BF16)
                act_s[r, cols] = act
                da = (dot_nt(dy, dn[cols, :]) * slope).astype(BF16)
                da_s[r, cols] = da
                oc, hc = dot(act, dn[cols, :]), dot_nt(da, u[:, cols])
                o, h = (oc, hc) if o is None else (o + oc, h + hc)
            oacc[r, :] += o
            hacc[r, :] = h if p == 0 else hacc[r, :] + h
            for j in range(4):
                tick(i == j, *plan.get((p, j), []))
            return 0

        lax.fori_loop(0, 4, through, 0)
        if ring and p > 0:
            gathers[p].finish()

        def grads(j, _):
            cols = pl.ds(pl.multiple_of(j * HALF_D, HALF_D), HALF_D)
            ud[p, 0, cols, :] = dot_tn(h2_s[:, cols], da_s[...]).astype(BF16)
            ud[p, 1, cols, :] = dot_tn(act_s[:, cols], dy_s[...]).astype(BF16)
            return 0

        lax.fori_loop(0, d // HALF_D, grads, 0)
        if ring and p < PARTS - 1:
            scatters[p].start()
        if ring and p == 3:
            t_ud[0] = scatters[0].total(0)
    load_q.start()
    first_out = PARTS - 1 if ring else 0
    stored = [
        pltpu.make_async_copy(ud.at[p], g_o.at[pl.ds(2 * (p - first_out), 2)], osem.at[16 + p])
        for p in range(first_out, PARTS)
    ]
    for c in stored:
        c.start()
    tick(True, *send(2, "near"))
    if ring:
        t_ud[1] = scatters[1].total(0)
    load_q.wait()

    def after(i, _):
        r = here(i)
        normal, inv = normalize(x1_s[r, :].astype(F32))
        x1_s[r, :] = oacc[r, :].astype(BF16)
        pltpu.make_async_copy(x1_s.at[r], out_o.at[r], osem.at[i]).start()
        dh2 = hacc[r, :]
        dgacc[...] += rowsum8(dh2 * normal)
        dx = (norm_back(dh2, normal, inv, gain) + dy_s[r, :].astype(F32)).astype(BF16)
        dy_s[r, :] = dx
        pltpu.make_async_copy(dy_s.at[r], dx_o.at[r], osem.at[4 + i]).start()
        dmix = dot_nt(dx, wo_s[...]).astype(BF16)
        h2_s[r, :] = dmix
        pltpu.make_async_copy(h2_s.at[r], dmix_o.at[r], osem.at[8 + i]).start()
        ones_bd = jnp.where(head_mask(), 1.0, 0.0).astype(BF16)
        for g in range(NG):
            dm = dmix[:, gs(g)]
            f = f_s[r, gs(g)]
            df = dot_nt(dm, wbd[g])
            gwacc[g] += dot_tn(f, dm)
            ff32 = f.astype(F32)
            prod = df * ff32
            hi, lo = split(prod)
            ds = (ff32 * (df - (dot(hi, ones_bd) + dot(lo, ones_bd)))).astype(BF16)
            da_s[r, gs(g)] = dot(ds, bdk[g]).astype(BF16)
            dktacc[g] += dot_tn(ds, q_s[r, gs(g)])
        pltpu.make_async_copy(da_s.at[r], dqf_o.at[r], osem.at[12 + i]).start()
        return 0

    lax.fori_loop(0, 4, after, 0)

    def grad_o(j, _):
        cols = pl.ds(pl.multiple_of(j * HALF_D, HALF_D), HALF_D)
        wo_s[cols, :] = dot_tn(mix_s[:, cols], dy_s[...]).astype(BF16)
        return 0

    lax.fori_loop(0, d // HALF_D, grad_o, 0)
    stored.append(pltpu.make_async_copy(wo_s, g_o.at[2 * (PARTS - first_out)], osem.at[20]))
    stored[-1].start()
    for g in range(NG):
        put_tall(gw_ref, g, collect(gwacc[g]))
        dkt_ref[:, gs(g)] = collect(dktacc[g])
    if gw_ref.shape[0] > 6 * M:
        gw_ref[6 * M :] = jnp.zeros((gw_ref.shape[0] - 6 * M, 128), F32)
    dg_ref[...] = jnp.broadcast_to(jnp.sum(dgacc[...], axis=0, keepdims=True), dg_ref.shape)
    if ring:
        t_ud[2] = scatters[2].total(0)
        for sc in scatters:
            sc.finish()
    for i in range(4):
        for b, src, dst in ((0, x1_s, out_o), (4, dy_s, dx_o), (8, h2_s, dmix_o), (12, da_s, dqf_o)):
            pltpu.make_async_copy(src.at[here(i)], dst.at[here(i)], osem.at[b + i]).wait()
    for c in stored:
        c.wait()


def middle(x, dy, f, q, conv, wo, ud, ud_own, gains, mk, uz, p, gw_rows, n):
    ring = ud_own is not None
    t, d = x.shape
    big = sds((t, d), BF16)
    outs = [big] * 4 + [sds((3 if ring else 2 * PARTS + 1, d, d), BF16)]
    outs += [sds((gw_rows, 128), F32), sds((M, d), F32), sds((8, d), F32)]
    extra = []
    if ring:
        cell = (2, d // CHIPS, d // 2)
        outs += [sds((PARTS - 1, *cell), F32)]
        extra = GatherMesh.scratch(1) * (PARTS - 1) + ScatterMesh.scratch([(cell, BF16)], True) * (PARTS - 1)
    square = pltpu.VMEM((NG, GROUP, GROUP), BF16)
    square_f = pltpu.VMEM((NG, GROUP, GROUP), F32)
    return pl.pallas_call(
        functools.partial(middle_kernel, n=n, ring=ring),
        in_specs=[ANYW] * 7 + [VM] * (5 if ring else 4),
        out_specs=[ANYW] * 5 + [VM] * (len(outs) - 5),
        out_shape=outs,
        scratch_shapes=[pltpu.VMEM((t, d), BF16)] * 7
        + [
            pltpu.VMEM((d, d), BF16),
            pltpu.VMEM((PARTS, 2, d, d), BF16),
            pltpu.VMEM((t, d), F32),
            pltpu.VMEM((t, d), F32),
            square,
            square,
            square_f,
            square_f,
            pltpu.VMEM((8, d), F32),
            DMA((8,)),
            DMA((21,)),
        ]
        + extra,
        compiler_params=pltpu.CompilerParams(
            collective_id=4 if ring else None, has_side_effects=True, vmem_limit_bytes=61 * 1024 * 1024
        ),
        name="middle",
    )(x, dy, f, q, conv, wo, ud, *((ud_own,) if ring else ()), gains, mk, uz, p)


def rear_kernel(*refs, n, ring, seg_len):
    take = Refs(refs)
    bodies = take(5)
    x_a, dx_a, h1_a, w_a = take(4)
    if ring:
        grads = take(1)
    gw_part, uz, a_ref, z_ref, az_ref, t2_ref, t3_ref, mq, mk, vl, vr, taps, dkt_ref, dg2_ref, gains = take(15)
    if ring:
        t_ud = take.one()
    ig_o, gvec_o, gqkv_o, dg_o = take(4)
    if ring:
        r_uo, r_down, r_vec, r_qkv = take(4)
    v_s, g_s, e_s, k_s, dqf_s, dqkv, gvec = take(7)
    vext, gext, tapacc, gl, gr, gw, gz, da, dubd, rowadd, dqtacc, bdq, pay, slots, own = take(15)
    w_s, gqkv, part, dslots, dgacc, gsem = take(6)
    isem, osem, hsem, wsem = take(4)
    sum_bufs = take(3)
    me = lax.axis_index("seq")
    t, d = v_s.shape
    loads = [
        pltpu.make_async_copy(b, s, isem.at[i]) for i, (b, s) in enumerate(zip(bodies, (v_s, g_s, e_s, k_s, dqf_s)))
    ]
    for c in loads:
        c.start()
    load_x = pltpu.make_async_copy(x_a, v_s, isem.at[5])
    load_dx = pltpu.make_async_copy(dx_a, g_s, isem.at[6])
    load_h1 = pltpu.make_async_copy(h1_a, e_s, isem.at[7])
    load_w = pltpu.make_async_copy(w_a, w_s, isem.at[8])
    load_w.start()
    if ring:
        place = Place()
        greet(me, n, [place.twin])
        big = ScatterMesh.take(take, place, (STACK,), grads)
        vec = ScatterMesh.take(take, place, (LINES,), (gvec,))
        late = ScatterMesh.take(take, place, (HALF,) * 3, [gqkv.at[i] for i in range(3)], in_place=True)
        fuo, fd, fq, fsem = take(4)
    else:
        greet(me, n, [])
    summing = SeqSum(me, n, gw_part, gw, *sum_bufs)
    loads[1].wait()
    halos = halo_copies(g_s, gl, gr, me, n, hsem)
    for c in halos:
        c.start()
    summing.start()
    if ring:
        big.start()

    def tick(cond, *acts):
        if ring:

            @pl.when(cond)
            def _():
                for act, k in acts:
                    act(k)

    tapacc[...] = jnp.zeros_like(tapacc)
    loads[0].wait()
    if not ring:
        big = vec = None
    far = (lambda k: big.far(k))
    mid = (lambda k: big.mid(k))
    near = (lambda k: big.near(k))

    def inner(i, _):
        fill_inner(vext, v_s, i * CTILE)
        fill_inner(gext, g_s, i * CTILE)
        conv_backward(vext, gext, taps, dqkv, tapacc, i * CTILE)


        @pl.when(i == 2)
        def _():
            summing.turn()

        tick(i == 2, (far, 0))
        return 0

    beside = NSITER // 2
    split_at = t // CTILE - 1 - beside
    lax.fori_loop(1, split_at, inner, 0)
    for c in halos:
        c.wait()
    mask_halos(gl, gr, me, n)

    def edge(i, _):
        fill_edge(vext, v_s, vl, vr, i == 0)
        fill_edge(gext, g_s, gl, gr, i == 0)
        conv_backward(vext, gext, taps, dqkv, tapacc, i * (t - CTILE))
        return 0

    lax.fori_loop(0, 2, edge, 0)
    summing.finish()
    for g in range(NG):
        z = zt_group(uz, g)
        bv = u_group(uz, g) / z
        gwg = u_group(gw, g)
        gz[:, gs(g)] = flip(dot_nt(gwg, spread(bv), HI))
        dbv = dot(flip(z_ref[NSITER, :, gs(g)]), spread(gwg), HI)
        dubd[g] = spread(dbv / z).astype(BF16)
        rowadd[g] = dot_nt(jnp.ones((8, GROUP), F32), spread(dbv * bv / z), HI)
        bdq[g] = spread(mq[:, gs(g)])
    da[...] = jnp.zeros_like(da)

    def newton(j, _):
        row0 = pl.multiple_of((split_at + lax.div(j, 2)) * CTILE, CTILE)

        @pl.when(lax.rem(j, 2) == 0)
        def _():
            fill_inner(vext, v_s, row0)
            fill_inner(gext, g_s, row0)

        base = lax.rem(j, 2) * (CTILE // 2)
        for h in range(2):
            conv_back_chunk(vext, gext, taps, dqkv, tapacc, row0, pl.multiple_of(base + h * CHUNK, CHUNK))
        pinv_back_step(NSITER - 1 - j, a_ref, z_ref, az_ref, t2_ref, t3_ref, gz, da)
        tick(j == 0, (mid, 0))
        tick(j == 3, (near, 0))
        return 0

    lax.fori_loop(0, NSITER, newton, 0)
    load_dx.start()
    dtap = jnp.sum(tapacc[...], axis=1)
    lines = jnp.concatenate([jnp.zeros((1, d), F32), dg2_ref[0:1, :], dtap, jnp.zeros((128 - 42, d), F32)], axis=0)
    gvec[...] = jnp.transpose(lines)
    if ring:
        vec.start()
    else:
        save_vec = pltpu.make_async_copy(gvec, gvec_o, osem.at[1])
        save_vec.start()
    loads[2].wait()
    loads[3].wait()
    dqtacc[...] = jnp.zeros_like(dqtacc)

    def cols(part, g):
        return slice(part * d + g * GROUP, part * d + (g + 1) * GROUP)

    def through(i, _):
        here = pl.ds(pl.multiple_of(i * (t // 4), t // 4), t // 4)
        for g in range(NG):
            e = e_s[here, gs(g)]
            de = dot_nt(v_s[here, gs(g)], dubd[g]) - rowadd[g, 0:1, :]
            ds = (e.astype(F32) * de).astype(BF16)
            dqkv[here, cols(2, g)] = (dot(e, dubd[g]) + dqkv[here, cols(2, g)].astype(F32)).astype(BF16)
            dqkv[here, cols(1, g)] = dot(ds, bdq[g]).astype(BF16)
            dqtacc[g] += dot_tn(ds, k_s[here, gs(g)])
        tick(i == 0, (lambda k: vec.far(k), 0))
        tick(i == 2, (lambda k: vec.mid(k), 0))
        return 0

    lax.fori_loop(0, 4, through, 0)
    load_x.start()
    load_h1.start()

    rows_dev = max(M // n, 1)
    per_mark = n * rows_dev // M
    if rows_dev < 4:
        pay[...] = jnp.zeros_like(pay)
    for g in range(NG):
        ds = pinv_back_end(g, a_ref, gz, da)
        dq = collect(dqtacc[g]) + dot(ds, spread(mk[:, gs(g)].astype(F32)), HI) * (1.0 / n)
        dk = dkt_ref[:, gs(g)] + dot(flip(ds), spread(mq[:, gs(g)].astype(F32)), HI) * (1.0 / n)
        for i in range(n):
            row = i * rows_dev // per_mark
            pay[i, 0:rows_dev, gs(g)] = dq[row : row + rows_dev]
            pay[i, 4 : 4 + rows_dev, gs(g)] = dk[row : row + rows_dev]

    def mark(j, peer):
        return remote(pay.at[peer], slots.at[me], wsem.at[0, j], wsem.at[1, j], {"seq": peer})

    each_peer(me, n, mark, lambda c: c.start())
    slots[pl.ds(me, 1)] = pay[pl.ds(me, 1)]

    def project_back(p, scale):
        def body(j, _):
            cols = pl.ds(pl.multiple_of(j * HALF_D, HALF_D), HALF_D)
            gqkv[p, cols, :] = (dot_tn(e_s[:, cols], dqkv[:, p * d : (p + 1) * d]) * scale).astype(BF16)
            return 0

        lax.fori_loop(0, d // HALF_D, body, 0)
        if ring:
            late.start((p,))

    load_h1.wait()
    project_back(2, 1.0)
    if ring:
        last_ud = big.total(0)
        for p in range(PARTS - 1):
            fuo[p] = t_ud[p, 0]
            fd[p] = t_ud[p, 1]
        fuo[PARTS - 1] = last_ud[0]
        fd[PARTS - 1] = last_ud[1]
        fuo[PARTS] = last_ud[2]
        cols = at(place.rep, d // 2, 128)
        back = [swap_rows(fuo, r_uo, place, fsem.at[0])]
        for j in range(2):
            r_down[j, :, cols] = fd[2 * place.rep + j]
            src = fd.at[2 * (1 - place.rep) + j]
            back.append(remote(src, r_down.at[j, :, cols], fsem.at[1 + j, 0], fsem.at[1 + j, 1], place.twin))
        for c in back:
            c.start()
        vec.near(0)
        late.far(2)
    loads[4].wait()
    each_peer(me, n, mark, lambda c: c.wait())
    own[...] = lax.fori_loop(1, n, lambda i, acc: acc + slots[i], slots[0]) * (1.0 / seg_len)

    def landed(i, _):
        here = pl.ds(pl.multiple_of(i * (t // 4), t // 4), t // 4)
        row = lax.div(i * rows_dev, 4)
        dqkv[here, 0:d] = (dqf_s[here, :].astype(F32) + own[pl.ds(row, 1), :]).astype(BF16)
        dqkv[here, d : 2 * d] = (dqkv[here, d : 2 * d].astype(F32) + own[pl.ds(row + 4, 1), :]).astype(BF16)
        return 0

    lax.fori_loop(0, 4, landed, 0)
    project_back(1, QK_SCALE)
    project_back(0, QK_SCALE)
    tick(True, (lambda k: late.far(k), 1), (lambda k: late.far(k), 0), (lambda k: late.mid(k), 2))
    for c in (load_w, load_x, load_dx):
        c.wait()
    dgacc[...] = jnp.zeros_like(dgacc)

    def back_through(i, _):
        here = pl.ds(pl.multiple_of(i * (t // 4), t // 4), t // 4)
        dq, dk, dv = (dqkv[here, p * d : (p + 1) * d] for p in range(3))
        dh = (dot_nt(dq, w_s[0]) + dot_nt(dk, w_s[1])) * QK_SCALE + dot_nt(dv, w_s[2])
        normal, inv = normalize(v_s[here, :].astype(F32))
        dgacc[...] += rowsum8(dh * normal)
        ig = norm_back(dh, normal, inv, gains[0:1, :]) + g_s[here, :].astype(F32)
        v_s[here, :] = ig.astype(BF16)
        pltpu.make_async_copy(v_s.at[here], ig_o.at[here], osem.at[2 + i]).start()
        tick(i == 1, (lambda k: late.near(k), 2), (lambda k: late.mid(k), 1))
        tick(i == 2, (lambda k: late.mid(k), 0))
        return 0

    lax.fori_loop(0, 4, back_through, 0)
    row = jnp.sum(dgacc[...], axis=0, keepdims=True)
    part[...] = jnp.concatenate(
        [row[:, c : c + 128] for c in range(0, d, 128)] + [jnp.zeros((8 - d // 128, 128), F32)], axis=0
    )

    def send(j, peer):
        return remote(part, dslots.at[me], gsem.at[0, j], gsem.at[1, j], {"seq": peer})

    each_peer(me, n, send, lambda c: c.start())
    dslots[pl.ds(me, 1)] = part[...][None]
    tick(True, (lambda k: late.near(k), 1), (lambda k: late.near(k), 0))
    each_peer(me, n, send, lambda c: c.wait())
    total = lax.fori_loop(1, n, lambda i, acc: acc + dslots[i], dslots[0])
    dg_o[0] = total
    if ring:
        twin_sum = remote(dg_o.at[0], dg_o.at[1], gsem.at[0, 0], gsem.at[1, 0], place.twin)
        twin_sum.start()
        r_vec[...] = vec.total(0)
        for p in (2, 1, 0):
            fq[p] = late.total(p)
        back.append(swap_rows(fq, r_qkv, place, fsem.at[3]))
        back[-1].start()
        twin_sum.wait()
        big.finish()
        vec.finish()
        late.finish()
        for c in back:
            c.wait()
    else:
        dg_o[1] = jnp.zeros_like(total)
        save_vec.wait()
        save_g = pltpu.make_async_copy(gqkv, gqkv_o, osem.at[0])
        save_g.start()
        save_g.wait()
    for i in range(4):
        here = pl.ds(i * (t // 4), t // 4)
        pltpu.make_async_copy(v_s.at[here], ig_o.at[here], osem.at[2 + i]).wait()


def rear(bodies, more, grads, gw, uz, a, z, az, t2, t3, mq, mk, vl, vr, taps, dkt, dg2, gains, t_ud, n, seg_len):
    ring = grads is not None
    t, d = bodies[0].shape
    r = gw.shape[0]
    outs = [sds((t, d), BF16), sds((d, 128), F32), sds((3, d, d), BF16), sds((2, 8, 128), F32)]
    extra = []
    if ring:
        own = d // (2 * CHIPS)
        outs += [sds((PARTS + 1, own, d), F32), sds((2, 2 * own, d), F32), sds((own, 128), F32), sds((3, own, d), F32)]
        extra = ScatterMesh.scratch([((3, 2 * own, d // 2), BF16)]) + ScatterMesh.scratch([((own, 128), F32)])
        extra += ScatterMesh.scratch([((2 * own, d // 2), BF16)] * 3, True) + [
            pltpu.VMEM((PARTS + 1, 2 * own, d // 2), F32),
            pltpu.VMEM((PARTS, 2 * own, d // 2), F32),
            pltpu.VMEM((3, 2 * own, d // 2), F32),
            DMA((4, 2)),
        ]
    ext = pltpu.VMEM((d // 128, CTILE + 2 * RAD, 128), F32)
    halo = pltpu.VMEM((RAD, d), BF16)
    small = pltpu.VMEM((M, d), F32)
    return pl.pallas_call(
        functools.partial(rear_kernel, n=n, ring=ring, seg_len=seg_len),
        in_specs=[ANYW] * (9 + (1 if ring else 0)) + [VM] * (15 + (1 if ring else 0)),
        out_specs=[ANYW] * 3 + [VM] * (len(outs) - 3),
        out_shape=outs,
        scratch_shapes=[pltpu.VMEM((t, d), BF16)] * 5
        + [
            pltpu.VMEM((t, 3 * d), BF16),
            pltpu.VMEM((d, 128), F32),
            ext,
            ext,
            pltpu.VMEM((40, 8, d), F32),
            halo,
            halo,
            pltpu.VMEM((r, 128), F32),
            small,
            small,
            pltpu.VMEM((NG, GROUP, GROUP), BF16),
            pltpu.VMEM((NG, 8, GROUP), F32),
            pltpu.VMEM((NG, GROUP, GROUP), F32),
            pltpu.VMEM((NG, GROUP, GROUP), BF16),
            pltpu.VMEM((n, 8, d), F32),
            pltpu.VMEM((n, 8, d), F32),
            pltpu.VMEM((8, d), F32),
            pltpu.VMEM((3, d, d), BF16),
            pltpu.VMEM((3, d, d), BF16),
            pltpu.VMEM((8, 128), F32),
            pltpu.VMEM((n, 8, 128), F32),
            pltpu.VMEM((8, d), F32),
            DMA((2, n)),
            DMA((9,)),
            DMA((6,)),
            DMA((4,)),
            DMA((2, n)),
        ]
        + SeqSum.scratch(r, n)
        + extra,
        compiler_params=pltpu.CompilerParams(
            collective_id=2, has_side_effects=True, vmem_limit_bytes=61 * 1024 * 1024
        ),
        name="rear",
    )(*bodies, *more, *(grads if ring else ()), gw, uz, a, z, az, t2, t3, mq, mk, vl, vr, taps, dkt, dg2, gains, *((t_ud,) if ring else ()))


def adam_into(grad, at_in, at_out, rate):
    w, m, v = at_in
    moment = BETA_ONE * m[...] + (1.0 - BETA_ONE) * grad
    second = BETA_TWO * v[...] + (1.0 - BETA_TWO) * grad * grad
    first_hat = moment * (1.0 / (1.0 - BETA_ONE**STEP))
    second_hat = second * (1.0 / (1.0 - BETA_TWO**STEP))
    at_out[0][...] = w[...] - rate * (first_hat / (jnp.sqrt(second_hat) + ADAM_EPS) + DECAY_RATE * w[...])
    at_out[1][...] = moment
    at_out[2][...] = second


def adam_kernel(*refs):
    take = Refs(refs)
    r_qkv, r_uo, r_down = take(3)
    attn, up, down = take(3), take(3), take(3)
    attn_n, up_n, down_n = take(3), take(3), take(3)
    for i in range(4):
        grad = r_qkv[i] if i < 3 else r_uo[PARTS]
        adam_into(grad, [r.at[i] for r in attn], [r.at[i] for r in attn_n], LEARN_RATE)
    rows_chip = r_down.shape[1]
    wide = PARTS * rows_chip
    for c in range(0, up[0].shape[1], 2 * wide):
        got = [r_uo[p, :, (c + h * wide) // PARTS : (c + h * wide) // PARTS + rows_chip] for h in range(2) for p in range(PARTS)]
        cols = slice(c, c + 2 * wide)
        adam_into(jnp.concatenate(got, axis=1), [r.at[:, cols] for r in up], [r.at[:, cols] for r in up_n], LEARN_RATE)
    for j in range(2):
        rows_j = slice(j * rows_chip, (j + 1) * rows_chip)
        adam_into(r_down[j], [r.at[rows_j, :] for r in down], [r.at[rows_j, :] for r in down_n], LEARN_RATE)


def adam_all(r_qkv, r_uo, r_down, state):
    return pl.pallas_call(
        adam_kernel,
        in_specs=[VM] * 12,
        out_specs=[VM] * 9,
        out_shape=[sds(x.shape, F32) for x in state],
        compiler_params=pltpu.CompilerParams(vmem_limit_bytes=VMEM_LIMIT),
        name="adam_all",
    )(r_qkv, r_uo, r_down, *state)


def adam_step(weight, grad_vec, moment, second, rate_value):
    moment_new = BETA_ONE * moment + (1.0 - BETA_ONE) * grad_vec
    second_new = BETA_TWO * second + (1.0 - BETA_TWO) * grad_vec * grad_vec
    first_hat = moment_new / (1.0 - BETA_ONE**STEP)
    second_hat = second_new / (1.0 - BETA_TWO**STEP)
    weight_new = weight - rate_value * (
        first_hat / (jnp.sqrt(second_hat) + ADAM_EPS) + DECAY_RATE * weight
    )
    return (weight_new, moment_new, second_new)


def per_device(tokens, cotangent, attn_w, w_up, w_down, vectors, attn_m, attn_v, up_m, up_v, down_m, down_v, vec_m, vec_v):
    both = ("seq", "rep")
    x = tokens[0]
    dy = cotangent[0]
    t, d = x.shape
    n = lax.axis_size("seq")
    seg_len = t * n // M
    ring = n == CHIPS and lax.axis_size("rep") == 2

    rown = d // n
    if ring:
        weights = (attn_w, w_up, w_down.reshape(2, rown, d), vectors)
    else:
        w_attn = lax.all_gather(attn_w.astype(BF16), both, axis=1, tiled=True)
        vec = lax.all_gather(vectors.astype(BF16), both, axis=0, tiled=True).astype(F32)
        weights = (w_attn[:3], jnp.pad(vec, ((0, 0), (0, 128 - vec.shape[1]))))
    (w_qkv, wo, ud, ud_own, gains, taps, h1, q, k, v, conv, f, e, mq, mk, uz, a, z, az, t2, t3, vl, vr, pinverse) = front(
        x, weights, n, ring
    )
    if not ring:
        w_qkv, wo = w_attn[:3], w_attn[3]
        up = lax.all_gather(w_up.astype(BF16), both, axis=0, tiled=True)
        down = lax.all_gather(w_down.astype(BF16), both, axis=0, tiled=True)
        ud = jnp.stack([jnp.transpose(up.reshape(d, PARTS, d), (1, 0, 2)), down.reshape(PARTS, d, d)], axis=1)
    else:
        ud = ud[None]
    res = middle(x, dy, f, q, conv, wo, ud, ud_own, gains, mk, uz, pinverse, padded_rows(6 * M, n), n)
    out, dx, dmix, dqf, g_last, gw, dkt, dg2 = res[:8]
    res = rear(
        (v, dmix, e, k, dqf),
        (x, dx, h1, w_qkv),
        (g_last,) if ring else None,
        gw, uz, a, z, az, t2, t3, mq, mk, vl, vr, taps, dkt, dg2, gains,
        res[8] if ring else None,
        n, seg_len,
    )
    ig, g_vec, g_qkv, dg = res[:4]
    dg1 = (dg[0] + dg[1])[: d // 128].reshape(d)
    if ring:
        r_uo, r_down, red_vec, r_qkv = res[4:]
        own = d // (2 * n)
        start = (lax.axis_index("seq") * 2 + lax.axis_index("rep")) * own
        dg1_own = lax.dynamic_slice_in_dim(dg1, start, own, 0)
        red_vec = jnp.concatenate([dg1_own[:, None], red_vec[:, 1 : vectors.shape[1]]], axis=1)
        state = (attn_w, attn_m, attn_v, w_up, up_m, up_v, w_down, down_m, down_v)
        news = adam_all(r_qkv, r_uo, r_down, state)
    else:
        g_attn = jnp.concatenate([g_qkv, g_last[2 * PARTS :]], axis=0)
        g_pairs = g_last[: 2 * PARTS].reshape(PARTS, 2, d, d)
        g_up = jnp.transpose(g_pairs[:, 0], (1, 0, 2)).reshape(d, PARTS * d)
        g_down = g_pairs[:, 1].reshape(PARTS * d, d)
        red_attn = lax.psum_scatter(g_attn, both, scatter_dimension=1, tiled=True).astype(F32)
        red_up = lax.psum_scatter(g_up, both, scatter_dimension=0, tiled=True).astype(F32)
        red_down = lax.psum_scatter(g_down, both, scatter_dimension=0, tiled=True).astype(F32)
        g_vec = jnp.concatenate([dg1[:, None] / n, g_vec[:, 1 : vectors.shape[1]]], axis=1)
        red_vec = lax.psum_scatter(g_vec, both, scatter_dimension=0, tiled=True)
        news = (
            *adam_step(attn_w, red_attn, attn_m, attn_v, LEARN_RATE),
            *adam_step(w_up, red_up, up_m, up_v, LEARN_RATE),
            *adam_step(w_down, red_down, down_m, down_v, LEARN_RATE),
        )
    return (out[None], ig[None], *news, *adam_step(vectors, red_vec, vec_m, vec_v, VECTOR_RATE))


def solution(mesh):
    tok = P("rep", "seq", None)
    att = P(None, ("seq", "rep"), None)
    mat = P(("seq", "rep"), None)
    return jax.shard_map(
        per_device,
        mesh=mesh,
        in_specs=(tok, tok, att, mat, mat, mat, att, att, mat, mat, mat, mat, mat, mat),
        out_specs=(tok, tok, att, att, att) + (mat,) * 9,
        check_vma=False,
    )
```

```python
import functools

import jax
import jax.numpy as jnp
from jax import lax
from jax.experimental import pallas as pl
from jax.experimental.pallas import tpu as pltpu
from jax.sharding import PartitionSpec as P

H = 12
HD = 64
M = 64
KC = 33
NSITER = 6
STEP = 10
EPS_NORM = 1e-05
BETA_ONE = 0.9
BETA_TWO = 0.999
ADAM_EPS = 1e-08
LEARN_RATE = 0.03
VECTOR_RATE = 0.15
DECAY_RATE = 0.1

F32 = jnp.float32
BF16 = jnp.bfloat16
GROUP = 256
NG = 3
RAD = 16
QK_SCALE = HD ** (-0.25)
HI = lax.Precision.HIGHEST
VMEM_LIMIT = 58 * 1024 * 1024


def dot(a, b, precision=None):
    return lax.dot_general(a, b, (((1,), (0,)), ((), ())), precision=precision, preferred_element_type=F32)


def dot_nt(a, b, precision=None):
    return lax.dot_general(a, b, (((1,), (1,)), ((), ())), precision=precision, preferred_element_type=F32)


def dot_tn(a, b, precision=None):
    return lax.dot_general(a, b, (((0,), (0,)), ((), ())), precision=precision, preferred_element_type=F32)


def split(x):
    hi = x.astype(BF16)
    return hi, (x - hi.astype(F32)).astype(BF16)


def dot3(a, b):
    return dot(a[0], b[0]) + (dot(a[0], b[1]) + dot(a[1], b[0]))


def spread2(a):
    return spread(a[0]), spread(a[1])


def head_mask(shape=(GROUP, GROUP)):
    rows = lax.broadcasted_iota(jnp.int32, shape, 0)
    cols = lax.broadcasted_iota(jnp.int32, shape, 1)
    return lax.shift_right_logical(rows, 6) == lax.shift_right_logical(cols, 6)


def spread(wide):
    tall = jnp.concatenate([wide, wide, wide, wide], axis=0)
    return jnp.where(head_mask(), tall, jnp.zeros_like(tall))


def collect(full):
    kept = jnp.where(head_mask(), full, jnp.zeros_like(full))
    return (kept[0:64] + kept[64:128]) + (kept[128:192] + kept[192:256])


def flip(wide):
    turned = jnp.transpose(spread(wide))
    return (turned[0:64] + turned[64:128]) + (turned[128:192] + turned[192:256])


def gs(g):
    return slice(g * GROUP, (g + 1) * GROUP)


def half_reduce(x, op, init):
    parts = []
    for c in range(x.shape[1] // 128):
        col = x[:, c * 128 : (c + 1) * 128]
        low = lax.broadcasted_iota(jnp.int32, col.shape, 1) < 64
        a = op(jnp.where(low, col, init), axis=1, keepdims=True)
        b = op(jnp.where(low, init, col), axis=1, keepdims=True)
        parts.append(jnp.where(low, a, b))
    return jnp.concatenate(parts, axis=1)


def normalize(x):
    center = x - jnp.mean(x, axis=-1, keepdims=True)
    inv = lax.rsqrt(jnp.mean(center * center, axis=-1, keepdims=True) + EPS_NORM)
    return center * inv, inv


def norm_back(up, normal, inv, gain):
    scaled = up * gain
    centered = scaled - jnp.mean(scaled, axis=-1, keepdims=True)
    return inv * (centered - normal * jnp.mean(scaled * normal, axis=-1, keepdims=True))


def rowsum8(x):
    return jnp.sum(x.reshape(x.shape[0] // 8, 8, x.shape[1]), axis=0)


def gelu_parts(a):
    z = jnp.abs(a)
    t = 1.0 / (1.0 + (0.3275911 * 0.7071067811865476) * z)
    e = jnp.exp(-0.5 * a * a)
    poly = t * (0.127414796 + t * (-0.142248368 + t * (0.7107068705 + t * (-0.7265760135 + t * 0.5307027145))))
    tail = poly * e
    phi = jnp.where(a >= 0, 1.0 - tail, tail)
    return a * phi, phi + a * (e * 0.3989422804014327)


def whole(shape):
    zeros = (0,) * len(shape)
    return pl.BlockSpec(shape, lambda i: zeros, pipeline_mode=pl.Buffered(1))


def rows(tile, width):
    return pl.BlockSpec((tile, width), lambda i: (i, 0))


def sds(shape, dtype):
    return jax.ShapeDtypeStruct(shape, dtype)


def params():
    return pltpu.CompilerParams(dimension_semantics=("arbitrary",), vmem_limit_bytes=VMEM_LIMIT)


def widen(zt, g):
    return jnp.concatenate(
        [jnp.broadcast_to(zt[:, h : h + 1], (M, HD)) for h in range(4 * g, 4 * g + 4)], axis=1
    )


def u_group(ref, g):
    return jnp.concatenate([ref[2 * g * M : (2 * g + 1) * M, :], ref[(2 * g + 1) * M : (2 * g + 2) * M, :]], axis=1)


def zt_group(ref, g):
    return widen(ref[6 * M : 7 * M, :], g)


def put_tall(ref, g, wide):
    ref[2 * g * M : (2 * g + 1) * M, :] = wide[:, :128]
    ref[(2 * g + 1) * M : (2 * g + 2) * M, :] = wide[:, 128:]


def padded_rows(r, n):
    return -(-r // (8 * n)) * 8 * n


MESH = pl.DeviceIdType.MESH
DMA = pltpu.SemaphoreType.DMA
VM = pl.BlockSpec(memory_space=pltpu.VMEM)
ANYW = pl.BlockSpec(memory_space=pl.ANY)


def remote(src, dst, send, recv, where):
    return pltpu.make_async_remote_copy(
        src_ref=src, dst_ref=dst, send_sem=send, recv_sem=recv, device_id=where, device_id_type=MESH
    )


def greet(me, n, others):
    bar = pltpu.get_barrier_semaphore()

    def hello(j, _):
        pl.semaphore_signal(bar, inc=1, device_id={"seq": lax.rem(me + j, n)}, device_id_type=MESH)
        return 0

    lax.fori_loop(1, n, hello, 0)
    for peer in others:
        pl.semaphore_signal(bar, inc=1, device_id=peer, device_id_type=MESH)
    pl.semaphore_wait(bar, n - 1 + len(others))


def each_peer(me, n, make, act):
    def body(j, _):
        act(make(j, lax.rem(me + j, n)))
        return 0

    lax.fori_loop(1, n, body, 0)


def halo_copies(body_ref, left_ref, right_ref, me, n, sems):
    t = body_ref.shape[0]
    right = {"seq": lax.rem(me + 1, n)}
    left = {"seq": lax.rem(me + n - 1, n)}
    return (
        remote(body_ref.at[pl.ds(t - RAD, RAD)], left_ref, sems.at[0], sems.at[1], right),
        remote(body_ref.at[pl.ds(0, RAD)], right_ref, sems.at[2], sems.at[3], left),
    )


def mask_halos(left_ref, right_ref, me, n):
    left_ref[...] = jnp.where(me > 0, left_ref[...], jnp.zeros_like(left_ref))
    right_ref[...] = jnp.where(me < n - 1, right_ref[...], jnp.zeros_like(right_ref))


class SeqSum:
    def __init__(self, me, n, x, out, slots, total, sems):
        self.me, self.n, self.x, self.out, self.slots, self.total, self.sems = me, n, x, out, slots, total, sems
        self.chunk = x.shape[0] // n
        self.here = pl.ds(pl.multiple_of(me * self.chunk, 8), self.chunk)

    def first(self, j, peer):
        src = self.x.at[pl.ds(pl.multiple_of(peer * self.chunk, 8), self.chunk)]
        return remote(src, self.slots.at[self.me], self.sems.at[0, j], self.sems.at[1, j], {"seq": peer})

    def second(self, j, peer):
        return remote(self.total, self.out.at[self.here], self.sems.at[2, j], self.sems.at[3, j], {"seq": peer})

    def start(self):
        each_peer(self.me, self.n, self.first, lambda c: c.start())
        self.slots[pl.ds(self.me, 1)] = self.x[self.here, :][None]

    def turn(self):
        each_peer(self.me, self.n, self.first, lambda c: c.wait())
        summed = lax.fori_loop(1, self.n, lambda i, acc: acc + self.slots[i], self.slots[0])
        self.total[...] = summed
        each_peer(self.me, self.n, self.second, lambda c: c.start())
        self.out[self.here, :] = summed

    def finish(self):
        each_peer(self.me, self.n, self.second, lambda c: c.wait())

    @staticmethod
    def scratch(r, n):
        return [pltpu.VMEM((n, r // n, 128), F32), pltpu.VMEM((r // n, 128), F32), DMA((4, n))]


CHIPS = 16
STACK, HALF, ROWS, LINES = range(4)


def at(i, size, unit):
    return pl.ds(pl.multiple_of(i * size, unit), size)


def piece(kind, ref, seq, rep):
    if kind == STACK:
        half = ref.shape[2] // 2
        return ref.at[:, at(seq, ref.shape[1] // CHIPS, 16), at(rep, half, 128)]
    if kind == HALF:
        half = ref.shape[1] // 2
        return ref.at[at(seq, ref.shape[0] // CHIPS, 16), at(rep, half, 128)]
    return ref.at[at(seq * 2 + rep, ref.shape[0] // (2 * CHIPS), 8 if kind == LINES else 16), :]


class Place:
    def __init__(self):
        self.seq = lax.axis_index("seq")
        self.rep = lax.axis_index("rep")
        self.x = lax.rem(self.seq, 2)
        self.y = lax.rem(lax.div(self.seq, 2), 2)
        self.z = lax.div(self.seq, 4)
        self.twin = {"rep": 1 - self.rep}
        self.across = ({"seq": self.chip(4, self.rep)}, {"seq": self.chip(8, self.rep)})

    def chip(self, i, rep):
        j, b, a = lax.rem(i, 4), lax.rem(lax.div(i, 4), 2), lax.div(i, 8)
        z = lax.rem(self.z + 4 - j, 4)
        fx = a + rep * (b - a)
        fy = b + rep * (a - b)
        x = self.x + fx * (1 - 2 * self.x)
        y = self.y + fy * (1 - 2 * self.y)
        return z * 4 + y * 2 + x

    def above(self, j):
        return {"seq": self.chip(4 - j, self.rep)}

    def below(self, j):
        return {"seq": self.chip(j, self.rep)}


class GatherMesh:
    def __init__(self, place, kinds, outs, own, sems):
        self.place, self.kinds, self.outs, self.own = place, kinds, outs, own
        self.zsend, self.send1, self.send2, self.ssend, self.recv, self.srecv = sems

    def block(self, i, k, rep):
        return piece(self.kinds[k], self.outs[k], self.place.chip(i, rep), rep)

    def copy(self, i, k, send, recv, where):
        b = self.block(i, k, self.place.rep)
        src = b if self.own[k] is None or not (isinstance(i, int) and i == 0) else self.own[k]
        return remote(src, b, send, recv, where)

    def to_z(self, j, k):
        return self.copy(0, k, self.zsend.at[j, k], self.recv.at[j, k], self.place.above(j))

    def to_first(self, i, k):
        return self.copy(i, k, self.send1.at[i, k], self.recv.at[i + 4, k], self.place.across[0])

    def to_second(self, i, k):
        return self.copy(i, k, self.send2.at[i, k], self.recv.at[i + 8, k], self.place.across[1])

    def share(self, i, k):
        return self.copy(i, k, self.ssend.at[i, k], self.srecv.at[i, k], self.place.twin)

    def arrival(self, i, k):
        b = self.block(i, k, self.place.rep)
        return remote(b, b, self.ssend.at[i, k], self.recv.at[i, k], self.place.twin)

    def shared(self, i, k):
        b = self.block(i, k, 1 - self.place.rep)
        return remote(b, b, self.ssend.at[i, k], self.srecv.at[i, k], self.place.twin)

    def start_z(self):
        for k in range(len(self.kinds)):
            for j in (1, 2, 3):
                self.to_z(j, k).start()

    def start_across(self, which=None):
        for k in range(len(self.kinds)) if which is None else which:
            self.to_second(0, k).start()
            self.to_first(0, k).start()
            self.share(0, k).start()

    def each(self, low, high, which, act):
        def body(i, _):
            for k in which:
                act(i, k)
            return 0

        lax.fori_loop(low, high, body, 0)

    def line(self, which):
        def act(i, k):
            self.arrival(i, k).wait_recv()
            self.to_first(i, k).start()
            self.share(i, k).start()

        self.each(1, 4, which, act)

    def line_on(self, which):
        self.each(1, 4, which, lambda i, k: self.to_second(i, k).start())

    def plane(self, which):
        def act(i, k):
            self.arrival(i, k).wait_recv()
            self.to_second(i, k).start()
            self.share(i, k).start()

        self.each(4, 8, which, act)

    def space(self, which):
        def act(i, k):
            self.arrival(i, k).wait_recv()
            self.share(i, k).start()

        self.each(8, CHIPS, which, act)

    def shares_in(self, which):
        self.shared_first(which)
        self.each(1, CHIPS, which, lambda i, k: self.shared(i, k).wait_recv())

    def shared_first(self, which):
        for k in which:
            self.shared(0, k).wait_recv()

    def finish(self):
        which = range(len(self.kinds))
        for k in which:
            for j in (1, 2, 3):
                self.to_z(j, k).wait_send()
            self.to_first(0, k).wait_send()
            self.to_second(0, k).wait_send()
            self.share(0, k).wait_send()

        def act(i, k):
            @pl.when(i < 4)
            def _():
                self.to_first(i, k).wait_send()

            @pl.when(i < 8)
            def _():
                self.to_second(i, k).wait_send()

            self.share(i, k).wait_send()

        self.each(1, CHIPS, which, act)

    @staticmethod
    def scratch(k):
        return [DMA((4, k)), DMA((4, k)), DMA((8, k))] + [DMA((CHIPS, k))] * 3


class ScatterMesh:
    def __init__(self, place, kinds, grads, mine, twins, in2, in1, inz, sems):
        self.place, self.kinds, self.grads = place, kinds, grads
        self.mine, self.twins, self.in2, self.in1, self.inz = mine, twins, in2, in1, inz
        self.lsem, self.tsend, self.trecv, self.s2, self.r2, self.s1, self.r1, self.sz, self.rz = sems

    def source(self, i, k):
        return piece(self.kinds[k], self.grads[k], self.place.chip(i, self.place.rep), self.place.rep)

    def cell(self, i, k):
        return self.source(i, k) if self.mine is None else self.mine[k].at[i]

    def load(self, i, k):
        return pltpu.make_async_copy(self.source(i, k), self.mine[k].at[i], self.lsem.at[i, k])

    def give(self, i, k):
        other = 1 - self.place.rep
        src = piece(self.kinds[k], self.grads[k], self.place.chip(i, other), other)
        return remote(src, self.twins[k].at[i], self.tsend.at[i, k], self.trecv.at[i, k], self.place.twin)

    def out2(self, i, k):
        return remote(self.cell(i, k), self.in2[k].at[i - 8], self.s2.at[i - 8, k], self.r2.at[i - 8, k], self.place.across[1])

    def out1(self, i, k):
        return remote(self.cell(i, k), self.in1[k].at[i - 4], self.s1.at[i - 4, k], self.r1.at[i - 4, k], self.place.across[0])

    def outz(self, j, k):
        return remote(self.cell(j, k), self.inz[k].at[j], self.sz.at[j, k], self.rz.at[j, k], self.place.below(j))

    def start(self, which=None):
        for low in (8, 0):
            for k in range(len(self.kinds)) if which is None else which:

                def body(j, _):
                    self.give(low + 7 - j, k).start()
                    if self.mine is not None:
                        self.load(low + 7 - j, k).start()
                    return 0

                lax.fori_loop(0, 8, body, 0)

    def terms(self, i, k):
        if self.mine is not None:
            self.load(i, k).wait()
        self.give(i, k).wait()
        return self.cell(i, k)[...].astype(F32) + self.twins[k].at[i][...].astype(F32)

    def keep(self, i, k, value):
        cell = self.cell(i, k)
        cell[...] = value.astype(cell.dtype)

    def far(self, k):
        def body(j, _):
            i = CHIPS - 1 - j
            self.keep(i, k, self.terms(i, k))
            self.out2(i, k).start()
            return 0

        lax.fori_loop(0, 8, body, 0)

    def mid(self, k):
        def body(j, _):
            i = 7 - j
            own = self.terms(i, k)
            self.out2(i + 8, k).wait_recv()
            self.keep(i, k, own + self.in2[k].at[i][...].astype(F32))
            self.out1(i, k).start()
            return 0

        lax.fori_loop(0, 4, body, 0)

    def closer(self, i, k):
        own = self.terms(i, k)
        self.out2(i + 8, k).wait_recv()
        self.out1(i + 4, k).wait_recv()
        return own + (self.in2[k].at[i][...].astype(F32) + self.in1[k].at[i][...].astype(F32))

    def near(self, k):
        def body(j, _):
            i = 3 - j
            self.keep(i, k, self.closer(i, k))
            self.outz(i, k).start()
            return 0

        lax.fori_loop(0, 3, body, 0)

    def total(self, k):
        acc = self.closer(0, k)
        for j in (1, 2, 3):
            self.outz(j, k).wait_recv()
            acc = acc + self.inz[k][j].astype(F32)
        return acc

    def finish(self):
        for k in range(len(self.kinds)):

            def body(i, _):
                @pl.when(i >= 8)
                def _():
                    self.out2(i, k).wait_send()

                @pl.when((i >= 4) & (i < 8))
                def _():
                    self.out1(i, k).wait_send()

                @pl.when(i < 4)
                def _():
                    self.outz(i, k).wait_send()

                return 0

            lax.fori_loop(1, CHIPS, body, 0)

    @staticmethod
    def scratch(blocks, in_place=False):
        k = len(blocks)
        return (
            ([] if in_place else [pltpu.VMEM((CHIPS, *s), t) for s, t in blocks])
            + [pltpu.VMEM((CHIPS, *s), t) for s, t in blocks]
            + [pltpu.VMEM((8, *s), t) for s, t in blocks]
            + [pltpu.VMEM((4, *s), t) for s, t in blocks]
            + [pltpu.VMEM((4, *s), t) for s, t in blocks]
            + [DMA((CHIPS, k))] * 3
            + [DMA((8, k))] * 2
            + [DMA((4, k))] * 4
        )

    @staticmethod
    def take(take, place, kinds, grads, in_place=False):
        k = len(kinds)
        mine = None if in_place else take(k)
        bufs = [take(k) for _ in range(4)]
        return ScatterMesh(place, kinds, grads, mine, *bufs, take(9))


def swap_rows(total, out, place, sems):
    rows_own = total.shape[-2] // 2
    half = total.shape[-1]
    theirs, mine = at(1 - place.rep, rows_own, 8), at(place.rep, rows_own, 8)
    cols = at(place.rep, half, 128)
    if len(total.shape) == 3:
        out[:, :, cols] = total[:, mine, :]
        return remote(total.at[:, theirs, :], out.at[:, :, cols], sems.at[0], sems.at[1], place.twin)
    out[:, cols] = total[mine, :]
    return remote(total.at[theirs, :], out.at[:, cols], sems.at[0], sems.at[1], place.twin)


CHUNK = 64
CTILE = 256


def fill_inner(ext, body_ref, start):
    count = ext.shape[1]
    rows_in = pl.ds(pl.multiple_of(start - RAD, RAD), count)
    for c in range(ext.shape[0]):
        ext[c] = body_ref[rows_in, c * 128 : (c + 1) * 128].astype(F32)


def fill_edge(ext, body_ref, left_ref, right_ref, first):
    tile = ext.shape[1] - 2 * RAD
    t = body_ref.shape[0]
    start = pl.multiple_of(jnp.where(first, 0, t - tile), tile)
    for c in range(ext.shape[0]):
        cols = slice(c * 128, (c + 1) * 128)
        ext[c, RAD : RAD + tile, :] = body_ref[pl.ds(start, tile), cols].astype(F32)
        ext[c, 0:RAD, :] = jnp.where(first, left_ref[:, cols], body_ref[t - tile - RAD : t - tile, cols]).astype(F32)
        ext[c, RAD + tile :, :] = jnp.where(first, body_ref[tile : tile + RAD, cols], right_ref[:, cols]).astype(F32)


def conv_forward(ext, tap_ref, out, row0):
    def step(r, _):
        base = pl.multiple_of(r * CHUNK, CHUNK)
        for c in range(ext.shape[0]):
            cols = slice(c * 128, (c + 1) * 128)
            acc = jnp.zeros((CHUNK, 128), F32)
            for b in range(8):
                reach = 4 if b == 0 else 3
                win = ext[c, pl.ds(base + b, CHUNK + 8 * reach), :]
                for m in range(reach + 1):
                    o = 8 * m + b
                    acc = acc + tap_ref[o : o + 1, cols] * win[8 * m : 8 * m + CHUNK]
            out[pl.ds(pl.multiple_of(row0 + base, CHUNK), CHUNK), cols] = acc.astype(out.dtype)
        return 0

    lax.fori_loop(0, CTILE // CHUNK, step, 0)


def conv_back_chunk(vext, gext, tap_ref, out, tapacc, row0, base):
    width = out.shape[1] // 3
    for c in range(vext.shape[0]):
        cols = slice(c * 128, (c + 1) * 128)
        acc = jnp.zeros((CHUNK, 128), F32)
        here = gext[c, pl.ds(base + RAD, CHUNK), :]
        for b in range(8):
            reach = 4 if b == 0 else 3
            win = gext[c, pl.ds(base + b, CHUNK + 8 * reach), :]
            for m in range(reach + 1):
                o = KC - 1 - (8 * m + b)
                acc = acc + tap_ref[o : o + 1, cols] * win[8 * m : 8 * m + CHUNK]
            win = vext[c, pl.ds(base + b, CHUNK + 8 * reach), :]
            for m in range(reach + 1):
                o = 8 * m + b
                tapacc[o, :, cols] += rowsum8(here * win[8 * m : 8 * m + CHUNK])
        into = slice(2 * width + c * 128, 2 * width + (c + 1) * 128)
        out[pl.ds(pl.multiple_of(row0 + base, CHUNK), CHUNK), into] = acc.astype(out.dtype)


def conv_backward(vext, gext, tap_ref, out, tapacc, row0):
    def step(r, _):
        conv_back_chunk(vext, gext, tap_ref, out, tapacc, row0, pl.multiple_of(r * CHUNK, CHUNK))
        return 0

    lax.fori_loop(0, CTILE // CHUNK, step, 0)


def wide_eye():
    lane = lax.broadcasted_iota(jnp.int32, (M, GROUP), 1) & 63
    return jnp.where(lane == lax.broadcasted_iota(jnp.int32, (M, GROUP), 0), 1.0, 0.0)


def head_sums(row):
    ones = jnp.where(head_mask(), 1.0, 0.0)
    return dot(jnp.broadcast_to(row, (8, GROUP)), ones, HI)[0:1]


def pinv_begin(mq_ref, mk_ref, a_ref, z_ref):
    for g in range(NG):
        s = dot_nt(mq_ref[:, gs(g)], spread(mk_ref[:, gs(g)]))
        e = jnp.exp(s - half_reduce(s, jnp.max, -jnp.inf))
        a = e / half_reduce(e, jnp.sum, 0.0)
        a_ref[:, gs(g)] = a
        col = jnp.sum(a, axis=0, keepdims=True)
        z_ref[0, :, gs(g)] = flip(a) / jnp.sqrt(head_sums(col * col))


def pinv_step(it, a_ref, z_ref, az_ref, t2_ref, t3_ref):
    eye = wide_eye()
    R = range(NG)
    z = [split(z_ref[it, :, gs(g)]) for g in R]
    az = [dot3(split(a_ref[:, gs(g)]), spread2(z[g])) for g in R]
    azs = [split(az[g]) for g in R]
    t2 = [15.0 * eye - dot3(azs[g], spread2(split(7.0 * eye - az[g]))) for g in R]
    t3 = [13.0 * eye - dot3(azs[g], spread2(split(t2[g]))) for g in R]
    for g in R:
        z_ref[it + 1, :, gs(g)] = 0.25 * dot3(z[g], spread2(split(t3[g])))
        az_ref[it, :, gs(g)] = az[g]
        t2_ref[it, :, gs(g)] = t2[g]
        t3_ref[it, :, gs(g)] = t3[g]


def pinv_back_step(it, a_ref, z_ref, az_ref, t2_ref, t3_ref, gz_ref, da_ref):
    eye = wide_eye()
    R = range(NG)
    az = [az_ref[it, :, gs(g)] for g in R]
    zs = [split(z_ref[it, :, gs(g)]) for g in R]
    gzs = [split(0.25 * gz_ref[:, gs(g)]) for g in R]
    baz = [spread2(split(az[g])) for g in R]
    d3 = [split(dot3(gzs[g], spread2(zs[g]))) for g in R]
    d2 = [split(-dot3(d3[g], baz[g])) for g in R]
    d1 = [-dot3(d2[g], baz[g]) for g in R]
    daz = [
        split(
            -dot3(split(t2_ref[it, :, gs(g)]), spread2(d3[g]))
            - dot3(split(7.0 * eye - az[g]), spread2(d2[g]))
            - d1[g]
        )
        for g in R
    ]
    for g in R:
        da_ref[:, gs(g)] += dot3(zs[g], spread2(daz[g]))
        gz_ref[:, gs(g)] = dot3(split(t3_ref[it, :, gs(g)]), spread2(gzs[g])) + dot3(
            daz[g], spread2(split(a_ref[:, gs(g)]))
        )


def pinv_back_end(g, a_ref, gz_ref, da_ref):
    a = a_ref[:, gs(g)]
    gz = gz_ref[:, gs(g)]
    col = jnp.sum(a, axis=0, keepdims=True)
    bound = jnp.sqrt(head_sums(col * col))
    tot = head_sums(jnp.sum(gz * a, axis=0, keepdims=True))
    full = flip(da_ref[:, gs(g)]) + gz / bound - (tot / (bound * bound * bound)) * col
    return a * (full - half_reduce(full * a, jnp.sum, 0.0))


def gather_marks(slots, outs, n):
    per = 4 * n // M
    half = slots.shape[2]
    for out, base in zip(outs, (0, 4)):
        if per == 1:
            got = [slots[i].astype(F32) for i in range(n)]
            for h in range(2):
                tall = jnp.concatenate([x[8 * h + base : 8 * h + base + 4] for x in got], axis=0)
                out[:, h * half : (h + 1) * half] = tall.astype(BF16)
        else:
            for h in range(2):
                lines = []
                for m in range(M):
                    total = jnp.zeros((1, half), F32)
                    for s in range(per // 4):
                        part = slots[m * (per // 4) + s].astype(F32)[8 * h + base : 8 * h + base + 4]
                        total = total + jnp.sum(part, axis=0, keepdims=True)
                    lines.append(total * (1.0 / per))
                out[:, h * half : (h + 1) * half] = jnp.concatenate(lines, axis=0).astype(BF16)


class Refs:
    def __init__(self, refs):
        self.it = iter(refs)

    def __call__(self, count):
        return [next(self.it) for _ in range(count)]

    def one(self):
        return next(self.it)


def front_kernel(*refs, n, ring):
    take = Refs(refs)
    x_any = take.one()
    if ring:
        wa, wu, wd, wv = take(4)
        wqkv_o, wo_o, ud0_o, ud_own = take(4)
    else:
        wq, vec = take(2)
    gains, taps = take(2)
    outs = take(7)
    mq, mk, uz, a_ref, z_ref, az_ref, t2_ref, t3_ref, vl, vr, p_ref = take(11)
    xs = take.one()
    stage = take(7)
    h_s, q_s, k_s, v_s, conv_s, f_s, e_s = stage
    means, pay, slots, ext, bdk, bdq, uacc, zacc, upart = take(9)
    xsem, osem, msem, hsem = take(4)
    sum_bufs = take(3)
    me = lax.axis_index("seq")
    t, d = xs.shape
    half = d // 2
    load_x = pltpu.make_async_copy(x_any, xs, xsem.at[0])
    load_x.start()
    drains = [pltpu.make_async_copy(s, o, osem.at[i]) for i, (s, o) in enumerate(zip(stage, outs))]
    if ring:
        wq, vec, sa, su, sd, so, co, wperm, psem, lsem = take(10)
        ring_one, ring_two = take(6), take(6)
        place = Place()
        greet(me, n, [place.twin])
        rep, seq = place.rep, place.seq
        rows_own = d // (2 * CHIPS)
        mine = at(rep, rows_own, 8)
        theirs = 1 - rep
        swaps = [
            remote(wa.at[0:3, :, at(theirs, half, 128)], sa.at[:, mine, :], psem.at[0], psem.at[1], place.twin),
            remote(wa.at[3, :, at(theirs, half, 128)], so.at[mine, :], psem.at[2], psem.at[3], place.twin),
            remote(wd.at[:, :, at(theirs, half, 128)], sd.at[pl.ds(2 * rep, 2)], psem.at[6], psem.at[7], place.twin),
        ]
        for c in swaps:
            c.start()
        sa[:, mine, :] = wa[0:3, :, at(rep, half, 128)]
        so[mine, :] = wa[3, :, at(rep, half, 128)]
        sd[pl.ds(2 * rep, 2)] = wd[:, :, at(rep, half, 128)]
        vec[at(seq * 2 + rep, rows_own, 8), :] = jnp.zeros((rows_own, 128), F32)
        vec[at(seq * 2 + rep, rows_own, 8), 0 : wv.shape[1]] = wv[...]
        swaps[0].wait()
        wq[:, at(seq, 2 * rows_own, 16), at(rep, half, 128)] = sa[...].astype(BF16)
        first = GatherMesh(place, (LINES, HALF, HALF, HALF), (vec, wq.at[2], wq.at[1], wq.at[0]), (None,) * 4, ring_one)
        first.start_z()
        first.start_across((0, 1))
        rows_chip = 2 * rows_own
        for p in range(PARTS):
            for c in range(0, CHIPS, 8):
                got = [
                    wu[:, (PARTS * (c + h) + p) * rows_chip : (PARTS * (c + h) + p + 1) * rows_chip] for h in range(8)
                ]
                wperm[p, :, c * rows_chip : (c + 8) * rows_chip] = jnp.concatenate(got, axis=1)
        swaps.append(
            remote(wperm.at[:, :, at(theirs, half, 128)], su.at[:, mine, :], psem.at[4], psem.at[5], place.twin)
        )
        swaps[-1].start()
        su[:, mine, :] = wperm[:, :, at(rep, half, 128)]
        for c in swaps[1:]:
            c.wait()
        co[...] = so[...].astype(BF16)
        ud_own[:, 0] = su[...].astype(BF16)
        ud_own[:, 1] = sd[...].astype(BF16)
        rest = GatherMesh(place, (STACK, HALF), (ud0_o, wo_o), (ud_own.at[0], co), ring_two)
        local = [
            pltpu.make_async_copy(src, piece(kind, out, seq, rep), lsem.at[i])
            for i, (src, kind, out) in enumerate(zip(rest.own, rest.kinds, rest.outs))
        ]

        rest.start_z()
        for c in local:
            c.start()
        first.line((0, 1))
        first.line_on((0, 1))
        first.start_across((2, 3))
        first.plane((0, 1))
        for which in ((2,), (3,)):
            first.line(which)
            first.line_on(which)
        first.space((0,))
        first.shares_in((0,))
        save_w = pltpu.make_async_copy(wq, wqkv_o, xsem.at[1])
    else:
        greet(me, n, [])

    turned = jnp.transpose(vec[...]).astype(BF16).astype(F32)
    gains[...] = turned[0:8]
    taps[...] = turned[2:42]
    load_x.wait()

    def tile(i):
        return pl.ds(pl.multiple_of(i * (t // 4), t // 4), t // 4)

    def norm(i, _):
        normal, _inv = normalize(xs[tile(i), :].astype(F32))
        h_s[tile(i), :] = (normal * gains[0:1, :]).astype(BF16)
        return 0

    def project_v(i, _):
        v_s[tile(i), :] = dot(h_s[tile(i), :], wq[2]).astype(BF16)
        return 0

    def project_k(i, _):
        k = (dot(h_s[tile(i), :], wq[1]) * QK_SCALE).astype(BF16)
        k_s[tile(i), :] = k
        means[pl.ds(i + 4, 1), :] = jnp.mean(k.astype(F32), axis=0, keepdims=True)
        return 0

    def project_q(i, _):
        q = (dot(h_s[tile(i), :], wq[0]) * QK_SCALE).astype(BF16)
        q_s[tile(i), :] = q
        means[pl.ds(i, 1), :] = jnp.mean(q.astype(F32), axis=0, keepdims=True)
        return 0

    def inner(i, _):
        fill_inner(ext, v_s, i * CTILE)
        conv_forward(ext, taps, conv_s, i * CTILE)
        if ring:

            @pl.when(i == 4)
            def _():
                rest.line_on((0,))

            @pl.when(i == 5)
            def _():
                rest.line((1,))
                rest.line_on((1,))

        return 0

    tiles = t // CTILE
    lax.fori_loop(0, 4, norm, 0)
    if ring:
        first.plane((2,))
        first.space((1,))
        first.shares_in((1,))
    lax.fori_loop(0, 4, project_v, 0)
    halos = halo_copies(v_s, vl, vr, me, n, hsem)
    for c in halos:
        c.start()
    if ring:
        first.plane((3,))
        rest.start_across()
    lax.fori_loop(1, tiles // 2, inner, 0)
    if ring:
        first.space((2,))
        first.shares_in((2,))
    lax.fori_loop(0, 4, project_k, 0)
    if ring:
        first.space((3,))
        first.shares_in((3,))
        save_w.start()
        rest.line((0,))
    lax.fori_loop(0, 4, project_q, 0)

    pay[...] = jnp.concatenate([means[:, :half], means[:, half:]], axis=0).astype(BF16)

    def mark(j, peer):
        return remote(pay, slots.at[me], msem.at[0, j], msem.at[1, j], {"seq": peer})

    each_peer(me, n, mark, lambda c: c.start())
    slots[pl.ds(me, 1)] = pay[...][None]
    for c in drains[:4]:
        c.start()

    lax.fori_loop(tiles // 2, tiles - 1, inner, 0)
    for c in halos:
        c.wait()
    mask_halos(vl, vr, me, n)

    def edge(i, _):
        fill_edge(ext, v_s, vl, vr, i == 0)
        conv_forward(ext, taps, conv_s, i * (t - CTILE))
        return 0

    lax.fori_loop(0, 2, edge, 0)
    drains[4].start()
    each_peer(me, n, mark, lambda c: c.wait())
    gather_marks(slots, (mq, mk), n)
    for g in range(NG):
        bdk[g] = spread(mk[:, gs(g)])
        bdq[g] = spread(mq[:, gs(g)])
    uacc[...] = jnp.zeros_like(uacc)
    zacc[...] = jnp.zeros_like(zacc)
    ones_bd = jnp.where(head_mask(), 1.0, 0.0).astype(BF16)

    def expand(i, _):
        for g in range(NG):
            e = jnp.exp(dot_nt(k_s[tile(i), gs(g)], bdq[g])).astype(BF16)
            e_s[tile(i), gs(g)] = e
            uacc[g] += dot_tn(e, v_s[tile(i), gs(g)])
            zacc[g] += dot_tn(e, jnp.ones((t // 4, 128), BF16))
        if ring:

            @pl.when(i == 0)
            def _():
                rest.plane((0,))

            @pl.when(i == 1)
            def _():
                rest.plane((1,))

        return 0

    def attend(i, _):
        for g in range(NG):
            s = dot_nt(q_s[tile(i), gs(g)], bdk[g])
            ex = jnp.exp(s - half_reduce(s, jnp.max, -jnp.inf))
            den = dot(ex.astype(BF16), ones_bd)
            f_s[tile(i), gs(g)] = (ex / den).astype(BF16)
        return 0

    lax.fori_loop(0, 4, expand, 0)
    lane = lax.broadcasted_iota(jnp.int32, (M, 128), 1)
    zt = jnp.zeros((M, 128), F32)
    for g in range(NG):
        put_tall(upart, g, collect(uacc[g]))
        for h in range(4):
            zt = zt + jnp.where(lane == 4 * g + h, zacc[g, h * 64 : h * 64 + 64, :], 0.0)
    upart[6 * M : 7 * M, :] = zt
    upart[7 * M :, :] = jnp.zeros((upart.shape[0] - 7 * M, 128), F32)
    summing = SeqSum(me, n, upart, uz, *sum_bufs)
    summing.start()
    pinv_begin(mq, mk, a_ref, z_ref)

    def newton(it, _):
        pinv_step(it, a_ref, z_ref, az_ref, t2_ref, t3_ref)
        return 0

    lax.fori_loop(0, 4, attend, 0)
    for c in drains[5:]:
        c.start()
    summing.turn()
    lax.fori_loop(0, NSITER, newton, 0)
    summing.finish()
    p_ref[...] = z_ref[NSITER]
    for c in drains:
        c.wait()
    if ring:
        for c in local:
            c.wait()
        save_w.wait()
        rest.space((0, 1))
        rest.shares_in((0, 1))
        first.finish()
        rest.finish()


def front(x, weights, n, ring):
    t, d = x.shape
    if ring:
        rown = d // CHIPS
        own4 = (4, rown, d // 2)
        extra_out = [sds((3, d, d), BF16), sds((d, d), BF16), sds((2, d, d), BF16), sds((4, 2, rown, d // 2), BF16)]
        extra = [
            pltpu.VMEM((3, d, d), BF16),
            pltpu.VMEM((d, 128), F32),
            pltpu.VMEM((3, rown, d // 2), F32),
            pltpu.VMEM(own4, F32),
            pltpu.VMEM(own4, F32),
            pltpu.VMEM((rown, d // 2), F32),
            pltpu.VMEM((rown, d // 2), BF16),
            pltpu.VMEM((PARTS, rown // 2, d), F32),
            DMA((8,)),
            DMA((2,)),
        ] + GatherMesh.scratch(4) + GatherMesh.scratch(2)
    else:
        extra_out, extra = [], []
    r = padded_rows(7 * M, n)
    big = sds((t, d), BF16)
    steps = sds((NSITER, M, d), F32)
    res = pl.pallas_call(
        functools.partial(front_kernel, n=n, ring=ring),
        in_specs=[ANYW] + [VM] * len(weights),
        out_specs=([ANYW] * 3 + [VM] if ring else []) + [VM] * 2 + [ANYW] * 7 + [VM] * 11,
        out_shape=extra_out
        + [sds((8, d), F32), sds((40, d), F32)]
        + [big] * 7
        + [sds((M, d), BF16)] * 2
        + [sds((r, 128), F32), sds((M, d), F32), sds((NSITER + 1, M, d), F32), steps, steps, steps]
        + [sds((RAD, d), BF16)] * 2
        + [sds((M, d), F32)],
        scratch_shapes=[pltpu.VMEM((t, d), BF16)] * 8
        + [
            pltpu.VMEM((8, d), F32),
            pltpu.VMEM((16, d // 2), BF16),
            pltpu.VMEM((n, 16, d // 2), BF16),
            pltpu.VMEM((d // 128, CTILE + 2 * RAD, 128), F32),
            pltpu.VMEM((NG, GROUP, GROUP), BF16),
            pltpu.VMEM((NG, GROUP, GROUP), BF16),
            pltpu.VMEM((NG, GROUP, GROUP), F32),
            pltpu.VMEM((NG, GROUP, 128), F32),
            pltpu.VMEM((r, 128), F32),
            DMA((2,)),
            DMA((7,)),
            DMA((2, n)),
            DMA((4,)),
        ]
        + SeqSum.scratch(r, n)
        + extra,
        compiler_params=pltpu.CompilerParams(collective_id=1, has_side_effects=True, vmem_limit_bytes=VMEM_LIMIT),
        name="front",
    )(x, *weights)
    return res if ring else [None] * 4 + list(res)


PARTS = 4
HALF_D = 384
PART = 768


def middle_kernel(*refs, n, ring):
    take = Refs(refs)
    x_a, dy_a, f_a, q_a, conv_a, wo_a, ud_a = take(7)
    if ring:
        ud_own = take.one()
    gains, mk, uz, p_ref = take(4)
    out_o, dx_o, dmix_o, dqf_o, g_o = take(5)
    gw_ref, dkt_ref, dg_ref = take(3)
    if ring:
        t_ud = take.one()
    x_s, dy_s, f_s, mix_s, h2_s, da_s, x1_s, wo_s, ud = take(9)
    oacc, hacc, wbd, bdk, gwacc, dktacc, dgacc = take(7)
    isem, osem = take(2)
    t, d = x_s.shape
    tile = t // 4
    act_s, q_s = x_s, x_s
    seq = lax.axis_index("seq")
    parts_in = 1 if ring else PARTS
    gain = gains[1:2, :]

    def here(i):
        return pl.ds(pl.multiple_of(i * tile, tile), tile)

    load_q = pltpu.make_async_copy(q_a, q_s, isem.at[7])
    loads = [
        pltpu.make_async_copy(a, b, isem.at[i])
        for i, (a, b) in enumerate(
            ((f_a, f_s), (conv_a, mix_s), (x_a, x_s), (wo_a, wo_s), (ud_a, ud.at[pl.ds(0, parts_in)]), (dy_a, dy_s))
        )
    ]
    for c in loads:
        c.start()
    if ring:
        place = Place()
        gathers = [None] + [
            GatherMesh(place, (STACK,), (ud.at[p],), (ud_own.at[p],), take(6)) for p in range(1, PARTS)
        ]
        scatters = [
            ScatterMesh.take(take, place, (STACK,), (ud.at[p],), in_place=True) for p in range(PARTS - 1)
        ]
        greet(seq, n, [place.twin])
        for g in gathers[1:]:
            g.start_z()
        for p in range(1, PARTS):
            gathers[p].start_across()
            ud[p, :, at(seq, d // CHIPS, 16), at(place.rep, d // 2, 128)] = ud_own[p]

    def tick(cond, *acts):
        if ring and acts:

            @pl.when(cond)
            def _():
                for act in acts:
                    act()

    K = (0,)

    def move(p, *names):
        return [functools.partial(getattr(gathers[p], name), K) for name in names] if ring else []

    def send(p, *names):
        return [functools.partial(getattr(scatters[p], name), 0) for name in names] if ring else []

    gwacc[...] = jnp.zeros_like(gwacc)
    dktacc[...] = jnp.zeros_like(dktacc)
    dgacc[...] = jnp.zeros_like(dgacc)
    for g in range(NG):
        bv = u_group(uz, g) / zt_group(uz, g)
        wbd[g] = spread(dot(p_ref[:, gs(g)], spread(bv), HI)).astype(BF16)
        bdk[g] = spread(mk[:, gs(g)])
    for c in loads[:4]:
        c.wait()

    def before(i, _):
        r = here(i)
        for g in range(NG):
            mix_s[r, gs(g)] = (dot(f_s[r, gs(g)], wbd[g]) + mix_s[r, gs(g)].astype(F32)).astype(BF16)
        x1 = x_s[r, :].astype(F32) + dot(mix_s[r, :], wo_s[...])
        oacc[r, :] = x1
        x1_s[r, :] = x1.astype(BF16)
        normal, _inv = normalize(x1)
        h2_s[r, :] = (normal * gain).astype(BF16)
        tick(i == 1, *move(1, "line", "line_on"))
        tick(i == 3, *move(1, "plane"))
        return 0

    lax.fori_loop(0, 4, before, 0)
    loads[4].wait()
    loads[5].wait()
    plan = {
        (0, 0): move(2, "line", "line_on"),
        (0, 2): move(1, "space") + move(2, "plane"),
        (0, 3): move(3, "line", "line_on"),
        (1, 0): move(3, "plane") + send(0, "far"),
        (1, 1): move(2, "space"),
        (1, 3): send(0, "mid") + move(3, "space"),
        (2, 0): send(1, "far"),
        (2, 1): send(0, "near"),
        (2, 3): send(1, "mid"),
        (3, 0): send(2, "far"),
        (3, 1): send(1, "near"),
        (3, 3): send(2, "mid"),
    }
    for p in range(PARTS):
        if ring and p > 0:
            gathers[p].shares_in(K)
        u, dn = ud.at[p, 0], ud.at[p, 1]

        def through(i, _):
            r = here(i)
            h2 = h2_s[r, :]
            dy = dy_s[r, :]
            o = h = None
            for c in range(0, d, PART):
                cols = slice(c, c + PART)
                act, slope = gelu_parts(dot(h2, u[:, cols]))
                act = act.astype(BF16)
                act_s[r, cols] = act
                da = (dot_nt(dy, dn[cols, :]) * slope).astype(BF16)
                da_s[r, cols] = da
                oc, hc = dot(act, dn[cols, :]), dot_nt(da, u[:, cols])
                o, h = (oc, hc) if o is None else (o + oc, h + hc)
            oacc[r, :] += o
            hacc[r, :] = h if p == 0 else hacc[r, :] + h
            for j in range(4):
                tick(i == j, *plan.get((p, j), []))
            return 0

        lax.fori_loop(0, 4, through, 0)
        if ring and p > 0:
            gathers[p].finish()

        def grads(j, _):
            cols = pl.ds(pl.multiple_of(j * HALF_D, HALF_D), HALF_D)
            ud[p, 0, cols, :] = dot_tn(h2_s[:, cols], da_s[...]).astype(BF16)
            ud[p, 1, cols, :] = dot_tn(act_s[:, cols], dy_s[...]).astype(BF16)
            return 0

        lax.fori_loop(0, d // HALF_D, grads, 0)
        if ring and p < PARTS - 1:
            scatters[p].start()
        if ring and p == 3:
            t_ud[0] = scatters[0].total(0)
    load_q.start()
    first_out = PARTS - 1 if ring else 0
    stored = [
        pltpu.make_async_copy(ud.at[p], g_o.at[pl.ds(2 * (p - first_out), 2)], osem.at[16 + p])
        for p in range(first_out, PARTS)
    ]
    for c in stored:
        c.start()
    tick(True, *send(2, "near"))
    if ring:
        t_ud[1] = scatters[1].total(0)
    load_q.wait()

    def after(i, _):
        r = here(i)
        normal, inv = normalize(x1_s[r, :].astype(F32))
        x1_s[r, :] = oacc[r, :].astype(BF16)
        pltpu.make_async_copy(x1_s.at[r], out_o.at[r], osem.at[i]).start()
        dh2 = hacc[r, :]
        dgacc[...] += rowsum8(dh2 * normal)
        dx = (norm_back(dh2, normal, inv, gain) + dy_s[r, :].astype(F32)).astype(BF16)
        dy_s[r, :] = dx
        pltpu.make_async_copy(dy_s.at[r], dx_o.at[r], osem.at[4 + i]).start()
        dmix = dot_nt(dx, wo_s[...]).astype(BF16)
        h2_s[r, :] = dmix
        pltpu.make_async_copy(h2_s.at[r], dmix_o.at[r], osem.at[8 + i]).start()
        ones_bd = jnp.where(head_mask(), 1.0, 0.0).astype(BF16)
        for g in range(NG):
            dm = dmix[:, gs(g)]
            f = f_s[r, gs(g)]
            df = dot_nt(dm, wbd[g])
            gwacc[g] += dot_tn(f, dm)
            ff32 = f.astype(F32)
            prod = df * ff32
            hi, lo = split(prod)
            ds = (ff32 * (df - (dot(hi, ones_bd) + dot(lo, ones_bd)))).astype(BF16)
            da_s[r, gs(g)] = dot(ds, bdk[g]).astype(BF16)
            dktacc[g] += dot_tn(ds, q_s[r, gs(g)])
        pltpu.make_async_copy(da_s.at[r], dqf_o.at[r], osem.at[12 + i]).start()
        return 0

    lax.fori_loop(0, 4, after, 0)

    def grad_o(j, _):
        cols = pl.ds(pl.multiple_of(j * HALF_D, HALF_D), HALF_D)
        wo_s[cols, :] = dot_tn(mix_s[:, cols], dy_s[...]).astype(BF16)
        return 0

    lax.fori_loop(0, d // HALF_D, grad_o, 0)
    stored.append(pltpu.make_async_copy(wo_s, g_o.at[2 * (PARTS - first_out)], osem.at[20]))
    stored[-1].start()
    for g in range(NG):
        put_tall(gw_ref, g, collect(gwacc[g]))
        dkt_ref[:, gs(g)] = collect(dktacc[g])
    if gw_ref.shape[0] > 6 * M:
        gw_ref[6 * M :] = jnp.zeros((gw_ref.shape[0] - 6 * M, 128), F32)
    dg_ref[...] = jnp.broadcast_to(jnp.sum(dgacc[...], axis=0, keepdims=True), dg_ref.shape)
    if ring:
        t_ud[2] = scatters[2].total(0)
        for sc in scatters:
            sc.finish()
    for i in range(4):
        for b, src, dst in ((0, x1_s, out_o), (4, dy_s, dx_o), (8, h2_s, dmix_o), (12, da_s, dqf_o)):
            pltpu.make_async_copy(src.at[here(i)], dst.at[here(i)], osem.at[b + i]).wait()
    for c in stored:
        c.wait()


def middle(x, dy, f, q, conv, wo, ud, ud_own, gains, mk, uz, p, gw_rows, n):
    ring = ud_own is not None
    t, d = x.shape
    big = sds((t, d), BF16)
    outs = [big] * 4 + [sds((3 if ring else 2 * PARTS + 1, d, d), BF16)]
    outs += [sds((gw_rows, 128), F32), sds((M, d), F32), sds((8, d), F32)]
    extra = []
    if ring:
        cell = (2, d // CHIPS, d // 2)
        outs += [sds((PARTS - 1, *cell), F32)]
        extra = GatherMesh.scratch(1) * (PARTS - 1) + ScatterMesh.scratch([(cell, BF16)], True) * (PARTS - 1)
    square = pltpu.VMEM((NG, GROUP, GROUP), BF16)
    square_f = pltpu.VMEM((NG, GROUP, GROUP), F32)
    return pl.pallas_call(
        functools.partial(middle_kernel, n=n, ring=ring),
        in_specs=[ANYW] * 7 + [VM] * (5 if ring else 4),
        out_specs=[ANYW] * 5 + [VM] * (len(outs) - 5),
        out_shape=outs,
        scratch_shapes=[pltpu.VMEM((t, d), BF16)] * 7
        + [
            pltpu.VMEM((d, d), BF16),
            pltpu.VMEM((PARTS, 2, d, d), BF16),
            pltpu.VMEM((t, d), F32),
            pltpu.VMEM((t, d), F32),
            square,
            square,
            square_f,
            square_f,
            pltpu.VMEM((8, d), F32),
            DMA((8,)),
            DMA((21,)),
        ]
        + extra,
        compiler_params=pltpu.CompilerParams(
            collective_id=4 if ring else None, has_side_effects=True, vmem_limit_bytes=61 * 1024 * 1024
        ),
        name="middle",
    )(x, dy, f, q, conv, wo, ud, *((ud_own,) if ring else ()), gains, mk, uz, p)


def rear_kernel(*refs, n, ring, seg_len):
    take = Refs(refs)
    bodies = take(5)
    x_a, dx_a, h1_a, w_a = take(4)
    if ring:
        grads = take(1)
    gw_part, uz, a_ref, z_ref, az_ref, t2_ref, t3_ref, mq, mk, vl, vr, taps, dkt_ref, dg2_ref, gains = take(15)
    if ring:
        t_ud = take.one()
    ig_o, gvec_o, gqkv_o, dg_o = take(4)
    if ring:
        r_uo, r_down, r_vec, r_qkv = take(4)
    v_s, g_s, e_s, k_s, dqf_s, dqkv, gvec = take(7)
    vext, gext, tapacc, gl, gr, gw, gz, da, dubd, rowadd, dqtacc, bdq, pay, slots, own = take(15)
    w_s, gqkv, part, dslots, dgacc, gsem = take(6)
    isem, osem, hsem, wsem = take(4)
    sum_bufs = take(3)
    me = lax.axis_index("seq")
    t, d = v_s.shape
    loads = [
        pltpu.make_async_copy(b, s, isem.at[i]) for i, (b, s) in enumerate(zip(bodies, (v_s, g_s, e_s, k_s, dqf_s)))
    ]
    for c in loads:
        c.start()
    load_x = pltpu.make_async_copy(x_a, v_s, isem.at[5])
    load_dx = pltpu.make_async_copy(dx_a, g_s, isem.at[6])
    load_h1 = pltpu.make_async_copy(h1_a, e_s, isem.at[7])
    load_w = pltpu.make_async_copy(w_a, w_s, isem.at[8])
    load_w.start()
    if ring:
        place = Place()
        greet(me, n, [place.twin])
        big = ScatterMesh.take(take, place, (STACK,), grads)
        vec = ScatterMesh.take(take, place, (LINES,), (gvec,))
        late = ScatterMesh.take(take, place, (HALF,) * 3, [gqkv.at[i] for i in range(3)], in_place=True)
        fuo, fd, fq, fsem = take(4)
    else:
        greet(me, n, [])
    summing = SeqSum(me, n, gw_part, gw, *sum_bufs)
    loads[1].wait()
    halos = halo_copies(g_s, gl, gr, me, n, hsem)
    for c in halos:
        c.start()
    summing.start()
    if ring:
        big.start()

    def tick(cond, *acts):
        if ring:

            @pl.when(cond)
            def _():
                for act, k in acts:
                    act(k)

    tapacc[...] = jnp.zeros_like(tapacc)
    loads[0].wait()
    if not ring:
        big = vec = None
    far = (lambda k: big.far(k))
    mid = (lambda k: big.mid(k))
    near = (lambda k: big.near(k))

    def inner(i, _):
        fill_inner(vext, v_s, i * CTILE)
        fill_inner(gext, g_s, i * CTILE)
        conv_backward(vext, gext, taps, dqkv, tapacc, i * CTILE)


        @pl.when(i == 2)
        def _():
            summing.turn()

        tick(i == 2, (far, 0))
        return 0

    beside = NSITER // 2
    split_at = t // CTILE - 1 - beside
    lax.fori_loop(1, split_at, inner, 0)
    for c in halos:
        c.wait()
    mask_halos(gl, gr, me, n)

    def edge(i, _):
        fill_edge(vext, v_s, vl, vr, i == 0)
        fill_edge(gext, g_s, gl, gr, i == 0)
        conv_backward(vext, gext, taps, dqkv, tapacc, i * (t - CTILE))
        return 0

    lax.fori_loop(0, 2, edge, 0)
    summing.finish()
    for g in range(NG):
        z = zt_group(uz, g)
        bv = u_group(uz, g) / z
        gwg = u_group(gw, g)
        gz[:, gs(g)] = flip(dot_nt(gwg, spread(bv), HI))
        dbv = dot(flip(z_ref[NSITER, :, gs(g)]), spread(gwg), HI)
        dubd[g] = spread(dbv / z).astype(BF16)
        rowadd[g] = dot_nt(jnp.ones((8, GROUP), F32), spread(dbv * bv / z), HI)
        bdq[g] = spread(mq[:, gs(g)])
    da[...] = jnp.zeros_like(da)

    def newton(j, _):
        row0 = pl.multiple_of((split_at + lax.div(j, 2)) * CTILE, CTILE)

        @pl.when(lax.rem(j, 2) == 0)
        def _():
            fill_inner(vext, v_s, row0)
            fill_inner(gext, g_s, row0)

        base = lax.rem(j, 2) * (CTILE // 2)
        for h in range(2):
            conv_back_chunk(vext, gext, taps, dqkv, tapacc, row0, pl.multiple_of(base + h * CHUNK, CHUNK))
        pinv_back_step(NSITER - 1 - j, a_ref, z_ref, az_ref, t2_ref, t3_ref, gz, da)
        tick(j == 0, (mid, 0))
        tick(j == 3, (near, 0))
        return 0

    lax.fori_loop(0, NSITER, newton, 0)
    load_dx.start()
    dtap = jnp.sum(tapacc[...], axis=1)
    lines = jnp.concatenate([jnp.zeros((1, d), F32), dg2_ref[0:1, :], dtap, jnp.zeros((128 - 42, d), F32)], axis=0)
    gvec[...] = jnp.transpose(lines)
    if ring:
        vec.start()
    else:
        save_vec = pltpu.make_async_copy(gvec, gvec_o, osem.at[1])
        save_vec.start()
    loads[2].wait()
    loads[3].wait()
    dqtacc[...] = jnp.zeros_like(dqtacc)

    def cols(part, g):
        return slice(part * d + g * GROUP, part * d + (g + 1) * GROUP)

    def through(i, _):
        here = pl.ds(pl.multiple_of(i * (t // 4), t // 4), t // 4)
        for g in range(NG):
            e = e_s[here, gs(g)]
            de = dot_nt(v_s[here, gs(g)], dubd[g]) - rowadd[g, 0:1, :]
            ds = (e.astype(F32) * de).astype(BF16)
            dqkv[here, cols(2, g)] = (dot(e, dubd[g]) + dqkv[here, cols(2, g)].astype(F32)).astype(BF16)
            dqkv[here, cols(1, g)] = dot(ds, bdq[g]).astype(BF16)
            dqtacc[g] += dot_tn(ds, k_s[here, gs(g)])
        tick(i == 0, (lambda k: vec.far(k), 0))
        tick(i == 2, (lambda k: vec.mid(k), 0))
        return 0

    lax.fori_loop(0, 4, through, 0)
    load_x.start()
    load_h1.start()

    rows_dev = max(M // n, 1)
    per_mark = n * rows_dev // M
    if rows_dev < 4:
        pay[...] = jnp.zeros_like(pay)
    for g in range(NG):
        ds = pinv_back_end(g, a_ref, gz, da)
        dq = collect(dqtacc[g]) + dot(ds, spread(mk[:, gs(g)].astype(F32)), HI) * (1.0 / n)
        dk = dkt_ref[:, gs(g)] + dot(flip(ds), spread(mq[:, gs(g)].astype(F32)), HI) * (1.0 / n)
        for i in range(n):
            row = i * rows_dev // per_mark
            pay[i, 0:rows_dev, gs(g)] = dq[row : row + rows_dev]
            pay[i, 4 : 4 + rows_dev, gs(g)] = dk[row : row + rows_dev]

    def mark(j, peer):
        return remote(pay.at[peer], slots.at[me], wsem.at[0, j], wsem.at[1, j], {"seq": peer})

    each_peer(me, n, mark, lambda c: c.start())
    slots[pl.ds(me, 1)] = pay[pl.ds(me, 1)]

    def project_back(p, scale):
        def body(j, _):
            cols = pl.ds(pl.multiple_of(j * HALF_D, HALF_D), HALF_D)
            gqkv[p, cols, :] = (dot_tn(e_s[:, cols], dqkv[:, p * d : (p + 1) * d]) * scale).astype(BF16)
            return 0

        lax.fori_loop(0, d // HALF_D, body, 0)
        if ring:
            late.start((p,))

    load_h1.wait()
    project_back(2, 1.0)
    if ring:
        last_ud = big.total(0)
        for p in range(PARTS - 1):
            fuo[p] = t_ud[p, 0]
            fd[p] = t_ud[p, 1]
        fuo[PARTS - 1] = last_ud[0]
        fd[PARTS - 1] = last_ud[1]
        fuo[PARTS] = last_ud[2]
        cols = at(place.rep, d // 2, 128)
        back = [swap_rows(fuo, r_uo, place, fsem.at[0])]
        for j in range(2):
            r_down[j, :, cols] = fd[2 * place.rep + j]
            src = fd.at[2 * (1 - place.rep) + j]
            back.append(remote(src, r_down.at[j, :, cols], fsem.at[1 + j, 0], fsem.at[1 + j, 1], place.twin))
        for c in back:
            c.start()
        vec.near(0)
        late.far(2)
    loads[4].wait()
    each_peer(me, n, mark, lambda c: c.wait())
    own[...] = lax.fori_loop(1, n, lambda i, acc: acc + slots[i], slots[0]) * (1.0 / seg_len)

    def landed(i, _):
        here = pl.ds(pl.multiple_of(i * (t // 4), t // 4), t // 4)
        row = lax.div(i * rows_dev, 4)
        dqkv[here, 0:d] = (dqf_s[here, :].astype(F32) + own[pl.ds(row, 1), :]).astype(BF16)
        dqkv[here, d : 2 * d] = (dqkv[here, d : 2 * d].astype(F32) + own[pl.ds(row + 4, 1), :]).astype(BF16)
        return 0

    lax.fori_loop(0, 4, landed, 0)
    project_back(1, QK_SCALE)
    tick(True, (lambda k: late.mid(k), 2), (lambda k: late.far(k), 1))
    project_back(0, QK_SCALE)
    tick(True, (lambda k: late.far(k), 0))
    for c in (load_w, load_x, load_dx):
        c.wait()
    dgacc[...] = jnp.zeros_like(dgacc)

    def back_through(i, _):
        here = pl.ds(pl.multiple_of(i * (t // 4), t // 4), t // 4)
        dq, dk, dv = (dqkv[here, p * d : (p + 1) * d] for p in range(3))
        dh = (dot_nt(dq, w_s[0]) + dot_nt(dk, w_s[1])) * QK_SCALE + dot_nt(dv, w_s[2])
        normal, inv = normalize(v_s[here, :].astype(F32))
        dgacc[...] += rowsum8(dh * normal)
        ig = norm_back(dh, normal, inv, gains[0:1, :]) + g_s[here, :].astype(F32)
        v_s[here, :] = ig.astype(BF16)
        pltpu.make_async_copy(v_s.at[here], ig_o.at[here], osem.at[2 + i]).start()
        tick(i == 1, (lambda k: late.near(k), 2), (lambda k: late.mid(k), 1))
        tick(i == 2, (lambda k: late.mid(k), 0))
        return 0

    lax.fori_loop(0, 4, back_through, 0)
    row = jnp.sum(dgacc[...], axis=0, keepdims=True)
    part[...] = jnp.concatenate(
        [row[:, c : c + 128] for c in range(0, d, 128)] + [jnp.zeros((8 - d // 128, 128), F32)], axis=0
    )

    def send(j, peer):
        return remote(part, dslots.at[me], gsem.at[0, j], gsem.at[1, j], {"seq": peer})

    each_peer(me, n, send, lambda c: c.start())
    dslots[pl.ds(me, 1)] = part[...][None]
    tick(True, (lambda k: late.near(k), 1), (lambda k: late.near(k), 0))
    each_peer(me, n, send, lambda c: c.wait())
    total = lax.fori_loop(1, n, lambda i, acc: acc + dslots[i], dslots[0])
    dg_o[0] = total
    if ring:
        twin_sum = remote(dg_o.at[0], dg_o.at[1], gsem.at[0, 0], gsem.at[1, 0], place.twin)
        twin_sum.start()
        r_vec[...] = vec.total(0)
        for p in (2, 1, 0):
            fq[p] = late.total(p)
        back.append(swap_rows(fq, r_qkv, place, fsem.at[3]))
        back[-1].start()
        twin_sum.wait()
        big.finish()
        vec.finish()
        late.finish()
        for c in back:
            c.wait()
    else:
        dg_o[1] = jnp.zeros_like(total)
        save_vec.wait()
        save_g = pltpu.make_async_copy(gqkv, gqkv_o, osem.at[0])
        save_g.start()
        save_g.wait()
    for i in range(4):
        here = pl.ds(i * (t // 4), t // 4)
        pltpu.make_async_copy(v_s.at[here], ig_o.at[here], osem.at[2 + i]).wait()


def rear(bodies, more, grads, gw, uz, a, z, az, t2, t3, mq, mk, vl, vr, taps, dkt, dg2, gains, t_ud, n, seg_len):
    ring = grads is not None
    t, d = bodies[0].shape
    r = gw.shape[0]
    outs = [sds((t, d), BF16), sds((d, 128), F32), sds((3, d, d), BF16), sds((2, 8, 128), F32)]
    extra = []
    if ring:
        own = d // (2 * CHIPS)
        outs += [sds((PARTS + 1, own, d), F32), sds((2, 2 * own, d), F32), sds((own, 128), F32), sds((3, own, d), F32)]
        extra = ScatterMesh.scratch([((3, 2 * own, d // 2), BF16)]) + ScatterMesh.scratch([((own, 128), F32)])
        extra += ScatterMesh.scratch([((2 * own, d // 2), BF16)] * 3, True) + [
            pltpu.VMEM((PARTS + 1, 2 * own, d // 2), F32),
            pltpu.VMEM((PARTS, 2 * own, d // 2), F32),
            pltpu.VMEM((3, 2 * own, d // 2), F32),
            DMA((4, 2)),
        ]
    ext = pltpu.VMEM((d // 128, CTILE + 2 * RAD, 128), F32)
    halo = pltpu.VMEM((RAD, d), BF16)
    small = pltpu.VMEM((M, d), F32)
    return pl.pallas_call(
        functools.partial(rear_kernel, n=n, ring=ring, seg_len=seg_len),
        in_specs=[ANYW] * (9 + (1 if ring else 0)) + [VM] * (15 + (1 if ring else 0)),
        out_specs=[ANYW] * 3 + [VM] * (len(outs) - 3),
        out_shape=outs,
        scratch_shapes=[pltpu.VMEM((t, d), BF16)] * 5
        + [
            pltpu.VMEM((t, 3 * d), BF16),
            pltpu.VMEM((d, 128), F32),
            ext,
            ext,
            pltpu.VMEM((40, 8, d), F32),
            halo,
            halo,
            pltpu.VMEM((r, 128), F32),
            small,
            small,
            pltpu.VMEM((NG, GROUP, GROUP), BF16),
            pltpu.VMEM((NG, 8, GROUP), F32),
            pltpu.VMEM((NG, GROUP, GROUP), F32),
            pltpu.VMEM((NG, GROUP, GROUP), BF16),
            pltpu.VMEM((n, 8, d), F32),
            pltpu.VMEM((n, 8, d), F32),
            pltpu.VMEM((8, d), F32),
            pltpu.VMEM((3, d, d), BF16),
            pltpu.VMEM((3, d, d), BF16),
            pltpu.VMEM((8, 128), F32),
            pltpu.VMEM((n, 8, 128), F32),
            pltpu.VMEM((8, d), F32),
            DMA((2, n)),
            DMA((9,)),
            DMA((6,)),
            DMA((4,)),
            DMA((2, n)),
        ]
        + SeqSum.scratch(r, n)
        + extra,
        compiler_params=pltpu.CompilerParams(
            collective_id=2, has_side_effects=True, vmem_limit_bytes=61 * 1024 * 1024
        ),
        name="rear",
    )(*bodies, *more, *(grads if ring else ()), gw, uz, a, z, az, t2, t3, mq, mk, vl, vr, taps, dkt, dg2, gains, *((t_ud,) if ring else ()))


def adam_into(grad, at_in, at_out, rate):
    w, m, v = at_in
    moment = BETA_ONE * m[...] + (1.0 - BETA_ONE) * grad
    second = BETA_TWO * v[...] + (1.0 - BETA_TWO) * grad * grad
    first_hat = moment * (1.0 / (1.0 - BETA_ONE**STEP))
    second_hat = second * (1.0 / (1.0 - BETA_TWO**STEP))
    at_out[0][...] = w[...] - rate * (first_hat / (jnp.sqrt(second_hat) + ADAM_EPS) + DECAY_RATE * w[...])
    at_out[1][...] = moment
    at_out[2][...] = second


def adam_kernel(*refs):
    take = Refs(refs)
    r_qkv, r_uo, r_down = take(3)
    attn, up, down = take(3), take(3), take(3)
    attn_n, up_n, down_n = take(3), take(3), take(3)
    for i in range(4):
        grad = r_qkv[i] if i < 3 else r_uo[PARTS]
        adam_into(grad, [r.at[i] for r in attn], [r.at[i] for r in attn_n], LEARN_RATE)
    rows_chip = r_down.shape[1]
    wide = PARTS * rows_chip
    for c in range(0, up[0].shape[1], 2 * wide):
        got = [r_uo[p, :, (c + h * wide) // PARTS : (c + h * wide) // PARTS + rows_chip] for h in range(2) for p in range(PARTS)]
        cols = slice(c, c + 2 * wide)
        adam_into(jnp.concatenate(got, axis=1), [r.at[:, cols] for r in up], [r.at[:, cols] for r in up_n], LEARN_RATE)
    for j in range(2):
        rows_j = slice(j * rows_chip, (j + 1) * rows_chip)
        adam_into(r_down[j], [r.at[rows_j, :] for r in down], [r.at[rows_j, :] for r in down_n], LEARN_RATE)


def adam_all(r_qkv, r_uo, r_down, state):
    return pl.pallas_call(
        adam_kernel,
        in_specs=[VM] * 12,
        out_specs=[VM] * 9,
        out_shape=[sds(x.shape, F32) for x in state],
        compiler_params=pltpu.CompilerParams(vmem_limit_bytes=VMEM_LIMIT),
        name="adam_all",
    )(r_qkv, r_uo, r_down, *state)


def adam_step(weight, grad_vec, moment, second, rate_value):
    moment_new = BETA_ONE * moment + (1.0 - BETA_ONE) * grad_vec
    second_new = BETA_TWO * second + (1.0 - BETA_TWO) * grad_vec * grad_vec
    first_hat = moment_new / (1.0 - BETA_ONE**STEP)
    second_hat = second_new / (1.0 - BETA_TWO**STEP)
    weight_new = weight - rate_value * (
        first_hat / (jnp.sqrt(second_hat) + ADAM_EPS) + DECAY_RATE * weight
    )
    return (weight_new, moment_new, second_new)


def per_device(tokens, cotangent, attn_w, w_up, w_down, vectors, attn_m, attn_v, up_m, up_v, down_m, down_v, vec_m, vec_v):
    both = ("seq", "rep")
    x = tokens[0]
    dy = cotangent[0]
    t, d = x.shape
    n = lax.axis_size("seq")
    seg_len = t * n // M
    ring = n == CHIPS and lax.axis_size("rep") == 2

    rown = d // n
    if ring:
        weights = (attn_w, w_up, w_down.reshape(2, rown, d), vectors)
    else:
        w_attn = lax.all_gather(attn_w.astype(BF16), both, axis=1, tiled=True)
        vec = lax.all_gather(vectors.astype(BF16), both, axis=0, tiled=True).astype(F32)
        weights = (w_attn[:3], jnp.pad(vec, ((0, 0), (0, 128 - vec.shape[1]))))
    (w_qkv, wo, ud, ud_own, gains, taps, h1, q, k, v, conv, f, e, mq, mk, uz, a, z, az, t2, t3, vl, vr, pinverse) = front(
        x, weights, n, ring
    )
    if not ring:
        w_qkv, wo = w_attn[:3], w_attn[3]
        up = lax.all_gather(w_up.astype(BF16), both, axis=0, tiled=True)
        down = lax.all_gather(w_down.astype(BF16), both, axis=0, tiled=True)
        ud = jnp.stack([jnp.transpose(up.reshape(d, PARTS, d), (1, 0, 2)), down.reshape(PARTS, d, d)], axis=1)
    else:
        ud = ud[None]
    res = middle(x, dy, f, q, conv, wo, ud, ud_own, gains, mk, uz, pinverse, padded_rows(6 * M, n), n)
    out, dx, dmix, dqf, g_last, gw, dkt, dg2 = res[:8]
    res = rear(
        (v, dmix, e, k, dqf),
        (x, dx, h1, w_qkv),
        (g_last,) if ring else None,
        gw, uz, a, z, az, t2, t3, mq, mk, vl, vr, taps, dkt, dg2, gains,
        res[8] if ring else None,
        n, seg_len,
    )
    ig, g_vec, g_qkv, dg = res[:4]
    dg1 = (dg[0] + dg[1])[: d // 128].reshape(d)
    if ring:
        r_uo, r_down, red_vec, r_qkv = res[4:]
        own = d // (2 * n)
        start = (lax.axis_index("seq") * 2 + lax.axis_index("rep")) * own
        dg1_own = lax.dynamic_slice_in_dim(dg1, start, own, 0)
        red_vec = jnp.concatenate([dg1_own[:, None], red_vec[:, 1 : vectors.shape[1]]], axis=1)
        state = (attn_w, attn_m, attn_v, w_up, up_m, up_v, w_down, down_m, down_v)
        news = adam_all(r_qkv, r_uo, r_down, state)
    else:
        g_attn = jnp.concatenate([g_qkv, g_last[2 * PARTS :]], axis=0)
        g_pairs = g_last[: 2 * PARTS].reshape(PARTS, 2, d, d)
        g_up = jnp.transpose(g_pairs[:, 0], (1, 0, 2)).reshape(d, PARTS * d)
        g_down = g_pairs[:, 1].reshape(PARTS * d, d)
        red_attn = lax.psum_scatter(g_attn, both, scatter_dimension=1, tiled=True).astype(F32)
        red_up = lax.psum_scatter(g_up, both, scatter_dimension=0, tiled=True).astype(F32)
        red_down = lax.psum_scatter(g_down, both, scatter_dimension=0, tiled=True).astype(F32)
        g_vec = jnp.concatenate([dg1[:, None] / n, g_vec[:, 1 : vectors.shape[1]]], axis=1)
        red_vec = lax.psum_scatter(g_vec, both, scatter_dimension=0, tiled=True)
        news = (
            *adam_step(attn_w, red_attn, attn_m, attn_v, LEARN_RATE),
            *adam_step(w_up, red_up, up_m, up_v, LEARN_RATE),
            *adam_step(w_down, red_down, down_m, down_v, LEARN_RATE),
        )
    return (out[None], ig[None], *news, *adam_step(vectors, red_vec, vec_m, vec_v, VECTOR_RATE))


def solution(mesh):
    tok = P("rep", "seq", None)
    att = P(None, ("seq", "rep"), None)
    mat = P(("seq", "rep"), None)
    return jax.shard_map(
        per_device,
        mesh=mesh,
        in_specs=(tok, tok, att, mat, mat, mat, att, att, mat, mat, mat, mat, mat, mat),
        out_specs=(tok, tok, att, att, att) + (mat,) * 9,
        check_vma=False,
    )
```
